32 devices in a mesh: pipe: 2 (over x), dp: 4 (over z), tensor: 4 (over y, core).
Axes of the slice: x: 2, y: 2, z: 4, core: 2. Of those that a mesh axis runs over, the one named last changes fastest.
Arguments:
- layer_inputs: bfloat16 [2, 480, 8, 768], P('pipe', 'tensor', 'dp'), may hold values from -6 to 6
- segment_ids: int32 [2, 8, 480], P(None, 'dp'), may hold values from 0 to 23, never falling along the last dimension, each value on 1 to 40 neighbouring positions
- slot_ids: int32 [480, 8], P('tensor', 'dp'), may hold values from 0 to 4095
- memory_table: bfloat16 [4096, 768], replicated, may hold values from -6 to 6
- buckets: int32 [960], replicated, may hold values from 0 to 31, as said below
- self_qkv: bfloat16 [2, 768, 3, 768], P('pipe', 'dp', None, 'tensor'), may hold values from -0.21875 to 0.21875
- self_out: bfloat16 [2, 768, 768], P('pipe', 'tensor', 'dp'), may hold values from -0.875 to 0.875
- source_kv: bfloat16 [2, 768, 2, 768], P('pipe', 'dp', None, 'tensor'), may hold values from -0.21875 to 0.21875
- ff_in: bfloat16 [2, 768, 3072], P('pipe', 'dp', 'tensor'), may hold values from -0.21875 to 0.21875
- ff_out: bfloat16 [2, 3072, 768], P('pipe', 'tensor', 'dp'), may hold values from -0.109375 to 0.109375
- rel_bias: bfloat16 [2, 32, 12], P('pipe', 'dp', 'tensor'), may hold values from -4 to 4
- gains: bfloat16 [2, 3, 768], P('pipe', None, 'dp'), may hold values from 0.5 to 1.5
- cross_query: bfloat16 [768, 768], P(('pipe', 'dp'), 'tensor'), may hold values from -0.21875 to 0.21875
- cross_out: bfloat16 [768, 768], P('tensor', ('pipe', 'dp')), may hold values from -0.875 to 0.875
- cross_gain: bfloat16 [768], P(('pipe', 'dp')), may hold values from 0.5 to 1.5
- cotangents: bfloat16 [2, 480, 8, 768], P('pipe', 'tensor', 'dp'), may hold values from -6 to 6
Outputs:
- section_outputs: bfloat16 [2, 480, 8, 768], P('pipe', 'tensor', 'dp')
- input_grads: float32 [2, 480, 8, 768], P('pipe', 'tensor', 'dp')
- grad_self_qkv: float32 [2, 768, 3, 768], P('pipe', 'dp', None, 'tensor')
- grad_self_out: float32 [2, 768, 768], P('pipe', 'tensor', 'dp')
- grad_source_kv: float32 [2, 768, 2, 768], P('pipe', 'dp', None, 'tensor')
- grad_ff_in: float32 [2, 768, 3072], P('pipe', 'dp', 'tensor')
- grad_ff_out: float32 [2, 3072, 768], P('pipe', 'tensor', 'dp')
- grad_rel_bias: float32 [2, 32, 12], P('pipe', 'dp', 'tensor')
- grad_gains: float32 [2, 3, 768], P('pipe', None, 'dp')
- grad_cross_query: float32 [768, 768], P(('pipe', 'dp'), 'tensor')
- grad_cross_out: float32 [768, 768], P('tensor', ('pipe', 'dp'))
- grad_cross_gain: float32 [768], P(('pipe', 'dp'))
The draws below stay inside these ranges and needn't reach their ends.
Inputs may be any that keep to these rules, and one draw needn't show every extreme that they name: Entry o + 480 is the bucket of the offset o (key position minus query position) for -480 < o < 480; entry 0 is not read. Offsets below zero take buckets under 32/2, the others 32/2 and up; the bucket never falls as |o| grows.
All inputs are finite; a program needn't handle non-finite values.
Results may differ from the reference program's by a relative error of at most 0.025.
Values may be sent and summed in bfloat16 or wider, within the bound.
A program may use at most 192 MiB of HBM per device.

```python
import math
import jax
import jax.numpy as jnp
import numpy as np
from jax import lax

D = 768
HEADS = 12
HD = 64
FF = 3072
NB = 32
MEM = 20
QPR = 24
TABLE = 4096
ROW = 480
ROWS = 8


def bucket_side(key, half):
    increments = jax.random.randint(key, (ROW,), 0, 2)
    increments = increments.at[0].set(0).at[ROW - 1].set(half)
    return jnp.minimum(jnp.cumsum(increments), half - 1).astype(jnp.int32)


def draw_buckets(key, part):
    key = jax.random.fold_in(key, 5)
    half = NB // 2
    ahead_key, behind_key = jax.random.split(key)
    ahead = half + bucket_side(ahead_key, half)
    behind = bucket_side(behind_key, half)
    return jnp.concatenate([jnp.zeros((1,), jnp.int32), behind[1:][::-1], ahead]).astype(jnp.int32)


def set_ends(result, stream_key, low, largest):
    spot = [jax.random.randint(jax.random.fold_in(stream_key, axis), (), 0, length) for axis, length in enumerate(result.shape)]
    main_axis = result.shape.index(max(result.shape))
    next_to = spot[:main_axis] + [(spot[main_axis] + 1) % result.shape[main_axis]] + spot[main_axis + 1:]
    return result.at[tuple(spot)].set(low).at[tuple(next_to)].set(largest)


def raised(result, own_key, source, target, blocks, factor):
    owner, partner = [(jnp.arange(result.shape[dim]) // (result.shape[dim] // blocks)).reshape([-1 if axis == dim else 1 for axis in range(result.ndim)]) for dim in (source, target)]
    chosen = jax.random.permutation(own_key, blocks)[partner]
    strong = (owner == chosen) | (owner == (partner + blocks // 2) % blocks)
    return jnp.where(strong, factor * result, result)


def block_levels(stream_key, extent, pieces, least, largest):
    def one(axis_at, shards_of):
        heights = jax.random.uniform(jax.random.fold_in(jax.random.fold_in(stream_key, 6), axis_at), (shards_of,), jnp.float32, least / len(pieces), largest / len(pieces))
        return jnp.repeat(jnp.exp(heights), extent[axis_at] // shards_of).reshape((-1,) + (1,) * (len(extent) - axis_at - 1))

    level = one(*pieces[0])
    for cut in pieces[1:]:
        level = level * one(*cut)
    return level


def profile(number_of, total, limit, lean):
    loads = [(1 << 20) // math.isqrt(rank ** lean) + 1 for rank in range(2, number_of + 1)]
    rest, given = total - limit - (number_of - 1), [1] * (number_of - 1)
    while rest > 0:
        free = [i for i in range(number_of - 1) if given[i] < limit]
        mass, left = sum([loads[i] for i in free]), rest
        for i in free:
            extra = min(limit - given[i], max(1, left * loads[i] // mass), rest)
            given[i] = given[i] + extra
            rest = rest - extra
    return np.array([limit] + given)


def ragged_sizes(own_key, count, total, bound, lean):
    if count == 2:
        one = jax.random.randint(own_key, (), max(1, total - bound), min(bound, total - 1) + 1)
        return jnp.stack([one, total - one])
    sizes = jnp.asarray(profile(count, total, bound, lean), jnp.int32)
    couples = (count - 1) // 2
    source_of, receiver = sizes[1:1 + 2 * couples:2], sizes[2:2 + 2 * couples:2]
    margin = jnp.minimum(source_of - 1, bound - receiver)
    moved = jax.random.randint(jax.random.fold_in(own_key, 1), (couples,), 0, 1 << 20) % (margin + 1)
    sizes = sizes.at[1:1 + 2 * couples:2].set(source_of - moved).at[2:2 + 2 * couples:2].set(receiver + moved)
    return sizes[jax.random.permutation(jax.random.fold_in(own_key, 2), count)]


def gaussian(stream_key, shape, scale, most, cuts=(), kind=jnp.bfloat16):
    drawn = jax.random.normal(stream_key, shape, jnp.float32) * scale
    if len(cuts) > 0:
        drawn = block_levels(stream_key, shape, cuts, -0.22, 0.18) * drawn
    return jnp.clip(drawn, min=-most, max=most).astype(kind)


def bell_draw_with(rng, extent, spread, limit, pieces, heavy, kind=jnp.bfloat16):
    drawn = spread * jax.random.normal(rng, extent, jnp.float32)
    if pieces:
        drawn = drawn * block_levels(rng, extent, pieces, -0.22, 0.18)
    return jnp.clip(raised(drawn, jax.random.fold_in(rng, 3), *heavy), -limit, limit).astype(kind)


def setup_inputs(seed: int = 0) -> dict:
    seeds = jax.random.split(jax.random.key(seed), 17)
    layer_inputs = gaussian(seeds[0], (2, ROW, ROWS, D), 1.0, 6.0, ((0, 2), (1, 4), (2, 4)))
    segment_ids = jax.vmap(lambda own: jnp.searchsorted(jnp.cumsum(ragged_sizes(own, QPR, ROW, 2 * MEM, 1)), jnp.arange(ROW), side="right"))(jax.random.split(seeds[1], 2 * ROWS)).reshape((2, ROWS, ROW)).astype(jnp.int32)
    slot_ids = set_ends(jax.random.randint(seeds[2], (ROW, ROWS), 0, TABLE), jax.random.fold_in(seeds[2], 1), 0, TABLE - 1).astype(jnp.int32)
    memory_table = gaussian(seeds[3], (TABLE, D), 1.0, 6.0)
    buckets = draw_buckets(jax.random.fold_in(seeds[16], 71), 0)
    self_qkv = gaussian(seeds[5], (2, D, 3, D), D ** -0.5, 0.21875, ((0, 2), (1, 4), (3, 4)))
    self_out = gaussian(seeds[6], (2, D, D), (D // 16) ** -0.5, 0.875, ((0, 2), (1, 4), (2, 4)))
    source_kv = gaussian(seeds[7], (2, D, 2, D), D ** -0.5, 0.21875, ((0, 2), (1, 4), (3, 4)))
    ff_in = gaussian(seeds[8], (2, D, FF), D ** -0.5, 0.21875, ((0, 2), (1, 4), (2, 4)))
    ff_out = gaussian(seeds[9], (2, FF, D), FF ** -0.5, 0.109375, ((0, 2), (1, 4), (2, 4)))
    rel_bias = gaussian(seeds[10], (2, NB, HEADS), 1.0, 4.0, ((0, 2), (1, 4), (2, 4)))
    gains = jnp.clip(1.0 + 0.1 * jax.random.normal(seeds[11], (2, 3, D), jnp.float32), 0.5, 1.5).astype(jnp.bfloat16)
    cross_query = gaussian(seeds[12], (D, D), D ** -0.5, 0.21875, ((0, 8), (1, 4)))
    cross_out = gaussian(seeds[13], (D, D), (D // 16) ** -0.5, 0.875, ((0, 4), (1, 8)))
    cross_gain = jnp.clip(1.0 + 0.1 * jax.random.normal(seeds[14], (D,), jnp.float32), 0.5, 1.5).astype(jnp.bfloat16)
    cotangents = bell_draw_with(seeds[15], (2, ROW, ROWS, D), 1.0, 6.0, ((0, 2), (1, 4), (2, 4)), (2, 3, 4, 2.0))
    return {"layer_inputs": layer_inputs, "segment_ids": segment_ids, "slot_ids": slot_ids, "memory_table": memory_table, "buckets": buckets, "self_qkv": self_qkv, "self_out": self_out, "source_kv": source_kv, "ff_in": ff_in, "ff_out": ff_out, "rel_bias": rel_bias, "gains": gains, "cross_query": cross_query, "cross_out": cross_out, "cross_gain": cross_gain, "cotangents": cotangents}


EPSILON = 1e-06
HIGHEST = lax.Precision.HIGHEST

@jax.custom_vjp
def low(v):
    return lax.optimization_barrier(v.astype(jnp.bfloat16)).astype(jnp.float32)

@jax.custom_vjp
def low_back(v):
    return v

def low_keep(v):
    return (low(v), None)

def low_pass(kept, grad):
    return (grad,)

def back_keep(v):
    return (v, None)

def back_low(kept, grad):
    return (low(grad),)
low.defvjp(low_keep, low_pass)
low_back.defvjp(back_keep, back_low)

def rounded(value):
    return low(low_back(value))

def norm_apply(values, gain):
    return values * lax.rsqrt(lax.optimization_barrier(jnp.mean(values * values, axis=-1, keepdims=True)) + EPSILON) * gain

def offset_index(first_row, row_count, seq_width):
    query_pos = first_row + jnp.arange(row_count, dtype=jnp.int32)[:, None]
    key_pos = jnp.arange(seq_width, dtype=jnp.int32)[None, :]
    return key_pos - query_pos + seq_width

def matmul(left, right):
    return jnp.dot(left, right, precision=HIGHEST, preferred_element_type=jnp.float32)

def attention(queries, key_rows, values, offset_bias, allowed):
    seq_width = queries.shape[0]
    key_len = key_rows.shape[0]
    half = seq_width // 2
    scale = queries.shape[2] ** (-0.5)
    blocks = queries.reshape(2, half, queries.shape[1], queries.shape[2])
    firsts = jnp.arange(2, dtype=jnp.int32) * half

    def one_block(args):
        query_blk, first_row = args
        scores = jnp.einsum('qhd,khd->hqk', query_blk, key_rows, precision=HIGHEST) * scale
        if offset_bias is not None:
            own_part = offset_bias[:, offset_index(first_row, half, seq_width)]
            lead_part = jnp.zeros((own_part.shape[0], half, key_len - seq_width), jnp.float32)
            scores = scores + jnp.concatenate([lead_part, own_part], -1)
        scores = low_back(jnp.where(allowed(first_row, half)[None], scores, -1000000000.0))
        weights = low(jax.nn.softmax(scores, axis=-1))
        return jnp.einsum('hqk,khd->qhd', weights, values, precision=HIGHEST)
    results = lax.map(jax.checkpoint(one_block), (blocks, firsts))
    return rounded(results.reshape(seq_width, -1))

def feed_forward(values, w_in, w_ffo, gain):
    normed_c = low(norm_apply(values, gain))
    hidden = low(jax.nn.gelu(low_back(matmul(normed_c, w_in))))
    return values + low_back(matmul(hidden, w_ffo))

def source_pairs(source, w_kv, gain, head_count):
    width = source.shape[1]
    normed_src = low(norm_apply(source, gain))
    return rounded(matmul(normed_src, w_kv.reshape(width, -1))).reshape(-1, 2, head_count, HD)

def encoder_layer(inputs, source, weights, offset_bias, allow_self):
    w_qkv, w_out, w_kv, w_in, w_ffo, gain = weights
    width = inputs.shape[1]
    head_count = width // HD
    normed_a = low(norm_apply(inputs, gain[0]))
    qkv = rounded(matmul(normed_a, w_qkv.reshape(width, -1))).reshape(-1, 3, head_count, HD)
    kv_src = source_pairs(source, w_kv, gain[2], head_count)
    key_rows = jnp.concatenate([kv_src[:, 0], qkv[:, 1]], 0)
    value_rows = jnp.concatenate([kv_src[:, 1], qkv[:, 2]], 0)
    mixed_a = attention(qkv[:, 0], key_rows, value_rows, offset_bias, allow_self)
    x_mid = inputs + low_back(matmul(mixed_a, w_out))
    return feed_forward(x_mid, w_in, w_ffo, gain[1])

def decoder_layer(inputs, source, weights, offset_bias, allow_self, allow_cross):
    w_qkv, w_out, w_kv, w_in, w_ffo, gain, w_query, w_cross, gain_cross = weights
    width = inputs.shape[1]
    head_count = width // HD
    normed_a = low(norm_apply(inputs, gain[0]))
    qkv = rounded(matmul(normed_a, w_qkv.reshape(width, -1))).reshape(-1, 3, head_count, HD)
    mixed_a = attention(qkv[:, 0], qkv[:, 1], qkv[:, 2], offset_bias, allow_self)
    x_mid = inputs + low_back(matmul(mixed_a, w_out))
    normed_b = low(norm_apply(x_mid, gain_cross))
    query_b = rounded(matmul(normed_b, w_query)).reshape(-1, head_count, HD)
    kv_src = source_pairs(source, w_kv, gain[2], head_count)
    mixed_b = attention(query_b, kv_src[:, 0], kv_src[:, 1], None, allow_cross)
    x_late = x_mid + low_back(matmul(mixed_b, w_cross))
    return feed_forward(x_late, w_in, w_ffo, gain[1])

def reference(layer_inputs, segment_ids, slot_ids, memory_table, buckets, self_qkv, self_out, source_kv, ff_in, ff_out, rel_bias, gains, cross_query, cross_out, cross_gain, cotangents):
    params = tuple((member.astype(jnp.float32) for member in (self_qkv, self_out, source_kv, ff_in, ff_out, rel_bias, gains, cross_query, cross_out, cross_gain)))
    inputs = layer_inputs.astype(jnp.float32)
    memory = memory_table.astype(jnp.float32)
    bucket_hot = (buckets[:, None] == jnp.arange(NB, dtype=jnp.int32)[None, :]).astype(jnp.float32)
    positions = jnp.arange(ROW, dtype=jnp.int32)
    memory_seg = positions // MEM

    def forward(params, inputs):
        w_qkv, w_out, w_kv, w_in, w_ffo, rel, gain, w_query, w_cross, gain_cross = params

        def per_row(carry, row_no):
            seg_enc = segment_ids[0, row_no]
            seg_dec = segment_ids[1, row_no]
            enc_bias = matmul(bucket_hot, rel[0]).T
            dec_bias = matmul(bucket_hot, rel[1]).T

            def allow_enc(first_row, row_count):
                rows_seg = lax.dynamic_slice_in_dim(seg_enc, first_row, row_count)
                return jnp.concatenate([rows_seg[:, None] == memory_seg[None, :], rows_seg[:, None] == seg_enc[None, :]], 1)

            def allow_dec(first_row, row_count):
                rows_seg = lax.dynamic_slice_in_dim(seg_dec, first_row, row_count)
                query_pos = first_row + jnp.arange(row_count, dtype=jnp.int32)
                return (rows_seg[:, None] == seg_dec[None, :]) & (positions[None, :] <= query_pos[:, None])

            def allow_src(first_row, row_count):
                rows_seg = lax.dynamic_slice_in_dim(seg_dec, first_row, row_count)
                return rows_seg[:, None] == seg_enc[None, :]
            source = memory[slot_ids[:, row_no].astype(jnp.int32)]
            enc_out = encoder_layer(inputs[0, :, row_no], source, (w_qkv[0], w_out[0], w_kv[0], w_in[0], w_ffo[0], gain[0]), enc_bias, allow_enc)
            dec_out = decoder_layer(inputs[1, :, row_no], rounded(enc_out), (w_qkv[1], w_out[1], w_kv[1], w_in[1], w_ffo[1], gain[1], w_query, w_cross, gain_cross), dec_bias, allow_dec, allow_src)
            return (carry, (enc_out, dec_out))
        _, (enc_all, dec_all) = lax.scan(jax.checkpoint(per_row), jnp.zeros((), jnp.float32), jnp.arange(ROWS, dtype=jnp.int32))
        return jnp.stack([enc_all, dec_all]).transpose(0, 2, 1, 3)
    outputs, pullback = jax.vjp(forward, params, inputs)
    grad_params, grad_inputs = pullback(cotangents.astype(jnp.float32))
    return (outputs.astype(jnp.bfloat16), grad_inputs, grad_params[0], grad_params[1], grad_params[2], grad_params[3], grad_params[4], grad_params[5], grad_params[6], grad_params[7], grad_params[8], grad_params[9])
```

```python
import functools

import jax
import jax.numpy as jnp
from jax import lax
from jax.experimental import pallas as pl
from jax.experimental.pallas import tpu as pltpu
from jax.sharding import PartitionSpec as P

HD = 64
NB = 32
MEM = 20
HALO = 48
EXT = 128
REL_AT = 8
EPSILON = 1e-06
NEG = -1000000000.0
BF = jnp.bfloat16
F32 = jnp.float32
MESH = pl.DeviceIdType.MESH
CW = 256
RT = 48


def dot(a, b):
    return lax.dot_general(a, b, (((1,), (0,)), ((), ())), preferred_element_type=F32)


def dot_nt(a, b):
    return lax.dot_general(a, b, (((1,), (1,)), ((), ())), preferred_element_type=F32)


def dot_tn(a, b):
    return lax.dot_general(a, b, (((0,), (0,)), ((), ())), preferred_element_type=F32)


class Refs:
    pass


def kernel(dims, names, *refs):
    L, D, hs, fs, nz, qb_rows, win_w = dims
    hc, fc = 2 * hs, 2 * fs
    at_o, at_kv, at_ext = 3 * hs, 4 * hs, 6 * hs
    chunk_rows = D // nz
    cross_rows = chunk_rows // 2
    n_blk = L // qb_rows
    n_pair = hc // 128
    n_cw = D // CW
    o = Refs()
    for name, ref in zip(names, refs, strict=True):
        setattr(o, name, ref)
    p = lax.axis_index("pipe")
    d = lax.axis_index("dp")
    t = lax.axis_index("tensor")
    enc, dec = p == 0, p == 1
    core = lax.rem(t, 2)
    y = t // 2
    sibling = (p, d, t + 1 - 2 * core)
    across = (1 - p, d, t)
    beside = (p, d, lax.rem(t + 2, 4))
    half = L // 2
    held = L // 4
    A, B, C, X = range(4)
    shard = (o.sa, o.sb, o.sc, o.sx)
    W = (o.wa, o.wb, o.wc, o.wx)
    RY = (o.ya, o.yb, o.yc, o.yx)
    RZ = (o.za, o.zb, o.zc, o.zx)
    place = (
        [(o.oa, o.xmid, chunk_rows, 0, fs), (o.oa, o.xlate, chunk_rows, fs, 6 * hs + EXT - fs)],
        [(o.ob, o.xlate, 0, 0, fs)],
        [(o.oc, o.xmid, 0, 0, fs)],
    )
    ROWS = ((o.xs, o.xq), (o.cs, o.cq), (o.ms, o.mq))

    def chunk(k):
        return pl.ds(pl.multiple_of(k * chunk_rows, 16), chunk_rows)

    def remote(src, dst, send, recv, device):
        return pltpu.make_async_remote_copy(
            src_ref=src,
            dst_ref=dst,
            send_sem=send,
            recv_sem=recv,
            device_id=device,
            device_id_type=MESH,
        )


    def ag_right(g, k):
        slot = W[g].at[y, chunk(k)]
        return remote(slot, slot, o.gr.at[g, k], o.gz.at[g, k], (p, d + 1, t))

    def ag_left(g, k):
        slot = W[g].at[y, chunk(k)]
        return remote(slot, slot, o.gl.at[g, k], o.gz.at[g, k], (p, d - 1, t))

    def ag_beside(g, k):
        slot = W[g].at[y, chunk(k)]
        return remote(slot, slot, o.gs.at[g, k], o.gy.at[g, k], beside)

    def ag_came(g, k):
        slot = W[g].at[y, chunk(k)]
        remote(slot, slot, o.gr.at[g, k], o.gz.at[g, k], beside).wait_recv()

    def ag_each(g, h, act):
        if h == 0:
            act(d, d + 1 < nz, d > 0, True)
        else:
            act(d - h, d + 1 < nz, False, d - h >= 0)
            act(d + h, False, d > 0, d + h < nz)

    def when(cond, fn):
        if cond is True:
            fn()
        elif cond is not False:
            pl.when(cond)(fn)

    def ag_hop(g, h):
        if h >= nz:
            return

        def act(k, right, left, here):
            def go():
                if h > 0:
                    ag_came(g, k)
                if nz > 1:
                    when(right, lambda: ag_right(g, k).start())
                    when(left, lambda: ag_left(g, k).start())
                ag_beside(g, k).start()

            when(here, go)

        ag_each(g, h, act)

    def ag_wait(g):
        for k in range(nz):
            slot = W[g].at[1 - y, chunk(k)]
            remote(slot, slot, o.gs.at[g, k], o.gy.at[g, k], beside).wait_recv()

    def ag_finish(g):
        for h in range(nz):

            def act(k, right, left, here):
                def go():
                    if nz > 1:
                        when(right, lambda: ag_right(g, k).wait_send())
                        when(left, lambda: ag_left(g, k).wait_send())
                    ag_beside(g, k).wait_send()

                when(here, go)

            ag_each(g, h, act)

    def own_copy(g):
        return pltpu.make_async_copy(shard[g], W[g].at[y, chunk(d)], o.oc_sem.at[g])

    def cross_part(k, part):
        start = k * chunk_rows + part * cross_rows
        return pl.ds(pl.multiple_of(start, 16), cross_rows)

    cross_own = pltpu.make_async_copy(o.sx, W[X].at[y, cross_part(d, 1)], o.oc_sem.at[X])
    cross_in = remote(
        o.sx, W[X].at[y, cross_part(d, 0)], o.xw.at[0], o.xw.at[1], across
    )
    cross_out = remote(o.xo, o.xi, o.xw.at[2], o.xw.at[3], across)


    def rs_y(g, k):
        return remote(
            W[g].at[1 - y, chunk(k)], RY[g].at[chunk(k)], o.rs_s.at[g, k], o.rs_r.at[g, k], beside
        )

    def rs_z(g, k):
        away = lax.rem(d + nz - 1 - k, nz)
        return remote(
            RY[g].at[chunk(k)], RZ[g].at[away], o.rz_s.at[g, k], o.rz_r.at[g, away], (p, k, t)
        )

    def rs_z_came(g, i):
        remote(
            RY[g].at[chunk(d)], RZ[g].at[i], o.rz_s.at[g, d], o.rz_r.at[g, i], beside
        ).wait_recv()

    def rs_start(g):
        for i in range(nz):
            rs_y(g, lax.rem(d + 1 + i, nz)).start()

    def rs_mid(g):
        for i in range(nz):
            k = lax.rem(d + 1 + i, nz)
            rs_y(g, k).wait_recv()
            start = pl.multiple_of(k * chunk_rows, 16)

            @pl.loop(0, chunk_rows // 32)
            def _(r):
                rows = pl.ds(pl.multiple_of(start + r * 32, 16), 32)
                both = W[g][y, rows, :].astype(F32) + RY[g][rows, :].astype(F32)
                RY[g][rows, :] = both.astype(BF)

            if i < nz - 1:
                rs_z(g, k).start()

    def rs_end(g, put):
        for i in range(nz - 1):
            rs_z_came(g, i)
        start = pl.multiple_of(d * chunk_rows, 16)

        @pl.loop(0, chunk_rows // 32)
        def _(r):
            rows = pl.ds(pl.multiple_of(r * 32, 16), 32)
            total = RY[g][pl.ds(pl.multiple_of(start + r * 32, 16), 32), :].astype(F32)
            for i in range(nz - 1):
                total = total + RZ[g][i, rows, :].astype(F32)
            put(rows, total)

    def rs_sent(g):
        for i in range(nz):
            k = lax.rem(d + 1 + i, nz)
            rs_y(g, k).wait_send()
            if i < nz - 1:
                rs_z(g, k).wait_send()

    def rs_copies(g):
        return [
            pltpu.make_async_copy(
                buffer.at[pl.ds(first, chunk_rows), pl.ds(0, width)],
                out.at[:, pl.ds(at, width)],
                o.lc.at[g + 3 * i],
            )
            for i, (out, buffer, first, at, width) in enumerate(place[g])
        ]

    def rs_out(g):
        if nz == 1:
            start = 0

            @pl.loop(0, chunk_rows // 32)
            def _(r):
                rows = pl.ds(pl.multiple_of(r * 32, 16), 32)
                (o.oa, o.ob, o.oc)[g][rows, :] = RY[g][rows, :]

        else:

            def put(rows, total):
                for out, buffer, first, at, width in place[g]:
                    into = pl.ds(pl.multiple_of(rows.start + first, 16), 32)
                    buffer[into, :width] = total[:, at : at + width]

            rs_end(g, put)
            for copy in rs_copies(g):
                copy.start()
        rs_sent(g)


    def rows_sib(i, k, n):
        own, landing = ROWS[i]
        src = own.at[y] if n == 0 else landing.at[k]
        return remote(src, landing.at[k], o.qs.at[i, n], o.qr.at[i, n], sibling)

    def rows_beside(i, k):
        own, landing = ROWS[i]
        return remote(own.at[1 - y], landing.at[k], o.qs.at[i, 2], o.qr.at[i, 2], beside)

    def rows_own(i):
        own, landing = ROWS[i]
        return pltpu.make_async_copy(own.at[y], landing.at[t], o.ql.at[i])

    def rows_start(i):
        rows_own(i).start()
        rows_beside(i, t).start()
        rows_sib(i, t, 0).start()

    other = lax.rem(t + 2, 4)

    def rows_pass(i):
        rows_beside(i, other).wait_recv()
        rows_sib(i, other, 1).start()

    def rows_done(i):
        rows_own(i).wait()
        rows_sib(i, t, 0).wait()
        rows_sib(i, other, 1).wait()
        rows_beside(i, t).wait_send()

    def rows_join(i, out_ref):
        landing = ROWS[i][1]
        for k in range(0, 4, 2):
            value = jnp.concatenate(
                [landing[k, :held].astype(F32), landing[k + 1, :held].astype(F32)], axis=0
            )
            out_ref[k * held : (k + 2) * held, :] = value.astype(out_ref.dtype)


    def home_copy(i):
        return remote(o.hs.at[i], o.hr.at[i], o.hx.at[i], o.hy.at[i], beside)

    def home_block(buffer, k):
        value = buffer[pl.ds(pl.multiple_of(k * held, 8), held), :]
        pad = o.hs.shape[1] - held
        return jnp.concatenate([value, jnp.zeros((pad, D), F32)], axis=0).astype(BF)

    def home_send(i, buffer):
        o.hs[i] = home_block(buffer, other)
        home_copy(i).start()

    home_out = (
        pltpu.make_async_copy(o.ho, o.oh.at[y], o.lh.at[0]),
        pltpu.make_async_copy(o.hr.at[0], o.oh.at[1 - y], o.lh.at[1]),
        pltpu.make_async_copy(
            o.gres.at[pl.ds(pl.multiple_of(t * held, 8), held)], o.gh.at[y], o.lh.at[2]
        ),
        pltpu.make_async_copy(o.ext.at[pl.ds(0, held)], o.gh.at[1 - y], o.lh.at[3]),
    )

    barrier = pltpu.get_barrier_semaphore()
    for g in (A, B, C):
        own_copy(g).start()
    when(dec, cross_own.start)
    for peer in (sibling, across, beside):
        pl.semaphore_signal(barrier, inc=1, device_id=peer, device_id_type=MESH)
    for i in range(1, nz):
        pl.semaphore_signal(
            barrier, inc=1, device_id=(p, lax.rem(d + i, nz), t), device_id_type=MESH
        )
    pl.semaphore_wait(barrier, 3 + nz - 1)
    rows_start(0)
    when(enc, lambda: rows_start(2))
    own_copy(A).wait()
    ag_hop(A, 0)
    when(enc, cross_in.start)
    own_copy(B).wait()
    ag_hop(B, 0)
    own_copy(C).wait()

    lane = lax.broadcasted_iota(jnp.int32, (1, 128), 1)
    lo = jnp.where(lane < 64, 1.0, 0.0).astype(BF)
    hi = jnp.where(lane < 64, 0.0, 1.0).astype(BF)

    def rows_loop(fn, step=RT):
        @pl.loop(0, L // step)
        def _(i):
            fn(pl.ds(pl.multiple_of(i * step, step), step))

    def norm_rows(x_ref, gain_no, out_ref):
        def one(rows):
            v = x_ref[rows, :].astype(F32)
            r = lax.rsqrt(jnp.mean(v * v, axis=-1, keepdims=True) + EPSILON)
            out_ref[rows, :] = (v * r * o.g[gain_no : gain_no + 1, :]).astype(BF)

        rows_loop(one)

    def exchange(slot, chunk_fn):
        copies = []
        for n in range(n_cw):
            o.exs[slot, n] = chunk_fn(n).astype(BF)
            copy = remote(
                o.exs.at[slot, n], o.exr.at[slot, n], o.ss.at[slot, n], o.rs.at[slot, n], sibling
            )
            copy.start()
            copies.append(copy)
        return copies

    def landed(copies):
        for copy in copies:
            copy.wait()

    def ex_rows(slot, rows):
        parts = [
            o.exs[slot, n, rows, :].astype(F32) + o.exr[slot, n, rows, :].astype(F32)
            for n in range(n_cw)
        ]
        return jnp.concatenate(parts, axis=1)

    def residual(slot, base_ref, put):
        def one(rows):
            put(rows, base_ref[rows, :].astype(F32) + ex_rows(slot, rows))

        rows_loop(one)

    def keep(ref):
        def put(rows, value):
            ref[rows, :] = value

        return put

    def norm_back(slot, x_ref, gain_no, put):
        o.dgacc[gain_no] = jnp.zeros((8, D), F32)

        def one(rows):
            dh = ex_rows(slot, rows)
            v = x_ref[rows, :].astype(F32)
            r = lax.rsqrt(jnp.mean(v * v, axis=-1, keepdims=True) + EPSILON)
            n = v * r
            dhg = dh * o.g[gain_no : gain_no + 1, :]
            mu = jnp.mean(dhg * n, axis=-1, keepdims=True)
            put(rows, r * (dhg - n * mu))
            o.dgacc[gain_no] += jnp.sum((dh * n).reshape(RT // 8, 8, D), axis=0)

        rows_loop(one)

    def split(a):
        return slice(a * hs, (a + 1) * hs)

    def kv_project():
        for a in range(2):
            r = dot(o.ns[...], W[A][a, :, at_kv:at_ext]).astype(BF)
            o.ks[:, split(a)] = r[:, :hs]
            o.vs[:, split(a)] = r[:, hs:]

    def pair_stack(block):
        return jnp.concatenate([block * lo, block * hi], axis=0)

    def pair_pick(stacked):
        return jnp.where(lane < 64, stacked[:qb_rows], stacked[qb_rows:])

    def attn_fwd(q_ref, mix_ref, mem, own, causal, hooks=()):
        @pl.loop(0, n_blk)
        def _(b):
            for i, hook in enumerate(hooks):
                pl.when(b == i)(hook)
            rows = pl.ds(pl.multiple_of(b * qb_rows, 16), qb_rows)
            wrows = pl.ds(pl.multiple_of(b * qb_rows, 16), win_w)
            sq = o.segq[rows, :]
            if mem:
                o.mm[...] = jnp.where(sq == o.srcseg[...], 0.0, NEG)
            if own:
                allowed = sq == o.segw[b]
                if causal:
                    qi = lax.broadcasted_iota(jnp.int32, (qb_rows, win_w), 0)
                    kj = lax.broadcasted_iota(jnp.int32, (qb_rows, win_w), 1)
                    allowed = allowed & (kj - HALO <= qi)
                o.mo[...] = jnp.where(allowed, 0.0, NEG)

            @pl.loop(0, n_pair)
            def _(j):
                cols = pl.ds(pl.multiple_of(j * 128, 128), 128)
                q2 = pair_stack(q_ref[rows, cols])
                parts = []
                if mem:
                    s = dot_nt(q2, o.ks[:, cols]).reshape(2, qb_rows, L)
                    parts.append(s + o.mm[...][None])
                if own:
                    s = dot_nt(q2, o.kp[wrows, cols]).reshape(2, qb_rows, win_w)
                    parts.append(s + o.tb[pl.ds(2 * j, 2)] + o.mo[...][None])
                top = [jnp.max(s, axis=-1, keepdims=True) for s in parts]
                top = functools.reduce(jnp.maximum, top)
                exps = [jnp.exp(s - top) for s in parts]
                total = sum(jnp.sum(e, axis=-1, keepdims=True) for e in exps)
                inv = 1.0 / total
                probs = [(e * inv).astype(BF).reshape(2 * qb_rows, -1) for e in exps]
                mixed = 0.0
                if mem:
                    o.pm[b * n_pair + j] = probs[0]
                    mixed = mixed + dot(probs[0], o.vs[:, cols])
                if own:
                    o.po[b * n_pair + j] = probs[-1]
                    mixed = mixed + dot(probs[-1], o.vp[wrows, cols])
                mix_ref[rows, cols] = pair_pick(mixed).astype(BF)

    def attn_back(q_ref, mix_ref, mem, own):
        if mem:
            o.dks[...] = jnp.zeros(o.dks.shape, F32)
            o.dvs[...] = jnp.zeros(o.dvs.shape, F32)
        if own:
            o.dkp[...] = jnp.zeros(o.dkp.shape, F32)
            o.dvp[...] = jnp.zeros(o.dvp.shape, F32)
            o.tb[...] = jnp.zeros(o.tb.shape, F32)

        @pl.loop(0, n_blk)
        def _(b):
            rows = pl.ds(pl.multiple_of(b * qb_rows, 16), qb_rows)
            wrows = pl.ds(pl.multiple_of(b * qb_rows, 16), win_w)

            @pl.loop(0, n_pair)
            def _(j):
                cols = pl.ds(pl.multiple_of(j * 128, 128), 128)
                q2 = pair_stack(q_ref[rows, cols])
                do2 = pair_stack(o.dmix[rows, cols])
                mix = mix_ref[rows, cols].astype(F32)
                delta = jnp.sum(
                    do2.astype(F32).reshape(2, qb_rows, 128) * mix[None], axis=-1, keepdims=True
                ).reshape(2 * qb_rows, 1)
                dq2 = 0.0
                if mem:
                    probs = o.pm[b * n_pair + j]
                    dp = dot_nt(do2, o.vs[:, cols])
                    ds = (probs.astype(F32) * (dp - delta)).astype(BF)
                    dq2 = dq2 + dot(ds, o.ks[:, cols])
                    o.dks[:, cols] += dot_tn(ds, q2)
                    o.dvs[:, cols] += dot_tn(probs, do2)
                if own:
                    probs = o.po[b * n_pair + j]
                    dp = dot_nt(do2, o.vp[wrows, cols])
                    ds = (probs.astype(F32) * (dp - delta)).astype(BF)
                    dq2 = dq2 + dot(ds, o.kp[wrows, cols])
                    o.dkp[wrows, cols] += dot_tn(ds, q2)
                    o.dvp[wrows, cols] += dot_tn(probs, do2)
                    o.tb[pl.ds(2 * j, 2)] += ds.astype(F32).reshape(2, qb_rows, win_w)
                o.dq[rows, cols] = (pair_pick(dq2) * (HD**-0.5)).astype(BF)

    def out_project(slot, mix_ref, weight_ref, at):
        mixed = [mix_ref[:, split(a)] for a in range(2)]
        return exchange(
            slot,
            lambda n: sum(
                dot_nt(mixed[a], weight_ref[a, n * CW : (n + 1) * CW, at : at + hs])
                for a in range(2)
            ),
        )

    def mix_grads(weight_ref, at):
        for a in range(2):
            o.dmix[:, split(a)] = dot(o.gb[...], weight_ref[a, :, at : at + hs]).astype(BF)

    fw = fs // 2

    def ff_half(n):
        a = n // 2
        return a, pl.ds(pl.multiple_of((n - 2 * a) * fw, 128), fw)

    def ff_fwd(x_ref):
        norm_rows(x_ref, 1, o.nc)
        ag_wait(B)

        @pl.loop(0, 4)
        def _(n):
            a, half_cols = ff_half(n)
            cols = pl.ds(pl.multiple_of(n * fw, 128), fw)
            o.pre[...] = dot(o.nc[...], W[B][a, :, half_cols])

            def one(rows):
                v = o.pre[rows, :]
                v2 = v * v
                th = jnp.tanh(0.7978845608028654 * v * (1.0 + 0.044715 * v2))
                cdf = 0.5 * (1.0 + th)
                slope = (0.5 * 0.7978845608028654) * v * (1.0 - th * th)
                o.hidden[rows, cols] = (v * cdf).astype(BF)
                o.gp[rows, cols] = (cdf + slope * (1.0 + (3 * 0.044715) * v2)).astype(BF)

            rows_loop(one, 32)

        ag_wait(C)
        return exchange(
            2,
            lambda n: sum(
                dot_nt(o.hidden[:, a * fs : (a + 1) * fs], W[C][a, n * CW : (n + 1) * CW, :])
                for a in range(2)
            ),
        )

    def sides():
        return (1 - y, y)

    def side_cols(a, width):
        return pl.ds(pl.multiple_of(a * width, 128), width)

    def ff_back(x_ref):
        ag_finish(B)
        ag_finish(C)

        @pl.loop(0, 4)
        def _(n):
            a, half_cols = ff_half(n)
            cols = pl.ds(pl.multiple_of(n * fw, 128), fw)
            o.gp[:, cols] = (
                dot(o.gb[...], W[C][a, :, half_cols]) * o.gp[:, cols].astype(F32)
            ).astype(BF)

        copies = exchange(
            0,
            lambda n: sum(
                dot_nt(o.gp[:, a * fs : (a + 1) * fs], W[B][a, n * CW : (n + 1) * CW, :])
                for a in range(2)
            ),
        )
        for i, a in enumerate(sides()):
            W[C][a] = dot_tn(o.gb[...], o.hidden[:, side_cols(a, fs)]).astype(BF)
            if i == 0:
                rs_start(C)
        landed(copies)

        def put(rows, dv):
            new = o.gres[rows, :] + dv
            o.gres[rows, :] = new
            o.gb[rows, :] = new.astype(BF)

        norm_back(0, x_ref, 1, put)

    def ff_weights():
        for i, a in enumerate(sides()):
            W[B][a] = dot_tn(o.nc[...], o.gp[:, side_cols(a, fs)]).astype(BF)
            if i == 0:
                rs_start(B)

    def x_part():
        return pl.ds(pl.multiple_of(core * half, 16), half)

    def x_copy(way):
        rows = x_part()
        return remote(
            o.xsend.at[rows], o.xbuf.at[rows], o.xss.at[way, 0], o.xrs.at[way, 0], across
        )

    def x_recv(way):
        x_copy(way).wait_recv()
        rows = x_part()
        copy = remote(
            o.xbuf.at[rows], o.xbuf.at[rows], o.xss.at[way, 1], o.xrs.at[way, 1], sibling
        )
        copy.start()
        copy.wait()

    def dkv_grads():
        for a in range(2):
            o.dkv[a, :, :hs] = o.dks[:, split(a)].astype(BF)
            o.dkv[a, :, hs:] = o.dvs[:, split(a)].astype(BF)
        return exchange(
            2,
            lambda n: sum(
                dot_nt(o.dkv[a], W[A][a, n * CW : (n + 1) * CW, at_kv:at_ext]) for a in range(2)
            ),
        )

    rows_pass(0)
    when(enc, lambda: rows_pass(2))
    ag_hop(A, 1)
    rows_start(1)
    ag_hop(A, 2)
    ag_hop(C, 0)
    rows_pass(1)
    ag_hop(A, 3)
    rows_done(0)
    rows_join(0, o.x)

    @pl.when(dec)
    def _():
        cross_own.wait()
        cross_in.wait_recv()
        ag_hop(X, 0)

    ag_wait(A)
    o.g[...] = W[A][0, :, at_ext:].astype(F32).T[:8]
    rel_lanes = [dot_tn(W[A][a, :, at_ext:], o.hot[...]) for a in range(2)]
    for h in range(2 * n_pair):
        a = h // (hs // HD)
        row = REL_AT + h - a * (hs // HD)
        line = rel_lanes[a][row : row + 1, :]
        o.tb[h] = pltpu.roll(
            jnp.broadcast_to(line, (qb_rows, win_w)), 0, 1, stride=1, stride_axis=0
        )
    pad = jnp.zeros((HALO, hc), BF)
    for ref in (o.kp, o.vp):
        ref[:HALO, :] = pad
        ref[HALO + L :, :] = pad
    norm_rows(o.x, 0, o.na)
    for a in range(2):
        r = dot(o.na[...], W[A][a, :, :at_o]).astype(BF)
        o.q[:, split(a)] = (r[:, :hs] * (HD**-0.5)).astype(BF)
        o.kp[HALO : HALO + L, split(a)] = r[:, hs : 2 * hs]
        o.vp[HALO : HALO + L, split(a)] = r[:, 2 * hs :]
    ag_hop(B, 1)
    hooks = (
        lambda: ag_hop(C, 1),
        lambda: ag_hop(B, 2),
        lambda: ag_hop(C, 2),
    )

    @pl.when(enc)
    def _():
        rows_done(2)
        rows_join(2, o.nb)
        norm_rows(o.nb, 2, o.ns)
        kv_project()
        attn_fwd(o.q, o.mixa, True, True, False, hooks)

    @pl.when(dec)
    def _():
        attn_fwd(o.q, o.mixa, False, True, True, hooks)
        ag_hop(X, 1)

    ag_hop(B, 3)
    copies = out_project(0, o.mixa, W[A], at_o)
    ag_hop(C, 3)
    landed(copies)
    residual(0, o.x, keep(o.xmid))

    @pl.when(enc)
    def _():
        landed(ff_fwd(o.xmid))

        def put_out(rows, value):
            o.xlate[rows, :] = value
            o.xsend[rows, :] = value.astype(BF)

        residual(2, o.xmid, put_out)
        x_copy(0).start()
        home_send(0, o.xlate)
        o.ho[...] = home_block(o.xlate, t)
        home_out[0].start()
        ag_finish(A)
        rows_done(1)
        rows_join(1, o.gres)
        x_copy(0).wait_send()
        x_recv(1)

        def one(rows):
            value = o.gres[rows, :] + o.xbuf[rows, :].astype(F32)
            o.gres[rows, :] = value
            o.gb[rows, :] = value.astype(BF)

        rows_loop(one)
        ff_back(o.xmid)
        ff_weights()

    @pl.when(dec)
    def _():
        ag_hop(X, 2)
        ag_hop(X, 3)
        ag_wait(X)
        ag_finish(X)
        for a in range(2):
            for k in range(nz):
                for part in range(2):
                    at = part * (D // 2) + k * cross_rows
                    o.xg[a, at : at + cross_rows, :] = W[X][
                        a, k * chunk_rows + part * cross_rows :, :
                    ][:cross_rows]
        o.g[3:4, :] = o.xg[0, :, 2 * hs :].astype(F32).T[:1]
        norm_rows(o.xmid, 3, o.nb)
        for a in range(2):
            r = dot(o.nb[...], o.xg[a, :, :hs]).astype(BF)
            o.qb[:, split(a)] = (r * (HD**-0.5)).astype(BF)
        x_recv(0)
        norm_rows(o.xbuf, 2, o.ns)
        kv_project()
        attn_fwd(o.qb, o.mixb, True, False, False)
        landed(out_project(1, o.mixb, o.xg, hs))
        residual(1, o.xmid, keep(o.xlate))
        landed(ff_fwd(o.xlate))
        residual(2, o.xlate, keep(o.gres))
        home_send(0, o.gres)
        o.ho[...] = home_block(o.gres, t)
        home_out[0].start()
        rows_done(1)
        rows_join(1, o.gres)
        rows_join(1, o.gb)
        ff_back(o.xlate)
        mix_grads(o.xg, hs)
        attn_back(o.qb, o.mixb, True, False)
        copies = dkv_grads()
        parts = [o.dq[:, split(a)] for a in range(2)]
        more = exchange(
            1,
            lambda n: sum(
                dot_nt(parts[a], o.xg[a, n * CW : (n + 1) * CW, :hs]) for a in range(2)
            ),
        )
        ff_weights()
        landed(copies)

        def put_source(rows, dv):
            o.xsend[rows, :] = dv.astype(BF)

        norm_back(2, o.xbuf, 2, put_source)
        x_copy(1).start()
        landed(more)

        def put_mid(rows, dv):
            new = o.gres[rows, :] + dv
            o.gres[rows, :] = new
            o.nc[rows, :] = new.astype(BF)

        norm_back(1, o.xmid, 3, put_mid)
        line = jnp.sum(o.dgacc[3], axis=0, keepdims=True)
        tall = jnp.broadcast_to(line, (EXT, D)).T.astype(BF)
        for a in range(2):
            full = jnp.concatenate(
                [
                    dot_tn(o.nb[...], parts[a]).astype(BF),
                    dot_tn(o.gb[...], o.mixb[:, split(a)]).astype(BF),
                    tall,
                ],
                axis=1,
            )
            for k in range(nz):
                for part in range(2):
                    at = part * (D // 2) + k * cross_rows
                    to = k * chunk_rows + part * cross_rows
                    W[X][a, to : to + cross_rows, :] = full[at : at + cross_rows]
        rs_start(X)
        ag_finish(A)
        rs_mid(C)
        x_copy(1).wait_send()
        o.gb[...] = o.nc[...]

    mix_grads(W[A], at_o)
    for a in range(2):
        W[A][a, :, at_o : at_o + hs] = dot_tn(o.gb[...], o.mixa[:, split(a)]).astype(BF)

    @pl.when(enc)
    def _():
        attn_back(o.q, o.mixa, True, True)
        landed(dkv_grads())

        def put_source(rows, dv):
            pass

        norm_back(2, o.nb, 2, put_source)
        rs_mid(C)

    @pl.when(dec)
    def _():
        attn_back(o.q, o.mixa, False, True)
        rs_mid(B)

    for a in range(2):
        o.dqkv[a, :, :hs] = o.dq[:, split(a)]
        o.dqkv[a, :, hs : 2 * hs] = o.dkp[HALO : HALO + L, split(a)].astype(BF)
        o.dqkv[a, :, 2 * hs :] = o.dvp[HALO : HALO + L, split(a)].astype(BF)
    copies = exchange(
        0,
        lambda n: sum(
            dot_nt(o.dqkv[a], W[A][a, n * CW : (n + 1) * CW, :at_o]) for a in range(2)
        ),
    )
    heads = 2 * n_pair
    acc = jnp.zeros((heads * 8, win_w), F32)
    for k in range(qb_rows // 8):
        part = o.tb[:, 8 * k : 8 * k + 8, :].reshape(heads * 8, win_w)
        acc = acc + (part if k == 0 else pltpu.roll(part, win_w - 8 * k, 1))
    sub = lax.rem(lax.broadcasted_iota(jnp.int32, (heads * 8, win_w), 0), 8)
    diag = jnp.zeros((heads * 8, win_w), F32)
    for k in range(8):
        turned = acc if k == 0 else pltpu.roll(acc, win_w - k, 1)
        diag = diag + jnp.where(sub == k, turned, 0.0)
    lines = jnp.sum(diag.reshape(heads, 8, win_w), axis=1)
    landed(copies)

    def put_in(rows, dv):
        o.gres[rows, :] = o.gres[rows, :] + dv

    norm_back(0, o.x, 0, put_in)
    home_send(1, o.gres)
    home_out[2].start()
    for i, a in enumerate(sides()):
        W[A][a, :, :at_o] = dot_tn(o.na[...], o.dqkv[a]).astype(BF)
        W[A][a, :, at_kv:at_ext] = dot_tn(o.ns[...], o.dkv[a]).astype(BF)
    per = hs // HD
    for a in range(2):
        o.ext[...] = jnp.zeros(o.ext.shape, F32)
        for k in range(3):
            o.ext[k : k + 1, :] = jnp.sum(o.dgacc[k], axis=0, keepdims=True)
        tall = o.ext[...].T
        o.lines[...] = jnp.zeros((EXT, win_w), F32)
        o.lines[REL_AT : REL_AT + per, :] = lines[per * a : per * (a + 1), :]
        whole = o.lines[...]
        high = whole.astype(BF)
        low = (whole - high.astype(F32)).astype(BF)
        tall = tall + dot_nt(o.hot[...], high) + dot_nt(o.hot[...], low)
        W[A][a, :, at_ext:] = tall.astype(BF)
    rs_start(A)
    home_copy(0).wait()
    home_out[1].start()

    @pl.when(enc)
    def _():
        rs_mid(B)

    rs_out(C)

    @pl.when(dec)
    def _():
        rs_mid(X)

    rs_mid(A)
    rs_out(B)

    @pl.when(dec)
    def _():
        def put(rows, total):
            o.xt[rows, :] = total

        rs_end(X, put)
        rs_sent(X)
        o.xo[...] = o.xt[:cross_rows, :]
        cross_out.start()
        o.ox[...] = o.xt[cross_rows:, :].astype(o.ox.dtype)
        cross_out.wait_send()

    @pl.when(enc)
    def _():
        cross_in.wait_send()
        cross_out.wait_recv()
        o.ox[...] = o.xi[...].astype(o.ox.dtype)

    home_copy(1).wait()
    o.ext[...] = o.hr[1].astype(F32)
    home_out[3].start()
    rs_out(A)
    for copy in home_out:
        copy.wait()
    if nz > 1:
        for g in (A, B, C):
            for copy in rs_copies(g):
                copy.wait()


def run_kernel(dims, given):
    L, D, hs, fs, nz, qb_rows, win_w = dims
    hc, fc = 2 * hs, 2 * fs
    n_blk, n_pair, n_cw = L // qb_rows, hc // 128, D // CW
    LP = L + 2 * HALO
    LBP = -(-(L // 4) // 16) * 16
    CR = D // nz
    widths = dict(a=6 * hs + EXT, b=fs, c=fs, x=2 * hs + EXT)
    S = jax.ShapeDtypeStruct
    SUM = F32 if nz > 1 else BF
    outs = dict(
        oh=S((2, LBP, D), BF),
        gh=S((2, L // 4, D), F32),
        oa=S((CR, widths["a"]), SUM),
        ob=S((CR, widths["b"]), SUM),
        oc=S((CR, widths["c"]), SUM),
        ox=S((CR // 2, widths["x"]), SUM),
    )
    V = pltpu.VMEM
    LD, LH, LF = (L, D), (L, hc), (L, fc)
    scratch = dict(
        na=V(LD, BF), ns=V(LD, BF), nb=V(LD, BF), nc=V(LD, BF),
        xmid=V(LD, F32), xlate=V(LD, F32), gres=V(LD, F32),
        q=V(LH, BF), kp=V((LP, hc), BF), vp=V((LP, hc), BF), ks=V(LH, BF), vs=V(LH, BF),
        qb=V(LH, BF), mixa=V(LH, BF), mixb=V(LH, BF),
        pm=V((n_blk * n_pair, 2 * qb_rows, L), BF), po=V((n_blk * n_pair, 2 * qb_rows, win_w), BF),
        hidden=V(LF, BF), gp=V(LF, BF), pre=V((L, fs // 2), F32),
        tb=V((2 * n_pair, qb_rows, win_w), F32),
        mm=V((qb_rows, L), F32), mo=V((qb_rows, win_w), F32),
        dmix=V(LH, BF), dq=V(LH, BF), dqkv=V((2, L, 3 * hs), BF), dkv=V((2, L, 2 * hs), BF),
        dkp=V((LP, hc), F32), dvp=V((LP, hc), F32), dks=V(LH, F32), dvs=V(LH, F32),
        gb=V(LD, BF), xbuf=V(LD, BF), xsend=V(LD, BF),
        exs=V((3, n_cw, L, CW), BF), exr=V((3, n_cw, L, CW), BF), dgacc=V((4, 8, D), F32),
        g=V((8, D), F32), ext=V((LBP, D), F32), lines=V((EXT, win_w), F32),
        x=V(LD, BF), xq=V((4, LBP, D), BF), cq=V((4, LBP, D), BF), mq=V((4, LBP, D), BF),
        hs=V((2, LBP, D), BF), hr=V((2, LBP, D), BF), ho=V((LBP, D), BF),
        xg=V((2, D, widths["x"]), BF), xt=V((CR, widths["x"]), F32),
        xo=V((CR // 2, widths["x"]), F32), xi=V((CR // 2, widths["x"]), F32),
    )
    for g, width in widths.items():
        scratch["w" + g] = V((2, D, width), BF)
        scratch["y" + g] = V((D, width), BF)
        scratch["z" + g] = V((nz - 1, CR, width) if nz > 1 else (1, 16, width), BF)
    sem = pltpu.SemaphoreType.DMA
    scratch.update(ss=sem((3, n_cw)), rs=sem((3, n_cw)), xss=sem((2, 2)), xrs=sem((2, 2)))
    scratch.update(xw=sem((4,)), oc_sem=sem((4,)), lc=sem((5,)), lh=sem((4,)))
    scratch.update(qs=sem((3, 3)), qr=sem((3, 3)), ql=sem((3,)), hx=sem((2,)), hy=sem((2,)))
    for name in ("gr", "gl", "gs", "gz", "gy", "rs_s", "rs_r", "rz_s", "rz_r"):
        scratch[name] = sem((4, nz))
    spec = pl.BlockSpec(memory_space=pltpu.VMEM)
    far = pl.BlockSpec(memory_space=pl.ANY)
    names = list(given) + list(outs) + list(scratch)
    FAR = ["sa", "sb", "sc", "sx", "xs", "cs", "ms", "oh", "gh"]
    if nz > 1:
        FAR += ["oa", "ob", "oc"]
    return pl.pallas_call(
        functools.partial(kernel, dims, names),
        out_shape=list(outs.values()),
        in_specs=[far if name in FAR else spec for name in given],
        out_specs=[far if name in FAR else spec for name in outs],
        scratch_shapes=list(scratch.values()),
        compiler_params=pltpu.CompilerParams(
            collective_id=0, has_side_effects=True, vmem_limit_bytes=63 << 20
        ),
        name="layers",
    )(*given.values())


def body(
    layer_inputs,
    segment_ids,
    slot_ids,
    memory_table,
    buckets,
    self_qkv,
    self_out,
    source_kv,
    ff_in,
    ff_out,
    rel_bias,
    gains,
    cross_query,
    cross_out,
    cross_gain,
    cotangents,
):
    section = lax.axis_index("pipe")
    t = lax.axis_index("tensor")
    nt = lax.axis_size("tensor")
    n_dp = lax.axis_size("dp")
    y = t // 2
    assert nt == 4 and layer_inputs.shape[2] == 2
    D = layer_inputs.shape[3]
    L = segment_ids.shape[2]
    hs = self_qkv.shape[3]
    fs = ff_in.shape[2]
    qb_rows, win_w = 160, 256
    rows = D // n_dp
    nz = n_dp if (rows // 2) % 32 == 0 else 1
    dims = (L, D, hs, fs, nz, qb_rows, win_w)

    held = L // nt
    fill = -(-held // 16) * 16 - held

    def by_row(block):
        return jnp.pad(block.transpose(1, 0, 2), ((0, 0), (0, fill), (0, 0)))

    xs = by_row(layer_inputs[0])
    cs = by_row(cotangents[0])
    ms = jnp.pad(memory_table[slot_ids.T], ((0, 0), (0, fill), (0, 0)))
    segs = lax.dynamic_index_in_dim(segment_ids, y, 1, keepdims=False)
    own_seg = lax.dynamic_index_in_dim(segs, section, 0, keepdims=False)
    padded = jnp.pad(own_seg, (HALO, HALO), constant_values=-1)
    segw = jnp.stack(
        [padded[b * qb_rows : b * qb_rows + win_w][None] for b in range(L // qb_rows)]
    )
    srcseg = jnp.where(section == 0, jnp.arange(L, dtype=jnp.int32) // MEM, segs[0])[None]

    heads = rel_bias.shape[2]
    nb_rows = rel_bias.shape[1]
    ext = jnp.pad(gains[0].T, ((0, 0), (0, EXT - gains.shape[1]))) + jnp.pad(
        rel_bias[0], ((0, rows - nb_rows), (REL_AT, EXT - REL_AT - heads))
    )
    shards = [
        jnp.concatenate(
            [
                self_qkv[0].reshape(rows, 3 * hs),
                self_out[0].T,
                source_kv[0].reshape(rows, 2 * hs),
                ext,
            ],
            axis=1,
        ),
        ff_in[0],
        ff_out[0].T,
        jnp.concatenate(
            [cross_query, cross_out.T, jnp.pad(cross_gain[:, None], ((0, 0), (0, EXT - 1)))],
            axis=1,
        ),
    ]
    if nz != n_dp:
        shards = [lax.all_gather(shard, "dp", axis=0, tiled=True) for shard in shards]
    window = jnp.concatenate([buckets[L - HALO : L + HALO], jnp.full((win_w - 2 * HALO,), -1)])
    place = jnp.arange(D, dtype=jnp.int32)
    bucket_at = jnp.where(place % rows < nb_rows, place // rows * nb_rows + place % rows, -2)
    hot = (window[None, :] == bucket_at[:, None]).astype(BF)

    given = dict(
        xs=xs, cs=cs, ms=ms, segq=own_seg[:, None], segw=segw, srcseg=srcseg, hot=hot,
        sa=shards[0], sb=shards[1], sc=shards[2], sx=shards[3],
    )
    oh, gh, *sums = run_kernel(dims, given)
    if nz != n_dp:
        sums = [
            lax.psum_scatter(full, "dp", scatter_dimension=0, tiled=True).astype(F32)
            for full in sums
        ]
    ga, gb, gc, gx = sums

    at_ext = 6 * hs
    return (
        oh[:, :held].transpose(1, 0, 2)[None],
        gh.transpose(1, 0, 2)[None],
        ga[:, : 3 * hs].reshape(1, rows, 3, hs),
        ga[:, 3 * hs : 4 * hs].T[None],
        ga[:, 4 * hs : at_ext].reshape(1, rows, 2, hs),
        gb[None],
        gc.T[None],
        ga[:nb_rows, at_ext + REL_AT : at_ext + REL_AT + heads][None],
        ga[:, at_ext : at_ext + gains.shape[1]].T[None],
        gx[:, :hs],
        gx[:, hs : 2 * hs].T,
        gx[:, 2 * hs],
    )


def solution(mesh):
    placed = (
        P("pipe", "tensor", "dp", None),
        P(None, "dp", None),
        P("tensor", "dp"),
        P(),
        P(),
        P("pipe", "dp", None, "tensor"),
        P("pipe", "tensor", "dp"),
        P("pipe", "dp", None, "tensor"),
        P("pipe", "dp", "tensor"),
        P("pipe", "tensor", "dp"),
        P("pipe", "dp", "tensor"),
        P("pipe", None, "dp"),
        P(("pipe", "dp"), "tensor"),
        P("tensor", ("pipe", "dp")),
        P(("pipe", "dp")),
        P("pipe", "tensor", "dp", None),
    )
    return jax.shard_map(
        body,
        mesh=mesh,
        in_specs=placed,
        out_specs=(
            P("pipe", "tensor", "dp", None),
            P("pipe", "tensor", "dp", None),
            P("pipe", "dp", None, "tensor"),
            P("pipe", "tensor", "dp"),
            P("pipe", "dp", None, "tensor"),
            P("pipe", "dp", "tensor"),
            P("pipe", "tensor", "dp"),
            P("pipe", "dp", "tensor"),
            P("pipe", None, "dp"),
            P(("pipe", "dp"), "tensor"),
            P("tensor", ("pipe", "dp")),
            P(("pipe", "dp")),
        ),
        check_vma=False,
    )
```

```python
import functools

import jax
import jax.numpy as jnp
from jax import lax
from jax.experimental import pallas as pl
from jax.experimental.pallas import tpu as pltpu
from jax.sharding import PartitionSpec as P

HD = 64
NB = 32
MEM = 20
HALO = 48
EXT = 128
REL_AT = 8
EPSILON = 1e-06
NEG = -1000000000.0
BF = jnp.bfloat16
F32 = jnp.float32
MESH = pl.DeviceIdType.MESH
CW = 256
RT = 48


def dot(a, b):
    return lax.dot_general(a, b, (((1,), (0,)), ((), ())), preferred_element_type=F32)


def dot_nt(a, b):
    return lax.dot_general(a, b, (((1,), (1,)), ((), ())), preferred_element_type=F32)


def dot_tn(a, b):
    return lax.dot_general(a, b, (((0,), (0,)), ((), ())), preferred_element_type=F32)


class Refs:
    pass


def kernel(dims, names, *refs):
    L, D, hs, fs, nz, qb_rows, win_w = dims
    hc, fc = 2 * hs, 2 * fs
    at_o, at_kv, at_ext = 3 * hs, 4 * hs, 6 * hs
    chunk_rows = D // nz
    cross_rows = chunk_rows // 2
    n_blk = L // qb_rows
    n_pair = hc // 128
    n_cw = D // CW
    o = Refs()
    for name, ref in zip(names, refs, strict=True):
        setattr(o, name, ref)
    p = lax.axis_index("pipe")
    d = lax.axis_index("dp")
    t = lax.axis_index("tensor")
    enc, dec = p == 0, p == 1
    core = lax.rem(t, 2)
    y = t // 2
    sibling = (p, d, t + 1 - 2 * core)
    across = (1 - p, d, t)
    beside = (p, d, lax.rem(t + 2, 4))
    half = L // 2
    held = L // 4
    A, B, C, X = range(4)
    shard = (o.sa, o.sb, o.sc, o.sx)
    W = (o.wa, o.wb, o.wc, o.wx)
    RY = (o.ya, o.yb, o.yc, o.yx)
    RZ = (o.za, o.zb, o.zc, o.zx)
    place = (
        [(o.oa, o.xmid, chunk_rows, 0, fs), (o.oa, o.xlate, chunk_rows, fs, 6 * hs + EXT - fs)],
        [(o.ob, o.xlate, 0, 0, fs)],
        [(o.oc, o.xmid, 0, 0, fs)],
    )
    ROWS = ((o.xs, o.xq), (o.cs, o.cq), (o.ms, o.mq))

    def chunk(k):
        return pl.ds(pl.multiple_of(k * chunk_rows, 16), chunk_rows)

    def remote(src, dst, send, recv, device):
        return pltpu.make_async_remote_copy(
            src_ref=src,
            dst_ref=dst,
            send_sem=send,
            recv_sem=recv,
            device_id=device,
            device_id_type=MESH,
        )


    def ag_right(g, k):
        slot = W[g].at[y, chunk(k)]
        return remote(slot, slot, o.gr.at[g, k], o.gz.at[g, k], (p, d + 1, t))

    def ag_left(g, k):
        slot = W[g].at[y, chunk(k)]
        return remote(slot, slot, o.gl.at[g, k], o.gz.at[g, k], (p, d - 1, t))

    def ag_beside(g, k):
        slot = W[g].at[y, chunk(k)]
        return remote(slot, slot, o.gs.at[g, k], o.gy.at[g, k], beside)

    def ag_came(g, k):
        slot = W[g].at[y, chunk(k)]
        remote(slot, slot, o.gr.at[g, k], o.gz.at[g, k], beside).wait_recv()

    def ag_each(g, h, act):
        if h == 0:
            act(d, d + 1 < nz, d > 0, True)
        else:
            act(d - h, d + 1 < nz, False, d - h >= 0)
            act(d + h, False, d > 0, d + h < nz)

    def when(cond, fn):
        if cond is True:
            fn()
        elif cond is not False:
            pl.when(cond)(fn)

    def ag_hop(g, h):
        if h >= nz:
            return

        def act(k, right, left, here):
            def go():
                if h > 0:
                    ag_came(g, k)
                if nz > 1:
                    when(right, lambda: ag_right(g, k).start())
                    when(left, lambda: ag_left(g, k).start())
                ag_beside(g, k).start()

            when(here, go)

        ag_each(g, h, act)

    def ag_wait(g):
        for k in range(nz):
            slot = W[g].at[1 - y, chunk(k)]
            remote(slot, slot, o.gs.at[g, k], o.gy.at[g, k], beside).wait_recv()

    def ag_finish(g):
        for h in range(nz):

            def act(k, right, left, here):
                def go():
                    if nz > 1:
                        when(right, lambda: ag_right(g, k).wait_send())
                        when(left, lambda: ag_left(g, k).wait_send())
                    ag_beside(g, k).wait_send()

                when(here, go)

            ag_each(g, h, act)

    def own_copy(g):
        return pltpu.make_async_copy(shard[g], W[g].at[y, chunk(d)], o.oc_sem.at[g])

    def cross_part(k, part):
        start = k * chunk_rows + part * cross_rows
        return pl.ds(pl.multiple_of(start, 16), cross_rows)

    cross_own = pltpu.make_async_copy(o.sx, W[X].at[y, cross_part(d, 1)], o.oc_sem.at[X])
    cross_in = remote(
        o.sx, W[X].at[y, cross_part(d, 0)], o.xw.at[0], o.xw.at[1], across
    )
    cross_out = remote(o.xo, o.xi, o.xw.at[2], o.xw.at[3], across)


    def rs_y(g, k):
        return remote(
            W[g].at[1 - y, chunk(k)], RY[g].at[chunk(k)], o.rs_s.at[g, k], o.rs_r.at[g, k], beside
        )

    def rs_z(g, k):
        away = lax.rem(d + nz - 1 - k, nz)
        return remote(
            RY[g].at[chunk(k)], RZ[g].at[away], o.rz_s.at[g, k], o.rz_r.at[g, away], (p, k, t)
        )

    def rs_z_came(g, i):
        remote(
            RY[g].at[chunk(d)], RZ[g].at[i], o.rz_s.at[g, d], o.rz_r.at[g, i], beside
        ).wait_recv()

    def rs_start(g):
        for i in range(nz):
            rs_y(g, lax.rem(d + 1 + i, nz)).start()

    def rs_mid(g):
        for i in range(nz):
            k = lax.rem(d + 1 + i, nz)
            rs_y(g, k).wait_recv()
            start = pl.multiple_of(k * chunk_rows, 16)

            @pl.loop(0, chunk_rows // 32)
            def _(r):
                rows = pl.ds(pl.multiple_of(start + r * 32, 16), 32)
                both = W[g][y, rows, :].astype(F32) + RY[g][rows, :].astype(F32)
                RY[g][rows, :] = both.astype(BF)

            if i < nz - 1:
                rs_z(g, k).start()

    def rs_end(g, put):
        for i in range(nz - 1):
            rs_z_came(g, i)
        start = pl.multiple_of(d * chunk_rows, 16)

        @pl.loop(0, chunk_rows // 32)
        def _(r):
            rows = pl.ds(pl.multiple_of(r * 32, 16), 32)
            total = RY[g][pl.ds(pl.multiple_of(start + r * 32, 16), 32), :].astype(F32)
            for i in range(nz - 1):
                total = total + RZ[g][i, rows, :].astype(F32)
            put(rows, total)

    def rs_sent(g):
        for i in range(nz):
            k = lax.rem(d + 1 + i, nz)
            rs_y(g, k).wait_send()
            if i < nz - 1:
                rs_z(g, k).wait_send()

    def rs_copies(g):
        return [
            pltpu.make_async_copy(
                buffer.at[pl.ds(first, chunk_rows), pl.ds(0, width)],
                out.at[:, pl.ds(at, width)],
                o.lc.at[g + 3 * i],
            )
            for i, (out, buffer, first, at, width) in enumerate(place[g])
        ]

    def rs_out(g):
        if nz == 1:
            start = 0

            @pl.loop(0, chunk_rows // 32)
            def _(r):
                rows = pl.ds(pl.multiple_of(r * 32, 16), 32)
                (o.oa, o.ob, o.oc)[g][rows, :] = RY[g][rows, :]

        else:

            def put(rows, total):
                for out, buffer, first, at, width in place[g]:
                    into = pl.ds(pl.multiple_of(rows.start + first, 16), 32)
                    buffer[into, :width] = total[:, at : at + width]

            rs_end(g, put)
            for copy in rs_copies(g):
                copy.start()
        rs_sent(g)


    def rows_sib(i, k, n):
        own, landing = ROWS[i]
        src = own.at[y] if n == 0 else landing.at[k]
        return remote(src, landing.at[k], o.qs.at[i, n], o.qr.at[i, n], sibling)

    def rows_beside(i, k):
        own, landing = ROWS[i]
        return remote(own.at[1 - y], landing.at[k], o.qs.at[i, 2], o.qr.at[i, 2], beside)

    def rows_own(i):
        own, landing = ROWS[i]
        return pltpu.make_async_copy(own.at[y], landing.at[t], o.ql.at[i])

    def rows_start(i):
        rows_own(i).start()
        rows_beside(i, t).start()
        rows_sib(i, t, 0).start()

    other = lax.rem(t + 2, 4)

    def rows_pass(i):
        rows_beside(i, other).wait_recv()
        rows_sib(i, other, 1).start()

    def rows_done(i):
        rows_own(i).wait()
        rows_sib(i, t, 0).wait()
        rows_sib(i, other, 1).wait()
        rows_beside(i, t).wait_send()

    def rows_join(i, out_ref):
        landing = ROWS[i][1]
        for k in range(0, 4, 2):
            value = jnp.concatenate(
                [landing[k, :held].astype(F32), landing[k + 1, :held].astype(F32)], axis=0
            )
            out_ref[k * held : (k + 2) * held, :] = value.astype(out_ref.dtype)


    def home_copy(i):
        return remote(o.hs.at[i], o.hr.at[i], o.hx.at[i], o.hy.at[i], beside)

    def home_block(buffer, k):
        value = buffer[pl.ds(pl.multiple_of(k * held, 8), held), :]
        pad = o.hs.shape[1] - held
        return jnp.concatenate([value, jnp.zeros((pad, D), F32)], axis=0).astype(BF)

    def home_send(i, buffer):
        o.hs[i] = home_block(buffer, other)
        home_copy(i).start()

    home_out = (
        pltpu.make_async_copy(o.ho, o.oh.at[y], o.lh.at[0]),
        pltpu.make_async_copy(o.hr.at[0], o.oh.at[1 - y], o.lh.at[1]),
        pltpu.make_async_copy(
            o.gres.at[pl.ds(pl.multiple_of(t * held, 8), held)], o.gh.at[y], o.lh.at[2]
        ),
        pltpu.make_async_copy(o.ext.at[pl.ds(0, held)], o.gh.at[1 - y], o.lh.at[3]),
    )

    barrier = pltpu.get_barrier_semaphore()
    for g in (A, B, C):
        own_copy(g).start()
    when(dec, cross_own.start)
    for peer in (sibling, across, beside):
        pl.semaphore_signal(barrier, inc=1, device_id=peer, device_id_type=MESH)
    for i in range(1, nz):
        pl.semaphore_signal(
            barrier, inc=1, device_id=(p, lax.rem(d + i, nz), t), device_id_type=MESH
        )
    pl.semaphore_wait(barrier, 3 + nz - 1)
    rows_start(0)
    when(enc, lambda: rows_start(2))
    own_copy(A).wait()
    ag_hop(A, 0)
    when(enc, cross_in.start)
    own_copy(B).wait()
    ag_hop(B, 0)
    own_copy(C).wait()

    lane = lax.broadcasted_iota(jnp.int32, (1, 128), 1)
    lo = jnp.where(lane < 64, 1.0, 0.0).astype(BF)
    hi = jnp.where(lane < 64, 0.0, 1.0).astype(BF)

    def rows_loop(fn, step=RT):
        @pl.loop(0, L // step)
        def _(i):
            fn(pl.ds(pl.multiple_of(i * step, step), step))

    def norm_rows(x_ref, gain_no, out_ref):
        def one(rows):
            v = x_ref[rows, :].astype(F32)
            r = lax.rsqrt(jnp.mean(v * v, axis=-1, keepdims=True) + EPSILON)
            out_ref[rows, :] = (v * r * o.g[gain_no : gain_no + 1, :]).astype(BF)

        rows_loop(one)

    def exchange(slot, chunk_fn):
        copies = []
        for n in range(n_cw):
            o.exs[slot, n] = chunk_fn(n).astype(BF)
            copy = remote(
                o.exs.at[slot, n], o.exr.at[slot, n], o.ss.at[slot, n], o.rs.at[slot, n], sibling
            )
            copy.start()
            copies.append(copy)
        return copies

    def landed(copies):
        for copy in copies:
            copy.wait()

    def ex_rows(slot, rows):
        parts = [
            o.exs[slot, n, rows, :].astype(F32) + o.exr[slot, n, rows, :].astype(F32)
            for n in range(n_cw)
        ]
        return jnp.concatenate(parts, axis=1)

    def residual(slot, base_ref, put):
        def one(rows):
            put(rows, base_ref[rows, :].astype(F32) + ex_rows(slot, rows))

        rows_loop(one)

    def keep(ref):
        def put(rows, value):
            ref[rows, :] = value

        return put

    def norm_back(slot, x_ref, gain_no, put):
        o.dgacc[gain_no] = jnp.zeros((8, D), F32)

        def one(rows):
            dh = ex_rows(slot, rows)
            v = x_ref[rows, :].astype(F32)
            r = lax.rsqrt(jnp.mean(v * v, axis=-1, keepdims=True) + EPSILON)
            n = v * r
            dhg = dh * o.g[gain_no : gain_no + 1, :]
            mu = jnp.mean(dhg * n, axis=-1, keepdims=True)
            put(rows, r * (dhg - n * mu))
            o.dgacc[gain_no] += jnp.sum((dh * n).reshape(RT // 8, 8, D), axis=0)

        rows_loop(one)

    def split(a):
        return slice(a * hs, (a + 1) * hs)

    def kv_project():
        for a in range(2):
            r = dot(o.ns[...], W[A][a, :, at_kv:at_ext]).astype(BF)
            o.ks[:, split(a)] = r[:, :hs]
            o.vs[:, split(a)] = r[:, hs:]

    def pair_stack(block):
        return jnp.concatenate([block * lo, block * hi], axis=0)

    def pair_pick(stacked):
        return jnp.where(lane < 64, stacked[:qb_rows], stacked[qb_rows:])

    def attn_fwd(q_ref, mix_ref, mem, own, causal, hooks=()):
        @pl.loop(0, n_blk)
        def _(b):
            for i, hook in enumerate(hooks):
                pl.when(b == i)(hook)
            rows = pl.ds(pl.multiple_of(b * qb_rows, 16), qb_rows)
            wrows = pl.ds(pl.multiple_of(b * qb_rows, 16), win_w)
            sq = o.segq[rows, :]
            if mem:
                o.mm[...] = jnp.where(sq == o.srcseg[...], 0.0, NEG)
            if own:
                allowed = sq == o.segw[b]
                if causal:
                    qi = lax.broadcasted_iota(jnp.int32, (qb_rows, win_w), 0)
                    kj = lax.broadcasted_iota(jnp.int32, (qb_rows, win_w), 1)
                    allowed = allowed & (kj - HALO <= qi)
                o.mo[...] = jnp.where(allowed, 0.0, NEG)

            @pl.loop(0, n_pair)
            def _(j):
                cols = pl.ds(pl.multiple_of(j * 128, 128), 128)
                q2 = pair_stack(q_ref[rows, cols])
                parts = []
                if mem:
                    s = dot_nt(q2, o.ks[:, cols]).reshape(2, qb_rows, L)
                    parts.append(s + o.mm[...][None])
                if own:
                    s = dot_nt(q2, o.kp[wrows, cols]).reshape(2, qb_rows, win_w)
                    parts.append(s + o.tb[pl.ds(2 * j, 2)] + o.mo[...][None])
                top = [jnp.max(s, axis=-1, keepdims=True) for s in parts]
                top = functools.reduce(jnp.maximum, top)
                exps = [jnp.exp(s - top) for s in parts]
                total = sum(jnp.sum(e, axis=-1, keepdims=True) for e in exps)
                inv = 1.0 / total
                probs = [(e * inv).astype(BF).reshape(2 * qb_rows, -1) for e in exps]
                mixed = 0.0
                if mem:
                    o.pm[b * n_pair + j] = probs[0]
                    mixed = mixed + dot(probs[0], o.vs[:, cols])
                if own:
                    o.po[b * n_pair + j] = probs[-1]
                    mixed = mixed + dot(probs[-1], o.vp[wrows, cols])
                mix_ref[rows, cols] = pair_pick(mixed).astype(BF)

    def attn_back(q_ref, mix_ref, mem, own):
        if mem:
            o.dks[...] = jnp.zeros(o.dks.shape, F32)
            o.dvs[...] = jnp.zeros(o.dvs.shape, F32)
        if own:
            o.dkp[...] = jnp.zeros(o.dkp.shape, F32)
            o.dvp[...] = jnp.zeros(o.dvp.shape, F32)
            o.tb[...] = jnp.zeros(o.tb.shape, F32)

        @pl.loop(0, n_blk)
        def _(b):
            rows = pl.ds(pl.multiple_of(b * qb_rows, 16), qb_rows)
            wrows = pl.ds(pl.multiple_of(b * qb_rows, 16), win_w)

            @pl.loop(0, n_pair)
            def _(j):
                cols = pl.ds(pl.multiple_of(j * 128, 128), 128)
                q2 = pair_stack(q_ref[rows, cols])
                do2 = pair_stack(o.dmix[rows, cols])
                mix = mix_ref[rows, cols].astype(F32)
                delta = jnp.sum(
                    do2.astype(F32).reshape(2, qb_rows, 128) * mix[None], axis=-1, keepdims=True
                ).reshape(2 * qb_rows, 1)
                dq2 = 0.0
                if mem:
                    probs = o.pm[b * n_pair + j]
                    dp = dot_nt(do2, o.vs[:, cols])
                    ds = (probs.astype(F32) * (dp - delta)).astype(BF)
                    dq2 = dq2 + dot(ds, o.ks[:, cols])
                    o.dks[:, cols] += dot_tn(ds, q2)
                    o.dvs[:, cols] += dot_tn(probs, do2)
                if own:
                    probs = o.po[b * n_pair + j]
                    dp = dot_nt(do2, o.vp[wrows, cols])
                    ds = (probs.astype(F32) * (dp - delta)).astype(BF)
                    dq2 = dq2 + dot(ds, o.kp[wrows, cols])
                    o.dkp[wrows, cols] += dot_tn(ds, q2)
                    o.dvp[wrows, cols] += dot_tn(probs, do2)
                    o.tb[pl.ds(2 * j, 2)] += ds.astype(F32).reshape(2, qb_rows, win_w)
                o.dq[rows, cols] = (pair_pick(dq2) * (HD**-0.5)).astype(BF)

    def out_project(slot, mix_ref, weight_ref, at):
        mixed = [mix_ref[:, split(a)] for a in range(2)]
        return exchange(
            slot,
            lambda n: sum(
                dot_nt(mixed[a], weight_ref[a, n * CW : (n + 1) * CW, at : at + hs])
                for a in range(2)
            ),
        )

    def mix_grads(weight_ref, at):
        for a in range(2):
            o.dmix[:, split(a)] = dot(o.gb[...], weight_ref[a, :, at : at + hs]).astype(BF)

    fw = fs // 2

    def ff_half(n):
        a = n // 2
        return a, pl.ds(pl.multiple_of((n - 2 * a) * fw, 128), fw)

    def ff_fwd(x_ref):
        norm_rows(x_ref, 1, o.nc)
        ag_wait(B)

        @pl.loop(0, 4)
        def _(n):
            a, half_cols = ff_half(n)
            cols = pl.ds(pl.multiple_of(n * fw, 128), fw)
            o.pre[...] = dot(o.nc[...], W[B][a, :, half_cols])

            def one(rows):
                v = o.pre[rows, :]
                v2 = v * v
                th = jnp.tanh(0.7978845608028654 * v * (1.0 + 0.044715 * v2))
                cdf = 0.5 * (1.0 + th)
                slope = (0.5 * 0.7978845608028654) * v * (1.0 - th * th)
                o.hidden[rows, cols] = (v * cdf).astype(BF)
                o.gp[rows, cols] = (cdf + slope * (1.0 + (3 * 0.044715) * v2)).astype(BF)

            rows_loop(one, 32)

        ag_wait(C)
        return exchange(
            2,
            lambda n: sum(
                dot_nt(o.hidden[:, a * fs : (a + 1) * fs], W[C][a, n * CW : (n + 1) * CW, :])
                for a in range(2)
            ),
        )

    def sides():
        return (1 - y, y)

    def side_cols(a, width):
        return pl.ds(pl.multiple_of(a * width, 128), width)

    def ff_back(x_ref):
        ag_finish(B)
        ag_finish(C)

        @pl.loop(0, 4)
        def _(n):
            a, half_cols = ff_half(n)
            cols = pl.ds(pl.multiple_of(n * fw, 128), fw)
            o.gp[:, cols] = (
                dot(o.gb[...], W[C][a, :, half_cols]) * o.gp[:, cols].astype(F32)
            ).astype(BF)

        copies = exchange(
            0,
            lambda n: sum(
                dot_nt(o.gp[:, a * fs : (a + 1) * fs], W[B][a, n * CW : (n + 1) * CW, :])
                for a in range(2)
            ),
        )
        for i, a in enumerate(sides()):
            W[C][a] = dot_tn(o.gb[...], o.hidden[:, side_cols(a, fs)]).astype(BF)
            if i == 0:
                rs_start(C)
        landed(copies)

        def put(rows, dv):
            new = o.gres[rows, :] + dv
            o.gres[rows, :] = new
            o.gb[rows, :] = new.astype(BF)

        norm_back(0, x_ref, 1, put)

    def ff_weights():
        for i, a in enumerate(sides()):
            W[B][a] = dot_tn(o.nc[...], o.gp[:, side_cols(a, fs)]).astype(BF)
            if i == 0:
                rs_start(B)

    def x_part():
        return pl.ds(pl.multiple_of(core * half, 16), half)

    def x_copy(way):
        rows = x_part()
        return remote(
            o.xsend.at[rows], o.xbuf.at[rows], o.xss.at[way, 0], o.xrs.at[way, 0], across
        )

    def x_recv(way):
        x_copy(way).wait_recv()
        rows = x_part()
        copy = remote(
            o.xbuf.at[rows], o.xbuf.at[rows], o.xss.at[way, 1], o.xrs.at[way, 1], sibling
        )
        copy.start()
        copy.wait()

    def dkv_grads():
        for a in range(2):
            o.dkv[a, :, :hs] = o.dks[:, split(a)].astype(BF)
            o.dkv[a, :, hs:] = o.dvs[:, split(a)].astype(BF)
        return exchange(
            2,
            lambda n: sum(
                dot_nt(o.dkv[a], W[A][a, n * CW : (n + 1) * CW, at_kv:at_ext]) for a in range(2)
            ),
        )

    rows_pass(0)
    when(enc, lambda: rows_pass(2))
    ag_hop(A, 1)
    rows_start(1)
    ag_hop(A, 2)
    ag_hop(C, 0)
    rows_pass(1)
    ag_hop(A, 3)
    rows_done(0)
    rows_join(0, o.x)

    @pl.when(dec)
    def _():
        cross_own.wait()
        cross_in.wait_recv()
        ag_hop(X, 0)

    ag_wait(A)
    o.g[...] = W[A][0, :, at_ext:].astype(F32).T[:8]
    rel_lanes = [dot_tn(W[A][a, :, at_ext:], o.hot[...]) for a in range(2)]
    for h in range(2 * n_pair):
        a = h // (hs // HD)
        row = REL_AT + h - a * (hs // HD)
        line = rel_lanes[a][row : row + 1, :]
        o.tb[h] = pltpu.roll(
            jnp.broadcast_to(line, (qb_rows, win_w)), 0, 1, stride=1, stride_axis=0
        )
    pad = jnp.zeros((HALO, hc), BF)
    for ref in (o.kp, o.vp):
        ref[:HALO, :] = pad
        ref[HALO + L :, :] = pad
    norm_rows(o.x, 0, o.na)
    for a in range(2):
        r = dot(o.na[...], W[A][a, :, :at_o]).astype(BF)
        o.q[:, split(a)] = (r[:, :hs] * (HD**-0.5)).astype(BF)
        o.kp[HALO : HALO + L, split(a)] = r[:, hs : 2 * hs]
        o.vp[HALO : HALO + L, split(a)] = r[:, 2 * hs :]
    ag_hop(B, 1)
    hooks = (
        lambda: ag_hop(C, 1),
        lambda: ag_hop(B, 2),
        lambda: ag_hop(C, 2),
    )

    @pl.when(enc)
    def _():
        rows_done(2)
        rows_join(2, o.nb)
        norm_rows(o.nb, 2, o.ns)
        kv_project()
        attn_fwd(o.q, o.mixa, True, True, False, hooks)

    @pl.when(dec)
    def _():
        attn_fwd(o.q, o.mixa, False, True, True, hooks)
        ag_hop(X, 1)

    ag_hop(B, 3)
    copies = out_project(0, o.mixa, W[A], at_o)
    ag_hop(C, 3)
    landed(copies)
    residual(0, o.x, keep(o.xmid))

    @pl.when(enc)
    def _():
        landed(ff_fwd(o.xmid))

        def put_out(rows, value):
            o.xlate[rows, :] = value
            o.xsend[rows, :] = value.astype(BF)

        residual(2, o.xmid, put_out)
        x_copy(0).start()
        home_send(0, o.xlate)
        o.ho[...] = home_block(o.xlate, t)
        home_out[0].start()
        ag_finish(A)
        rows_done(1)
        rows_join(1, o.gres)
        x_copy(0).wait_send()
        x_recv(1)

        def one(rows):
            value = o.gres[rows, :] + o.xbuf[rows, :].astype(F32)
            o.gres[rows, :] = value
            o.gb[rows, :] = value.astype(BF)

        rows_loop(one)
        ff_back(o.xmid)
        ff_weights()

    @pl.when(dec)
    def _():
        ag_hop(X, 2)
        ag_hop(X, 3)
        ag_wait(X)
        ag_finish(X)
        for a in range(2):
            for k in range(nz):
                for part in range(2):
                    at = part * (D // 2) + k * cross_rows
                    o.xg[a, at : at + cross_rows, :] = W[X][
                        a, k * chunk_rows + part * cross_rows :, :
                    ][:cross_rows]
        o.g[3:4, :] = o.xg[0, :, 2 * hs :].astype(F32).T[:1]
        norm_rows(o.xmid, 3, o.nb)
        for a in range(2):
            r = dot(o.nb[...], o.xg[a, :, :hs]).astype(BF)
            o.qb[:, split(a)] = (r * (HD**-0.5)).astype(BF)
        x_recv(0)
        norm_rows(o.xbuf, 2, o.ns)
        kv_project()
        attn_fwd(o.qb, o.mixb, True, False, False)
        landed(out_project(1, o.mixb, o.xg, hs))
        residual(1, o.xmid, keep(o.xlate))
        landed(ff_fwd(o.xlate))
        residual(2, o.xlate, keep(o.gres))
        home_send(0, o.gres)
        o.ho[...] = home_block(o.gres, t)
        home_out[0].start()
        rows_done(1)
        rows_join(1, o.gres)
        rows_join(1, o.gb)
        ff_back(o.xlate)
        mix_grads(o.xg, hs)
        attn_back(o.qb, o.mixb, True, False)
        copies = dkv_grads()
        parts = [o.dq[:, split(a)] for a in range(2)]
        more = exchange(
            1,
            lambda n: sum(
                dot_nt(parts[a], o.xg[a, n * CW : (n + 1) * CW, :hs]) for a in range(2)
            ),
        )
        ff_weights()
        landed(copies)

        def put_source(rows, dv):
            o.xsend[rows, :] = dv.astype(BF)

        norm_back(2, o.xbuf, 2, put_source)
        x_copy(1).start()
        landed(more)

        def put_mid(rows, dv):
            new = o.gres[rows, :] + dv
            o.gres[rows, :] = new
            o.nc[rows, :] = new.astype(BF)

        norm_back(1, o.xmid, 3, put_mid)
        line = jnp.sum(o.dgacc[3], axis=0, keepdims=True)
        tall = jnp.broadcast_to(line, (EXT, D)).T.astype(BF)
        for a in range(2):
            full = jnp.concatenate(
                [
                    dot_tn(o.nb[...], parts[a]).astype(BF),
                    dot_tn(o.gb[...], o.mixb[:, split(a)]).astype(BF),
                    tall,
                ],
                axis=1,
            )
            for k in range(nz):
                for part in range(2):
                    at = part * (D // 2) + k * cross_rows
                    to = k * chunk_rows + part * cross_rows
                    W[X][a, to : to + cross_rows, :] = full[at : at + cross_rows]
        rs_start(X)
        ag_finish(A)
        rs_mid(C)
        x_copy(1).wait_send()
        o.gb[...] = o.nc[...]

    mix_grads(W[A], at_o)
    for a in range(2):
        W[A][a, :, at_o : at_o + hs] = dot_tn(o.gb[...], o.mixa[:, split(a)]).astype(BF)

    @pl.when(enc)
    def _():
        attn_back(o.q, o.mixa, True, True)
        landed(dkv_grads())

        def put_source(rows, dv):
            pass

        norm_back(2, o.nb, 2, put_source)
        rs_mid(C)

    @pl.when(dec)
    def _():
        attn_back(o.q, o.mixa, False, True)
        rs_mid(B)

    for a in range(2):
        o.dqkv[a, :, :hs] = o.dq[:, split(a)]
        o.dqkv[a, :, hs : 2 * hs] = o.dkp[HALO : HALO + L, split(a)].astype(BF)
        o.dqkv[a, :, 2 * hs :] = o.dvp[HALO : HALO + L, split(a)].astype(BF)
    copies = exchange(
        0,
        lambda n: sum(
            dot_nt(o.dqkv[a], W[A][a, n * CW : (n + 1) * CW, :at_o]) for a in range(2)
        ),
    )
    heads = 2 * n_pair
    acc = jnp.zeros((heads * 8, win_w), F32)
    for k in range(qb_rows // 8):
        part = o.tb[:, 8 * k : 8 * k + 8, :].reshape(heads * 8, win_w)
        acc = acc + (part if k == 0 else pltpu.roll(part, win_w - 8 * k, 1))
    sub = lax.rem(lax.broadcasted_iota(jnp.int32, (heads * 8, win_w), 0), 8)
    diag = jnp.zeros((heads * 8, win_w), F32)
    for k in range(8):
        turned = acc if k == 0 else pltpu.roll(acc, win_w - k, 1)
        diag = diag + jnp.where(sub == k, turned, 0.0)
    lines = jnp.sum(diag.reshape(heads, 8, win_w), axis=1)
    landed(copies)

    def put_in(rows, dv):
        o.gres[rows, :] = o.gres[rows, :] + dv

    norm_back(0, o.x, 0, put_in)
    home_send(1, o.gres)
    home_out[2].start()
    for i, a in enumerate(sides()):
        W[A][a, :, :at_o] = dot_tn(o.na[...], o.dqkv[a]).astype(BF)
        W[A][a, :, at_kv:at_ext] = dot_tn(o.ns[...], o.dkv[a]).astype(BF)
    per = hs // HD
    for a in range(2):
        o.ext[...] = jnp.zeros(o.ext.shape, F32)
        for k in range(3):
            o.ext[k : k + 1, :] = jnp.sum(o.dgacc[k], axis=0, keepdims=True)
        tall = o.ext[...].T
        o.lines[...] = jnp.zeros((EXT, win_w), F32)
        o.lines[REL_AT : REL_AT + per, :] = lines[per * a : per * (a + 1), :]
        whole = o.lines[...]
        high = whole.astype(BF)
        low = (whole - high.astype(F32)).astype(BF)
        tall = tall + dot_nt(o.hot[...], high) + dot_nt(o.hot[...], low)
        W[A][a, :, at_ext:] = tall.astype(BF)
    rs_start(A)
    home_copy(0).wait()
    home_out[1].start()

    @pl.when(enc)
    def _():
        rs_mid(B)

    rs_out(C)

    @pl.when(dec)
    def _():
        rs_mid(X)

    rs_mid(A)
    rs_out(B)

    @pl.when(dec)
    def _():
        def put(rows, total):
            o.xt[rows, :] = total

        rs_end(X, put)
        rs_sent(X)
        o.xo[...] = o.xt[:cross_rows, :]
        cross_out.start()
        o.ox[...] = o.xt[cross_rows:, :].astype(o.ox.dtype)
        cross_out.wait_send()

    @pl.when(enc)
    def _():
        cross_in.wait_send()
        cross_out.wait_recv()
        o.ox[...] = o.xi[...].astype(o.ox.dtype)

    home_copy(1).wait()
    o.ext[...] = o.hr[1].astype(F32)
    home_out[3].start()
    rs_out(A)
    for copy in home_out:
        copy.wait()
    if nz > 1:
        for g in (A, B, C):
            for copy in rs_copies(g):
                copy.wait()


def run_kernel(dims, given):
    L, D, hs, fs, nz, qb_rows, win_w = dims
    hc, fc = 2 * hs, 2 * fs
    n_blk, n_pair, n_cw = L // qb_rows, hc // 128, D // CW
    LP = L + 2 * HALO
    LBP = -(-(L // 4) // 16) * 16
    CR = D // nz
    widths = dict(a=6 * hs + EXT, b=fs, c=fs, x=2 * hs + EXT)
    S = jax.ShapeDtypeStruct
    SUM = F32 if nz > 1 else BF
    outs = dict(
        oh=S((2, LBP, D), BF),
        gh=S((2, L // 4, D), F32),
        oa=S((CR, widths["a"]), SUM),
        ob=S((CR, widths["b"]), SUM),
        oc=S((CR, widths["c"]), SUM),
        ox=S((CR // 2, widths["x"]), SUM),
    )
    V = pltpu.VMEM
    LD, LH, LF = (L, D), (L, hc), (L, fc)
    scratch = dict(
        na=V(LD, BF), ns=V(LD, BF), nb=V(LD, BF), nc=V(LD, BF),
        xmid=V(LD, F32), xlate=V(LD, F32), gres=V(LD, F32),
        q=V(LH, BF), kp=V((LP, hc), BF), vp=V((LP, hc), BF), ks=V(LH, BF), vs=V(LH, BF),
        qb=V(LH, BF), mixa=V(LH, BF), mixb=V(LH, BF),
        pm=V((n_blk * n_pair, 2 * qb_rows, L), BF), po=V((n_blk * n_pair, 2 * qb_rows, win_w), BF),
        hidden=V(LF, BF), gp=V(LF, BF), pre=V((L, fs // 2), F32),
        tb=V((2 * n_pair, qb_rows, win_w), F32),
        mm=V((qb_rows, L), F32), mo=V((qb_rows, win_w), F32),
        dmix=V(LH, BF), dq=V(LH, BF), dqkv=V((2, L, 3 * hs), BF), dkv=V((2, L, 2 * hs), BF),
        dkp=V((LP, hc), F32), dvp=V((LP, hc), F32), dks=V(LH, F32), dvs=V(LH, F32),
        gb=V(LD, BF), xbuf=V(LD, BF), xsend=V(LD, BF),
        exs=V((3, n_cw, L, CW), BF), exr=V((3, n_cw, L, CW), BF), dgacc=V((4, 8, D), F32),
        g=V((8, D), F32), ext=V((LBP, D), F32), lines=V((EXT, win_w), F32),
        x=V(LD, BF), xq=V((4, LBP, D), BF), cq=V((4, LBP, D), BF), mq=V((4, LBP, D), BF),
        hs=V((2, LBP, D), BF), hr=V((2, LBP, D), BF), ho=V((LBP, D), BF),
        xg=V((2, D, widths["x"]), BF), xt=V((CR, widths["x"]), F32),
        xo=V((CR // 2, widths["x"]), F32), xi=V((CR // 2, widths["x"]), F32),
    )
    for g, width in widths.items():
        scratch["w" + g] = V((2, D, width), BF)
        scratch["y" + g] = V((D, width), BF)
        scratch["z" + g] = V((nz - 1, CR, width) if nz > 1 else (1, 16, width), BF)
    sem = pltpu.SemaphoreType.DMA
    scratch.update(ss=sem((3, n_cw)), rs=sem((3, n_cw)), xss=sem((2, 2)), xrs=sem((2, 2)))
    scratch.update(xw=sem((4,)), oc_sem=sem((4,)), lc=sem((5,)), lh=sem((4,)))
    scratch.update(qs=sem((3, 3)), qr=sem((3, 3)), ql=sem((3,)), hx=sem((2,)), hy=sem((2,)))
    for name in ("gr", "gl", "gs", "gz", "gy", "rs_s", "rs_r", "rz_s", "rz_r"):
        scratch[name] = sem((4, nz))
    spec = pl.BlockSpec(memory_space=pltpu.VMEM)
    far = pl.BlockSpec(memory_space=pl.ANY)
    names = list(given) + list(outs) + list(scratch)
    FAR = ["sa", "sb", "sc", "sx", "xs", "cs", "ms", "oh", "gh"]
    if nz > 1:
        FAR += ["oa", "ob", "oc"]
    return pl.pallas_call(
        functools.partial(kernel, dims, names),
        out_shape=list(outs.values()),
        in_specs=[far if name in FAR else spec for name in given],
        out_specs=[far if name in FAR else spec for name in outs],
        scratch_shapes=list(scratch.values()),
        compiler_params=pltpu.CompilerParams(
            collective_id=0, has_side_effects=True, vmem_limit_bytes=63 << 20
        ),
        name="layers",
    )(*given.values())


def prep_kernel(dims, n_dp, names, *refs):
    L, D, hs, fs, nz, qb_rows, win_w = dims
    o = Refs()
    for name, ref in zip(names, refs, strict=True):
        setattr(o, name, ref)
    section = lax.axis_index("pipe")
    y = lax.axis_index("tensor") // 2
    rows = D // n_dp
    held = L // 4
    for raw, out in ((o.li, o.xs), (o.co, o.cs)):
        o.tmp[...] = raw[...].astype(F32)
        pad = jnp.zeros((out.shape[1] - held, D), F32)
        for r in range(2):
            out[r] = jnp.concatenate([o.tmp[:, r, :], pad], axis=0).astype(BF)
    for i in range(3):
        o.sa[:, i * hs : (i + 1) * hs] = o.qkv[i]
    o.sa[:, 3 * hs : 4 * hs] = o.so[...].astype(F32).T.astype(BF)
    for i in range(2):
        o.kvt[...] = o.kv[...].astype(F32)
        o.sa[:, (4 + i) * hs : (5 + i) * hs] = o.kvt[:, i, :].astype(BF)
    n_gain = o.gain.shape[0]
    o.ext[...] = jnp.zeros(o.ext.shape, F32)
    o.ext[:n_gain, :rows] = o.gain[...].astype(F32)
    tall = o.ext[...].T
    o.wide[...] = tall
    nb_rows, heads = o.rel.shape
    o.wide[:nb_rows, REL_AT : REL_AT + heads] = o.rel[...].astype(F32)
    o.sa[:, 6 * hs :] = o.wide[:rows, :].astype(BF)
    o.sx[:, :hs] = o.cq[...]
    o.sx[:, hs : 2 * hs] = o.cw[...].astype(F32).T.astype(BF)
    half = o.cg.shape[1]
    o.ext[...] = jnp.zeros(o.ext.shape, F32)
    o.ext[:1, :half] = o.cg[...].astype(F32)
    o.wide[...] = o.ext[...].T
    o.sx[:, 2 * hs :] = o.wide[:half, :].astype(BF)
    own = o.seg[section, pl.ds(y, 1), :]
    first = o.seg[0, pl.ds(y, 1), :]
    o.segq[...] = jnp.broadcast_to(own.astype(F32), (8, L)).T[:, :1].astype(jnp.int32)
    slots = lax.broadcasted_iota(jnp.int32, (1, L), 1).astype(F32)
    slots = jnp.floor((slots + 0.5) * (1.0 / MEM)).astype(jnp.int32)
    o.srcseg[...] = jnp.where(section == 0, slots, first)
    o.line[...] = jnp.full(o.line.shape, -1, jnp.int32)
    o.line[:, HALO : HALO + L] = own
    for b in range(L // qb_rows):
        o.segw[b] = o.line[:, b * qb_rows : b * qb_rows + win_w]
    at = lax.broadcasted_iota(jnp.int32, (rows, win_w), 0)
    for k in range(n_dp):
        same = (at < nb_rows) & (o.win[...] == at + k * nb_rows)
        o.hotf[k * rows : (k + 1) * rows, :] = jnp.where(same, 1.0, 0.0)
    o.hot[...] = o.hotf[...].astype(BF)


def run_prep(dims, n_dp, given):
    L, D, hs, fs, nz, qb_rows, win_w = dims
    rows, held = D // n_dp, L // 4
    LBP = -(-held // 16) * 16
    S = jax.ShapeDtypeStruct
    outs = dict(
        xs=S((2, LBP, D), BF),
        cs=S((2, LBP, D), BF),
        sa=S((rows, 6 * hs + EXT), BF),
        sx=S((rows // 2, 2 * hs + EXT), BF),
        segq=S((L, 1), jnp.int32),
        segw=S((L // qb_rows, 1, win_w), jnp.int32),
        srcseg=S((1, L), jnp.int32),
        hot=S((D, win_w), BF),
    )
    V = pltpu.VMEM
    up = -(-rows // 128) * 128
    scratch = dict(
        tmp=V((held, 2, D), F32),
        kvt=V((rows, 2, hs), F32),
        ext=V((EXT, up), F32),
        wide=V((up, EXT), F32),
        line=V((1, L + 2 * HALO), jnp.int32),
        hotf=V((D, win_w), F32),
    )
    spec = pl.BlockSpec(memory_space=pltpu.VMEM)
    names = list(given) + list(outs) + list(scratch)
    return pl.pallas_call(
        functools.partial(prep_kernel, dims, n_dp, names),
        out_shape=list(outs.values()),
        in_specs=[spec] * len(given),
        out_specs=[spec] * len(outs),
        scratch_shapes=list(scratch.values()),
        compiler_params=pltpu.CompilerParams(vmem_limit_bytes=60 << 20),
        name="prep",
    )(*given.values())


def finish_kernel(dims, names, *refs):
    L, D, hs, fs, nz, qb_rows, win_w = dims
    o = Refs()
    for name, ref in zip(names, refs, strict=True):
        setattr(o, name, ref)
    o.ffi[...] = o.gb[...]
    o.ffo[...] = o.gc[...]
    for r in range(2):
        o.gin[:, r, :] = o.gh[r]
        o.tmp[:, r, :] = o.oh[r, : L // 4].astype(F32)
    o.out[...] = o.tmp[...].astype(BF)
    for i in range(3):
        o.qkv[i] = o.ga[:, i * hs : (i + 1) * hs]
    o.so[...] = o.ga[:, 3 * hs : 4 * hs].T
    for i in range(2):
        o.kv[:, i, :] = o.ga[:, (4 + i) * hs : (5 + i) * hs]
    ext = o.ga[:, 6 * hs :].T
    for i in range(o.gain.shape[0]):
        o.gain[i] = ext[i : i + 1]
    heads, _, nb_rows = o.rel.shape
    for i in range(heads):
        o.rel[i] = ext[REL_AT + i : REL_AT + i + 1, :nb_rows]
    o.cq[...] = o.gx[:, :hs]
    o.co[...] = o.gx[:, hs : 2 * hs].T
    o.cg[...] = o.gx[:, 2 * hs :].T[:1]


def run_finish(dims, rel_shape, sums):
    L, D, hs, fs, nz, qb_rows, win_w = dims
    rows = sums[2].shape[0]
    held = L // 4
    S = jax.ShapeDtypeStruct
    outs = dict(
        out=S((held, 2, D), BF),
        gin=S((held, 2, D), F32),
        qkv=S((3, rows, hs), F32),
        so=S((hs, rows), F32),
        kv=S((rows, 2, hs), F32),
        rel=S((rel_shape[1], 1, rel_shape[0]), F32),
        gain=S((3, 1, rows), F32),
        cq=S((rows // 2, hs), F32),
        co=S((hs, rows // 2), F32),
        cg=S((1, rows // 2), F32),
        ffi=S((rows, fs), F32),
        ffo=S((rows, fs), F32),
    )
    spec = pl.BlockSpec(memory_space=pltpu.VMEM)
    return pl.pallas_call(
        functools.partial(
            finish_kernel, dims, ["oh", "gh", "ga", "gb", "gc", "gx", *outs, "tmp"]
        ),
        out_shape=list(outs.values()),
        in_specs=[spec] * 6,
        out_specs=[spec] * len(outs),
        scratch_shapes=[pltpu.VMEM((held, 2, D), F32)],
        compiler_params=pltpu.CompilerParams(vmem_limit_bytes=60 << 20),
        name="finish",
    )(*sums)


def body(
    layer_inputs,
    segment_ids,
    slot_ids,
    memory_table,
    buckets,
    self_qkv,
    self_out,
    source_kv,
    ff_in,
    ff_out,
    rel_bias,
    gains,
    cross_query,
    cross_out,
    cross_gain,
    cotangents,
):
    nt = lax.axis_size("tensor")
    n_dp = lax.axis_size("dp")
    assert nt == 4 and layer_inputs.shape[2] == 2
    D = layer_inputs.shape[3]
    L = segment_ids.shape[2]
    hs = self_qkv.shape[3]
    fs = ff_in.shape[2]
    qb_rows, win_w = 160, 256
    rows = D // n_dp
    nz = n_dp if (rows // 2) % 32 == 0 else 1
    dims = (L, D, hs, fs, nz, qb_rows, win_w)
    held = L // nt
    fill = -(-held // 16) * 16 - held
    ids = jnp.pad(slot_ids.T, ((0, 0), (0, fill)))
    ms = memory_table.at[ids].get(mode="promise_in_bounds")
    window = jnp.pad(
        buckets[L - HALO : L + HALO], (0, win_w - 2 * HALO), constant_values=-1
    )
    prepared = run_prep(
        dims,
        n_dp,
        dict(
            li=layer_inputs[0],
            co=cotangents[0],
            qkv=self_qkv[0].transpose(1, 0, 2),
            so=self_out[0],
            kv=source_kv[0],
            gain=gains[0],
            rel=rel_bias[0],
            cq=cross_query,
            cw=cross_out,
            cg=cross_gain[None],
            seg=segment_ids,
            win=window[None],
        ),
    )
    xs, cs, sa, sx, segq, segw, srcseg, hot = prepared
    shards = [sa, ff_in[0], ff_out[0].T, sx]
    if nz != n_dp:
        shards = [lax.all_gather(shard, "dp", axis=0, tiled=True) for shard in shards]
    given = dict(
        xs=xs, cs=cs, ms=ms, segq=segq, segw=segw, srcseg=srcseg, hot=hot,
        sa=shards[0], sb=shards[1], sc=shards[2], sx=shards[3],
    )
    oh, gh, *sums = run_kernel(dims, given)
    if nz != n_dp:
        sums = [
            lax.psum_scatter(full, "dp", scatter_dimension=0, tiled=True).astype(F32)
            for full in sums
        ]
    done = run_finish(dims, rel_bias.shape[1:], [oh, gh, *sums])
    out, gin, qkv, so, kv, rel, gain, cq, co, cg, ff_i, ff_o = done
    return (
        out[None],
        gin[None],
        qkv.transpose(1, 0, 2)[None],
        so[None],
        kv[None],
        ff_i[None],
        ff_o.T[None],
        rel.transpose(1, 2, 0),
        gain.transpose(1, 0, 2),
        cq,
        co,
        cg[0],
    )


def solution(mesh):
    placed = (
        P("pipe", "tensor", "dp", None),
        P(None, "dp", None),
        P("tensor", "dp"),
        P(),
        P(),
        P("pipe", "dp", None, "tensor"),
        P("pipe", "tensor", "dp"),
        P("pipe", "dp", None, "tensor"),
        P("pipe", "dp", "tensor"),
        P("pipe", "tensor", "dp"),
        P("pipe", "dp", "tensor"),
        P("pipe", None, "dp"),
        P(("pipe", "dp"), "tensor"),
        P("tensor", ("pipe", "dp")),
        P(("pipe", "dp")),
        P("pipe", "tensor", "dp", None),
    )
    return jax.shard_map(
        body,
        mesh=mesh,
        in_specs=placed,
        out_specs=(
            P("pipe", "tensor", "dp", None),
            P("pipe", "tensor", "dp", None),
            P("pipe", "dp", None, "tensor"),
            P("pipe", "tensor", "dp"),
            P("pipe", "dp", None, "tensor"),
            P("pipe", "dp", "tensor"),
            P("pipe", "tensor", "dp"),
            P("pipe", "dp", "tensor"),
            P("pipe", None, "dp"),
            P(("pipe", "dp"), "tensor"),
            P("tensor", ("pipe", "dp")),
            P(("pipe", "dp")),
        ),
        check_vma=False,
    )
```

```python
import functools

import jax
import jax.numpy as jnp
from jax import lax
from jax.experimental import pallas as pl
from jax.experimental.pallas import tpu as pltpu
from jax.sharding import PartitionSpec as P

HD = 64
NB = 32
MEM = 20
HALO = 48
EXT = 128
REL_AT = 8
EPSILON = 1e-06
NEG = -1000000000.0
BF = jnp.bfloat16
F32 = jnp.float32
MESH = pl.DeviceIdType.MESH
RT = 48


def dot(a, b):
    return lax.dot_general(a, b, (((1,), (0,)), ((), ())), preferred_element_type=F32)


def dot_nt(a, b):
    return lax.dot_general(a, b, (((1,), (1,)), ((), ())), preferred_element_type=F32)


def dot_tn(a, b):
    return lax.dot_general(a, b, (((0,), (0,)), ((), ())), preferred_element_type=F32)


class Refs:
    pass


def kernel(dims, names, *refs):
    L, D, hs, fs, nz, qb_rows, win_w = dims
    hc, fc = 2 * hs, 2 * fs
    at_o, at_kv, at_ext = 3 * hs, 4 * hs, 6 * hs
    chunk_rows = D // nz
    cross_rows = chunk_rows // 2
    n_blk = L // qb_rows
    n_pair = hc // 128
    o = Refs()
    for name, ref in zip(names, refs, strict=True):
        setattr(o, name, ref)
    p = lax.axis_index("pipe")
    d = lax.axis_index("dp")
    t = lax.axis_index("tensor")
    enc, dec = p == 0, p == 1
    core = lax.rem(t, 2)
    y = t // 2
    z = d if nz > 1 else 0
    skew = (1 - p, d, lax.rem(t + 2, 4))
    sibling = (p, d, t + 1 - 2 * core)
    across = (1 - p, d, t)
    beside = (p, d, lax.rem(t + 2, 4))
    half = L // 2
    held = L // 4
    A, B, C, X = range(4)
    shard = (o.sa, o.sb, o.sc, o.sx)
    W = (o.wa, o.wb, o.wc, o.wx)
    RY = (o.ya, o.yb, o.yc, o.yx)
    RZ = (o.za, o.zb, o.zc, o.zx)
    RB, RC, RX, RQ, RK, RG = range(6)
    REDUCE = {
        RB: (B, 0, fs),
        RC: (C, 0, fs),
        RX: (X, 0, 2 * hs + EXT),
        RQ: (A, 0, at_kv),
        RK: (A, at_kv, 2 * hs),
        RG: (A, at_ext, EXT),
    }
    LEAVE = {
        RB: (o.ob, o.xlate, 0, 0),
        RC: (o.oc, o.xmid, 0, 0),
        RQ: (o.oa, o.xmid, chunk_rows, 0),
        RK: (o.oa, o.xlate, chunk_rows, 0),
        RG: (o.oa, o.xlate, chunk_rows, 2 * hs),
    }
    STAGE = {} if nz == 1 else {
        A: o.hidden.at[pl.ds(0, chunk_rows), pl.ds(0, 6 * hs + EXT)],
        B: o.gp.at[pl.ds(0, chunk_rows), pl.ds(0, fs)],
        C: o.gp.at[pl.ds(0, chunk_rows), pl.ds(fs, fs)],
    }
    ROWS = ((o.xs, o.xq), (o.cs, o.cq), (o.ms, o.mq))

    def chunk(k):
        return pl.ds(pl.multiple_of(k * chunk_rows, 16), chunk_rows)

    def remote(src, dst, send, recv, device):
        return pltpu.make_async_remote_copy(
            src_ref=src,
            dst_ref=dst,
            send_sem=send,
            recv_sem=recv,
            device_id=device,
            device_id_type=MESH,
        )


    def ag_right(g, k):
        slot = W[g].at[y, chunk(k)]
        return remote(slot, slot, o.gr.at[g, k], o.gz.at[g, k], (p, d + 1, t))

    def ag_left(g, k):
        slot = W[g].at[y, chunk(k)]
        return remote(slot, slot, o.gl.at[g, k], o.gz.at[g, k], (p, d - 1, t))

    def ag_beside(g, k):
        slot = W[g].at[y, chunk(k)]
        return remote(slot, slot, o.gs.at[g, k], o.gy.at[g, k], beside)

    def ag_came(g, k):
        slot = W[g].at[y, chunk(k)]
        remote(slot, slot, o.gr.at[g, k], o.gz.at[g, k], beside).wait_recv()

    def ag_each(g, h, act):
        if h == 0:
            act(z, z + 1 < nz, z > 0, True)
        else:
            act(z - h, z + 1 < nz, False, z - h >= 0)
            act(z + h, False, z > 0, z + h < nz)

    def when(cond, fn):
        if cond is True:
            fn()
        elif cond is not False:
            pl.when(cond)(fn)


    def ag_skew(g):
        return remote(W[g].at[y, chunk(z)], STAGE[g], o.gd.at[g, 0], o.gd.at[g, 1], skew)

    def ag_relay(g):
        slot = W[g].at[1 - y, chunk(z)]
        return remote(STAGE[g], slot, o.gd.at[g, 2], o.gy.at[g, z], across)

    def ag_pass_on(g):
        ag_skew(g).wait_recv()
        ag_relay(g).start()

    def ag_aside(g, k, own, wait):
        act = (lambda c: c.wait_send()) if wait else (lambda c: c.start())
        if own and g in STAGE:
            pl.when(enc)(lambda: act(ag_skew(g)))
            pl.when(dec)(lambda: act(ag_beside(g, k)))
        elif not own and g == C:
            pl.when(enc)(lambda: act(ag_beside(g, k)))
        else:
            act(ag_beside(g, k))


    def ag_also(k, way):
        slot = W[C].at[1 - y, chunk(k)]
        return remote(slot, slot, o.ga.at[way, k], o.gb2.at[k], (p, d + (1, -1)[way], t))

    def ag_also_hop(h):
        if h >= nz or nz == 1:
            return

        def act(k, right, left, here):
            def go():
                slot = W[C].at[1 - y, chunk(k)]
                if h == 0:
                    remote(slot, slot, o.gs.at[C, k], o.gy.at[C, k], beside).wait_recv()
                else:
                    remote(slot, slot, o.ga.at[0, k], o.gb2.at[k], beside).wait_recv()
                when(right, lambda: ag_also(k, 0).start())
                when(left, lambda: ag_also(k, 1).start())

            when(here, go)

        ag_each(C, h, act)

    def ag_also_sent():
        for h in range(nz):

            def act(k, right, left, here):
                def go():
                    when(right, lambda: ag_also(k, 0).wait_send())
                    when(left, lambda: ag_also(k, 1).wait_send())

                when(here, go)

            ag_each(C, h, act)

    def ag_hop(g, h, aside=True):
        if h >= nz:
            return

        def act(k, right, left, here):
            def go():
                if h > 0:
                    ag_came(g, k)
                if nz > 1:
                    when(right, lambda: ag_right(g, k).start())
                    when(left, lambda: ag_left(g, k).start())
                if aside:
                    ag_aside(g, k, h == 0, False)

            when(here, go)

        ag_each(g, h, act)

    def ag_side(g, h):
        if h >= nz:
            return

        def act(k, right, left, here):
            when(here, lambda: ag_aside(g, k, h == 0, False))

        ag_each(g, h, act)

    def ag_wait(g):
        if g == C and nz > 1:
            pl.when(enc)(lambda: ag_wait_all(g))
        else:
            ag_wait_all(g)

    def ag_wait_all(g):
        for k in range(nz):
            slot = W[g].at[1 - y, chunk(k)]
            remote(slot, slot, o.gs.at[g, k], o.gy.at[g, k], beside).wait_recv()

    def ag_finish(g):
        for h in range(nz):

            def act(k, right, left, here):
                def go():
                    if nz > 1:
                        when(right, lambda: ag_right(g, k).wait_send())
                        when(left, lambda: ag_left(g, k).wait_send())
                    ag_aside(g, k, h == 0, True)

                when(here, go)

            ag_each(g, h, act)

    def own_copy(g):
        return pltpu.make_async_copy(shard[g], W[g].at[y, chunk(z)], o.oc_sem.at[g])

    def cross_part(k, part):
        start = k * chunk_rows + part * cross_rows
        return pl.ds(pl.multiple_of(start, 16), cross_rows)

    cross_own = pltpu.make_async_copy(o.sx, W[X].at[y, cross_part(z, 1)], o.oc_sem.at[X])
    cross_in = remote(
        o.sx, W[X].at[y, cross_part(z, 0)], o.xw.at[0], o.xw.at[1], across
    )
    cross_out = remote(o.xo, o.xi, o.xw.at[2], o.xw.at[3], across)


    def rs_y(r, k):
        g, at, width = REDUCE[r]
        cols = pl.ds(at, width)
        return remote(
            W[g].at[1 - y, chunk(k), cols],
            RY[g].at[chunk(k), cols],
            o.rs_s.at[r, k],
            o.rs_r.at[r, k],
            beside,
        )

    def rs_z(r, k):
        g, at, width = REDUCE[r]
        cols = pl.ds(at, width)
        away = lax.rem(z + nz - 1 - k, nz)
        return remote(
            RY[g].at[chunk(k), cols],
            RZ[g].at[away, :, cols],
            o.rz_s.at[r, k],
            o.rz_r.at[r, away],
            (p, k, t),
        )

    def rs_z_came(r, i):
        g, at, width = REDUCE[r]
        cols = pl.ds(at, width)
        remote(
            RY[g].at[chunk(z), cols],
            RZ[g].at[i, :, cols],
            o.rz_s.at[r, z],
            o.rz_r.at[r, i],
            beside,
        ).wait_recv()

    def rs_start(r):
        for i in range(nz):
            rs_y(r, lax.rem(z + 1 + i, nz)).start()

    def rs_mid(r, first=0, last=nz):
        g, at, width = REDUCE[r]
        cols = slice(at, at + width)

        @pl.loop(min(first, nz), min(last, nz))
        def _(i):
            k = lax.rem(z + 1 + i, nz)
            rs_y(r, k).wait_recv()
            start = pl.multiple_of(k * chunk_rows, 16)

            @pl.loop(0, chunk_rows // 32)
            def _(n):
                rows = pl.ds(pl.multiple_of(start + n * 32, 16), 32)
                both = W[g][y, rows, cols].astype(F32) + RY[g][rows, cols].astype(F32)
                RY[g][rows, cols] = both.astype(BF)

            if nz > 1:
                pl.when(i < nz - 1)(lambda: rs_z(r, k).start())

    def rs_end(r, put):
        g, at, width = REDUCE[r]
        cols = slice(at, at + width)
        for i in range(nz - 1):
            rs_z_came(r, i)
        start = pl.multiple_of(z * chunk_rows, 16)

        @pl.loop(0, chunk_rows // 32)
        def _(n):
            rows = pl.ds(pl.multiple_of(n * 32, 16), 32)
            total = RY[g][pl.ds(pl.multiple_of(start + n * 32, 16), 32), cols].astype(F32)
            for i in range(nz - 1):
                total = total + RZ[g][i, rows, cols].astype(F32)
            put(rows, total)

    def rs_sent(r):
        for i in range(nz):
            k = lax.rem(z + 1 + i, nz)
            rs_y(r, k).wait_send()
            if i < nz - 1:
                rs_z(r, k).wait_send()

    def rs_leave(r):
        g, at, width = REDUCE[r]
        out, buffer, first, into = LEAVE[r]
        return pltpu.make_async_copy(
            buffer.at[pl.ds(first, chunk_rows), pl.ds(into, width)],
            out.at[:, pl.ds(at, width)],
            o.lc.at[r],
        )

    def rs_out(r):
        g, at, width = REDUCE[r]
        out, buffer, first, into = LEAVE[r]
        if nz == 1:

            @pl.loop(0, chunk_rows // 32)
            def _(n):
                rows = pl.ds(pl.multiple_of(n * 32, 16), 32)
                out[rows, at : at + width] = RY[g][rows, at : at + width]

        else:

            def put(rows, total):
                buffer[pl.ds(pl.multiple_of(rows.start + first, 16), 32), into : into + width] = (
                    total
                )

            rs_end(r, put)
            rs_leave(r).start()
        rs_sent(r)


    def rows_sib(i, k, n):
        own, landing = ROWS[i]
        src = own.at[y] if n == 0 else landing.at[k]
        return remote(src, landing.at[k], o.qs.at[i, n], o.qr.at[i, n], sibling)

    def rows_beside(i, k):
        own, landing = ROWS[i]
        return remote(own.at[1 - y], landing.at[k], o.qs.at[i, 2], o.qr.at[i, 2], beside)

    def rows_own(i):
        own, landing = ROWS[i]
        return pltpu.make_async_copy(own.at[y], landing.at[t], o.ql.at[i])

    def rows_start(i):
        rows_own(i).start()
        rows_beside(i, t).start()
        rows_sib(i, t, 0).start()

    other = lax.rem(t + 2, 4)

    def rows_pass(i):
        rows_beside(i, other).wait_recv()
        rows_sib(i, other, 1).start()

    def rows_done(i):
        rows_own(i).wait()
        rows_sib(i, t, 0).wait()
        rows_sib(i, other, 1).wait()
        rows_beside(i, t).wait_send()

    def rows_join(i, out_ref):
        landing = ROWS[i][1]
        wide = 256

        @pl.loop(0, 2)
        def _(k):
            @pl.loop(0, D // wide)
            def _(n):
                cols = pl.ds(pl.multiple_of(n * wide, 128), wide)
                value = jnp.concatenate(
                    [landing[2 * k + j, :held, cols].astype(F32) for j in range(2)], axis=0
                )
                rows = pl.ds(pl.multiple_of(2 * k * held, 16), 2 * held)
                out_ref[rows, cols] = value.astype(out_ref.dtype)


    def home_copy(i):
        return remote(o.hs.at[i], o.hr.at[i], o.hx.at[i], o.hy.at[i], beside)

    def home_block(buffer, k):
        value = buffer[pl.ds(pl.multiple_of(k * held, 8), held), :]
        pad = o.hs.shape[1] - held
        return jnp.concatenate([value, jnp.zeros((pad, D), F32)], axis=0).astype(BF)

    def home_send(i, buffer):
        o.hs[i] = home_block(buffer, other)
        home_copy(i).start()

    home_out = (
        pltpu.make_async_copy(o.ho, o.oh.at[y], o.lh.at[0]),
        pltpu.make_async_copy(o.hr.at[0], o.oh.at[1 - y], o.lh.at[1]),
        pltpu.make_async_copy(
            o.gres.at[pl.ds(pl.multiple_of(t * held, 8), held)], o.gh.at[y], o.lh.at[2]
        ),
        pltpu.make_async_copy(o.ext.at[pl.ds(0, held)], o.gh.at[1 - y], o.lh.at[3]),
    )

    barrier = pltpu.get_barrier_semaphore()
    for g in (A, B, C):
        own_copy(g).start()
    when(dec, cross_own.start)
    for peer in (sibling, across, beside, skew):
        pl.semaphore_signal(barrier, inc=1, device_id=peer, device_id_type=MESH)
    for i in range(1, nz):
        pl.semaphore_signal(
            barrier, inc=1, device_id=(p, lax.rem(d + i, nz), t), device_id_type=MESH
        )
    pl.semaphore_wait(barrier, 4 + nz - 1)
    rows_start(0)
    when(enc, lambda: rows_start(2))
    own_copy(A).wait()
    ag_hop(A, 0)
    when(enc, cross_in.start)
    own_copy(B).wait()
    ag_hop(B, 0, False)
    when(enc, lambda: ag_side(B, 0))
    own_copy(C).wait()

    lane = lax.broadcasted_iota(jnp.int32, (1, 128), 1)
    lo = jnp.where(lane < 64, 1.0, 0.0).astype(BF)
    hi = jnp.where(lane < 64, 0.0, 1.0).astype(BF)

    def rows_loop(fn, step=RT):
        @pl.loop(0, L // step)
        def _(i):
            fn(pl.ds(pl.multiple_of(i * step, step), step))

    def half_rows(h):
        return pl.ds(pl.multiple_of(h * half, 16), half)

    def half_loop(h, fn):
        @pl.loop(0, half // RT)
        def _(i):
            fn(pl.ds(pl.multiple_of(h * half + i * RT, 16), RT))

    def halves(fn, ready=None, after=None):
        @pl.loop(0, 2)
        def _(i):
            h = lax.rem(core + i, 2)
            if ready is not None:
                ready(i, h)
            half_loop(h, fn)
            if after is not None:
                pl.when(i == 0)(after)

    def normed(v, gain_no):
        r = lax.rsqrt(jnp.mean(v * v, axis=-1, keepdims=True) + EPSILON)
        return (v * r * o.g[gain_no : gain_no + 1, :]).astype(BF)

    def norm_rows(x_ref, gain_no, out_ref):
        def one(rows):
            out_ref[rows, :] = normed(x_ref[rows, :].astype(F32), gain_no)

        rows_loop(one)

    def ex_copy(slot, h):
        rows = half_rows(h)
        return remote(
            o.exs.at[slot, rows], o.exr.at[slot, rows], o.ss.at[slot, h], o.rs.at[slot, h], sibling
        )

    def exchange(slot, fn):
        @pl.loop(0, 2)
        def _(i):
            h = lax.rem(1 - core + i, 2)
            rows = half_rows(h)
            o.exs[slot, rows, :] = fn(rows).astype(BF)
            ex_copy(slot, h).start()

    def arrived(slot):
        return lambda i, h: ex_copy(slot, h).wait()

    def ex_rows(slot, rows):
        return o.exs[slot, rows, :].astype(F32) + o.exr[slot, rows, :].astype(F32)

    def residual(slot, base_ref, put, after=None):
        def one(rows):
            put(rows, base_ref[rows, :].astype(F32) + ex_rows(slot, rows))

        halves(one, arrived(slot), after)

    def keep(ref, gain_no=None, normed_ref=None):
        def put(rows, value):
            ref[rows, :] = value
            if gain_no is not None:
                normed_ref[rows, :] = normed(value, gain_no)

        return put

    def norm_back(slot, x_ref, gain_no, put, after=None):
        o.dgacc[gain_no] = jnp.zeros((8, D), F32)

        def one(rows):
            dh = ex_rows(slot, rows)
            v = x_ref[rows, :].astype(F32)
            r = lax.rsqrt(jnp.mean(v * v, axis=-1, keepdims=True) + EPSILON)
            n = v * r
            dhg = dh * o.g[gain_no : gain_no + 1, :]
            mu = jnp.mean(dhg * n, axis=-1, keepdims=True)
            put(rows, r * (dhg - n * mu))
            o.dgacc[gain_no] += jnp.sum((dh * n).reshape(RT // 8, 8, D), axis=0)

        halves(one, arrived(slot), after)

    def split(a):
        return slice(a * hs, (a + 1) * hs)

    def both_shards(fn):
        @pl.loop(0, 2)
        def _(a):
            fn(a)

    def side_first(fn, r):
        @pl.loop(0, 2)
        def _(i):
            fn(lax.rem(1 - y + i, 2))
            if r is not None:
                pl.when(i == 0)(lambda: rs_start(r))

    def kv_project():
        def one(a):
            o.dkv[a] = dot(o.ns[...], W[A][a, :, at_kv:at_ext]).astype(BF)

        both_shards(one)
        for a in range(2):
            o.ks[:, split(a)] = o.dkv[a, :, :hs]
            o.vs[:, split(a)] = o.dkv[a, :, hs:]

    def pair_stack(block):
        return jnp.concatenate([block * lo, block * hi], axis=0)

    def pair_pick(stacked):
        return jnp.where(lane < 64, stacked[:qb_rows], stacked[qb_rows:])

    def attn_fwd(q_ref, mix_ref, mem, own, causal, hooks=()):
        @pl.loop(0, n_blk)
        def _(b):
            for i, hook in enumerate(hooks):
                pl.when(b == i)(hook)
            rows = pl.ds(pl.multiple_of(b * qb_rows, 16), qb_rows)
            wrows = pl.ds(pl.multiple_of(b * qb_rows, 16), win_w)
            sq = o.segq[rows, :]
            if mem:
                o.mm[...] = jnp.where(sq == o.srcseg[...], 0.0, NEG)
            if own:
                allowed = sq == o.segw[b]
                if causal:
                    qi = lax.broadcasted_iota(jnp.int32, (qb_rows, win_w), 0)
                    kj = lax.broadcasted_iota(jnp.int32, (qb_rows, win_w), 1)
                    allowed = allowed & (kj - HALO <= qi)
                o.mo[...] = jnp.where(allowed, 0.0, NEG)

            @pl.loop(0, n_pair)
            def _(j):
                cols = pl.ds(pl.multiple_of(j * 128, 128), 128)
                q2 = pair_stack(q_ref[rows, cols])
                parts = []
                if mem:
                    s = dot_nt(q2, o.ks[:, cols]).reshape(2, qb_rows, L)
                    parts.append(s + o.mm[...][None])
                if own:
                    s = dot_nt(q2, o.kp[wrows, cols]).reshape(2, qb_rows, win_w)
                    parts.append(s + o.tb[pl.ds(2 * j, 2)] + o.mo[...][None])
                top = [jnp.max(s, axis=-1, keepdims=True) for s in parts]
                top = functools.reduce(jnp.maximum, top)
                exps = [jnp.exp(s - top) for s in parts]
                total = sum(jnp.sum(e, axis=-1, keepdims=True) for e in exps)
                inv = 1.0 / total
                probs = [(e * inv).astype(BF).reshape(2 * qb_rows, -1) for e in exps]
                mixed = 0.0
                if mem:
                    o.pm[b * n_pair + j] = probs[0]
                    mixed = mixed + dot(probs[0], o.vs[:, cols])
                if own:
                    o.po[b * n_pair + j] = probs[-1]
                    mixed = mixed + dot(probs[-1], o.vp[wrows, cols])
                mix_ref[rows, cols] = pair_pick(mixed).astype(BF)

    def attn_back(q_ref, mix_ref, mem, own, hooks=()):
        if mem:
            o.dks[...] = jnp.zeros(o.dks.shape, F32)
            o.dvs[...] = jnp.zeros(o.dvs.shape, F32)
        if own:
            o.dkp[...] = jnp.zeros(o.dkp.shape, F32)
            o.dvp[...] = jnp.zeros(o.dvp.shape, F32)
            o.tb[...] = jnp.zeros(o.tb.shape, F32)

        @pl.loop(0, n_blk)
        def _(b):
            for i, hook in enumerate(hooks):
                pl.when(b == i)(hook)
            rows = pl.ds(pl.multiple_of(b * qb_rows, 16), qb_rows)
            wrows = pl.ds(pl.multiple_of(b * qb_rows, 16), win_w)

            @pl.loop(0, n_pair)
            def _(j):
                cols = pl.ds(pl.multiple_of(j * 128, 128), 128)
                q2 = pair_stack(q_ref[rows, cols])
                do2 = pair_stack(o.dmix[rows, cols])
                mix = mix_ref[rows, cols].astype(F32)
                delta = jnp.sum(
                    do2.astype(F32).reshape(2, qb_rows, 128) * mix[None], axis=-1, keepdims=True
                ).reshape(2 * qb_rows, 1)
                dq2 = 0.0
                if mem:
                    probs = o.pm[b * n_pair + j]
                    dp = dot_nt(do2, o.vs[:, cols])
                    ds = (probs.astype(F32) * (dp - delta)).astype(BF)
                    dq2 = dq2 + dot(ds, o.ks[:, cols])
                    o.dks[:, cols] += dot_tn(ds, q2)
                    o.dvs[:, cols] += dot_tn(probs, do2)
                if own:
                    probs = o.po[b * n_pair + j]
                    dp = dot_nt(do2, o.vp[wrows, cols])
                    ds = (probs.astype(F32) * (dp - delta)).astype(BF)
                    dq2 = dq2 + dot(ds, o.kp[wrows, cols])
                    o.dkp[wrows, cols] += dot_tn(ds, q2)
                    o.dvp[wrows, cols] += dot_tn(probs, do2)
                    o.tb[pl.ds(2 * j, 2)] += ds.astype(F32).reshape(2, qb_rows, win_w)
                o.dq[rows, cols] = (pair_pick(dq2) * (HD**-0.5)).astype(BF)

    def out_project(slot, mix_ref, weight_ref, at):
        exchange(
            slot,
            lambda rows: sum(
                dot_nt(mix_ref[rows, split(a)], weight_ref[a, :, at : at + hs]) for a in range(2)
            ),
        )

    def mix_grads(weight_ref, at):
        for a in range(2):
            o.dmix[:, split(a)] = dot(o.gb[...], weight_ref[a, :, at : at + hs]).astype(BF)

    fw = fs // 2

    def ff_half(n):
        a = n // 2
        return a, pl.ds(pl.multiple_of((n - 2 * a) * fw, 128), fw)

    def shard_cols(a):
        return slice(a * fs, (a + 1) * fs)

    def ff_fwd():
        ag_wait(B)

        @pl.loop(0, 4)
        def _(n):
            a, half_cols = ff_half(n)
            cols = pl.ds(pl.multiple_of(n * fw, 128), fw)
            o.pre[...] = dot(o.nc[...], W[B][a, :, half_cols])

            def one(rows):
                v = o.pre[rows, :]
                v2 = v * v
                th = jnp.tanh(0.7978845608028654 * v * (1.0 + 0.044715 * v2))
                cdf = 0.5 * (1.0 + th)
                slope = (0.5 * 0.7978845608028654) * v * (1.0 - th * th)
                o.hidden[rows, cols] = (v * cdf).astype(BF)
                o.gp[rows, cols] = (cdf + slope * (1.0 + (3 * 0.044715) * v2)).astype(BF)

            rows_loop(one, 32)

        ag_wait(C)
        when(dec, lambda: ag_also_hop(3))
        exchange(
            2,
            lambda rows: sum(dot_nt(o.hidden[rows, shard_cols(a)], W[C][a]) for a in range(2)),
        )

    def side_cols(a, width):
        return pl.ds(pl.multiple_of(a * width, 128), width)

    def ff_pre(n):
        a, half_cols = ff_half(n)
        cols = pl.ds(pl.multiple_of(n * fw, 128), fw)
        o.gp[:, cols] = (
            dot(o.gb[...], W[C][a, :, half_cols]) * o.gp[:, cols].astype(F32)
        ).astype(BF)

    def ff_out_weights():
        def one(a):
            W[C][a] = dot_tn(o.gb[...], o.hidden[:, side_cols(a, fs)]).astype(BF)

        side_first(one, RC)

    def ff_in_weights():
        def one(a):
            W[B][a] = dot_tn(o.nc[...], o.gp[:, side_cols(a, fs)]).astype(BF)

        side_first(one, RB)

    def ff_back():
        ag_finish(B)
        ag_finish(C)
        if nz > 1:
            when(dec, ag_also_sent)

        @pl.loop(0, 4)
        def _(n):
            ff_pre(n)

        exchange(
            0, lambda rows: sum(dot_nt(o.gp[rows, shard_cols(a)], W[B][a]) for a in range(2))
        )
        ff_out_weights()

        def put(rows, dv):
            new = o.gres[rows, :] + dv
            o.gres[rows, :] = new
            o.gb[rows, :] = new.astype(BF)

        norm_back(0, o.xlate, 1, put)

    def x_copy(way):
        rows = half_rows(core)
        return remote(
            o.xsend.at[rows], o.xbuf.at[rows], o.xss.at[way, 0], o.xrs.at[way, 0], across
        )

    def x_pass(way, h):
        rows = half_rows(h)
        return remote(
            o.xbuf.at[rows], o.xbuf.at[rows], o.xss.at[way, 1], o.xrs.at[way, 1], sibling
        )

    def x_halves(way, fn):
        x_copy(way).wait_recv()
        x_pass(way, core).start()

        def ready(i, h):
            pl.when(i == 1)(lambda: x_pass(way, h).wait_recv())

        halves(fn, ready)
        x_pass(way, core).wait_send()

    def kv_weights():
        def one(a):
            W[A][a, :, at_kv:at_ext] = dot_tn(o.ns[...], o.dkv[a]).astype(BF)

        side_first(one, RK)

    def dkv_grads():
        for a in range(2):
            o.dkv[a, :, :hs] = o.dks[:, split(a)].astype(BF)
            o.dkv[a, :, hs:] = o.dvs[:, split(a)].astype(BF)
        exchange(
            2,
            lambda rows: sum(
                dot_nt(o.dkv[a, rows, :], W[A][a, :, at_kv:at_ext]) for a in range(2)
            ),
        )

    rows_pass(0)
    when(enc, lambda: rows_pass(2))

    def first_cross():
        cross_own.wait()
        cross_in.wait_recv()
        ag_hop(X, 0)

    when(dec, first_cross)
    ag_hop(A, 1)
    ag_hop(C, 0, False)
    if STAGE:
        when(dec, lambda: ag_pass_on(A))
    ag_side(C, 0)
    ag_hop(A, 2)
    ag_hop(B, 1, False)
    if STAGE:
        when(dec, lambda: ag_pass_on(B))
    when(dec, lambda: ag_hop(X, 1))
    ag_hop(C, 1, False)
    if STAGE:
        when(dec, lambda: ag_pass_on(C))
    ag_hop(A, 3)
    when(dec, lambda: ag_hop(X, 2))
    rows_done(0)
    rows_join(0, o.x)
    when(dec, lambda: ag_hop(X, 3))

    when(dec, lambda: ag_side(B, 0))
    ag_side(B, 1)
    ag_side(C, 1)
    when(dec, lambda: rows_start(1))
    ag_wait(A)
    o.g[...] = W[A][0, :, at_ext:].astype(F32).T[:8]
    rel_lanes = [dot_tn(W[A][a, :, at_ext:], o.hot[...]) for a in range(2)]
    for h in range(2 * n_pair):
        a = h // (hs // HD)
        row = REL_AT + h - a * (hs // HD)
        line = rel_lanes[a][row : row + 1, :]
        o.tb[h] = pltpu.roll(
            jnp.broadcast_to(line, (qb_rows, win_w)), 0, 1, stride=1, stride_axis=0
        )
    pad = jnp.zeros((HALO, hc), BF)
    for ref in (o.kp, o.vp):
        ref[:HALO, :] = pad
        ref[HALO + L :, :] = pad
    norm_rows(o.x, 0, o.na)

    def project_own(a):
        o.dqkv[a] = dot(o.na[...], W[A][a, :, :at_o]).astype(BF)

    both_shards(project_own)
    for a in range(2):
        o.q[:, split(a)] = (o.dqkv[a, :, :hs] * (HD**-0.5)).astype(BF)
        o.kp[HALO : HALO + L, split(a)] = o.dqkv[a, :, hs : 2 * hs]
        o.vp[HALO : HALO + L, split(a)] = o.dqkv[a, :, 2 * hs :]
    ag_hop(B, 2)
    hooks = (
        lambda: ag_hop(C, 2),
        lambda: ag_hop(B, 3),
        lambda: ag_hop(C, 3),
    )

    @pl.when(enc)
    def _():
        rows_done(2)
        rows_join(2, o.nb)
        norm_rows(o.nb, 2, o.ns)
        kv_project()
        attn_fwd(o.q, o.mixa, True, True, False, hooks)

    @pl.when(dec)
    def _():
        attn_fwd(o.q, o.mixa, False, True, True, hooks)
        ag_also_hop(0)

    out_project(0, o.mixa, W[A], at_o)

    @pl.when(enc)
    def _():
        residual(0, o.x, keep(o.xlate, 1, o.nc))

    @pl.when(dec)
    def _():
        ag_wait(X)
        ag_finish(X)
        if STAGE:
            ag_relay(A).wait_send()
            ag_relay(B).wait_send()
            ag_relay(C).wait_send()

        def whole(a):
            for k in range(nz):
                for part in range(2):
                    at = part * (D // 2) + k * cross_rows
                    start = k * chunk_rows + part * cross_rows
                    o.xg[a, at : at + cross_rows, :] = W[X][a, start : start + cross_rows, :]

        both_shards(whole)
        o.g[3:4, :] = o.xg[0, :, 2 * hs :].astype(F32).T[:1]
        residual(0, o.x, keep(o.xmid, 3, o.nb))
        for a in range(2):
            r = dot(o.nb[...], o.xg[a, :, :hs]).astype(BF)
            o.qb[:, split(a)] = (r * (HD**-0.5)).astype(BF)

        def one(rows):
            o.ns[rows, :] = normed(o.xbuf[rows, :].astype(F32), 2)

        x_halves(0, one)
        kv_project()
        attn_fwd(o.qb, o.mixb, True, False, False)
        ag_also_hop(1)
        out_project(1, o.mixb, o.xg, hs)
        residual(1, o.xmid, keep(o.xlate, 1, o.nc))
        ag_also_hop(2)


    when(dec, lambda: rows_pass(1))
    ff_fwd()

    def put_out(rows, value):
        o.gres[rows, :] = value
        o.xsend[rows, :] = value.astype(BF)

    residual(2, o.xlate, put_out, lambda: pl.when(enc)(lambda: x_copy(0).start()))
    when(enc, lambda: rows_start(1))
    home_send(0, o.gres)
    o.ho[...] = home_block(o.gres, t)
    home_out[0].start()
    ag_finish(A)
    when(enc, lambda: rows_pass(1))
    rows_done(1)
    rows_join(1, o.gres)

    @pl.when(enc)
    def _():
        x_copy(0).wait_send()

        def one(rows):
            value = o.gres[rows, :] + o.xbuf[rows, :].astype(F32)
            o.gres[rows, :] = value
            o.gb[rows, :] = value.astype(BF)

        x_halves(1, one)

    when(dec, lambda: rows_join(1, o.gb))


    ff_back()

    @pl.when(dec)
    def _():
        mix_grads(o.xg, hs)
        attn_back(o.qb, o.mixb, True, False)
        dkv_grads()
        exchange(
            1, lambda rows: sum(dot_nt(o.dq[rows, split(a)], o.xg[a, :, :hs]) for a in range(2))
        )

        def put_source(rows, dv):
            o.xsend[rows, :] = dv.astype(BF)

        norm_back(2, o.xbuf, 2, put_source, lambda: x_copy(1).start())
        rs_mid(RC, 0, 2)

        def put_mid(rows, dv):
            new = o.gres[rows, :] + dv
            o.gres[rows, :] = new
            o.xbuf[rows, :] = new.astype(BF)

        norm_back(1, o.xmid, 3, put_mid)
        line = jnp.sum(o.dgacc[3], axis=0, keepdims=True)
        tall = jnp.broadcast_to(line, (EXT, D)).T.astype(BF)
        for a in range(2):
            full = jnp.concatenate(
                [
                    dot_tn(o.nb[...], o.dq[:, split(a)]).astype(BF),
                    dot_tn(o.gb[...], o.mixb[:, split(a)]).astype(BF),
                    tall,
                ],
                axis=1,
            )
            for k in range(nz):
                for part in range(2):
                    at = part * (D // 2) + k * cross_rows
                    to = k * chunk_rows + part * cross_rows
                    W[X][a, to : to + cross_rows, :] = full[at : at + cross_rows]
        rs_start(RX)
        x_copy(1).wait_send()
        o.gb[...] = o.xbuf[...]

    ff_in_weights()
    mix_grads(W[A], at_o)
    for a in range(2):
        W[A][a, :, at_o : at_o + hs] = dot_tn(o.gb[...], o.mixa[:, split(a)]).astype(BF)
    steps = tuple(functools.partial(rs_mid, RC, i, i + 1) for i in range(3))

    @pl.when(enc)
    def _():
        attn_back(o.q, o.mixa, True, True, steps)
        dkv_grads()

    @pl.when(dec)
    def _():
        attn_back(o.q, o.mixa, False, True)
        rs_mid(RC, 2, 3)

    kv_weights()
    rs_mid(RC, 3)
    for a in range(2):
        o.dqkv[a, :, :hs] = o.dq[:, split(a)]
        o.dqkv[a, :, hs : 2 * hs] = o.dkp[HALO : HALO + L, split(a)].astype(BF)
        o.dqkv[a, :, 2 * hs :] = o.dvp[HALO : HALO + L, split(a)].astype(BF)
    last_slot = 1 - p
    exchange(
        last_slot,
        lambda rows: sum(dot_nt(o.dqkv[a, rows, :], W[A][a, :, :at_o]) for a in range(2)),
    )

    def own_weights(a):
        W[A][a, :, :at_o] = dot_tn(o.na[...], o.dqkv[a]).astype(BF)

    side_first(own_weights, RQ)

    @pl.when(enc)
    def _():
        def put_source(rows, dv):
            pass

        norm_back(2, o.nb, 2, put_source)
        rs_mid(RB, 0, 2)

    heads = 2 * n_pair
    acc = jnp.zeros((heads * 8, win_w), F32)
    for k in range(qb_rows // 8):
        part = o.tb[:, 8 * k : 8 * k + 8, :].reshape(heads * 8, win_w)
        acc = acc + (part if k == 0 else pltpu.roll(part, win_w - 8 * k, 1))
    sub = lax.rem(lax.broadcasted_iota(jnp.int32, (heads * 8, win_w), 0), 8)
    diag = jnp.zeros((heads * 8, win_w), F32)
    for k in range(8):
        turned = acc if k == 0 else pltpu.roll(acc, win_w - k, 1)
        diag = diag + jnp.where(sub == k, turned, 0.0)
    lines = jnp.sum(diag.reshape(heads, 8, win_w), axis=1)

    def put_in(rows, dv):
        o.gres[rows, :] = o.gres[rows, :] + dv

    norm_back(last_slot, o.x, 0, put_in)
    home_send(1, o.gres)
    home_out[2].start()
    per = hs // HD
    for a in range(2):
        o.ext[...] = jnp.zeros(o.ext.shape, F32)
        for k in range(3):
            o.ext[k : k + 1, :] = jnp.sum(o.dgacc[k], axis=0, keepdims=True)
        tall = o.ext[...].T
        o.lines[...] = jnp.zeros((EXT, win_w), F32)
        o.lines[REL_AT : REL_AT + per, :] = lines[per * a : per * (a + 1), :]
        whole = o.lines[...]
        high = whole.astype(BF)
        low = (whole - high.astype(F32)).astype(BF)
        tall = tall + dot_nt(o.hot[...], high) + dot_nt(o.hot[...], low)
        W[A][a, :, at_ext:] = tall.astype(BF)
    rs_start(RG)
    home_copy(0).wait()
    home_out[1].start()
    when(enc, lambda: rs_mid(RB, 2))
    when(dec, lambda: rs_mid(RB))
    rs_mid(RK)
    rs_out(RC)

    @pl.when(dec)
    def _():
        rs_mid(RX)

    rs_mid(RQ)
    rs_out(RB)
    rs_mid(RG)
    rs_out(RK)

    @pl.when(dec)
    def _():
        def put(rows, total):
            o.xt[rows, :] = total

        rs_end(RX, put)
        rs_sent(RX)
        o.xo[...] = o.xt[:cross_rows, :]
        cross_out.start()
        o.ox[...] = o.xt[cross_rows:, :].astype(o.ox.dtype)
        cross_out.wait_send()

    @pl.when(enc)
    def _():
        cross_in.wait_send()
        cross_out.wait_recv()
        o.ox[...] = o.xi[...].astype(o.ox.dtype)

    home_copy(1).wait()
    o.ext[...] = o.hr[1].astype(F32)
    home_out[3].start()
    rs_out(RQ)
    rs_out(RG)
    for copy in home_out:
        copy.wait()
    if nz > 1:
        for r in LEAVE:
            rs_leave(r).wait()


def run_kernel(dims, given):
    L, D, hs, fs, nz, qb_rows, win_w = dims
    hc, fc = 2 * hs, 2 * fs
    n_blk, n_pair = L // qb_rows, hc // 128
    LP = L + 2 * HALO
    LBP = -(-(L // 4) // 16) * 16
    CR = D // nz
    widths = dict(a=6 * hs + EXT, b=fs, c=fs, x=2 * hs + EXT)
    S = jax.ShapeDtypeStruct
    SUM = F32 if nz > 1 else BF
    outs = dict(
        oh=S((2, LBP, D), BF),
        gh=S((2, L // 4, D), F32),
        oa=S((CR, widths["a"]), SUM),
        ob=S((CR, widths["b"]), SUM),
        oc=S((CR, widths["c"]), SUM),
        ox=S((CR // 2, widths["x"]), SUM),
    )
    V = pltpu.VMEM
    LD, LH, LF = (L, D), (L, hc), (L, fc)
    scratch = dict(
        na=V(LD, BF), ns=V(LD, BF), nb=V(LD, BF), nc=V(LD, BF),
        xmid=V(LD, F32), xlate=V(LD, F32), gres=V(LD, F32),
        q=V(LH, BF), kp=V((LP, hc), BF), vp=V((LP, hc), BF), ks=V(LH, BF), vs=V(LH, BF),
        qb=V(LH, BF), mixa=V(LH, BF), mixb=V(LH, BF),
        pm=V((n_blk * n_pair, 2 * qb_rows, L), BF), po=V((n_blk * n_pair, 2 * qb_rows, win_w), BF),
        hidden=V(LF, BF), gp=V(LF, BF), pre=V((L, fs // 2), F32),
        tb=V((2 * n_pair, qb_rows, win_w), F32),
        mm=V((qb_rows, L), F32), mo=V((qb_rows, win_w), F32),
        dmix=V(LH, BF), dq=V(LH, BF), dqkv=V((2, L, 3 * hs), BF), dkv=V((2, L, 2 * hs), BF),
        dkp=V((LP, hc), F32), dvp=V((LP, hc), F32), dks=V(LH, F32), dvs=V(LH, F32),
        gb=V(LD, BF), xbuf=V(LD, BF), xsend=V(LD, BF),
        exs=V((3, L, D), BF), exr=V((3, L, D), BF), dgacc=V((4, 8, D), F32),
        g=V((8, D), F32), ext=V((LBP, D), F32), lines=V((EXT, win_w), F32),
        x=V(LD, BF), xq=V((4, LBP, D), BF), cq=V((4, LBP, D), BF), mq=V((4, LBP, D), BF),
        hs=V((2, LBP, D), BF), hr=V((2, LBP, D), BF), ho=V((LBP, D), BF),
        xg=V((2, D, widths["x"]), BF), xt=V((CR, widths["x"]), F32),
        xo=V((CR // 2, widths["x"]), F32), xi=V((CR // 2, widths["x"]), F32),
    )
    for g, width in widths.items():
        scratch["w" + g] = V((2, D, width), BF)
        scratch["y" + g] = V((D, width), BF)
        scratch["z" + g] = V((nz - 1, CR, width) if nz > 1 else (1, 16, width), BF)
    sem = pltpu.SemaphoreType.DMA
    scratch.update(ss=sem((3, 2)), rs=sem((3, 2)), gd=sem((3, 3)), ga=sem((2, nz)), gb2=sem((nz,)), xss=sem((2, 2)), xrs=sem((2, 2)))
    scratch.update(xw=sem((4,)), oc_sem=sem((4,)), lc=sem((6,)), lh=sem((4,)))
    scratch.update(qs=sem((3, 3)), qr=sem((3, 3)), ql=sem((3,)), hx=sem((2,)), hy=sem((2,)))
    for name in ("gr", "gl", "gs", "gz", "gy"):
        scratch[name] = sem((4, nz))
    for name in ("rs_s", "rs_r", "rz_s", "rz_r"):
        scratch[name] = sem((6, nz))
    spec = pl.BlockSpec(memory_space=pltpu.VMEM)
    far = pl.BlockSpec(memory_space=pl.ANY)
    names = list(given) + list(outs) + list(scratch)
    FAR = ["sa", "sb", "sc", "sx", "xs", "cs", "ms", "oh", "gh"]
    if nz > 1:
        FAR += ["oa", "ob", "oc"]
    return pl.pallas_call(
        functools.partial(kernel, dims, names),
        out_shape=list(outs.values()),
        in_specs=[far if name in FAR else spec for name in given],
        out_specs=[far if name in FAR else spec for name in outs],
        scratch_shapes=list(scratch.values()),
        compiler_params=pltpu.CompilerParams(
            collective_id=0, has_side_effects=True, vmem_limit_bytes=63 << 20
        ),
        name="layers",
    )(*given.values())


def prep_kernel(dims, n_dp, names, *refs):
    L, D, hs, fs, nz, qb_rows, win_w = dims
    o = Refs()
    for name, ref in zip(names, refs, strict=True):
        setattr(o, name, ref)
    section = lax.axis_index("pipe")
    y = lax.axis_index("tensor") // 2
    rows = D // n_dp
    held = L // 4
    for raw, out in ((o.li, o.xs), (o.co, o.cs)):
        o.tmp[...] = raw[...].astype(F32)
        pad = jnp.zeros((out.shape[1] - held, D), F32)
        for r in range(2):
            out[r] = jnp.concatenate([o.tmp[:, r, :], pad], axis=0).astype(BF)
    for i in range(3):
        o.sa[:, i * hs : (i + 1) * hs] = o.qkv[i]
    o.sa[:, 3 * hs : 4 * hs] = o.so[...].astype(F32).T.astype(BF)
    for i in range(2):
        o.kvt[...] = o.kv[...].astype(F32)
        o.sa[:, (4 + i) * hs : (5 + i) * hs] = o.kvt[:, i, :].astype(BF)
    n_gain = o.gain.shape[0]
    o.ext[...] = jnp.zeros(o.ext.shape, F32)
    o.ext[:n_gain, :rows] = o.gain[...].astype(F32)
    tall = o.ext[...].T
    o.wide[...] = tall
    nb_rows, heads = o.rel.shape
    o.wide[:nb_rows, REL_AT : REL_AT + heads] = o.rel[...].astype(F32)
    o.sa[:, 6 * hs :] = o.wide[:rows, :].astype(BF)
    o.sx[:, :hs] = o.cq[...]
    o.sx[:, hs : 2 * hs] = o.cw[...].astype(F32).T.astype(BF)
    half = o.cg.shape[1]
    o.ext[...] = jnp.zeros(o.ext.shape, F32)
    o.ext[:1, :half] = o.cg[...].astype(F32)
    o.wide[...] = o.ext[...].T
    o.sx[:, 2 * hs :] = o.wide[:half, :].astype(BF)
    own = o.seg[section, pl.ds(y, 1), :]
    first = o.seg[0, pl.ds(y, 1), :]
    o.segq[...] = jnp.broadcast_to(own.astype(F32), (8, L)).T[:, :1].astype(jnp.int32)
    slots = lax.broadcasted_iota(jnp.int32, (1, L), 1).astype(F32)
    slots = jnp.floor((slots + 0.5) * (1.0 / MEM)).astype(jnp.int32)
    o.srcseg[...] = jnp.where(section == 0, slots, first)
    o.line[...] = jnp.full(o.line.shape, -1, jnp.int32)
    o.line[:, HALO : HALO + L] = own
    for b in range(L // qb_rows):
        o.segw[b] = o.line[:, b * qb_rows : b * qb_rows + win_w]
    at = lax.broadcasted_iota(jnp.int32, (rows, win_w), 0)
    for k in range(n_dp):
        same = (at < nb_rows) & (o.win[...] == at + k * nb_rows)
        o.hotf[k * rows : (k + 1) * rows, :] = jnp.where(same, 1.0, 0.0)
    o.hot[...] = o.hotf[...].astype(BF)


def run_prep(dims, n_dp, given):
    L, D, hs, fs, nz, qb_rows, win_w = dims
    rows, held = D // n_dp, L // 4
    LBP = -(-held // 16) * 16
    S = jax.ShapeDtypeStruct
    outs = dict(
        xs=S((2, LBP, D), BF),
        cs=S((2, LBP, D), BF),
        sa=S((rows, 6 * hs + EXT), BF),
        sx=S((rows // 2, 2 * hs + EXT), BF),
        segq=S((L, 1), jnp.int32),
        segw=S((L // qb_rows, 1, win_w), jnp.int32),
        srcseg=S((1, L), jnp.int32),
        hot=S((D, win_w), BF),
    )
    V = pltpu.VMEM
    up = -(-rows // 128) * 128
    scratch = dict(
        tmp=V((held, 2, D), F32),
        kvt=V((rows, 2, hs), F32),
        ext=V((EXT, up), F32),
        wide=V((up, EXT), F32),
        line=V((1, L + 2 * HALO), jnp.int32),
        hotf=V((D, win_w), F32),
    )
    spec = pl.BlockSpec(memory_space=pltpu.VMEM)
    names = list(given) + list(outs) + list(scratch)
    return pl.pallas_call(
        functools.partial(prep_kernel, dims, n_dp, names),
        out_shape=list(outs.values()),
        in_specs=[spec] * len(given),
        out_specs=[spec] * len(outs),
        scratch_shapes=list(scratch.values()),
        compiler_params=pltpu.CompilerParams(vmem_limit_bytes=60 << 20),
        name="prep",
    )(*given.values())


def finish_kernel(dims, names, *refs):
    L, D, hs, fs, nz, qb_rows, win_w = dims
    o = Refs()
    for name, ref in zip(names, refs, strict=True):
        setattr(o, name, ref)
    o.ffi[...] = o.gb[...]
    o.ffo[...] = o.gc[...]
    for r in range(2):
        o.gin[:, r, :] = o.gh[r]
        o.tmp[:, r, :] = o.oh[r, : L // 4].astype(F32)
    o.out[...] = o.tmp[...].astype(BF)
    for i in range(3):
        o.qkv[i] = o.ga[:, i * hs : (i + 1) * hs]
    o.so[...] = o.ga[:, 3 * hs : 4 * hs].T
    for i in range(2):
        o.kv[:, i, :] = o.ga[:, (4 + i) * hs : (5 + i) * hs]
    ext = o.ga[:, 6 * hs :].T
    for i in range(o.gain.shape[0]):
        o.gain[i] = ext[i : i + 1]
    heads, _, nb_rows = o.rel.shape
    for i in range(heads):
        o.rel[i] = ext[REL_AT + i : REL_AT + i + 1, :nb_rows]
    o.cq[...] = o.gx[:, :hs]
    o.co[...] = o.gx[:, hs : 2 * hs].T
    o.cg[...] = o.gx[:, 2 * hs :].T[:1]


def run_finish(dims, rel_shape, sums):
    L, D, hs, fs, nz, qb_rows, win_w = dims
    rows = sums[2].shape[0]
    held = L // 4
    S = jax.ShapeDtypeStruct
    outs = dict(
        out=S((held, 2, D), BF),
        gin=S((held, 2, D), F32),
        qkv=S((3, rows, hs), F32),
        so=S((hs, rows), F32),
        kv=S((rows, 2, hs), F32),
        rel=S((rel_shape[1], 1, rel_shape[0]), F32),
        gain=S((3, 1, rows), F32),
        cq=S((rows // 2, hs), F32),
        co=S((hs, rows // 2), F32),
        cg=S((1, rows // 2), F32),
        ffi=S((rows, fs), F32),
        ffo=S((rows, fs), F32),
    )
    spec = pl.BlockSpec(memory_space=pltpu.VMEM)
    return pl.pallas_call(
        functools.partial(
            finish_kernel, dims, ["oh", "gh", "ga", "gb", "gc", "gx", *outs, "tmp"]
        ),
        out_shape=list(outs.values()),
        in_specs=[spec] * 6,
        out_specs=[spec] * len(outs),
        scratch_shapes=[pltpu.VMEM((held, 2, D), F32)],
        compiler_params=pltpu.CompilerParams(vmem_limit_bytes=60 << 20),
        name="finish",
    )(*sums)


def body(
    layer_inputs,
    segment_ids,
    slot_ids,
    memory_table,
    buckets,
    self_qkv,
    self_out,
    source_kv,
    ff_in,
    ff_out,
    rel_bias,
    gains,
    cross_query,
    cross_out,
    cross_gain,
    cotangents,
):
    nt = lax.axis_size("tensor")
    n_dp = lax.axis_size("dp")
    assert nt == 4 and layer_inputs.shape[2] == 2
    D = layer_inputs.shape[3]
    L = segment_ids.shape[2]
    hs = self_qkv.shape[3]
    fs = ff_in.shape[2]
    qb_rows, win_w = 160, 256
    rows = D // n_dp
    nz = n_dp if (rows // 2) % 32 == 0 else 1
    dims = (L, D, hs, fs, nz, qb_rows, win_w)
    held = L // nt
    fill = -(-held // 16) * 16 - held
    ids = jnp.pad(slot_ids.T, ((0, 0), (0, fill)))
    ms = memory_table.at[ids].get(mode="promise_in_bounds")
    window = jnp.pad(
        buckets[L - HALO : L + HALO], (0, win_w - 2 * HALO), constant_values=-1
    )
    prepared = run_prep(
        dims,
        n_dp,
        dict(
            li=layer_inputs[0],
            co=cotangents[0],
            qkv=self_qkv[0].transpose(1, 0, 2),
            so=self_out[0],
            kv=source_kv[0],
            gain=gains[0],
            rel=rel_bias[0],
            cq=cross_query,
            cw=cross_out,
            cg=cross_gain[None],
            seg=segment_ids,
            win=window[None],
        ),
    )
    xs, cs, sa, sx, segq, segw, srcseg, hot = prepared
    shards = [sa, ff_in[0], ff_out[0].T, sx]
    if nz != n_dp:
        shards = [lax.all_gather(shard, "dp", axis=0, tiled=True) for shard in shards]
    given = dict(
        xs=xs, cs=cs, ms=ms, segq=segq, segw=segw, srcseg=srcseg, hot=hot,
        sa=shards[0], sb=shards[1], sc=shards[2], sx=shards[3],
    )
    oh, gh, *sums = run_kernel(dims, given)
    if nz != n_dp:
        sums = [
            lax.psum_scatter(full, "dp", scatter_dimension=0, tiled=True).astype(F32)
            for full in sums
        ]
    done = run_finish(dims, rel_bias.shape[1:], [oh, gh, *sums])
    out, gin, qkv, so, kv, rel, gain, cq, co, cg, ff_i, ff_o = done
    return (
        out[None],
        gin[None],
        qkv.transpose(1, 0, 2)[None],
        so[None],
        kv[None],
        ff_i[None],
        ff_o.T[None],
        rel.transpose(1, 2, 0),
        gain.transpose(1, 0, 2),
        cq,
        co,
        cg[0],
    )


def solution(mesh):
    placed = (
        P("pipe", "tensor", "dp", None),
        P(None, "dp", None),
        P("tensor", "dp"),
        P(),
        P(),
        P("pipe", "dp", None, "tensor"),
        P("pipe", "tensor", "dp"),
        P("pipe", "dp", None, "tensor"),
        P("pipe", "dp", "tensor"),
        P("pipe", "tensor", "dp"),
        P("pipe", "dp", "tensor"),
        P("pipe", None, "dp"),
        P(("pipe", "dp"), "tensor"),
        P("tensor", ("pipe", "dp")),
        P(("pipe", "dp")),
        P("pipe", "tensor", "dp", None),
    )
    return jax.shard_map(
        body,
        mesh=mesh,
        in_specs=placed,
        out_specs=(
            P("pipe", "tensor", "dp", None),
            P("pipe", "tensor", "dp", None),
            P("pipe", "dp", None, "tensor"),
            P("pipe", "tensor", "dp"),
            P("pipe", "dp", None, "tensor"),
            P("pipe", "dp", "tensor"),
            P("pipe", "tensor", "dp"),
            P("pipe", "dp", "tensor"),
            P("pipe", None, "dp"),
            P(("pipe", "dp"), "tensor"),
            P("tensor", ("pipe", "dp")),
            P(("pipe", "dp")),
        ),
        check_vma=False,
    )
```

```python
import functools

import jax
import jax.numpy as jnp
from jax import lax
from jax.experimental import pallas as pl
from jax.experimental.pallas import tpu as pltpu
from jax.sharding import PartitionSpec as P

HD = 64
NB = 32
MEM = 20
HALO = 48
TILE = 16
CROSS_AT = 3
REL_AT = 8
PIECE = 256
EPSILON = 1e-06
NEG = -1000000000.0
BF = jnp.bfloat16
F32 = jnp.float32
MESH = pl.DeviceIdType.MESH
RT = 48


def dot(a, b):
    return lax.dot_general(a, b, (((1,), (0,)), ((), ())), preferred_element_type=F32)


def dot_nt(a, b):
    return lax.dot_general(a, b, (((1,), (1,)), ((), ())), preferred_element_type=F32)


def dot_tn(a, b):
    return lax.dot_general(a, b, (((0,), (0,)), ((), ())), preferred_element_type=F32)


class Refs:
    pass


def kernel(dims, names, *refs):
    L, D, hs, fs, nz, qb_rows, win_w = dims
    hc, fc = 2 * hs, 2 * fs
    at_o, at_kv, at_ext = 3 * hs, 4 * hs, 6 * hs
    chunk_rows = D // nz
    cross_rows = chunk_rows // 2
    n_blk = L // qb_rows
    n_pair = hc // 128
    o = Refs()
    for name, ref in zip(names, refs, strict=True):
        setattr(o, name, ref)
    p = lax.axis_index("pipe")
    d = lax.axis_index("dp")
    t = lax.axis_index("tensor")
    enc, dec = p == 0, p == 1
    core = lax.rem(t, 2)
    y = t // 2
    z = d if nz > 1 else 0
    skew = (1 - p, d, lax.rem(t + 2, 4))
    sibling = (p, d, t + 1 - 2 * core)
    across = (1 - p, d, t)
    beside = (p, d, lax.rem(t + 2, 4))
    half = L // 2
    held = L // 4
    A, B, C, X = range(4)
    shard = (o.sa, o.sb, o.sc, o.sx)
    W = (o.wa, o.wb, o.wc, o.wx)
    RY = (o.ya, o.yb, o.yc, o.yx)
    RZ = (o.za, o.zb, o.zc, o.zx)
    RB, RC, RX, RQ, RK = range(5)
    REDUCE = {
        RB: (B, 0, fs),
        RC: (C, 0, fs),
        RX: (X, 0, 2 * hs),
        RQ: (A, 0, at_kv),
        RK: (A, at_kv, 2 * hs),
    }
    LEAVE = {
        RB: (o.ob, o.xlate, 0, 0),
        RC: (o.oc, o.xmid, 0, 0),
        RQ: (o.oa, o.xmid, chunk_rows, 0),
        RK: (o.oa, o.xlate, chunk_rows, 0),
    }
    STAGE = {} if nz == 1 else {
        A: o.hidden.at[pl.ds(0, chunk_rows), pl.ds(0, 6 * hs)],
        B: o.gp.at[pl.ds(0, chunk_rows), pl.ds(0, fs)],
        C: o.gp.at[pl.ds(0, chunk_rows), pl.ds(fs, fs)],
    }
    ROWS = ((o.xs, o.xq), (o.cs, o.cq), (o.ms, o.mq))

    def chunk(k):
        return pl.ds(pl.multiple_of(k * chunk_rows, 16), chunk_rows)

    def remote(src, dst, send, recv, device):
        return pltpu.make_async_remote_copy(
            src_ref=src,
            dst_ref=dst,
            send_sem=send,
            recv_sem=recv,
            device_id=device,
            device_id_type=MESH,
        )


    def ag_right(g, k):
        slot = W[g].at[y, chunk(k)]
        return remote(slot, slot, o.gr.at[g, k], o.gz.at[g, k], (p, d + 1, t))

    def ag_left(g, k):
        slot = W[g].at[y, chunk(k)]
        return remote(slot, slot, o.gl.at[g, k], o.gz.at[g, k], (p, d - 1, t))

    def ag_beside(g, k):
        slot = W[g].at[y, chunk(k)]
        return remote(slot, slot, o.gs.at[g, k], o.gy.at[g, k], beside)

    def ag_came(g, k):
        slot = W[g].at[y, chunk(k)]
        remote(slot, slot, o.gr.at[g, k], o.gz.at[g, k], beside).wait_recv()

    def ag_each(g, h, act):
        if h == 0:
            act(z, z + 1 < nz, z > 0, True)
        else:
            act(z - h, z + 1 < nz, False, z - h >= 0)
            act(z + h, False, z > 0, z + h < nz)

    def when(cond, fn):
        if cond is True:
            fn()
        elif cond is not False:
            pl.when(cond)(fn)


    def ag_skew(g):
        return remote(W[g].at[y, chunk(z)], STAGE[g], o.gd.at[g, 0], o.gd.at[g, 1], skew)

    def ag_relay(g):
        slot = W[g].at[1 - y, chunk(z)]
        return remote(STAGE[g], slot, o.gd.at[g, 2], o.gy.at[g, z], across)

    def ag_pass_on(g):
        ag_skew(g).wait_recv()
        ag_relay(g).start()

    def ag_aside(g, k, own, wait):
        act = (lambda c: c.wait_send()) if wait else (lambda c: c.start())
        if own and g in STAGE:
            pl.when(enc)(lambda: act(ag_skew(g)))
            pl.when(dec)(lambda: act(ag_beside(g, k)))
        elif not own and g == C:
            pl.when(enc)(lambda: act(ag_beside(g, k)))
        else:
            act(ag_beside(g, k))


    def ag_also(k, way):
        slot = W[C].at[1 - y, chunk(k)]
        return remote(slot, slot, o.ga.at[way, k], o.gb2.at[k], (p, d + (1, -1)[way], t))

    def ag_also_hop(h):
        if h >= nz or nz == 1:
            return

        def act(k, right, left, here):
            def go():
                slot = W[C].at[1 - y, chunk(k)]
                if h == 0:
                    remote(slot, slot, o.gs.at[C, k], o.gy.at[C, k], beside).wait_recv()
                else:
                    remote(slot, slot, o.ga.at[0, k], o.gb2.at[k], beside).wait_recv()
                when(right, lambda: ag_also(k, 0).start())
                when(left, lambda: ag_also(k, 1).start())

            when(here, go)

        ag_each(C, h, act)

    def ag_also_sent():
        for h in range(nz):

            def act(k, right, left, here):
                def go():
                    when(right, lambda: ag_also(k, 0).wait_send())
                    when(left, lambda: ag_also(k, 1).wait_send())

                when(here, go)

            ag_each(C, h, act)

    def ag_hop(g, h, aside=True):
        if h >= nz:
            return

        def act(k, right, left, here):
            def go():
                if h > 0:
                    ag_came(g, k)
                if nz > 1:
                    when(right, lambda: ag_right(g, k).start())
                    when(left, lambda: ag_left(g, k).start())
                if aside:
                    ag_aside(g, k, h == 0, False)

            when(here, go)

        ag_each(g, h, act)

    def ag_side(g, h):
        if h >= nz:
            return

        def act(k, right, left, here):
            when(here, lambda: ag_aside(g, k, h == 0, False))

        ag_each(g, h, act)

    def ag_wait(g):
        if g == C and nz > 1:
            pl.when(enc)(lambda: ag_wait_all(g))
        else:
            ag_wait_all(g)

    def ag_wait_all(g):
        for k in range(nz):
            slot = W[g].at[1 - y, chunk(k)]
            remote(slot, slot, o.gs.at[g, k], o.gy.at[g, k], beside).wait_recv()

    def ag_finish(g):
        for h in range(nz):

            def act(k, right, left, here):
                def go():
                    if nz > 1:
                        when(right, lambda: ag_right(g, k).wait_send())
                        when(left, lambda: ag_left(g, k).wait_send())
                    ag_aside(g, k, h == 0, True)

                when(here, go)

            ag_each(g, h, act)

    def own_copy(g):
        return pltpu.make_async_copy(shard[g], W[g].at[y, chunk(z)], o.oc_sem.at[g])

    def cross_part(k, part):
        start = k * chunk_rows + part * cross_rows
        return pl.ds(pl.multiple_of(start, 16), cross_rows)

    cross_own = pltpu.make_async_copy(o.sx, W[X].at[y, cross_part(z, 1)], o.oc_sem.at[X])
    cross_in = remote(
        o.sx, W[X].at[y, cross_part(z, 0)], o.xw.at[0], o.xw.at[1], across
    )
    cross_out = remote(o.xo, o.xi, o.xw.at[2], o.xw.at[3], across)


    nb_each = NB // nz
    n_rel = hs // HD

    def others(fn):
        if nz > 1:

            @pl.loop(1, nz)
            def _(i):
                fn(lax.rem(z + i, nz))

    def tile_z(a, k, to, sems):
        slot = o.m.at[a, k]
        return remote(slot, slot, o.mt.at[sems, to], o.mt.at[sems + 1, k], (p, to, t))

    def tile_beside(k):
        slot = o.m.at[y, k]
        return remote(slot, slot, o.mt.at[2, k], o.mt.at[3, k], beside)

    def tile_across():
        return remote(o.m.at[y, z], o.m.at[2, z], o.mx.at[0], o.mx.at[1], across)

    def tiles_start():
        o.m[y, z] = o.sm[...]

        @pl.when(enc)
        def _():
            o.m[2] = jnp.zeros(o.m.shape[1:], BF)

        others(lambda k: tile_z(y, z, k, 0).start())
        tile_beside(z).start()
        when(enc, lambda: tile_across().start())

    def tiles_pass():
        def one(k):
            tile_z(y, k, k, 0).wait_recv()
            tile_beside(k).start()

        others(one)

        @pl.when(dec)
        def _():
            tile_across().wait_recv()
            others(lambda k: tile_z(2, z, k, 4).start())

    def tiles_done():
        @pl.loop(0, nz)
        def _(k):
            slot = o.m.at[1 - y, k]
            remote(slot, slot, o.mt.at[2, k], o.mt.at[3, k], beside).wait_recv()
            tile_beside(k).wait_send()

        others(lambda k: tile_z(y, z, k, 0).wait_send())
        when(enc, lambda: tile_across().wait_send())

        @pl.when(dec)
        def _():
            others(lambda k: tile_z(2, k, k, 4).wait_recv())
            others(lambda k: tile_z(2, z, k, 4).wait_send())

        o.rl[...] = jnp.zeros(o.rl.shape, F32)
        for k in range(nz):
            block = o.m[y, k].astype(F32)
            o.g[:CROSS_AT, k * chunk_rows : (k + 1) * chunk_rows] = block[:CROSS_AT, :chunk_rows]
            for part in range(2):
                cross = block if part else o.m[2, k].astype(F32)
                at = part * (D // 2) + k * cross_rows
                o.g[CROSS_AT : CROSS_AT + 1, at : at + cross_rows] = cross[
                    CROSS_AT : CROSS_AT + 1, :cross_rows
                ]
            for a in range(2):
                rel = o.m[a, k].astype(F32)
                o.rl[a, :n_rel, k * nb_each : (k + 1) * nb_each] = rel[
                    REL_AT : REL_AT + n_rel, :nb_each
                ]

    def sums_y():
        return remote(o.ms1.at[1 - y], o.ms2, o.mx.at[2], o.mx.at[3], beside)

    def sums_z(k):
        away = lax.rem(z + nz - 1 - k, nz)
        return remote(o.ms2.at[k], o.ms3.at[away], o.mt.at[6, k], o.mt.at[7, away], (p, k, t))

    def sums_z_came(i):
        remote(o.ms2.at[z], o.ms3.at[i], o.mt.at[6, z], o.mt.at[7, i], beside).wait_recv()

    def sums_across():
        return remote(o.mo1, o.mo2, o.mx.at[4], o.mx.at[5], across)

    def sums_start(lines):
        o.dgl[...] = jnp.zeros(o.dgl.shape, F32)
        for i in range(4):
            o.dgl[i : i + 1, :] = jnp.sum(o.dgacc[i], axis=0, keepdims=True)
        for a in range(2):
            o.lines[...] = jnp.zeros(o.lines.shape, F32)
            o.lines[:n_rel, :] = lines[n_rel * a : n_rel * (a + 1), :]
            whole = o.lines[...]
            high = whole.astype(BF)
            low = (whole - high.astype(F32)).astype(BF)
            o.rl[a] = dot_nt(high, o.hot[...]) + dot_nt(low, o.hot[...])
            for k in range(nz):
                o.mf[...] = jnp.zeros(o.mf.shape, F32)
                o.mf[:CROSS_AT, :chunk_rows] = o.dgl[
                    :CROSS_AT, k * chunk_rows : (k + 1) * chunk_rows
                ]
                for part in range(2):
                    at = part * (D // 2) + k * cross_rows
                    row = CROSS_AT + part
                    o.mf[row : row + 1, :cross_rows] = o.dgl[
                        CROSS_AT : CROSS_AT + 1, at : at + cross_rows
                    ]
                o.mf[REL_AT : REL_AT + n_rel, :nb_each] = o.rl[
                    a, :n_rel, k * nb_each : (k + 1) * nb_each
                ]
                o.ms1[a, k] = o.mf[...].astype(BF)
        sums_y().start()

    def sums_mid():
        sums_y().wait()
        for k in range(nz):
            both = o.ms1[y, k].astype(F32) + o.ms2[k].astype(F32)
            o.ms2[k] = both.astype(BF)
        others(lambda k: sums_z(k).start())

    def sums_end():
        total = o.ms2[z].astype(F32)
        for i in range(nz - 1):
            sums_z_came(i)
            total = total + o.ms3[i].astype(F32)
        o.om[...] = total
        others(lambda k: sums_z(k).wait_send())

        @pl.when(dec)
        def _():
            o.mo1[...] = total
            sums_across().start()
            o.om[CROSS_AT : CROSS_AT + 1, :] = total[CROSS_AT + 1 : CROSS_AT + 2, :]
            sums_across().wait_send()

        @pl.when(enc)
        def _():
            sums_across().wait_recv()
            o.om[CROSS_AT : CROSS_AT + 1, :] = o.mo2[CROSS_AT : CROSS_AT + 1, :]


    def piece(c, slot):
        return pltpu.make_async_copy(
            o.table.at[pl.ds(pl.multiple_of(c * PIECE, PIECE), PIECE)],
            o.exs.at[slot, pl.ds(0, PIECE)],
            o.tg.at[slot],
        )

    def pick_rows():
        n_piece = o.table.shape[0] // PIECE
        piece(0, 0).start()
        rows_done(2)
        for k in range(4):
            o.idr[:, k * held : (k + 1) * held] = o.mq[k, 0:1, :held]
        o.gres[...] = jnp.zeros(o.gres.shape, F32)

        @pl.loop(0, n_piece)
        def _(c):
            slot = lax.rem(c, 2)
            pl.when(c + 1 < n_piece)(lambda: piece(c + 1, 1 - slot).start())
            at = lax.broadcasted_iota(jnp.int32, (PIECE, L), 0) + c * PIECE
            hit = jnp.where(at == o.idr[...], 1.0, 0.0).astype(BF)
            piece(c, slot).wait()
            o.gres[...] += dot_tn(hit, o.exs[slot, :PIECE, :])

        def one(rows):
            o.nb[rows, :] = o.gres[rows, :].astype(BF)

        rows_loop(one)


    def rs_y(r, k):
        g, at, width = REDUCE[r]
        cols = pl.ds(at, width)
        return remote(
            W[g].at[1 - y, chunk(k), cols],
            RY[g].at[chunk(k), cols],
            o.rs_s.at[r, k],
            o.rs_r.at[r, k],
            beside,
        )

    def rs_z(r, k):
        g, at, width = REDUCE[r]
        cols = pl.ds(at, width)
        away = lax.rem(z + nz - 1 - k, nz)
        return remote(
            RY[g].at[chunk(k), cols],
            RZ[g].at[away, :, cols],
            o.rz_s.at[r, k],
            o.rz_r.at[r, away],
            (p, k, t),
        )

    def rs_z_came(r, i):
        g, at, width = REDUCE[r]
        cols = pl.ds(at, width)
        remote(
            RY[g].at[chunk(z), cols],
            RZ[g].at[i, :, cols],
            o.rz_s.at[r, z],
            o.rz_r.at[r, i],
            beside,
        ).wait_recv()

    def rs_start(r):
        for i in range(nz):
            rs_y(r, lax.rem(z + 1 + i, nz)).start()

    def rs_mid(r, first=0, last=nz):
        g, at, width = REDUCE[r]
        cols = slice(at, at + width)

        @pl.loop(min(first, nz), min(last, nz))
        def _(i):
            k = lax.rem(z + 1 + i, nz)
            rs_y(r, k).wait_recv()
            start = pl.multiple_of(k * chunk_rows, 16)

            @pl.loop(0, chunk_rows // 32)
            def _(n):
                rows = pl.ds(pl.multiple_of(start + n * 32, 16), 32)
                both = W[g][y, rows, cols].astype(F32) + RY[g][rows, cols].astype(F32)
                RY[g][rows, cols] = both.astype(BF)

            if nz > 1:
                pl.when(i < nz - 1)(lambda: rs_z(r, k).start())

    def rs_end(r, put):
        g, at, width = REDUCE[r]
        cols = slice(at, at + width)
        for i in range(nz - 1):
            rs_z_came(r, i)
        start = pl.multiple_of(z * chunk_rows, 16)

        @pl.loop(0, chunk_rows // 32)
        def _(n):
            rows = pl.ds(pl.multiple_of(n * 32, 16), 32)
            total = RY[g][pl.ds(pl.multiple_of(start + n * 32, 16), 32), cols].astype(F32)
            for i in range(nz - 1):
                total = total + RZ[g][i, rows, cols].astype(F32)
            put(rows, total)

    def rs_sent(r):
        for i in range(nz):
            k = lax.rem(z + 1 + i, nz)
            rs_y(r, k).wait_send()
            if i < nz - 1:
                rs_z(r, k).wait_send()

    def rs_leave(r):
        g, at, width = REDUCE[r]
        out, buffer, first, into = LEAVE[r]
        return pltpu.make_async_copy(
            buffer.at[pl.ds(first, chunk_rows), pl.ds(into, width)],
            out.at[:, pl.ds(at, width)],
            o.lc.at[r],
        )

    def rs_out(r):
        g, at, width = REDUCE[r]
        out, buffer, first, into = LEAVE[r]
        if nz == 1:

            @pl.loop(0, chunk_rows // 32)
            def _(n):
                rows = pl.ds(pl.multiple_of(n * 32, 16), 32)
                out[rows, at : at + width] = RY[g][rows, at : at + width]

        else:

            def put(rows, total):
                buffer[pl.ds(pl.multiple_of(rows.start + first, 16), 32), into : into + width] = (
                    total
                )

            rs_end(r, put)
            rs_leave(r).start()
        rs_sent(r)


    def rows_sib(i, k, n):
        own, landing = ROWS[i]
        src = own.at[y] if n == 0 else landing.at[k]
        return remote(src, landing.at[k], o.qs.at[i, n], o.qr.at[i, n], sibling)

    def rows_beside(i, k):
        own, landing = ROWS[i]
        return remote(own.at[1 - y], landing.at[k], o.qs.at[i, 2], o.qr.at[i, 2], beside)

    def rows_own(i):
        own, landing = ROWS[i]
        return pltpu.make_async_copy(own.at[y], landing.at[t], o.ql.at[i])

    def rows_start(i):
        rows_own(i).start()
        rows_beside(i, t).start()
        rows_sib(i, t, 0).start()

    other = lax.rem(t + 2, 4)

    def rows_pass(i):
        rows_beside(i, other).wait_recv()
        rows_sib(i, other, 1).start()

    def rows_done(i):
        rows_own(i).wait()
        rows_sib(i, t, 0).wait()
        rows_sib(i, other, 1).wait()
        rows_beside(i, t).wait_send()

    def rows_join(i, out_ref):
        landing = ROWS[i][1]
        wide = 256

        @pl.loop(0, 2)
        def _(k):
            @pl.loop(0, D // wide)
            def _(n):
                cols = pl.ds(pl.multiple_of(n * wide, 128), wide)
                value = jnp.concatenate(
                    [landing[2 * k + j, :held, cols].astype(F32) for j in range(2)], axis=0
                )
                rows = pl.ds(pl.multiple_of(2 * k * held, 16), 2 * held)
                out_ref[rows, cols] = value.astype(out_ref.dtype)


    def home_copy(i):
        return remote(o.hs.at[i], o.hr.at[i], o.hx.at[i], o.hy.at[i], beside)

    def home_block(buffer, k):
        value = buffer[pl.ds(pl.multiple_of(k * held, 8), held), :]
        pad = o.hs.shape[1] - held
        return jnp.concatenate([value, jnp.zeros((pad, D), F32)], axis=0).astype(BF)

    def home_send(i, buffer):
        o.hs[i] = home_block(buffer, other)
        home_copy(i).start()

    home_out = (
        pltpu.make_async_copy(o.ho, o.oh.at[y], o.lh.at[0]),
        pltpu.make_async_copy(o.hr.at[0], o.oh.at[1 - y], o.lh.at[1]),
        pltpu.make_async_copy(
            o.gres.at[pl.ds(pl.multiple_of(t * held, 8), held)], o.gh.at[y], o.lh.at[2]
        ),
        pltpu.make_async_copy(o.ext.at[pl.ds(0, held)], o.gh.at[1 - y], o.lh.at[3]),
    )

    barrier = pltpu.get_barrier_semaphore()
    for g in (A, B, C):
        own_copy(g).start()
    when(dec, cross_own.start)
    for peer in (sibling, across, beside, skew):
        pl.semaphore_signal(barrier, inc=1, device_id=peer, device_id_type=MESH)
    for i in range(1, nz):
        pl.semaphore_signal(
            barrier, inc=1, device_id=(p, lax.rem(d + i, nz), t), device_id_type=MESH
        )
    pl.semaphore_wait(barrier, 4 + nz - 1)
    tiles_start()
    rows_start(0)
    when(enc, lambda: rows_start(2))
    own_copy(A).wait()
    ag_hop(A, 0)
    when(enc, cross_in.start)
    own_copy(B).wait()
    ag_hop(B, 0, False)
    when(enc, lambda: ag_side(B, 0))
    own_copy(C).wait()

    lane = lax.broadcasted_iota(jnp.int32, (1, 128), 1)
    lo = jnp.where(lane < 64, 1.0, 0.0).astype(BF)
    hi = jnp.where(lane < 64, 0.0, 1.0).astype(BF)

    def rows_loop(fn, step=RT):
        @pl.loop(0, L // step)
        def _(i):
            fn(pl.ds(pl.multiple_of(i * step, step), step))

    def half_rows(h):
        return pl.ds(pl.multiple_of(h * half, 16), half)

    def half_loop(h, fn):
        @pl.loop(0, half // RT)
        def _(i):
            fn(pl.ds(pl.multiple_of(h * half + i * RT, 16), RT))

    def halves(fn, ready=None, after=None):
        @pl.loop(0, 2)
        def _(i):
            h = lax.rem(core + i, 2)
            if ready is not None:
                ready(i, h)
            half_loop(h, fn)
            if after is not None:
                pl.when(i == 0)(after)

    def normed(v, gain_no):
        r = lax.rsqrt(jnp.mean(v * v, axis=-1, keepdims=True) + EPSILON)
        return (v * r * o.g[gain_no : gain_no + 1, :]).astype(BF)

    def norm_rows(x_ref, gain_no, out_ref):
        def one(rows):
            out_ref[rows, :] = normed(x_ref[rows, :].astype(F32), gain_no)

        rows_loop(one)

    def ex_copy(slot, h):
        rows = half_rows(h)
        return remote(
            o.exs.at[slot, rows], o.exr.at[slot, rows], o.ss.at[slot, h], o.rs.at[slot, h], sibling
        )

    def exchange(slot, fn):
        @pl.loop(0, 2)
        def _(i):
            h = lax.rem(1 - core + i, 2)
            rows = half_rows(h)
            o.exs[slot, rows, :] = fn(rows).astype(BF)
            ex_copy(slot, h).start()

    def arrived(slot):
        return lambda i, h: ex_copy(slot, h).wait()

    def ex_rows(slot, rows):
        return o.exs[slot, rows, :].astype(F32) + o.exr[slot, rows, :].astype(F32)

    def residual(slot, base_ref, put, after=None):
        def one(rows):
            put(rows, base_ref[rows, :].astype(F32) + ex_rows(slot, rows))

        halves(one, arrived(slot), after)

    def keep(ref, gain_no=None, normed_ref=None):
        def put(rows, value):
            ref[rows, :] = value
            if gain_no is not None:
                normed_ref[rows, :] = normed(value, gain_no)

        return put

    def norm_back(slot, x_ref, gain_no, put, after=None):
        o.dgacc[gain_no] = jnp.zeros((8, D), F32)

        def one(rows):
            dh = ex_rows(slot, rows)
            v = x_ref[rows, :].astype(F32)
            r = lax.rsqrt(jnp.mean(v * v, axis=-1, keepdims=True) + EPSILON)
            n = v * r
            dhg = dh * o.g[gain_no : gain_no + 1, :]
            mu = jnp.mean(dhg * n, axis=-1, keepdims=True)
            put(rows, r * (dhg - n * mu))
            o.dgacc[gain_no] += jnp.sum((dh * n).reshape(RT // 8, 8, D), axis=0)

        halves(one, arrived(slot), after)

    def split(a):
        return slice(a * hs, (a + 1) * hs)

    def both_shards(fn):
        @pl.loop(0, 2)
        def _(a):
            fn(a)

    def side_first(fn, r):
        @pl.loop(0, 2)
        def _(i):
            fn(lax.rem(1 - y + i, 2))
            if r is not None:
                pl.when(i == 0)(lambda: rs_start(r))

    def kv_project():
        def one(a):
            o.dkv[a] = dot(o.ns[...], W[A][a, :, at_kv:at_ext]).astype(BF)

        both_shards(one)
        for a in range(2):
            o.ks[:, split(a)] = o.dkv[a, :, :hs]
            o.vs[:, split(a)] = o.dkv[a, :, hs:]

    def pair_stack(block):
        return jnp.concatenate([block * lo, block * hi], axis=0)

    def pair_pick(stacked):
        return jnp.where(lane < 64, stacked[:qb_rows], stacked[qb_rows:])

    def attn_fwd(q_ref, mix_ref, mem, own, causal, hooks=()):
        @pl.loop(0, n_blk)
        def _(b):
            for i, hook in enumerate(hooks):
                pl.when(b == i)(hook)
            rows = pl.ds(pl.multiple_of(b * qb_rows, 16), qb_rows)
            wrows = pl.ds(pl.multiple_of(b * qb_rows, 16), win_w)
            sq = o.segq[rows, :]
            if mem:
                o.mm[...] = jnp.where(sq == o.srcseg[...], 0.0, NEG)
            if own:
                allowed = sq == o.segw[b]
                if causal:
                    qi = lax.broadcasted_iota(jnp.int32, (qb_rows, win_w), 0)
                    kj = lax.broadcasted_iota(jnp.int32, (qb_rows, win_w), 1)
                    allowed = allowed & (kj - HALO <= qi)
                o.mo[...] = jnp.where(allowed, 0.0, NEG)

            @pl.loop(0, n_pair)
            def _(j):
                cols = pl.ds(pl.multiple_of(j * 128, 128), 128)
                q2 = pair_stack(q_ref[rows, cols])
                parts = []
                if mem:
                    s = dot_nt(q2, o.ks[:, cols]).reshape(2, qb_rows, L)
                    parts.append(s + o.mm[...][None])
                if own:
                    s = dot_nt(q2, o.kp[wrows, cols]).reshape(2, qb_rows, win_w)
                    parts.append(s + o.tb[pl.ds(2 * j, 2)] + o.mo[...][None])
                top = [jnp.max(s, axis=-1, keepdims=True) for s in parts]
                top = functools.reduce(jnp.maximum, top)
                exps = [jnp.exp(s - top) for s in parts]
                total = sum(jnp.sum(e, axis=-1, keepdims=True) for e in exps)
                inv = 1.0 / total
                probs = [(e * inv).astype(BF).reshape(2 * qb_rows, -1) for e in exps]
                mixed = 0.0
                if mem:
                    o.pm[b * n_pair + j] = probs[0]
                    mixed = mixed + dot(probs[0], o.vs[:, cols])
                if own:
                    o.po[b * n_pair + j] = probs[-1]
                    mixed = mixed + dot(probs[-1], o.vp[wrows, cols])
                mix_ref[rows, cols] = pair_pick(mixed).astype(BF)

    def attn_back(q_ref, mix_ref, mem, own, hooks=()):
        if mem:
            o.dks[...] = jnp.zeros(o.dks.shape, F32)
            o.dvs[...] = jnp.zeros(o.dvs.shape, F32)
        if own:
            o.dkp[...] = jnp.zeros(o.dkp.shape, F32)
            o.dvp[...] = jnp.zeros(o.dvp.shape, F32)
            o.tb[...] = jnp.zeros(o.tb.shape, F32)

        @pl.loop(0, n_blk)
        def _(b):
            for i, hook in enumerate(hooks):
                pl.when(b == i)(hook)
            rows = pl.ds(pl.multiple_of(b * qb_rows, 16), qb_rows)
            wrows = pl.ds(pl.multiple_of(b * qb_rows, 16), win_w)

            @pl.loop(0, n_pair)
            def _(j):
                cols = pl.ds(pl.multiple_of(j * 128, 128), 128)
                q2 = pair_stack(q_ref[rows, cols])
                do2 = pair_stack(o.dmix[rows, cols])
                mix = mix_ref[rows, cols].astype(F32)
                delta = jnp.sum(
                    do2.astype(F32).reshape(2, qb_rows, 128) * mix[None], axis=-1, keepdims=True
                ).reshape(2 * qb_rows, 1)
                dq2 = 0.0
                if mem:
                    probs = o.pm[b * n_pair + j]
                    dp = dot_nt(do2, o.vs[:, cols])
                    ds = (probs.astype(F32) * (dp - delta)).astype(BF)
                    dq2 = dq2 + dot(ds, o.ks[:, cols])
                    o.dks[:, cols] += dot_tn(ds, q2)
                    o.dvs[:, cols] += dot_tn(probs, do2)
                if own:
                    probs = o.po[b * n_pair + j]
                    dp = dot_nt(do2, o.vp[wrows, cols])
                    ds = (probs.astype(F32) * (dp - delta)).astype(BF)
                    dq2 = dq2 + dot(ds, o.kp[wrows, cols])
                    o.dkp[wrows, cols] += dot_tn(ds, q2)
                    o.dvp[wrows, cols] += dot_tn(probs, do2)
                    o.tb[pl.ds(2 * j, 2)] += ds.astype(F32).reshape(2, qb_rows, win_w)
                o.dq[rows, cols] = (pair_pick(dq2) * (HD**-0.5)).astype(BF)

    def out_project(slot, mix_ref, weight_ref, at):
        exchange(
            slot,
            lambda rows: sum(
                dot_nt(mix_ref[rows, split(a)], weight_ref[a, :, at : at + hs]) for a in range(2)
            ),
        )

    def mix_grads(weight_ref, at):
        for a in range(2):
            o.dmix[:, split(a)] = dot(o.gb[...], weight_ref[a, :, at : at + hs]).astype(BF)

    fw = fs // 2

    def ff_half(n):
        a = n // 2
        return a, pl.ds(pl.multiple_of((n - 2 * a) * fw, 128), fw)

    def shard_cols(a):
        return slice(a * fs, (a + 1) * fs)

    def ff_fwd():
        ag_wait(B)

        @pl.loop(0, 4)
        def _(n):
            a, half_cols = ff_half(n)
            cols = pl.ds(pl.multiple_of(n * fw, 128), fw)
            o.pre[...] = dot(o.nc[...], W[B][a, :, half_cols])

            def one(rows):
                v = o.pre[rows, :]
                v2 = v * v
                th = jnp.tanh(0.7978845608028654 * v * (1.0 + 0.044715 * v2))
                cdf = 0.5 * (1.0 + th)
                slope = (0.5 * 0.7978845608028654) * v * (1.0 - th * th)
                o.hidden[rows, cols] = (v * cdf).astype(BF)
                o.gp[rows, cols] = (cdf + slope * (1.0 + (3 * 0.044715) * v2)).astype(BF)

            rows_loop(one, 32)

        ag_wait(C)
        when(dec, lambda: ag_also_hop(3))
        exchange(
            2,
            lambda rows: sum(dot_nt(o.hidden[rows, shard_cols(a)], W[C][a]) for a in range(2)),
        )

    def side_cols(a, width):
        return pl.ds(pl.multiple_of(a * width, 128), width)

    def ff_pre(n):
        a, half_cols = ff_half(n)
        cols = pl.ds(pl.multiple_of(n * fw, 128), fw)
        o.gp[:, cols] = (
            dot(o.gb[...], W[C][a, :, half_cols]) * o.gp[:, cols].astype(F32)
        ).astype(BF)

    def ff_out_weights():
        def one(a):
            W[C][a] = dot_tn(o.gb[...], o.hidden[:, side_cols(a, fs)]).astype(BF)

        side_first(one, RC)

    def ff_in_weights():
        def one(a):
            W[B][a] = dot_tn(o.nc[...], o.gp[:, side_cols(a, fs)]).astype(BF)

        side_first(one, RB)

    def ff_back():
        ag_finish(B)
        ag_finish(C)
        if nz > 1:
            when(dec, ag_also_sent)

        @pl.loop(0, 4)
        def _(n):
            ff_pre(n)

        exchange(
            0, lambda rows: sum(dot_nt(o.gp[rows, shard_cols(a)], W[B][a]) for a in range(2))
        )
        ff_out_weights()

        def put(rows, dv):
            new = o.gres[rows, :] + dv
            o.gres[rows, :] = new
            o.gb[rows, :] = new.astype(BF)

        norm_back(0, o.xlate, 1, put)

    def x_copy(way):
        rows = half_rows(core)
        return remote(
            o.xsend.at[rows], o.xbuf.at[rows], o.xss.at[way, 0], o.xrs.at[way, 0], across
        )

    def x_pass(way, h):
        rows = half_rows(h)
        return remote(
            o.xbuf.at[rows], o.xbuf.at[rows], o.xss.at[way, 1], o.xrs.at[way, 1], sibling
        )

    def x_halves(way, fn):
        x_copy(way).wait_recv()
        x_pass(way, core).start()

        def ready(i, h):
            pl.when(i == 1)(lambda: x_pass(way, h).wait_recv())

        halves(fn, ready)
        x_pass(way, core).wait_send()

    def kv_weights():
        def one(a):
            W[A][a, :, at_kv:at_ext] = dot_tn(o.ns[...], o.dkv[a]).astype(BF)

        side_first(one, RK)

    def dkv_grads():
        for a in range(2):
            o.dkv[a, :, :hs] = o.dks[:, split(a)].astype(BF)
            o.dkv[a, :, hs:] = o.dvs[:, split(a)].astype(BF)
        exchange(
            2,
            lambda rows: sum(
                dot_nt(o.dkv[a, rows, :], W[A][a, :, at_kv:at_ext]) for a in range(2)
            ),
        )

    tiles_pass()
    rows_pass(0)
    when(enc, lambda: rows_pass(2))

    def first_cross():
        cross_own.wait()
        cross_in.wait_recv()
        ag_hop(X, 0)

    when(dec, first_cross)
    ag_hop(A, 1)
    ag_hop(C, 0, False)
    if STAGE:
        when(dec, lambda: ag_pass_on(A))
    ag_side(C, 0)
    when(enc, pick_rows)
    ag_hop(A, 2)
    ag_hop(B, 1, False)
    if STAGE:
        when(dec, lambda: ag_pass_on(B))
    when(dec, lambda: ag_hop(X, 1))
    ag_hop(C, 1, False)
    if STAGE:
        when(dec, lambda: ag_pass_on(C))
    ag_hop(A, 3)
    when(dec, lambda: ag_hop(X, 2))
    rows_done(0)
    rows_join(0, o.x)
    when(dec, lambda: ag_hop(X, 3))

    when(dec, lambda: ag_side(B, 0))
    ag_side(B, 1)
    ag_side(C, 1)
    when(dec, lambda: rows_start(1))
    ag_wait(A)
    tiles_done()
    for a in range(2):
        rel_lines = dot(o.rl[a].astype(BF), o.hot[...])
        for h in range(n_rel):
            o.tb[a * n_rel + h] = pltpu.roll(
                jnp.broadcast_to(rel_lines[h : h + 1, :], (qb_rows, win_w)),
                0,
                1,
                stride=1,
                stride_axis=0,
            )
    pad = jnp.zeros((HALO, hc), BF)
    for ref in (o.kp, o.vp):
        ref[:HALO, :] = pad
        ref[HALO + L :, :] = pad
    norm_rows(o.x, 0, o.na)

    def project_own(a):
        o.dqkv[a] = dot(o.na[...], W[A][a, :, :at_o]).astype(BF)

    both_shards(project_own)
    for a in range(2):
        o.q[:, split(a)] = (o.dqkv[a, :, :hs] * (HD**-0.5)).astype(BF)
        o.kp[HALO : HALO + L, split(a)] = o.dqkv[a, :, hs : 2 * hs]
        o.vp[HALO : HALO + L, split(a)] = o.dqkv[a, :, 2 * hs :]
    ag_hop(B, 2)
    hooks = (
        lambda: ag_hop(C, 2),
        lambda: ag_hop(B, 3),
        lambda: ag_hop(C, 3),
    )

    @pl.when(enc)
    def _():
        norm_rows(o.nb, 2, o.ns)
        kv_project()
        attn_fwd(o.q, o.mixa, True, True, False, hooks)

    @pl.when(dec)
    def _():
        attn_fwd(o.q, o.mixa, False, True, True, hooks)
        ag_also_hop(0)

    out_project(0, o.mixa, W[A], at_o)

    @pl.when(enc)
    def _():
        residual(0, o.x, keep(o.xlate, 1, o.nc))

    @pl.when(dec)
    def _():
        ag_wait(X)
        ag_finish(X)
        if STAGE:
            ag_relay(A).wait_send()
            ag_relay(B).wait_send()
            ag_relay(C).wait_send()

        def whole(a):
            for k in range(nz):
                for part in range(2):
                    at = part * (D // 2) + k * cross_rows
                    start = k * chunk_rows + part * cross_rows
                    o.xg[a, at : at + cross_rows, :] = W[X][a, start : start + cross_rows, :]

        both_shards(whole)
        residual(0, o.x, keep(o.xmid, 3, o.nb))
        for a in range(2):
            r = dot(o.nb[...], o.xg[a, :, :hs]).astype(BF)
            o.qb[:, split(a)] = (r * (HD**-0.5)).astype(BF)

        def one(rows):
            o.ns[rows, :] = normed(o.xbuf[rows, :].astype(F32), 2)

        x_halves(0, one)
        kv_project()
        attn_fwd(o.qb, o.mixb, True, False, False)
        ag_also_hop(1)
        out_project(1, o.mixb, o.xg, hs)
        residual(1, o.xmid, keep(o.xlate, 1, o.nc))
        ag_also_hop(2)


    when(dec, lambda: rows_pass(1))
    ff_fwd()

    def put_out(rows, value):
        o.gres[rows, :] = value
        o.xsend[rows, :] = value.astype(BF)

    residual(2, o.xlate, put_out, lambda: pl.when(enc)(lambda: x_copy(0).start()))
    when(enc, lambda: rows_start(1))
    home_send(0, o.gres)
    o.ho[...] = home_block(o.gres, t)
    home_out[0].start()
    ag_finish(A)
    when(enc, lambda: rows_pass(1))
    rows_done(1)
    rows_join(1, o.gres)

    @pl.when(enc)
    def _():
        o.dgacc[3] = jnp.zeros((8, D), F32)
        x_copy(0).wait_send()

        def one(rows):
            value = o.gres[rows, :] + o.xbuf[rows, :].astype(F32)
            o.gres[rows, :] = value
            o.gb[rows, :] = value.astype(BF)

        x_halves(1, one)

    when(dec, lambda: rows_join(1, o.gb))


    ff_back()

    @pl.when(dec)
    def _():
        mix_grads(o.xg, hs)
        attn_back(o.qb, o.mixb, True, False)
        dkv_grads()
        exchange(
            1, lambda rows: sum(dot_nt(o.dq[rows, split(a)], o.xg[a, :, :hs]) for a in range(2))
        )

        def put_source(rows, dv):
            o.xsend[rows, :] = dv.astype(BF)

        norm_back(2, o.xbuf, 2, put_source, lambda: x_copy(1).start())
        rs_mid(RC, 0, 2)

        def put_mid(rows, dv):
            new = o.gres[rows, :] + dv
            o.gres[rows, :] = new
            o.xbuf[rows, :] = new.astype(BF)

        norm_back(1, o.xmid, 3, put_mid)
        for a in range(2):
            full = jnp.concatenate(
                [
                    dot_tn(o.nb[...], o.dq[:, split(a)]).astype(BF),
                    dot_tn(o.gb[...], o.mixb[:, split(a)]).astype(BF),
                ],
                axis=1,
            )
            for k in range(nz):
                for part in range(2):
                    at = part * (D // 2) + k * cross_rows
                    to = k * chunk_rows + part * cross_rows
                    W[X][a, to : to + cross_rows, :] = full[at : at + cross_rows]
        rs_start(RX)
        x_copy(1).wait_send()
        o.gb[...] = o.xbuf[...]

    ff_in_weights()
    mix_grads(W[A], at_o)
    for a in range(2):
        W[A][a, :, at_o : at_o + hs] = dot_tn(o.gb[...], o.mixa[:, split(a)]).astype(BF)
    steps = tuple(functools.partial(rs_mid, RC, i, i + 1) for i in range(3))

    @pl.when(enc)
    def _():
        attn_back(o.q, o.mixa, True, True, steps)
        dkv_grads()

    @pl.when(dec)
    def _():
        attn_back(o.q, o.mixa, False, True)
        rs_mid(RC, 2, 3)

    kv_weights()
    rs_mid(RC, 3)
    for a in range(2):
        o.dqkv[a, :, :hs] = o.dq[:, split(a)]
        o.dqkv[a, :, hs : 2 * hs] = o.dkp[HALO : HALO + L, split(a)].astype(BF)
        o.dqkv[a, :, 2 * hs :] = o.dvp[HALO : HALO + L, split(a)].astype(BF)
    last_slot = 1 - p
    exchange(
        last_slot,
        lambda rows: sum(dot_nt(o.dqkv[a, rows, :], W[A][a, :, :at_o]) for a in range(2)),
    )

    def own_weights(a):
        W[A][a, :, :at_o] = dot_tn(o.na[...], o.dqkv[a]).astype(BF)

    side_first(own_weights, RQ)

    @pl.when(enc)
    def _():
        def put_source(rows, dv):
            pass

        norm_back(2, o.nb, 2, put_source)
        rs_mid(RB, 0, 2)

    heads = 2 * n_pair
    acc = jnp.zeros((heads * 8, win_w), F32)
    for k in range(qb_rows // 8):
        part = o.tb[:, 8 * k : 8 * k + 8, :].reshape(heads * 8, win_w)
        acc = acc + (part if k == 0 else pltpu.roll(part, win_w - 8 * k, 1))
    sub = lax.rem(lax.broadcasted_iota(jnp.int32, (heads * 8, win_w), 0), 8)
    diag = jnp.zeros((heads * 8, win_w), F32)
    for k in range(8):
        turned = acc if k == 0 else pltpu.roll(acc, win_w - k, 1)
        diag = diag + jnp.where(sub == k, turned, 0.0)
    lines = jnp.sum(diag.reshape(heads, 8, win_w), axis=1)

    def put_in(rows, dv):
        o.gres[rows, :] = o.gres[rows, :] + dv

    norm_back(last_slot, o.x, 0, put_in)
    home_send(1, o.gres)
    home_out[2].start()
    sums_start(lines)
    home_copy(0).wait()
    home_out[1].start()
    when(enc, lambda: rs_mid(RB, 2))
    when(dec, lambda: rs_mid(RB))
    rs_mid(RK)
    rs_out(RC)

    @pl.when(dec)
    def _():
        rs_mid(RX)

    rs_mid(RQ)
    rs_out(RB)
    rs_out(RK)
    sums_mid()

    @pl.when(dec)
    def _():
        def put(rows, total):
            o.xt[rows, :] = total

        rs_end(RX, put)
        rs_sent(RX)
        o.xo[...] = o.xt[:cross_rows, :]
        cross_out.start()
        o.ox[...] = o.xt[cross_rows:, :].astype(o.ox.dtype)
        cross_out.wait_send()

    @pl.when(enc)
    def _():
        cross_in.wait_send()
        cross_out.wait_recv()
        o.ox[...] = o.xi[...].astype(o.ox.dtype)

    home_copy(1).wait()
    o.ext[...] = o.hr[1].astype(F32)
    home_out[3].start()
    rs_out(RQ)
    sums_end()
    for copy in home_out:
        copy.wait()
    if nz > 1:
        for r in LEAVE:
            rs_leave(r).wait()


def run_kernel(dims, given):
    L, D, hs, fs, nz, qb_rows, win_w = dims
    hc, fc = 2 * hs, 2 * fs
    n_blk, n_pair = L // qb_rows, hc // 128
    LP = L + 2 * HALO
    LBP = -(-(L // 4) // 16) * 16
    CR = D // nz
    widths = dict(a=6 * hs, b=fs, c=fs, x=2 * hs)
    MW = -(-CR // 128) * 128
    S = jax.ShapeDtypeStruct
    SUM = F32 if nz > 1 else BF
    outs = dict(
        oh=S((2, LBP, D), BF),
        gh=S((2, L // 4, D), F32),
        oa=S((CR, widths["a"]), SUM),
        ob=S((CR, widths["b"]), SUM),
        oc=S((CR, widths["c"]), SUM),
        ox=S((CR // 2, widths["x"]), SUM),
        om=S((TILE, MW), F32),
    )
    V = pltpu.VMEM
    LD, LH, LF = (L, D), (L, hc), (L, fc)
    scratch = dict(
        na=V(LD, BF), ns=V(LD, BF), nb=V(LD, BF), nc=V(LD, BF),
        xmid=V(LD, F32), xlate=V(LD, F32), gres=V(LD, F32),
        q=V(LH, BF), kp=V((LP, hc), BF), vp=V((LP, hc), BF), ks=V(LH, BF), vs=V(LH, BF),
        qb=V(LH, BF), mixa=V(LH, BF), mixb=V(LH, BF),
        pm=V((n_blk * n_pair, 2 * qb_rows, L), BF), po=V((n_blk * n_pair, 2 * qb_rows, win_w), BF),
        hidden=V(LF, BF), gp=V(LF, BF), pre=V((L, fs // 2), F32),
        tb=V((2 * n_pair, qb_rows, win_w), F32),
        mm=V((qb_rows, L), F32), mo=V((qb_rows, win_w), F32),
        dmix=V(LH, BF), dq=V(LH, BF), dqkv=V((2, L, 3 * hs), BF), dkv=V((2, L, 2 * hs), BF),
        dkp=V((LP, hc), F32), dvp=V((LP, hc), F32), dks=V(LH, F32), dvs=V(LH, F32),
        gb=V(LD, BF), xbuf=V(LD, BF), xsend=V(LD, BF),
        exs=V((3, L, D), BF), exr=V((3, L, D), BF), dgacc=V((4, 8, D), F32),
        g=V((8, D), F32), ext=V((LBP, D), F32), lines=V((TILE, win_w), F32),
        m=V((3, nz, TILE, MW), BF), ms1=V((2, nz, TILE, MW), BF), ms2=V((nz, TILE, MW), BF),
        ms3=V((max(nz - 1, 1), TILE, MW), BF), mf=V((TILE, MW), F32), mo1=V((TILE, MW), F32),
        mo2=V((TILE, MW), F32), dgl=V((8, D), F32), rl=V((2, TILE, 128), F32),
        idr=V((1, L), jnp.int32),
        x=V(LD, BF), xq=V((4, LBP, D), BF), cq=V((4, LBP, D), BF), mq=V((4, 8, 128), jnp.int32),
        hs=V((2, LBP, D), BF), hr=V((2, LBP, D), BF), ho=V((LBP, D), BF),
        xg=V((2, D, widths["x"]), BF), xt=V((CR, widths["x"]), F32),
        xo=V((CR // 2, widths["x"]), F32), xi=V((CR // 2, widths["x"]), F32),
    )
    for g, width in widths.items():
        scratch["w" + g] = V((2, D, width), BF)
        scratch["y" + g] = V((D, width), BF)
        scratch["z" + g] = V((nz - 1, CR, width) if nz > 1 else (1, 16, width), BF)
    sem = pltpu.SemaphoreType.DMA
    scratch.update(ss=sem((3, 2)), rs=sem((3, 2)), gd=sem((3, 3)), ga=sem((2, nz)), gb2=sem((nz,)), mt=sem((8, nz)), mx=sem((6,)), tg=sem((2,)), xss=sem((2, 2)), xrs=sem((2, 2)))
    scratch.update(xw=sem((4,)), oc_sem=sem((4,)), lc=sem((6,)), lh=sem((4,)))
    scratch.update(qs=sem((3, 3)), qr=sem((3, 3)), ql=sem((3,)), hx=sem((2,)), hy=sem((2,)))
    for name in ("gr", "gl", "gs", "gz", "gy"):
        scratch[name] = sem((4, nz))
    for name in ("rs_s", "rs_r", "rz_s", "rz_r"):
        scratch[name] = sem((6, nz))
    spec = pl.BlockSpec(memory_space=pltpu.VMEM)
    far = pl.BlockSpec(memory_space=pl.ANY)
    names = list(given) + list(outs) + list(scratch)
    FAR = ["sa", "sb", "sc", "sx", "xs", "cs", "ms", "table", "oh", "gh"]
    if nz > 1:
        FAR += ["oa", "ob", "oc"]
    return pl.pallas_call(
        functools.partial(kernel, dims, names),
        out_shape=list(outs.values()),
        in_specs=[far if name in FAR else spec for name in given],
        out_specs=[far if name in FAR else spec for name in outs],
        scratch_shapes=list(scratch.values()),
        compiler_params=pltpu.CompilerParams(
            collective_id=0, has_side_effects=True, vmem_limit_bytes=63 << 20
        ),
        name="layers",
    )(*given.values())


def prep_kernel(dims, n_dp, names, *refs):
    L, D, hs, fs, nz, qb_rows, win_w = dims
    o = Refs()
    for name, ref in zip(names, refs, strict=True):
        setattr(o, name, ref)
    section = lax.axis_index("pipe")
    y = lax.axis_index("tensor") // 2
    rows = D // n_dp
    held = L // 4
    for raw, out in ((o.li, o.xs), (o.co, o.cs)):
        o.tmp[...] = raw[...].astype(F32)
        pad = jnp.zeros((out.shape[1] - held, D), F32)
        for r in range(2):
            out[r] = jnp.concatenate([o.tmp[:, r, :], pad], axis=0).astype(BF)
    for i in range(3):
        o.sa[:, i * hs : (i + 1) * hs] = o.qkv[i]
    o.sa[:, 3 * hs : 4 * hs] = o.so[...].astype(F32).T.astype(BF)
    for i in range(2):
        o.kvt[...] = o.kv[...].astype(F32)
        o.sa[:, (4 + i) * hs : (5 + i) * hs] = o.kvt[:, i, :].astype(BF)
    n_gain = o.gain.shape[0]
    heads = o.rel.shape[0]
    o.mf[...] = jnp.zeros(o.mf.shape, F32)
    o.mf[:n_gain, : o.gain.shape[1]] = o.gain[...].astype(F32)
    o.mf[CROSS_AT : CROSS_AT + 1, : o.cg.shape[1]] = o.cg[...].astype(F32)
    o.mf[REL_AT : REL_AT + heads, : o.rel.shape[1]] = o.rel[...].astype(F32)
    o.sm[...] = o.mf[...].astype(BF)
    o.sx[:, :hs] = o.cq[...]
    o.sx[:, hs : 2 * hs] = o.cw[...].astype(F32).T.astype(BF)
    o.ms[...] = jnp.zeros(o.ms.shape, jnp.int32)
    for r in range(2):
        o.ms[r, 0:1, :held] = o.ids[r : r + 1, :]
    own = o.seg[section, pl.ds(y, 1), :]
    first = o.seg[0, pl.ds(y, 1), :]
    o.segq[...] = jnp.broadcast_to(own.astype(F32), (8, L)).T[:, :1].astype(jnp.int32)
    slots = lax.broadcasted_iota(jnp.int32, (1, L), 1).astype(F32)
    slots = jnp.floor((slots + 0.5) * (1.0 / MEM)).astype(jnp.int32)
    o.srcseg[...] = jnp.where(section == 0, slots, first)
    o.line[...] = jnp.full(o.line.shape, -1, jnp.int32)
    o.line[:, HALO : HALO + L] = own
    for b in range(L // qb_rows):
        o.segw[b] = o.line[:, b * qb_rows : b * qb_rows + win_w]
    o.win[...] = jnp.full(o.win.shape, -1, jnp.int32)
    o.win[:, : 2 * HALO] = o.buckets[:, L - HALO : L + HALO]
    at = lax.broadcasted_iota(jnp.int32, (128, win_w), 0)
    o.hot[...] = jnp.where(at == o.win[...], 1.0, 0.0).astype(BF)


def run_prep(dims, n_dp, given):
    L, D, hs, fs, nz, qb_rows, win_w = dims
    rows, held = D // n_dp, L // 4
    MW = -(-(D // nz) // 128) * 128
    LBP = -(-held // 16) * 16
    S = jax.ShapeDtypeStruct
    outs = dict(
        xs=S((2, LBP, D), BF),
        cs=S((2, LBP, D), BF),
        sa=S((rows, 6 * hs), BF),
        sx=S((rows // 2, 2 * hs), BF),
        sm=S((TILE, MW), BF),
        ms=S((2, 8, 128), jnp.int32),
        segq=S((L, 1), jnp.int32),
        segw=S((L // qb_rows, 1, win_w), jnp.int32),
        srcseg=S((1, L), jnp.int32),
        hot=S((128, win_w), BF),
    )
    V = pltpu.VMEM
    scratch = dict(
        tmp=V((held, 2, D), F32),
        kvt=V((rows, 2, hs), F32),
        mf=V((TILE, MW), F32),
        line=V((1, L + 2 * HALO), jnp.int32),
        win=V((1, win_w), jnp.int32),
    )
    spec = pl.BlockSpec(memory_space=pltpu.VMEM)
    names = list(given) + list(outs) + list(scratch)
    return pl.pallas_call(
        functools.partial(prep_kernel, dims, n_dp, names),
        out_shape=list(outs.values()),
        in_specs=[spec] * len(given),
        out_specs=[spec] * len(outs),
        scratch_shapes=list(scratch.values()),
        compiler_params=pltpu.CompilerParams(vmem_limit_bytes=60 << 20),
        name="prep",
    )(*given.values())


def finish_kernel(dims, names, *refs):
    L, D, hs, fs, nz, qb_rows, win_w = dims
    o = Refs()
    for name, ref in zip(names, refs, strict=True):
        setattr(o, name, ref)
    o.ffi[...] = o.gb[...]
    o.ffo[...] = o.gc[...]
    for r in range(2):
        o.gin[:, r, :] = o.gh[r]
        o.tmp[:, r, :] = o.oh[r, : L // 4].astype(F32)
    o.out[...] = o.tmp[...].astype(BF)
    for i in range(3):
        o.qkv[i] = o.ga[:, i * hs : (i + 1) * hs]
    o.so[...] = o.ga[:, 3 * hs : 4 * hs].T
    for i in range(2):
        o.kv[:, i, :] = o.ga[:, (4 + i) * hs : (5 + i) * hs]
    rows = o.ga.shape[0]
    for i in range(o.gain.shape[0]):
        o.gain[i] = o.gm[i : i + 1, :rows]
    heads, _, nb_rows = o.rel.shape
    for i in range(heads):
        o.rel[i] = o.gm[REL_AT + i : REL_AT + i + 1, :nb_rows]
    o.cq[...] = o.gx[:, :hs]
    o.co[...] = o.gx[:, hs : 2 * hs].T
    o.cg[...] = o.gm[CROSS_AT : CROSS_AT + 1, : rows // 2]


def run_finish(dims, rel_shape, sums):
    L, D, hs, fs, nz, qb_rows, win_w = dims
    rows = sums[2].shape[0]
    held = L // 4
    S = jax.ShapeDtypeStruct
    outs = dict(
        out=S((held, 2, D), BF),
        gin=S((held, 2, D), F32),
        qkv=S((3, rows, hs), F32),
        so=S((hs, rows), F32),
        kv=S((rows, 2, hs), F32),
        rel=S((rel_shape[1], 1, rel_shape[0]), F32),
        gain=S((3, 1, rows), F32),
        cq=S((rows // 2, hs), F32),
        co=S((hs, rows // 2), F32),
        cg=S((1, rows // 2), F32),
        ffi=S((rows, fs), F32),
        ffo=S((rows, fs), F32),
    )
    spec = pl.BlockSpec(memory_space=pltpu.VMEM)
    return pl.pallas_call(
        functools.partial(
            finish_kernel, dims, ["oh", "gh", "ga", "gb", "gc", "gx", "gm", *outs, "tmp"]
        ),
        out_shape=list(outs.values()),
        in_specs=[spec] * 7,
        out_specs=[spec] * len(outs),
        scratch_shapes=[pltpu.VMEM((held, 2, D), F32)],
        compiler_params=pltpu.CompilerParams(vmem_limit_bytes=60 << 20),
        name="finish",
    )(*sums)


def body(
    layer_inputs,
    segment_ids,
    slot_ids,
    memory_table,
    buckets,
    self_qkv,
    self_out,
    source_kv,
    ff_in,
    ff_out,
    rel_bias,
    gains,
    cross_query,
    cross_out,
    cross_gain,
    cotangents,
):
    nt = lax.axis_size("tensor")
    n_dp = lax.axis_size("dp")
    assert nt == 4 and layer_inputs.shape[2] == 2
    D = layer_inputs.shape[3]
    L = segment_ids.shape[2]
    hs = self_qkv.shape[3]
    fs = ff_in.shape[2]
    qb_rows, win_w = 160, 256
    rows = D // n_dp
    nz = n_dp if (rows // 2) % 32 == 0 else 1
    dims = (L, D, hs, fs, nz, qb_rows, win_w)
    held = L // nt
    gain, rel, cross_g = gains[0], rel_bias[0].T, cross_gain[None]
    if nz != n_dp:
        gain = lax.all_gather(gain, "dp", axis=1, tiled=True)
        rel = lax.all_gather(rel, "dp", axis=1, tiled=True)
        cross_g = lax.all_gather(cross_g, "dp", axis=1, tiled=True)
    prepared = run_prep(
        dims,
        n_dp,
        dict(
            li=layer_inputs[0],
            co=cotangents[0],
            qkv=self_qkv[0].transpose(1, 0, 2),
            so=self_out[0],
            kv=source_kv[0],
            gain=gain,
            rel=rel,
            cq=cross_query,
            cw=cross_out,
            cg=cross_g,
            seg=segment_ids,
            ids=slot_ids.T,
            buckets=buckets[None],
        ),
    )
    xs, cs, sa, sx, sm, ms, segq, segw, srcseg, hot = prepared
    shards = [sa, ff_in[0], ff_out[0].T, sx]
    if nz != n_dp:
        shards = [lax.all_gather(shard, "dp", axis=0, tiled=True) for shard in shards]
    given = dict(
        xs=xs, cs=cs, ms=ms, table=memory_table, sm=sm, segq=segq, segw=segw, srcseg=srcseg, hot=hot,
        sa=shards[0], sb=shards[1], sc=shards[2], sx=shards[3],
    )
    oh, gh, *sums, gm = run_kernel(dims, given)
    if nz != n_dp:
        sums = [
            lax.psum_scatter(full, "dp", scatter_dimension=0, tiled=True).astype(F32)
            for full in sums
        ]

        def share(first, count, width):
            mine = lax.psum_scatter(
                gm[first : first + count, :width], "dp", scatter_dimension=1, tiled=True
            )
            below = TILE - first - count
            return jnp.pad(mine, ((first, below), (0, 128 - mine.shape[1])))

        gm = (
            share(0, CROSS_AT, D)
            + share(CROSS_AT, 1, D // 2)
            + share(REL_AT, rel_bias.shape[2], NB)
        )
    done = run_finish(dims, rel_bias.shape[1:], [oh, gh, *sums, gm])
    out, gin, qkv, so, kv, rel, gain, cq, co, cg, ff_i, ff_o = done
    return (
        out[None],
        gin[None],
        qkv.transpose(1, 0, 2)[None],
        so[None],
        kv[None],
        ff_i[None],
        ff_o.T[None],
        rel.transpose(1, 2, 0),
        gain.transpose(1, 0, 2),
        cq,
        co,
        cg[0],
    )


def solution(mesh):
    placed = (
        P("pipe", "tensor", "dp", None),
        P(None, "dp", None),
        P("tensor", "dp"),
        P(),
        P(),
        P("pipe", "dp", None, "tensor"),
        P("pipe", "tensor", "dp"),
        P("pipe", "dp", None, "tensor"),
        P("pipe", "dp", "tensor"),
        P("pipe", "tensor", "dp"),
        P("pipe", "dp", "tensor"),
        P("pipe", None, "dp"),
        P(("pipe", "dp"), "tensor"),
        P("tensor", ("pipe", "dp")),
        P(("pipe", "dp")),
        P("pipe", "tensor", "dp", None),
    )
    return jax.shard_map(
        body,
        mesh=mesh,
        in_specs=placed,
        out_specs=(
            P("pipe", "tensor", "dp", None),
            P("pipe", "tensor", "dp", None),
            P("pipe", "dp", None, "tensor"),
            P("pipe", "tensor", "dp"),
            P("pipe", "dp", None, "tensor"),
            P("pipe", "dp", "tensor"),
            P("pipe", "tensor", "dp"),
            P("pipe", "dp", "tensor"),
            P("pipe", None, "dp"),
            P(("pipe", "dp"), "tensor"),
            P("tensor", ("pipe", "dp")),
            P(("pipe", "dp")),
        ),
        check_vma=False,
    )
```

```python
import functools

import jax
import jax.numpy as jnp
from jax import lax
from jax.experimental import pallas as pl
from jax.experimental.pallas import tpu as pltpu
from jax.sharding import PartitionSpec as P

HD = 64
NB = 32
MEM = 20
HALO = 48
TILE = 16
CROSS_AT = 3
REL_AT = 8
PIECE = 256
EPSILON = 1e-06
NEG = -1000000000.0
BF = jnp.bfloat16
F32 = jnp.float32
MESH = pl.DeviceIdType.MESH
RT = 48


def dot(a, b):
    return lax.dot_general(a, b, (((1,), (0,)), ((), ())), preferred_element_type=F32)


def dot_nt(a, b):
    return lax.dot_general(a, b, (((1,), (1,)), ((), ())), preferred_element_type=F32)


def dot_tn(a, b):
    return lax.dot_general(a, b, (((0,), (0,)), ((), ())), preferred_element_type=F32)


class Refs:
    pass


def kernel(dims, names, *refs):
    L, D, hs, fs, nz, qb_rows, win_w = dims
    hc, fc = 2 * hs, 2 * fs
    at_o, at_kv, at_ext = 3 * hs, 4 * hs, 6 * hs
    chunk_rows = D // nz
    cross_rows = chunk_rows // 2
    n_blk = L // qb_rows
    n_pair = hc // 128
    o = Refs()
    for name, ref in zip(names, refs, strict=True):
        setattr(o, name, ref)
    p = lax.axis_index("pipe")
    d = lax.axis_index("dp")
    t = lax.axis_index("tensor")
    enc, dec = p == 0, p == 1
    core = lax.rem(t, 2)
    y = t // 2
    z = d if nz > 1 else 0
    skew = (1 - p, d, lax.rem(t + 2, 4))
    sibling = (p, d, t + 1 - 2 * core)
    across = (1 - p, d, t)
    beside = (p, d, lax.rem(t + 2, 4))
    half = L // 2
    held = L // 4
    A, B, C, X = range(4)
    shard = (o.sa, o.sb, o.sc, o.sx)
    W = (o.wa, o.wb, o.wc, o.wx)
    RY = (o.ya, o.yb, o.yc, o.yx)
    RZ = (o.za, o.zb, o.zc, o.zx)
    RB, RC, RX, RQ, RK = range(5)
    REDUCE = {
        RB: (B, 0, fs),
        RC: (C, 0, fs),
        RX: (X, 0, 2 * hs),
        RQ: (A, 0, at_kv),
        RK: (A, at_kv, 2 * hs),
    }
    LEAVE = {
        RB: (o.ob, o.xlate, 0, 0),
        RC: (o.oc, o.xmid, 0, 0),
        RQ: (o.oa, o.xmid, chunk_rows, 0),
        RK: (o.oa, o.xlate, chunk_rows, 0),
    }
    STAGE = {} if nz == 1 else {
        A: o.hidden.at[pl.ds(0, chunk_rows), pl.ds(0, 6 * hs)],
        C: o.gp.at[pl.ds(0, chunk_rows), pl.ds(fs, fs)],
    }
    ROWS = ((o.xs, o.xq), (o.cs, o.cq), (o.ms, o.mq))

    def chunk(k):
        return pl.ds(pl.multiple_of(k * chunk_rows, 16), chunk_rows)

    def remote(src, dst, send, recv, device):
        return pltpu.make_async_remote_copy(
            src_ref=src,
            dst_ref=dst,
            send_sem=send,
            recv_sem=recv,
            device_id=device,
            device_id_type=MESH,
        )


    def ag_right(g, k):
        slot = W[g].at[y, chunk(k)]
        return remote(slot, slot, o.gr.at[g, k], o.gz.at[g, k], (p, d + 1, t))

    def ag_left(g, k):
        slot = W[g].at[y, chunk(k)]
        return remote(slot, slot, o.gl.at[g, k], o.gz.at[g, k], (p, d - 1, t))

    def ag_beside(g, k):
        slot = W[g].at[y, chunk(k)]
        return remote(slot, slot, o.gs.at[g, k], o.gy.at[g, k], beside)

    def ag_came(g, k):
        slot = W[g].at[y, chunk(k)]
        remote(slot, slot, o.gr.at[g, k], o.gz.at[g, k], beside).wait_recv()

    def ag_each(g, h, act):
        if h == 0:
            act(z, z + 1 < nz, z > 0, True)
        else:
            act(z - h, z + 1 < nz, False, z - h >= 0)
            act(z + h, False, z > 0, z + h < nz)

    def when(cond, fn):
        if cond is True:
            fn()
        elif cond is not False:
            pl.when(cond)(fn)


    def ag_skew(g):
        return remote(W[g].at[y, chunk(z)], STAGE[g], o.gd.at[g, 0], o.gd.at[g, 1], skew)

    def ag_relay(g):
        slot = W[g].at[1 - y, chunk(z)]
        return remote(STAGE[g], slot, o.gd.at[g, 2], o.gy.at[g, z], across)

    def ag_pass_on(g):
        ag_skew(g).wait_recv()
        ag_relay(g).start()

    def ag_aside(g, k, own, wait):
        act = (lambda c: c.wait_send()) if wait else (lambda c: c.start())
        if own and g in STAGE:
            pl.when(enc)(lambda: act(ag_skew(g)))
            pl.when(dec)(lambda: act(ag_beside(g, k)))
        elif not own and g == C:
            pl.when(enc)(lambda: act(ag_beside(g, k)))
        else:
            act(ag_beside(g, k))


    def ag_also(k, way):
        slot = W[C].at[1 - y, chunk(k)]
        return remote(slot, slot, o.ga.at[way, k], o.gb2.at[k], (p, d + (1, -1)[way], t))

    def ag_also_hop(h):
        if h >= nz or nz == 1:
            return

        def act(k, right, left, here):
            def go():
                slot = W[C].at[1 - y, chunk(k)]
                if h == 0:
                    remote(slot, slot, o.gs.at[C, k], o.gy.at[C, k], beside).wait_recv()
                else:
                    remote(slot, slot, o.ga.at[0, k], o.gb2.at[k], beside).wait_recv()
                when(right, lambda: ag_also(k, 0).start())
                when(left, lambda: ag_also(k, 1).start())

            when(here, go)

        ag_each(C, h, act)

    def ag_also_sent():
        for h in range(nz):

            def act(k, right, left, here):
                def go():
                    when(right, lambda: ag_also(k, 0).wait_send())
                    when(left, lambda: ag_also(k, 1).wait_send())

                when(here, go)

            ag_each(C, h, act)

    def ag_hop(g, h, aside=True):
        if h >= nz:
            return

        def act(k, right, left, here):
            def go():
                if h > 0:
                    ag_came(g, k)
                if nz > 1:
                    when(right, lambda: ag_right(g, k).start())
                    when(left, lambda: ag_left(g, k).start())
                if aside:
                    ag_aside(g, k, h == 0, False)

            when(here, go)

        ag_each(g, h, act)

    def ag_side(g, h):
        if h >= nz:
            return

        def act(k, right, left, here):
            when(here, lambda: ag_aside(g, k, h == 0, False))

        ag_each(g, h, act)

    def ag_wait(g):
        if g == C and nz > 1:
            pl.when(enc)(lambda: ag_wait_all(g))
        else:
            ag_wait_all(g)

    def ag_wait_all(g):
        for k in range(nz):
            slot = W[g].at[1 - y, chunk(k)]
            remote(slot, slot, o.gs.at[g, k], o.gy.at[g, k], beside).wait_recv()

    def ag_finish(g):
        for h in range(nz):

            def act(k, right, left, here):
                def go():
                    if nz > 1:
                        when(right, lambda: ag_right(g, k).wait_send())
                        when(left, lambda: ag_left(g, k).wait_send())
                    ag_aside(g, k, h == 0, True)

                when(here, go)

            ag_each(g, h, act)

    def own_copy(g):
        return pltpu.make_async_copy(shard[g], W[g].at[y, chunk(z)], o.oc_sem.at[g])

    def cross_part(k, part):
        start = k * chunk_rows + part * cross_rows
        return pl.ds(pl.multiple_of(start, 16), cross_rows)

    cross_own = pltpu.make_async_copy(o.sx, W[X].at[y, cross_part(z, 1)], o.oc_sem.at[X])
    cross_in = remote(
        o.sx, W[X].at[y, cross_part(z, 0)], o.xw.at[0], o.xw.at[1], across
    )
    cross_out = remote(o.xo, o.xi, o.xw.at[2], o.xw.at[3], across)


    nb_each = NB // nz
    n_rel = hs // HD

    def others(fn):
        if nz > 1:

            @pl.loop(1, nz)
            def _(i):
                fn(lax.rem(z + i, nz))

    def tile_z(a, k, to, sems):
        slot = o.m.at[a, k]
        return remote(slot, slot, o.mt.at[sems, to], o.mt.at[sems + 1, k], (p, to, t))

    def tile_beside(k):
        slot = o.m.at[y, k]
        return remote(slot, slot, o.mt.at[2, k], o.mt.at[3, k], beside)

    def tile_across():
        return remote(o.m.at[y, z], o.m.at[2, z], o.mx.at[0], o.mx.at[1], across)

    def tiles_start():
        o.m[y, z] = o.sm[...]

        @pl.when(enc)
        def _():
            o.m[2] = jnp.zeros(o.m.shape[1:], BF)

        others(lambda k: tile_z(y, z, k, 0).start())
        tile_beside(z).start()
        when(enc, lambda: tile_across().start())

    def tiles_pass():
        def one(k):
            tile_z(y, k, k, 0).wait_recv()
            tile_beside(k).start()

        others(one)

        @pl.when(dec)
        def _():
            tile_across().wait_recv()
            others(lambda k: tile_z(2, z, k, 4).start())

    def tiles_done():
        @pl.loop(0, nz)
        def _(k):
            slot = o.m.at[1 - y, k]
            remote(slot, slot, o.mt.at[2, k], o.mt.at[3, k], beside).wait_recv()
            tile_beside(k).wait_send()

        others(lambda k: tile_z(y, z, k, 0).wait_send())
        when(enc, lambda: tile_across().wait_send())

        @pl.when(dec)
        def _():
            others(lambda k: tile_z(2, k, k, 4).wait_recv())
            others(lambda k: tile_z(2, z, k, 4).wait_send())

        o.rl[...] = jnp.zeros(o.rl.shape, F32)
        for k in range(nz):
            block = o.m[y, k].astype(F32)
            o.g[:CROSS_AT, k * chunk_rows : (k + 1) * chunk_rows] = block[:CROSS_AT, :chunk_rows]
            for part in range(2):
                cross = block if part else o.m[2, k].astype(F32)
                at = part * (D // 2) + k * cross_rows
                o.g[CROSS_AT : CROSS_AT + 1, at : at + cross_rows] = cross[
                    CROSS_AT : CROSS_AT + 1, :cross_rows
                ]
            for a in range(2):
                rel = o.m[a, k].astype(F32)
                o.rl[a, :n_rel, k * nb_each : (k + 1) * nb_each] = rel[
                    REL_AT : REL_AT + n_rel, :nb_each
                ]

    def sums_y():
        return remote(o.ms1.at[1 - y], o.ms2, o.mx.at[2], o.mx.at[3], beside)

    def sums_z(k):
        away = lax.rem(z + nz - 1 - k, nz)
        return remote(o.ms2.at[k], o.ms3.at[away], o.mt.at[6, k], o.mt.at[7, away], (p, k, t))

    def sums_z_came(i):
        remote(o.ms2.at[z], o.ms3.at[i], o.mt.at[6, z], o.mt.at[7, i], beside).wait_recv()

    def sums_across():
        return remote(o.mo1, o.mo2, o.mx.at[4], o.mx.at[5], across)

    def sums_start(lines):
        o.dgl[...] = jnp.zeros(o.dgl.shape, F32)
        for i in range(4):
            o.dgl[i : i + 1, :] = jnp.sum(o.dgacc[i], axis=0, keepdims=True)
        for a in range(2):
            o.lines[...] = jnp.zeros(o.lines.shape, F32)
            o.lines[:n_rel, :] = lines[n_rel * a : n_rel * (a + 1), :]
            whole = o.lines[...]
            high = whole.astype(BF)
            low = (whole - high.astype(F32)).astype(BF)
            o.rl[a] = dot_nt(high, o.hot[...]) + dot_nt(low, o.hot[...])
            for k in range(nz):
                o.mf[...] = jnp.zeros(o.mf.shape, F32)
                o.mf[:CROSS_AT, :chunk_rows] = o.dgl[
                    :CROSS_AT, k * chunk_rows : (k + 1) * chunk_rows
                ]
                for part in range(2):
                    at = part * (D // 2) + k * cross_rows
                    row = CROSS_AT + part
                    o.mf[row : row + 1, :cross_rows] = o.dgl[
                        CROSS_AT : CROSS_AT + 1, at : at + cross_rows
                    ]
                o.mf[REL_AT : REL_AT + n_rel, :nb_each] = o.rl[
                    a, :n_rel, k * nb_each : (k + 1) * nb_each
                ]
                o.ms1[a, k] = o.mf[...].astype(BF)
        sums_y().start()

    def sums_mid():
        sums_y().wait()
        for k in range(nz):
            both = o.ms1[y, k].astype(F32) + o.ms2[k].astype(F32)
            o.ms2[k] = both.astype(BF)
        others(lambda k: sums_z(k).start())

    def sums_end():
        total = o.ms2[z].astype(F32)
        for i in range(nz - 1):
            sums_z_came(i)
            total = total + o.ms3[i].astype(F32)
        o.om[...] = total
        others(lambda k: sums_z(k).wait_send())

        @pl.when(dec)
        def _():
            o.mo1[...] = total
            sums_across().start()
            o.om[CROSS_AT : CROSS_AT + 1, :] = total[CROSS_AT + 1 : CROSS_AT + 2, :]
            sums_across().wait_send()

        @pl.when(enc)
        def _():
            sums_across().wait_recv()
            o.om[CROSS_AT : CROSS_AT + 1, :] = o.mo2[CROSS_AT : CROSS_AT + 1, :]


    def piece(c, slot):
        return pltpu.make_async_copy(
            o.table.at[pl.ds(pl.multiple_of(c * PIECE, PIECE), PIECE)],
            o.exs.at[slot, pl.ds(0, PIECE)],
            o.tg.at[slot],
        )

    def pick_rows(part):
        n_piece = o.table.shape[0] // PIECE // 2
        first = part * n_piece
        if part == 0:
            rows_done(2)
            for k in range(4):
                o.idr[:, k * held : (k + 1) * held] = o.mq[k, 0:1, :held]
            o.gres[...] = jnp.zeros(o.gres.shape, F32)
        piece(first, 0).start()

        @pl.loop(0, n_piece)
        def _(i):
            c = first + i
            slot = lax.rem(i, 2)
            pl.when(i + 1 < n_piece)(lambda: piece(c + 1, 1 - slot).start())
            at = lax.broadcasted_iota(jnp.int32, (PIECE, L), 0) + c * PIECE
            hit = jnp.where(at == o.idr[...], 1.0, 0.0).astype(BF)
            piece(c, slot).wait()
            o.gres[...] += dot_tn(hit, o.exs[slot, :PIECE, :])

        if part == 1:

            def one(rows):
                o.nb[rows, :] = o.gres[rows, :].astype(BF)

            rows_loop(one)


    def rs_y(r, k):
        g, at, width = REDUCE[r]
        cols = pl.ds(at, width)
        return remote(
            W[g].at[1 - y, chunk(k), cols],
            RY[g].at[chunk(k), cols],
            o.rs_s.at[r, k],
            o.rs_r.at[r, k],
            beside,
        )

    mate = z + 1 - 2 * lax.rem(z, 2)
    far = 2 - 2 * (z // 2)
    TAKES = (far + lax.rem(mate, 2), mate, far + lax.rem(z, 2), z)
    GOES = (mate, mate, far + lax.rem(z, 2), z)

    def by_step(i, values):
        if nz == 1:
            return z
        weights = (
            (1 - i) * (2 - i) * (3 - i) // 6,
            i * (2 - i) * (3 - i) // 2,
            i * (i - 1) * (3 - i) // 2,
            i * (i - 1) * (i - 2) // 6,
        )
        return sum(value * weight for value, weight in zip(values, weights))

    def rs_z(r, i):
        g, at, width = REDUCE[r]
        cols = pl.ds(at, width)
        return remote(
            RY[g].at[chunk(by_step(i, TAKES)), cols],
            RZ[g].at[i, :, cols],
            o.rz_s.at[r, i],
            o.rz_r.at[r, i],
            (p, by_step(i, GOES), t),
        )

    def rs_start(r):
        for i in range(nz):
            rs_y(r, by_step(i, TAKES)).start()


    kv_cols = slice(at_kv, at_ext)
    kv_lanes = pl.ds(at_kv, 2 * hs)

    def kv_slot(own, i):
        return RZ[A].at[i, :, kv_lanes] if own else RY[A].at[chunk(i), kv_lanes]

    def kv_z(own, i):
        a = y if own else 1 - y
        return remote(
            W[A].at[a, chunk(TAKES[i]), kv_lanes],
            kv_slot(own, i),
            o.kq.at[own, i],
            o.kq.at[2 + own, i],
            (p, GOES[i], t),
        )

    kv_y = remote(
        W[A].at[1 - y, chunk(z), kv_lanes],
        RY[A].at[chunk(nz - 1), kv_lanes],
        o.kq.at[0, nz - 1],
        o.kq.at[2, nz - 1],
        beside,
    )

    def kv_add(k, terms, put):
        start = pl.multiple_of(k * chunk_rows, 16)

        @pl.loop(0, chunk_rows // 32)
        def _(n):
            rows = pl.ds(pl.multiple_of(start + n * 32, 16), 32)
            near = pl.ds(pl.multiple_of(n * 32, 16), 32)
            put(rows, near, sum(term(rows, near).astype(F32) for term in terms))

    def kv_term(own, i):
        if own:
            return lambda rows, near: RZ[A][i, near, kv_cols]
        return lambda rows, near: RY[A][
            pl.ds(pl.multiple_of(i * chunk_rows + near.start, 16), 32), kv_cols
        ]

    def kv_mine(own):
        a = y if own else 1 - y
        return lambda rows, near: W[A][a, rows, kv_cols]

    def kv_keep(own):
        a = y if own else 1 - y

        def put(rows, near, value):
            W[A][a, rows, kv_cols] = value.astype(BF)

        return put

    def kv_start(own):
        if nz > 1:
            kv_z(own, 0).start()
            kv_z(own, 1).start()

    def kv_mid():
        if nz == 1:
            rs_mid(RK)
            return
        for own in (0, 1):
            kv_z(own, 0).wait_recv()
            kv_add(TAKES[2], [kv_mine(own), kv_term(own, 0)], kv_keep(own))
            kv_z(own, 2).start()

    def kv_cross():
        if nz == 1:
            return
        kv_z(0, 1).wait_recv()
        kv_z(0, 2).wait_recv()
        kv_add(z, [kv_mine(0), kv_term(0, 1), kv_term(0, 2)], kv_keep(0))
        kv_y.start()

    def kv_out():
        if nz == 1:
            rs_out(RK)
            return
        out, buffer, first, into = LEAVE[RK]
        kv_z(1, 1).wait_recv()
        kv_z(1, 2).wait_recv()
        kv_y.wait_recv()

        def put(rows, near, value):
            to = pl.ds(pl.multiple_of(near.start + first, 16), 32)
            buffer[to, into : into + 2 * hs] = value

        kv_add(
            z, [kv_mine(1), kv_term(1, 1), kv_term(1, 2), kv_term(0, nz - 1)], put
        )
        rs_leave(RK).start()
        for own in (0, 1):
            for i in range(nz - 1):
                kv_z(own, i).wait_send()
        kv_y.wait_send()

    def rs_mid(r, first=0, last=nz):
        g, at, width = REDUCE[r]
        cols = slice(at, at + width)

        @pl.loop(min(first, nz), min(last, nz))
        def _(i):
            k = by_step(i, TAKES)
            rs_y(r, k).wait_recv()
            start = pl.multiple_of(k * chunk_rows, 16)

            def add(more):
                @pl.loop(0, chunk_rows // 32)
                def _(n):
                    rows = pl.ds(pl.multiple_of(start + n * 32, 16), 32)
                    both = W[g][y, rows, cols].astype(F32) + RY[g][rows, cols].astype(F32)
                    if more:
                        near = pl.ds(pl.multiple_of(n * 32, 16), 32)
                        both = both + RZ[g][0, near, cols].astype(F32)
                    RY[g][rows, cols] = both.astype(BF)

            if nz == 1:
                add(False)
                return

            @pl.when(i == 2)
            def _():
                rs_z(r, 0).wait_recv()
                add(True)

            pl.when(i != 2)(lambda: add(False))
            pl.when(i < nz - 1)(lambda: rs_z(r, i).start())

    def rs_end(r, put):
        g, at, width = REDUCE[r]
        cols = slice(at, at + width)
        if nz > 1:
            rs_z(r, 1).wait_recv()
            rs_z(r, 2).wait_recv()
        start = pl.multiple_of(z * chunk_rows, 16)

        @pl.loop(0, chunk_rows // 32)
        def _(n):
            rows = pl.ds(pl.multiple_of(n * 32, 16), 32)
            total = RY[g][pl.ds(pl.multiple_of(start + n * 32, 16), 32), cols].astype(F32)
            if nz > 1:
                total = total + RZ[g][1, rows, cols].astype(F32)
                total = total + RZ[g][2, rows, cols].astype(F32)
            put(rows, total)

    def rs_sent(r):
        for i in range(nz):
            rs_y(r, by_step(i, TAKES)).wait_send()
            if i < nz - 1:
                rs_z(r, i).wait_send()

    def rs_leave(r):
        g, at, width = REDUCE[r]
        out, buffer, first, into = LEAVE[r]
        return pltpu.make_async_copy(
            buffer.at[pl.ds(first, chunk_rows), pl.ds(into, width)],
            out.at[:, pl.ds(at, width)],
            o.lc.at[r],
        )

    def rs_out(r):
        g, at, width = REDUCE[r]
        out, buffer, first, into = LEAVE[r]
        if nz == 1:

            @pl.loop(0, chunk_rows // 32)
            def _(n):
                rows = pl.ds(pl.multiple_of(n * 32, 16), 32)
                out[rows, at : at + width] = RY[g][rows, at : at + width]

        else:

            def put(rows, total):
                buffer[pl.ds(pl.multiple_of(rows.start + first, 16), 32), into : into + width] = (
                    total
                )

            rs_end(r, put)
            rs_leave(r).start()
        rs_sent(r)


    def rows_sib(i, k, n):
        own, landing = ROWS[i]
        src = own.at[y] if n == 0 else landing.at[k]
        return remote(src, landing.at[k], o.qs.at[i, n], o.qr.at[i, n], sibling)

    def rows_beside(i, k):
        own, landing = ROWS[i]
        return remote(own.at[1 - y], landing.at[k], o.qs.at[i, 2], o.qr.at[i, 2], beside)

    def rows_own(i):
        own, landing = ROWS[i]
        return pltpu.make_async_copy(own.at[y], landing.at[t], o.ql.at[i])

    def rows_start(i):
        rows_own(i).start()
        rows_beside(i, t).start()
        rows_sib(i, t, 0).start()

    other = lax.rem(t + 2, 4)

    def rows_pass(i):
        rows_beside(i, other).wait_recv()
        rows_sib(i, other, 1).start()

    def rows_done(i):
        rows_own(i).wait()
        rows_sib(i, t, 0).wait()
        rows_sib(i, other, 1).wait()
        rows_beside(i, t).wait_send()

    def rows_join(i, out_ref):
        landing = ROWS[i][1]
        wide = 256

        @pl.loop(0, 2)
        def _(k):
            @pl.loop(0, D // wide)
            def _(n):
                cols = pl.ds(pl.multiple_of(n * wide, 128), wide)
                value = jnp.concatenate(
                    [landing[2 * k + j, :held, cols].astype(F32) for j in range(2)], axis=0
                )
                rows = pl.ds(pl.multiple_of(2 * k * held, 16), 2 * held)
                out_ref[rows, cols] = value.astype(out_ref.dtype)


    def home_copy(i):
        return remote(o.hs.at[i], o.hr.at[i], o.hx.at[i], o.hy.at[i], beside)

    def home_block(buffer, k):
        value = buffer[pl.ds(pl.multiple_of(k * held, 8), held), :]
        pad = o.hs.shape[1] - held
        return jnp.concatenate([value, jnp.zeros((pad, D), F32)], axis=0).astype(BF)

    def home_send(i, buffer):
        o.hs[i] = home_block(buffer, other)
        home_copy(i).start()

    home_out = (
        pltpu.make_async_copy(o.ho, o.oh.at[y], o.lh.at[0]),
        pltpu.make_async_copy(o.hr.at[0], o.oh.at[1 - y], o.lh.at[1]),
        pltpu.make_async_copy(
            o.gres.at[pl.ds(pl.multiple_of(t * held, 8), held)], o.gh.at[y], o.lh.at[2]
        ),
        pltpu.make_async_copy(o.ext.at[pl.ds(0, held)], o.gh.at[1 - y], o.lh.at[3]),
    )

    barrier = pltpu.get_barrier_semaphore()
    for g in (A, B, C):
        own_copy(g).start()
    when(dec, cross_own.start)
    for peer in (sibling, across, beside, skew):
        pl.semaphore_signal(barrier, inc=1, device_id=peer, device_id_type=MESH)
    for i in range(1, nz):
        pl.semaphore_signal(
            barrier, inc=1, device_id=(p, lax.rem(d + i, nz), t), device_id_type=MESH
        )
    pl.semaphore_wait(barrier, 4 + nz - 1)
    tiles_start()
    rows_start(0)
    when(enc, lambda: rows_start(2))
    own_copy(A).wait()
    ag_hop(A, 0)
    when(enc, cross_in.start)
    own_copy(B).wait()
    ag_hop(B, 0, False)
    when(enc, lambda: ag_side(B, 0))
    own_copy(C).wait()

    lane = lax.broadcasted_iota(jnp.int32, (1, 128), 1)
    lo = jnp.where(lane < 64, 1.0, 0.0).astype(BF)
    hi = jnp.where(lane < 64, 0.0, 1.0).astype(BF)

    def rows_loop(fn, step=RT):
        @pl.loop(0, L // step)
        def _(i):
            fn(pl.ds(pl.multiple_of(i * step, step), step))

    def half_rows(h):
        return pl.ds(pl.multiple_of(h * half, 16), half)

    def half_loop(h, fn):
        @pl.loop(0, half // RT)
        def _(i):
            fn(pl.ds(pl.multiple_of(h * half + i * RT, 16), RT))

    def halves(fn, ready=None, after=None):
        @pl.loop(0, 2)
        def _(i):
            h = lax.rem(core + i, 2)
            if ready is not None:
                ready(i, h)
            half_loop(h, fn)
            if after is not None:
                pl.when(i == 0)(after)

    def normed(v, gain_no):
        r = lax.rsqrt(jnp.mean(v * v, axis=-1, keepdims=True) + EPSILON)
        return (v * r * o.g[gain_no : gain_no + 1, :]).astype(BF)

    def norm_rows(x_ref, gain_no, out_ref):
        def one(rows):
            out_ref[rows, :] = normed(x_ref[rows, :].astype(F32), gain_no)

        rows_loop(one)

    def ex_copy(slot, h):
        rows = half_rows(h)
        return remote(
            o.exs.at[slot, rows], o.exr.at[slot, rows], o.ss.at[slot, h], o.rs.at[slot, h], sibling
        )

    def exchange(slot, fn):
        @pl.loop(0, 2)
        def _(i):
            h = lax.rem(1 - core + i, 2)
            rows = half_rows(h)
            o.exs[slot, rows, :] = fn(rows).astype(BF)
            ex_copy(slot, h).start()

    def arrived(slot):
        return lambda i, h: ex_copy(slot, h).wait()

    def ex_rows(slot, rows):
        return o.exs[slot, rows, :].astype(F32) + o.exr[slot, rows, :].astype(F32)

    def residual(slot, base_ref, put, after=None):
        def one(rows):
            put(rows, base_ref[rows, :].astype(F32) + ex_rows(slot, rows))

        halves(one, arrived(slot), after)

    def keep(ref, gain_no=None, normed_ref=None):
        def put(rows, value):
            ref[rows, :] = value
            if gain_no is not None:
                normed_ref[rows, :] = normed(value, gain_no)

        return put

    def norm_back(slot, x_ref, gain_no, put, after=None):
        o.dgacc[gain_no] = jnp.zeros((8, D), F32)

        def one(rows):
            dh = ex_rows(slot, rows)
            v = x_ref[rows, :].astype(F32)
            r = lax.rsqrt(jnp.mean(v * v, axis=-1, keepdims=True) + EPSILON)
            n = v * r
            dhg = dh * o.g[gain_no : gain_no + 1, :]
            mu = jnp.mean(dhg * n, axis=-1, keepdims=True)
            put(rows, r * (dhg - n * mu))
            o.dgacc[gain_no] += jnp.sum((dh * n).reshape(RT // 8, 8, D), axis=0)

        halves(one, arrived(slot), after)

    def split(a):
        return slice(a * hs, (a + 1) * hs)

    def both_shards(fn):
        @pl.loop(0, 2)
        def _(a):
            fn(a)

    def side_first(fn, r):
        @pl.loop(0, 2)
        def _(i):
            fn(lax.rem(1 - y + i, 2))
            if r is not None:
                pl.when(i == 0)(lambda: rs_start(r))

    def kv_project():
        def one(a):
            o.dkv[a] = dot(o.ns[...], W[A][a, :, at_kv:at_ext]).astype(BF)

        both_shards(one)
        for a in range(2):
            o.ks[:, split(a)] = o.dkv[a, :, :hs]
            o.vs[:, split(a)] = o.dkv[a, :, hs:]

    def pair_stack(block):
        return jnp.concatenate([block * lo, block * hi], axis=0)

    def pair_pick(stacked):
        return jnp.where(lane < 64, stacked[:qb_rows], stacked[qb_rows:])

    def attn_fwd(q_ref, mix_ref, mem, own, causal, hooks=()):
        @pl.loop(0, n_blk)
        def _(b):
            for i, hook in enumerate(hooks):
                pl.when(b == i)(hook)
            rows = pl.ds(pl.multiple_of(b * qb_rows, 16), qb_rows)
            wrows = pl.ds(pl.multiple_of(b * qb_rows, 16), win_w)
            sq = o.segq[rows, :]
            if mem:
                o.mm[...] = jnp.where(sq == o.srcseg[...], 0.0, NEG)
            if own:
                allowed = sq == o.segw[b]
                if causal:
                    qi = lax.broadcasted_iota(jnp.int32, (qb_rows, win_w), 0)
                    kj = lax.broadcasted_iota(jnp.int32, (qb_rows, win_w), 1)
                    allowed = allowed & (kj - HALO <= qi)
                o.mo[...] = jnp.where(allowed, 0.0, NEG)

            @pl.loop(0, n_pair)
            def _(j):
                cols = pl.ds(pl.multiple_of(j * 128, 128), 128)
                q2 = pair_stack(q_ref[rows, cols])
                parts = []
                if mem:
                    s = dot_nt(q2, o.ks[:, cols]).reshape(2, qb_rows, L)
                    parts.append(s + o.mm[...][None])
                if own:
                    s = dot_nt(q2, o.kp[wrows, cols]).reshape(2, qb_rows, win_w)
                    parts.append(s + o.tb[pl.ds(2 * j, 2)] + o.mo[...][None])
                top = [jnp.max(s, axis=-1, keepdims=True) for s in parts]
                top = functools.reduce(jnp.maximum, top)
                exps = [jnp.exp(s - top) for s in parts]
                total = sum(jnp.sum(e, axis=-1, keepdims=True) for e in exps)
                inv = 1.0 / total
                probs = [(e * inv).astype(BF).reshape(2 * qb_rows, -1) for e in exps]
                mixed = 0.0
                if mem:
                    o.pm[b * n_pair + j] = probs[0]
                    mixed = mixed + dot(probs[0], o.vs[:, cols])
                if own:
                    o.po[b * n_pair + j] = probs[-1]
                    mixed = mixed + dot(probs[-1], o.vp[wrows, cols])
                mix_ref[rows, cols] = pair_pick(mixed).astype(BF)

    def attn_back(q_ref, mix_ref, mem, own, hooks=()):
        if mem:
            o.dks[...] = jnp.zeros(o.dks.shape, F32)
            o.dvs[...] = jnp.zeros(o.dvs.shape, F32)
        if own:
            o.dkp[...] = jnp.zeros(o.dkp.shape, F32)
            o.dvp[...] = jnp.zeros(o.dvp.shape, F32)
            o.tb[...] = jnp.zeros(o.tb.shape, F32)

        @pl.loop(0, n_blk)
        def _(b):
            for i, hook in enumerate(hooks):
                pl.when(b == i)(hook)
            rows = pl.ds(pl.multiple_of(b * qb_rows, 16), qb_rows)
            wrows = pl.ds(pl.multiple_of(b * qb_rows, 16), win_w)

            @pl.loop(0, n_pair)
            def _(j):
                cols = pl.ds(pl.multiple_of(j * 128, 128), 128)
                q2 = pair_stack(q_ref[rows, cols])
                do2 = pair_stack(o.dmix[rows, cols])
                mix = mix_ref[rows, cols].astype(F32)
                delta = jnp.sum(
                    do2.astype(F32).reshape(2, qb_rows, 128) * mix[None], axis=-1, keepdims=True
                ).reshape(2 * qb_rows, 1)
                dq2 = 0.0
                if mem:
                    probs = o.pm[b * n_pair + j]
                    dp = dot_nt(do2, o.vs[:, cols])
                    ds = (probs.astype(F32) * (dp - delta)).astype(BF)
                    dq2 = dq2 + dot(ds, o.ks[:, cols])
                    o.dks[:, cols] += dot_tn(ds, q2)
                    o.dvs[:, cols] += dot_tn(probs, do2)
                if own:
                    probs = o.po[b * n_pair + j]
                    dp = dot_nt(do2, o.vp[wrows, cols])
                    ds = (probs.astype(F32) * (dp - delta)).astype(BF)
                    dq2 = dq2 + dot(ds, o.kp[wrows, cols])
                    o.dkp[wrows, cols] += dot_tn(ds, q2)
                    o.dvp[wrows, cols] += dot_tn(probs, do2)
                    o.tb[pl.ds(2 * j, 2)] += ds.astype(F32).reshape(2, qb_rows, win_w)
                o.dq[rows, cols] = (pair_pick(dq2) * (HD**-0.5)).astype(BF)

    def out_project(slot, mix_ref, weight_ref, at):
        exchange(
            slot,
            lambda rows: sum(
                dot_nt(mix_ref[rows, split(a)], weight_ref[a, :, at : at + hs]) for a in range(2)
            ),
        )

    def mix_grads(weight_ref, at):
        for a in range(2):
            o.dmix[:, split(a)] = dot(o.gb[...], weight_ref[a, :, at : at + hs]).astype(BF)

    fw = fs // 2

    def ff_half(n):
        a = n // 2
        return a, pl.ds(pl.multiple_of((n - 2 * a) * fw, 128), fw)

    def shard_cols(a):
        return slice(a * fs, (a + 1) * fs)

    def ff_fwd():
        ag_wait(B)

        @pl.loop(0, 4)
        def _(n):
            a, half_cols = ff_half(n)
            cols = pl.ds(pl.multiple_of(n * fw, 128), fw)
            o.pre[...] = dot(o.nc[...], W[B][a, :, half_cols])

            def one(rows):
                v = o.pre[rows, :]
                v2 = v * v
                th = jnp.tanh(0.7978845608028654 * v * (1.0 + 0.044715 * v2))
                cdf = 0.5 * (1.0 + th)
                slope = (0.5 * 0.7978845608028654) * v * (1.0 - th * th)
                o.hidden[rows, cols] = (v * cdf).astype(BF)
                o.gp[rows, cols] = (cdf + slope * (1.0 + (3 * 0.044715) * v2)).astype(BF)

            rows_loop(one, 32)

        ag_wait(C)
        when(dec, lambda: ag_also_hop(3))
        exchange(
            2,
            lambda rows: sum(dot_nt(o.hidden[rows, shard_cols(a)], W[C][a]) for a in range(2)),
        )

    def side_cols(a, width):
        return pl.ds(pl.multiple_of(a * width, 128), width)

    def ff_pre(n):
        a, half_cols = ff_half(n)
        cols = pl.ds(pl.multiple_of(n * fw, 128), fw)
        o.gp[:, cols] = (
            dot(o.gb[...], W[C][a, :, half_cols]) * o.gp[:, cols].astype(F32)
        ).astype(BF)

    def ff_out_weights():
        def one(a):
            W[C][a] = dot_tn(o.gb[...], o.hidden[:, side_cols(a, fs)]).astype(BF)

        side_first(one, RC)

    def ff_in_weights():
        def one(a):
            W[B][a] = dot_tn(o.nc[...], o.gp[:, side_cols(a, fs)]).astype(BF)

        side_first(one, RB)

    def ff_back():
        ag_finish(B)
        ag_finish(C)
        if nz > 1:
            when(dec, ag_also_sent)

        @pl.loop(0, 4)
        def _(n):
            ff_pre(n)

        exchange(
            0, lambda rows: sum(dot_nt(o.gp[rows, shard_cols(a)], W[B][a]) for a in range(2))
        )
        ff_out_weights()

        def put(rows, dv):
            new = o.gres[rows, :] + dv
            o.gres[rows, :] = new
            o.gb[rows, :] = new.astype(BF)

        norm_back(0, o.xlate, 1, put)

    def x_copy(way):
        rows = half_rows(core)
        return remote(
            o.xsend.at[rows], o.xbuf.at[rows], o.xss.at[way, 0], o.xrs.at[way, 0], across
        )

    def x_pass(way, h):
        rows = half_rows(h)
        return remote(
            o.xbuf.at[rows], o.xbuf.at[rows], o.xss.at[way, 1], o.xrs.at[way, 1], sibling
        )

    def x_halves(way, fn):
        x_copy(way).wait_recv()
        x_pass(way, core).start()

        def ready(i, h):
            pl.when(i == 1)(lambda: x_pass(way, h).wait_recv())

        halves(fn, ready)
        x_pass(way, core).wait_send()

    def kv_weights():
        def one(a):
            W[A][a, :, at_kv:at_ext] = dot_tn(o.ns[...], o.dkv[a]).astype(BF)

        side_first(one, RK if nz == 1 else None)
        kv_start(0)
        kv_start(1)

    def dkv_grads():
        for a in range(2):
            o.dkv[a, :, :hs] = o.dks[:, split(a)].astype(BF)
            o.dkv[a, :, hs:] = o.dvs[:, split(a)].astype(BF)
        exchange(
            2,
            lambda rows: sum(
                dot_nt(o.dkv[a, rows, :], W[A][a, :, at_kv:at_ext]) for a in range(2)
            ),
        )

    when(enc, lambda: rows_pass(2))

    def first_cross():
        cross_own.wait()
        cross_in.wait_recv()
        ag_hop(X, 0)

    when(dec, first_cross)
    ag_hop(A, 1)
    ag_hop(C, 0, False)
    tiles_pass()
    if STAGE:
        when(dec, lambda: ag_pass_on(A))
    ag_side(C, 0)
    when(enc, lambda: pick_rows(0))
    when(enc, lambda: pick_rows(1))
    ag_hop(A, 2)
    ag_hop(B, 1, False)
    when(enc, lambda: ag_side(B, 1))
    when(dec, lambda: ag_hop(X, 1))
    rows_pass(0)
    ag_hop(C, 1, False)
    if STAGE:
        when(dec, lambda: ag_pass_on(C))
    ag_hop(A, 3)
    ag_side(C, 1)
    ag_hop(B, 2, False)
    when(enc, lambda: ag_side(B, 2))
    when(dec, lambda: ag_hop(X, 2))
    rows_done(0)
    rows_join(0, o.x)

    @pl.when(dec)
    def _():
        ag_hop(X, 3)
        ag_side(B, 0)
        ag_side(B, 1)
        ag_side(B, 2)

    ag_wait(A)
    ag_hop(C, 2)
    tiles_done()
    for a in range(2):
        rel_lines = dot(o.rl[a].astype(BF), o.hot[...])
        for h in range(n_rel):
            o.tb[a * n_rel + h] = pltpu.roll(
                jnp.broadcast_to(rel_lines[h : h + 1, :], (qb_rows, win_w)),
                0,
                1,
                stride=1,
                stride_axis=0,
            )
    pad = jnp.zeros((HALO, hc), BF)
    for ref in (o.kp, o.vp):
        ref[:HALO, :] = pad
        ref[HALO + L :, :] = pad
    norm_rows(o.x, 0, o.na)

    def project_own(a):
        o.dqkv[a] = dot(o.na[...], W[A][a, :, :at_o]).astype(BF)

    both_shards(project_own)
    for a in range(2):
        o.q[:, split(a)] = (o.dqkv[a, :, :hs] * (HD**-0.5)).astype(BF)
        o.kp[HALO : HALO + L, split(a)] = o.dqkv[a, :, hs : 2 * hs]
        o.vp[HALO : HALO + L, split(a)] = o.dqkv[a, :, 2 * hs :]
    hooks = (lambda: ag_hop(B, 3), lambda: ag_hop(C, 3))

    @pl.when(enc)
    def _():
        norm_rows(o.nb, 2, o.ns)
        kv_project()
        attn_fwd(o.q, o.mixa, True, True, False, hooks)

    @pl.when(dec)
    def _():
        ag_also_hop(0)
        attn_fwd(o.q, o.mixa, False, True, True, hooks)

    out_project(0, o.mixa, W[A], at_o)
    when(dec, lambda: rows_start(1))

    @pl.when(enc)
    def _():
        residual(0, o.x, keep(o.xlate, 1, o.nc))

    @pl.when(dec)
    def _():
        ag_wait(X)
        ag_finish(X)
        if STAGE:
            ag_relay(A).wait_send()
            ag_relay(C).wait_send()

        def whole(a):
            for k in range(nz):
                for part in range(2):
                    at = part * (D // 2) + k * cross_rows
                    start = k * chunk_rows + part * cross_rows
                    o.xg[a, at : at + cross_rows, :] = W[X][a, start : start + cross_rows, :]

        both_shards(whole)
        residual(0, o.x, keep(o.xmid, 3, o.nb))
        for a in range(2):
            r = dot(o.nb[...], o.xg[a, :, :hs]).astype(BF)
            o.qb[:, split(a)] = (r * (HD**-0.5)).astype(BF)

        def one(rows):
            o.ns[rows, :] = normed(o.xbuf[rows, :].astype(F32), 2)

        ag_also_hop(1)
        x_halves(0, one)
        kv_project()
        attn_fwd(o.qb, o.mixb, True, False, False)
        ag_also_hop(2)
        out_project(1, o.mixb, o.xg, hs)
        residual(1, o.xmid, keep(o.xlate, 1, o.nc))


    ff_fwd()

    def put_out(rows, value):
        o.gres[rows, :] = value
        o.xsend[rows, :] = value.astype(BF)

    residual(2, o.xlate, put_out, lambda: pl.when(enc)(lambda: x_copy(0).start()))
    when(enc, lambda: rows_start(1))
    home_send(0, o.gres)
    o.ho[...] = home_block(o.gres, t)
    home_out[0].start()
    ag_finish(A)
    rows_pass(1)
    rows_done(1)
    rows_join(1, o.gres)

    @pl.when(enc)
    def _():
        o.dgacc[3] = jnp.zeros((8, D), F32)
        x_copy(0).wait_send()

        def one(rows):
            value = o.gres[rows, :] + o.xbuf[rows, :].astype(F32)
            o.gres[rows, :] = value
            o.gb[rows, :] = value.astype(BF)

        x_halves(1, one)

    when(dec, lambda: rows_join(1, o.gb))


    ff_back()

    @pl.when(dec)
    def _():
        mix_grads(o.xg, hs)
        attn_back(o.qb, o.mixb, True, False)
        dkv_grads()
        exchange(
            1, lambda rows: sum(dot_nt(o.dq[rows, split(a)], o.xg[a, :, :hs]) for a in range(2))
        )

        def put_source(rows, dv):
            o.xsend[rows, :] = dv.astype(BF)

        norm_back(2, o.xbuf, 2, put_source, lambda: x_copy(1).start())
        rs_mid(RC, 0, 2)

        def put_mid(rows, dv):
            new = o.gres[rows, :] + dv
            o.gres[rows, :] = new
            o.xbuf[rows, :] = new.astype(BF)

        norm_back(1, o.xmid, 3, put_mid)
        for a in range(2):
            full = jnp.concatenate(
                [
                    dot_tn(o.nb[...], o.dq[:, split(a)]).astype(BF),
                    dot_tn(o.gb[...], o.mixb[:, split(a)]).astype(BF),
                ],
                axis=1,
            )
            for k in range(nz):
                for part in range(2):
                    at = part * (D // 2) + k * cross_rows
                    to = k * chunk_rows + part * cross_rows
                    W[X][a, to : to + cross_rows, :] = full[at : at + cross_rows]
        rs_start(RX)
        x_copy(1).wait_send()
        o.gb[...] = o.xbuf[...]

    ff_in_weights()
    mix_grads(W[A], at_o)
    for a in range(2):
        W[A][a, :, at_o : at_o + hs] = dot_tn(o.gb[...], o.mixa[:, split(a)]).astype(BF)
    steps = tuple(functools.partial(rs_mid, RC, i, i + 1) for i in range(3))

    @pl.when(enc)
    def _():
        attn_back(o.q, o.mixa, True, True, steps)
        dkv_grads()

    @pl.when(dec)
    def _():
        attn_back(o.q, o.mixa, False, True)
        rs_mid(RC, 2, 3)

    kv_weights()
    rs_mid(RC, 3)
    for a in range(2):
        o.dqkv[a, :, :hs] = o.dq[:, split(a)]
        o.dqkv[a, :, hs : 2 * hs] = o.dkp[HALO : HALO + L, split(a)].astype(BF)
        o.dqkv[a, :, 2 * hs :] = o.dvp[HALO : HALO + L, split(a)].astype(BF)
    last_slot = 1 - p
    exchange(
        last_slot,
        lambda rows: sum(dot_nt(o.dqkv[a, rows, :], W[A][a, :, :at_o]) for a in range(2)),
    )

    @pl.when(enc)
    def _():
        def put_source(rows, dv):
            pass

        norm_back(2, o.nb, 2, put_source)

    heads = 2 * n_pair
    acc = jnp.zeros((heads * 8, win_w), F32)
    for k in range(qb_rows // 8):
        part = o.tb[:, 8 * k : 8 * k + 8, :].reshape(heads * 8, win_w)
        acc = acc + (part if k == 0 else pltpu.roll(part, win_w - 8 * k, 1))
    sub = lax.rem(lax.broadcasted_iota(jnp.int32, (heads * 8, win_w), 0), 8)
    diag = jnp.zeros((heads * 8, win_w), F32)
    for k in range(8):
        turned = acc if k == 0 else pltpu.roll(acc, win_w - k, 1)
        diag = diag + jnp.where(sub == k, turned, 0.0)
    lines = jnp.sum(diag.reshape(heads, 8, win_w), axis=1)

    def put_in(rows, dv):
        o.gres[rows, :] = o.gres[rows, :] + dv

    norm_back(last_slot, o.x, 0, put_in)
    home_send(1, o.gres)
    home_out[2].start()
    sums_start(lines)

    def own_weights(a):
        W[A][a, :, :at_o] = dot_tn(o.na[...], o.dqkv[a]).astype(BF)

    side_first(own_weights, RQ)

    home_copy(0).wait()
    home_out[1].start()
    kv_mid()
    rs_mid(RB)
    rs_out(RC)
    kv_cross()
    sums_mid()
    when(dec, lambda: rs_mid(RX))
    rs_mid(RQ, 0, 2)
    rs_out(RB)
    sums_end()
    rs_mid(RQ, 2)
    kv_out()

    @pl.when(dec)
    def _():
        def put(rows, total):
            o.xt[rows, :] = total

        rs_end(RX, put)
        rs_sent(RX)
        o.xo[...] = o.xt[:cross_rows, :]
        cross_out.start()
        o.ox[...] = o.xt[cross_rows:, :].astype(o.ox.dtype)
        cross_out.wait_send()

    @pl.when(enc)
    def _():
        cross_in.wait_send()
        cross_out.wait_recv()
        o.ox[...] = o.xi[...].astype(o.ox.dtype)

    home_copy(1).wait()
    o.ext[...] = o.hr[1].astype(F32)
    home_out[3].start()
    rs_out(RQ)
    for copy in home_out:
        copy.wait()
    if nz > 1:
        for r in LEAVE:
            rs_leave(r).wait()


def run_kernel(dims, given):
    L, D, hs, fs, nz, qb_rows, win_w = dims
    hc, fc = 2 * hs, 2 * fs
    n_blk, n_pair = L // qb_rows, hc // 128
    LP = L + 2 * HALO
    LBP = -(-(L // 4) // 16) * 16
    CR = D // nz
    widths = dict(a=6 * hs, b=fs, c=fs, x=2 * hs)
    MW = -(-CR // 128) * 128
    S = jax.ShapeDtypeStruct
    SUM = F32 if nz > 1 else BF
    outs = dict(
        oh=S((2, LBP, D), BF),
        gh=S((2, L // 4, D), F32),
        oa=S((CR, widths["a"]), SUM),
        ob=S((CR, widths["b"]), SUM),
        oc=S((CR, widths["c"]), SUM),
        ox=S((CR // 2, widths["x"]), SUM),
        om=S((TILE, MW), F32),
    )
    V = pltpu.VMEM
    LD, LH, LF = (L, D), (L, hc), (L, fc)
    scratch = dict(
        na=V(LD, BF), ns=V(LD, BF), nb=V(LD, BF), nc=V(LD, BF),
        xmid=V(LD, F32), xlate=V(LD, F32), gres=V(LD, F32),
        q=V(LH, BF), kp=V((LP, hc), BF), vp=V((LP, hc), BF), ks=V(LH, BF), vs=V(LH, BF),
        qb=V(LH, BF), mixa=V(LH, BF), mixb=V(LH, BF),
        pm=V((n_blk * n_pair, 2 * qb_rows, L), BF), po=V((n_blk * n_pair, 2 * qb_rows, win_w), BF),
        hidden=V(LF, BF), gp=V(LF, BF), pre=V((L, fs // 2), F32),
        tb=V((2 * n_pair, qb_rows, win_w), F32),
        mm=V((qb_rows, L), F32), mo=V((qb_rows, win_w), F32),
        dmix=V(LH, BF), dq=V(LH, BF), dqkv=V((2, L, 3 * hs), BF), dkv=V((2, L, 2 * hs), BF),
        dkp=V((LP, hc), F32), dvp=V((LP, hc), F32), dks=V(LH, F32), dvs=V(LH, F32),
        gb=V(LD, BF), xbuf=V(LD, BF), xsend=V(LD, BF),
        exs=V((3, L, D), BF), exr=V((3, L, D), BF), dgacc=V((4, 8, D), F32),
        g=V((8, D), F32), ext=V((LBP, D), F32), lines=V((TILE, win_w), F32),
        m=V((3, nz, TILE, MW), BF), ms1=V((2, nz, TILE, MW), BF), ms2=V((nz, TILE, MW), BF),
        ms3=V((max(nz - 1, 1), TILE, MW), BF), mf=V((TILE, MW), F32), mo1=V((TILE, MW), F32),
        mo2=V((TILE, MW), F32), dgl=V((8, D), F32), rl=V((2, TILE, 128), F32),
        idr=V((1, L), jnp.int32),
        x=V(LD, BF), xq=V((4, LBP, D), BF), cq=V((4, LBP, D), BF), mq=V((4, 8, 128), jnp.int32),
        hs=V((2, LBP, D), BF), hr=V((2, LBP, D), BF), ho=V((LBP, D), BF),
        xg=V((2, D, widths["x"]), BF), xt=V((CR, widths["x"]), F32),
        xo=V((CR // 2, widths["x"]), F32), xi=V((CR // 2, widths["x"]), F32),
    )
    for g, width in widths.items():
        scratch["w" + g] = V((2, D, width), BF)
        scratch["y" + g] = V((D, width), BF)
        scratch["z" + g] = V((nz - 1, CR, width) if nz > 1 else (1, 16, width), BF)
    sem = pltpu.SemaphoreType.DMA
    scratch.update(ss=sem((3, 2)), rs=sem((3, 2)), gd=sem((3, 3)), ga=sem((2, nz)), gb2=sem((nz,)), mt=sem((8, nz)), mx=sem((6,)), tg=sem((2,)), xss=sem((2, 2)), xrs=sem((2, 2)))
    scratch.update(xw=sem((4,)), oc_sem=sem((4,)), kq=sem((4, nz)), lc=sem((6,)), lh=sem((4,)))
    scratch.update(qs=sem((3, 3)), qr=sem((3, 3)), ql=sem((3,)), hx=sem((2,)), hy=sem((2,)))
    for name in ("gr", "gl", "gs", "gz", "gy"):
        scratch[name] = sem((4, nz))
    for name in ("rs_s", "rs_r", "rz_s", "rz_r"):
        scratch[name] = sem((6, nz))
    spec = pl.BlockSpec(memory_space=pltpu.VMEM)
    far = pl.BlockSpec(memory_space=pl.ANY)
    names = list(given) + list(outs) + list(scratch)
    FAR = ["sa", "sb", "sc", "sx", "xs", "cs", "ms", "table", "oh", "gh"]
    if nz > 1:
        FAR += ["oa", "ob", "oc"]
    return pl.pallas_call(
        functools.partial(kernel, dims, names),
        out_shape=list(outs.values()),
        in_specs=[far if name in FAR else spec for name in given],
        out_specs=[far if name in FAR else spec for name in outs],
        scratch_shapes=list(scratch.values()),
        compiler_params=pltpu.CompilerParams(
            collective_id=0, has_side_effects=True, vmem_limit_bytes=63 << 20
        ),
        name="layers",
    )(*given.values())


def prep_kernel(dims, n_dp, names, *refs):
    L, D, hs, fs, nz, qb_rows, win_w = dims
    o = Refs()
    for name, ref in zip(names, refs, strict=True):
        setattr(o, name, ref)
    section = lax.axis_index("pipe")
    y = lax.axis_index("tensor") // 2
    rows = D // n_dp
    held = L // 4
    for raw, out in ((o.li, o.xs), (o.co, o.cs)):
        o.tmp[...] = raw[...].astype(F32)
        pad = jnp.zeros((out.shape[1] - held, D), F32)
        for r in range(2):
            out[r] = jnp.concatenate([o.tmp[:, r, :], pad], axis=0).astype(BF)
    for i in range(3):
        o.sa[:, i * hs : (i + 1) * hs] = o.qkv[i]
    o.sa[:, 3 * hs : 4 * hs] = o.so[...].astype(F32).T.astype(BF)
    for i in range(2):
        o.kvt[...] = o.kv[...].astype(F32)
        o.sa[:, (4 + i) * hs : (5 + i) * hs] = o.kvt[:, i, :].astype(BF)
    n_gain = o.gain.shape[0]
    heads = o.rel.shape[0]
    o.mf[...] = jnp.zeros(o.mf.shape, F32)
    o.mf[:n_gain, : o.gain.shape[1]] = o.gain[...].astype(F32)
    o.mf[CROSS_AT : CROSS_AT + 1, : o.cg.shape[1]] = o.cg[...].astype(F32)
    o.mf[REL_AT : REL_AT + heads, : o.rel.shape[1]] = o.rel[...].astype(F32)
    o.sm[...] = o.mf[...].astype(BF)
    o.sx[:, :hs] = o.cq[...]
    o.sx[:, hs : 2 * hs] = o.cw[...].astype(F32).T.astype(BF)
    o.ms[...] = jnp.zeros(o.ms.shape, jnp.int32)
    for r in range(2):
        o.ms[r, 0:1, :held] = o.ids[r : r + 1, :]
    own = o.seg[section, pl.ds(y, 1), :]
    first = o.seg[0, pl.ds(y, 1), :]
    o.segq[...] = jnp.broadcast_to(own.astype(F32), (8, L)).T[:, :1].astype(jnp.int32)
    slots = lax.broadcasted_iota(jnp.int32, (1, L), 1).astype(F32)
    slots = jnp.floor((slots + 0.5) * (1.0 / MEM)).astype(jnp.int32)
    o.srcseg[...] = jnp.where(section == 0, slots, first)
    o.line[...] = jnp.full(o.line.shape, -1, jnp.int32)
    o.line[:, HALO : HALO + L] = own
    for b in range(L // qb_rows):
        o.segw[b] = o.line[:, b * qb_rows : b * qb_rows + win_w]
    o.win[...] = jnp.full(o.win.shape, -1, jnp.int32)
    o.win[:, : 2 * HALO] = o.buckets[:, L - HALO : L + HALO]
    at = lax.broadcasted_iota(jnp.int32, (128, win_w), 0)
    o.hot[...] = jnp.where(at == o.win[...], 1.0, 0.0).astype(BF)


def run_prep(dims, n_dp, given):
    L, D, hs, fs, nz, qb_rows, win_w = dims
    rows, held = D // n_dp, L // 4
    MW = -(-(D // nz) // 128) * 128
    LBP = -(-held // 16) * 16
    S = jax.ShapeDtypeStruct
    outs = dict(
        xs=S((2, LBP, D), BF),
        cs=S((2, LBP, D), BF),
        sa=S((rows, 6 * hs), BF),
        sx=S((rows // 2, 2 * hs), BF),
        sm=S((TILE, MW), BF),
        ms=S((2, 8, 128), jnp.int32),
        segq=S((L, 1), jnp.int32),
        segw=S((L // qb_rows, 1, win_w), jnp.int32),
        srcseg=S((1, L), jnp.int32),
        hot=S((128, win_w), BF),
    )
    V = pltpu.VMEM
    scratch = dict(
        tmp=V((held, 2, D), F32),
        kvt=V((rows, 2, hs), F32),
        mf=V((TILE, MW), F32),
        line=V((1, L + 2 * HALO), jnp.int32),
        win=V((1, win_w), jnp.int32),
    )
    spec = pl.BlockSpec(memory_space=pltpu.VMEM)
    names = list(given) + list(outs) + list(scratch)
    return pl.pallas_call(
        functools.partial(prep_kernel, dims, n_dp, names),
        out_shape=list(outs.values()),
        in_specs=[spec] * len(given),
        out_specs=[spec] * len(outs),
        scratch_shapes=list(scratch.values()),
        compiler_params=pltpu.CompilerParams(vmem_limit_bytes=60 << 20),
        name="prep",
    )(*given.values())


def finish_kernel(dims, names, *refs):
    L, D, hs, fs, nz, qb_rows, win_w = dims
    o = Refs()
    for name, ref in zip(names, refs, strict=True):
        setattr(o, name, ref)
    o.ffi[...] = o.gb[...]
    o.ffo[...] = o.gc[...]
    for r in range(2):
        o.gin[:, r, :] = o.gh[r]
        o.tmp[:, r, :] = o.oh[r, : L // 4].astype(F32)
    o.out[...] = o.tmp[...].astype(BF)
    for i in range(3):
        o.qkv[i] = o.ga[:, i * hs : (i + 1) * hs]
    o.so[...] = o.ga[:, 3 * hs : 4 * hs].T
    for i in range(2):
        o.kv[:, i, :] = o.ga[:, (4 + i) * hs : (5 + i) * hs]
    rows = o.ga.shape[0]
    for i in range(o.gain.shape[0]):
        o.gain[i] = o.gm[i : i + 1, :rows]
    heads, _, nb_rows = o.rel.shape
    for i in range(heads):
        o.rel[i] = o.gm[REL_AT + i : REL_AT + i + 1, :nb_rows]
    o.cq[...] = o.gx[:, :hs]
    o.co[...] = o.gx[:, hs : 2 * hs].T
    o.cg[...] = o.gm[CROSS_AT : CROSS_AT + 1, : rows // 2]


def run_finish(dims, rel_shape, sums):
    L, D, hs, fs, nz, qb_rows, win_w = dims
    rows = sums[2].shape[0]
    held = L // 4
    S = jax.ShapeDtypeStruct
    outs = dict(
        out=S((held, 2, D), BF),
        gin=S((held, 2, D), F32),
        qkv=S((3, rows, hs), F32),
        so=S((hs, rows), F32),
        kv=S((rows, 2, hs), F32),
        rel=S((rel_shape[1], 1, rel_shape[0]), F32),
        gain=S((3, 1, rows), F32),
        cq=S((rows // 2, hs), F32),
        co=S((hs, rows // 2), F32),
        cg=S((1, rows // 2), F32),
        ffi=S((rows, fs), F32),
        ffo=S((rows, fs), F32),
    )
    spec = pl.BlockSpec(memory_space=pltpu.VMEM)
    return pl.pallas_call(
        functools.partial(
            finish_kernel, dims, ["oh", "gh", "ga", "gb", "gc", "gx", "gm", *outs, "tmp"]
        ),
        out_shape=list(outs.values()),
        in_specs=[spec] * 7,
        out_specs=[spec] * len(outs),
        scratch_shapes=[pltpu.VMEM((held, 2, D), F32)],
        compiler_params=pltpu.CompilerParams(vmem_limit_bytes=60 << 20),
        name="finish",
    )(*sums)


def body(
    layer_inputs,
    segment_ids,
    slot_ids,
    memory_table,
    buckets,
    self_qkv,
    self_out,
    source_kv,
    ff_in,
    ff_out,
    rel_bias,
    gains,
    cross_query,
    cross_out,
    cross_gain,
    cotangents,
):
    nt = lax.axis_size("tensor")
    n_dp = lax.axis_size("dp")
    assert nt == 4 and layer_inputs.shape[2] == 2
    D = layer_inputs.shape[3]
    L = segment_ids.shape[2]
    hs = self_qkv.shape[3]
    fs = ff_in.shape[2]
    qb_rows, win_w = 160, 256
    rows = D // n_dp
    nz = 4 if n_dp == 4 and (rows // 2) % 32 == 0 else 1
    dims = (L, D, hs, fs, nz, qb_rows, win_w)
    held = L // nt
    gain, rel, cross_g = gains[0], rel_bias[0].T, cross_gain[None]
    if nz != n_dp:
        gain = lax.all_gather(gain, "dp", axis=1, tiled=True)
        rel = lax.all_gather(rel, "dp", axis=1, tiled=True)
        cross_g = lax.all_gather(cross_g, "dp", axis=1, tiled=True)
    prepared = run_prep(
        dims,
        n_dp,
        dict(
            li=layer_inputs[0],
            co=cotangents[0],
            qkv=self_qkv[0].transpose(1, 0, 2),
            so=self_out[0],
            kv=source_kv[0],
            gain=gain,
            rel=rel,
            cq=cross_query,
            cw=cross_out,
            cg=cross_g,
            seg=segment_ids,
            ids=slot_ids.T,
            buckets=buckets[None],
        ),
    )
    xs, cs, sa, sx, sm, ms, segq, segw, srcseg, hot = prepared
    shards = [sa, ff_in[0], ff_out[0].T, sx]
    if nz != n_dp:
        shards = [lax.all_gather(shard, "dp", axis=0, tiled=True) for shard in shards]
    given = dict(
        xs=xs, cs=cs, ms=ms, table=memory_table, sm=sm, segq=segq, segw=segw, srcseg=srcseg, hot=hot,
        sa=shards[0], sb=shards[1], sc=shards[2], sx=shards[3],
    )
    oh, gh, *sums, gm = run_kernel(dims, given)
    if nz != n_dp:
        sums = [
            lax.psum_scatter(full, "dp", scatter_dimension=0, tiled=True).astype(F32)
            for full in sums
        ]

        def share(first, count, width):
            mine = lax.psum_scatter(
                gm[first : first + count, :width], "dp", scatter_dimension=1, tiled=True
            )
            below = TILE - first - count
            return jnp.pad(mine, ((first, below), (0, 128 - mine.shape[1])))

        gm = (
            share(0, CROSS_AT, D)
            + share(CROSS_AT, 1, D // 2)
            + share(REL_AT, rel_bias.shape[2], NB)
        )
    done = run_finish(dims, rel_bias.shape[1:], [oh, gh, *sums, gm])
    out, gin, qkv, so, kv, rel, gain, cq, co, cg, ff_i, ff_o = done
    return (
        out[None],
        gin[None],
        qkv.transpose(1, 0, 2)[None],
        so[None],
        kv[None],
        ff_i[None],
        ff_o.T[None],
        rel.transpose(1, 2, 0),
        gain.transpose(1, 0, 2),
        cq,
        co,
        cg[0],
    )


def solution(mesh):
    placed = (
        P("pipe", "tensor", "dp", None),
        P(None, "dp", None),
        P("tensor", "dp"),
        P(),
        P(),
        P("pipe", "dp", None, "tensor"),
        P("pipe", "tensor", "dp"),
        P("pipe", "dp", None, "tensor"),
        P("pipe", "dp", "tensor"),
        P("pipe", "tensor", "dp"),
        P("pipe", "dp", "tensor"),
        P("pipe", None, "dp"),
        P(("pipe", "dp"), "tensor"),
        P("tensor", ("pipe", "dp")),
        P(("pipe", "dp")),
        P("pipe", "tensor", "dp", None),
    )
    return jax.shard_map(
        body,
        mesh=mesh,
        in_specs=placed,
        out_specs=(
            P("pipe", "tensor", "dp", None),
            P("pipe", "tensor", "dp", None),
            P("pipe", "dp", None, "tensor"),
            P("pipe", "tensor", "dp"),
            P("pipe", "dp", None, "tensor"),
            P("pipe", "dp", "tensor"),
            P("pipe", "tensor", "dp"),
            P("pipe", "dp", "tensor"),
            P("pipe", None, "dp"),
            P(("pipe", "dp"), "tensor"),
            P("tensor", ("pipe", "dp")),
            P(("pipe", "dp")),
        ),
        check_vma=False,
    )
```

```python
import functools

import jax
import jax.numpy as jnp
from jax import lax
from jax.experimental import pallas as pl
from jax.experimental.pallas import tpu as pltpu
from jax.sharding import PartitionSpec as P

HD = 64
NB = 32
MEM = 20
HALO = 48
TILE = 16
CROSS_AT = 3
REL_AT = 8
PIECE = 256
EPSILON = 1e-06
NEG = -1000000000.0
BF = jnp.bfloat16
F32 = jnp.float32
MESH = pl.DeviceIdType.MESH
RT = 48


def dot(a, b):
    return lax.dot_general(a, b, (((1,), (0,)), ((), ())), preferred_element_type=F32)


def dot_nt(a, b):
    return lax.dot_general(a, b, (((1,), (1,)), ((), ())), preferred_element_type=F32)


def dot_tn(a, b):
    return lax.dot_general(a, b, (((0,), (0,)), ((), ())), preferred_element_type=F32)


class Refs:
    pass


def kernel(dims, names, *refs):
    L, D, hs, fs, nz, qb_rows, win_w = dims
    hc, fc = 2 * hs, 2 * fs
    at_o, at_kv, at_ext = 3 * hs, 4 * hs, 6 * hs
    chunk_rows = D // nz
    cross_rows = chunk_rows // 2
    n_blk = L // qb_rows
    n_pair = hc // 128
    o = Refs()
    for name, ref in zip(names, refs, strict=True):
        setattr(o, name, ref)
    p = lax.axis_index("pipe")
    d = lax.axis_index("dp")
    t = lax.axis_index("tensor")
    enc, dec = p == 0, p == 1
    core = lax.rem(t, 2)
    y = t // 2
    z = d if nz > 1 else 0
    skew = (1 - p, d, lax.rem(t + 2, 4))
    sibling = (p, d, t + 1 - 2 * core)
    across = (1 - p, d, t)
    beside = (p, d, lax.rem(t + 2, 4))
    half = L // 2
    held = L // 4
    A, B, C, X = range(4)
    shard = (o.sa, o.sb, o.sc, o.sx)
    W = (o.wa, o.wb, o.wc, o.wx)
    RY = (o.ya, o.yb, o.yc, o.yx)
    RZ = (o.za, o.zb, o.zc, o.zx)
    RB, RC, RX, RQ, RK = range(5)
    REDUCE = {
        RB: (B, 0, fs),
        RC: (C, 0, fs),
        RX: (X, 0, 2 * hs),
        RQ: (A, 0, at_kv),
        RK: (A, at_kv, 2 * hs),
    }
    LEAVE = {
        RB: (o.ob, o.xlate, 0, 0),
        RC: (o.oc, o.xmid, 0, 0),
        RQ: (o.oa, o.xmid, chunk_rows, 0),
        RK: (o.oa, o.xlate, chunk_rows, 0),
    }
    STAGE = {} if nz == 1 else {
        A: o.hidden.at[pl.ds(0, chunk_rows), pl.ds(0, 6 * hs)],
        C: o.gp.at[pl.ds(0, chunk_rows), pl.ds(fs, fs)],
    }
    ROWS = ((o.xs, o.xq), (o.cs, o.cq), (o.ms, o.mq))

    def chunk(k):
        return pl.ds(pl.multiple_of(k * chunk_rows, 16), chunk_rows)

    def remote(src, dst, send, recv, device):
        return pltpu.make_async_remote_copy(
            src_ref=src,
            dst_ref=dst,
            send_sem=send,
            recv_sem=recv,
            device_id=device,
            device_id_type=MESH,
        )


    def ag_right(g, k):
        slot = W[g].at[y, chunk(k)]
        return remote(slot, slot, o.gr.at[g, k], o.gz.at[g, k], (p, d + 1, t))

    def ag_left(g, k):
        slot = W[g].at[y, chunk(k)]
        return remote(slot, slot, o.gl.at[g, k], o.gz.at[g, k], (p, d - 1, t))

    def ag_beside(g, k):
        slot = W[g].at[y, chunk(k)]
        return remote(slot, slot, o.gs.at[g, k], o.gy.at[g, k], beside)

    def ag_came(g, k):
        slot = W[g].at[y, chunk(k)]
        remote(slot, slot, o.gr.at[g, k], o.gz.at[g, k], beside).wait_recv()

    def ag_each(g, h, act):
        if h == 0:
            act(z, z + 1 < nz, z > 0, True)
        else:
            act(z - h, z + 1 < nz, False, z - h >= 0)
            act(z + h, False, z > 0, z + h < nz)

    def when(cond, fn):
        if cond is True:
            fn()
        elif cond is not False:
            pl.when(cond)(fn)


    def ag_skew(g):
        return remote(W[g].at[y, chunk(z)], STAGE[g], o.gd.at[g, 0], o.gd.at[g, 1], skew)

    def ag_relay(g):
        slot = W[g].at[1 - y, chunk(z)]
        return remote(STAGE[g], slot, o.gd.at[g, 2], o.gy.at[g, z], across)

    def ag_pass_on(g):
        ag_skew(g).wait_recv()
        ag_relay(g).start()

    def ag_aside(g, k, own, wait):
        act = (lambda c: c.wait_send()) if wait else (lambda c: c.start())
        if own and g in STAGE:
            pl.when(enc)(lambda: act(ag_skew(g)))
            pl.when(dec)(lambda: act(ag_beside(g, k)))
        elif not own and g == C:
            pl.when(enc)(lambda: act(ag_beside(g, k)))
        else:
            act(ag_beside(g, k))


    def ag_also(k, way):
        slot = W[C].at[1 - y, chunk(k)]
        return remote(slot, slot, o.ga.at[way, k], o.gb2.at[k], (p, d + (1, -1)[way], t))

    def ag_also_hop(h):
        if h >= nz or nz == 1:
            return

        def act(k, right, left, here):
            def go():
                slot = W[C].at[1 - y, chunk(k)]
                if h == 0:
                    remote(slot, slot, o.gs.at[C, k], o.gy.at[C, k], beside).wait_recv()
                else:
                    remote(slot, slot, o.ga.at[0, k], o.gb2.at[k], beside).wait_recv()
                when(right, lambda: ag_also(k, 0).start())
                when(left, lambda: ag_also(k, 1).start())

            when(here, go)

        ag_each(C, h, act)

    def ag_also_sent():
        for h in range(nz):

            def act(k, right, left, here):
                def go():
                    when(right, lambda: ag_also(k, 0).wait_send())
                    when(left, lambda: ag_also(k, 1).wait_send())

                when(here, go)

            ag_each(C, h, act)

    def ag_hop(g, h, aside=True):
        if h >= nz:
            return

        def act(k, right, left, here):
            def go():
                if h > 0:
                    ag_came(g, k)
                if nz > 1:
                    when(right, lambda: ag_right(g, k).start())
                    when(left, lambda: ag_left(g, k).start())
                if aside:
                    ag_aside(g, k, h == 0, False)

            when(here, go)

        ag_each(g, h, act)

    def ag_side(g, h):
        if h >= nz:
            return

        def act(k, right, left, here):
            when(here, lambda: ag_aside(g, k, h == 0, False))

        ag_each(g, h, act)

    def ag_wait(g):
        if g == C and nz > 1:
            pl.when(enc)(lambda: ag_wait_all(g))
        else:
            ag_wait_all(g)

    def ag_wait_all(g):
        for k in range(nz):
            slot = W[g].at[1 - y, chunk(k)]
            remote(slot, slot, o.gs.at[g, k], o.gy.at[g, k], beside).wait_recv()

    def ag_finish(g):
        for h in range(nz):

            def act(k, right, left, here):
                def go():
                    if nz > 1:
                        when(right, lambda: ag_right(g, k).wait_send())
                        when(left, lambda: ag_left(g, k).wait_send())
                    ag_aside(g, k, h == 0, True)

                when(here, go)

            ag_each(g, h, act)

    def own_copy(g):
        return pltpu.make_async_copy(shard[g], W[g].at[y, chunk(z)], o.oc_sem.at[g])

    def cross_part(k, part):
        start = k * chunk_rows + part * cross_rows
        return pl.ds(pl.multiple_of(start, 16), cross_rows)

    cross_own = pltpu.make_async_copy(o.sx, W[X].at[y, cross_part(z, 1)], o.oc_sem.at[X])
    cross_in = remote(
        o.sx, W[X].at[y, cross_part(z, 0)], o.xw.at[0], o.xw.at[1], across
    )
    cross_out = remote(o.xo, o.xi, o.xw.at[2], o.xw.at[3], across)


    nb_each = NB // nz
    n_rel = hs // HD

    def others(fn):
        if nz > 1:

            @pl.loop(1, nz)
            def _(i):
                fn(lax.rem(z + i, nz))

    def tile_z(a, k, to, sems):
        slot = o.m.at[a, k]
        return remote(slot, slot, o.mt.at[sems, to], o.mt.at[sems + 1, k], (p, to, t))

    def tile_beside(k):
        slot = o.m.at[y, k]
        return remote(slot, slot, o.mt.at[2, k], o.mt.at[3, k], beside)

    def tile_across():
        return remote(o.m.at[y, z], o.m.at[2, z], o.mx.at[0], o.mx.at[1], across)

    def tiles_start():
        o.m[y, z] = o.sm[...]

        @pl.when(enc)
        def _():
            o.m[2] = jnp.zeros(o.m.shape[1:], BF)

        others(lambda k: tile_z(y, z, k, 0).start())
        tile_beside(z).start()
        when(enc, lambda: tile_across().start())

    def tiles_pass():
        def one(k):
            tile_z(y, k, k, 0).wait_recv()
            tile_beside(k).start()

        others(one)

        @pl.when(dec)
        def _():
            tile_across().wait_recv()
            others(lambda k: tile_z(2, z, k, 4).start())

    def tiles_done():
        @pl.loop(0, nz)
        def _(k):
            slot = o.m.at[1 - y, k]
            remote(slot, slot, o.mt.at[2, k], o.mt.at[3, k], beside).wait_recv()
            tile_beside(k).wait_send()

        others(lambda k: tile_z(y, z, k, 0).wait_send())
        when(enc, lambda: tile_across().wait_send())

        @pl.when(dec)
        def _():
            others(lambda k: tile_z(2, k, k, 4).wait_recv())
            others(lambda k: tile_z(2, z, k, 4).wait_send())

        o.rl[...] = jnp.zeros(o.rl.shape, F32)
        for k in range(nz):
            block = o.m[y, k].astype(F32)
            o.g[:CROSS_AT, k * chunk_rows : (k + 1) * chunk_rows] = block[:CROSS_AT, :chunk_rows]
            for part in range(2):
                cross = block if part else o.m[2, k].astype(F32)
                at = part * (D // 2) + k * cross_rows
                o.g[CROSS_AT : CROSS_AT + 1, at : at + cross_rows] = cross[
                    CROSS_AT : CROSS_AT + 1, :cross_rows
                ]
            for a in range(2):
                rel = o.m[a, k].astype(F32)
                o.rl[a, :n_rel, k * nb_each : (k + 1) * nb_each] = rel[
                    REL_AT : REL_AT + n_rel, :nb_each
                ]

    def sums_y():
        return remote(o.ms1.at[1 - y], o.ms2, o.mx.at[2], o.mx.at[3], beside)

    def sums_z(k):
        away = lax.rem(z + nz - 1 - k, nz)
        return remote(o.ms2.at[k], o.ms3.at[away], o.mt.at[6, k], o.mt.at[7, away], (p, k, t))

    def sums_z_came(i):
        remote(o.ms2.at[z], o.ms3.at[i], o.mt.at[6, z], o.mt.at[7, i], beside).wait_recv()

    def sums_across():
        return remote(o.mo1, o.mo2, o.mx.at[4], o.mx.at[5], across)

    def sums_start(lines):
        o.dgl[...] = jnp.zeros(o.dgl.shape, F32)
        for i in range(4):
            o.dgl[i : i + 1, :] = jnp.sum(o.dgacc[i], axis=0, keepdims=True)
        for a in range(2):
            o.lines[...] = jnp.zeros(o.lines.shape, F32)
            o.lines[:n_rel, :] = lines[n_rel * a : n_rel * (a + 1), :]
            whole = o.lines[...]
            high = whole.astype(BF)
            low = (whole - high.astype(F32)).astype(BF)
            o.rl[a] = dot_nt(high, o.hot[...]) + dot_nt(low, o.hot[...])
            for k in range(nz):
                o.mf[...] = jnp.zeros(o.mf.shape, F32)
                o.mf[:CROSS_AT, :chunk_rows] = o.dgl[
                    :CROSS_AT, k * chunk_rows : (k + 1) * chunk_rows
                ]
                for part in range(2):
                    at = part * (D // 2) + k * cross_rows
                    row = CROSS_AT + part
                    o.mf[row : row + 1, :cross_rows] = o.dgl[
                        CROSS_AT : CROSS_AT + 1, at : at + cross_rows
                    ]
                o.mf[REL_AT : REL_AT + n_rel, :nb_each] = o.rl[
                    a, :n_rel, k * nb_each : (k + 1) * nb_each
                ]
                o.ms1[a, k] = o.mf[...].astype(BF)
        sums_y().start()

    def sums_mid():
        sums_y().wait()
        for k in range(nz):
            both = o.ms1[y, k].astype(F32) + o.ms2[k].astype(F32)
            o.ms2[k] = both.astype(BF)
        others(lambda k: sums_z(k).start())

    def sums_end():
        total = o.ms2[z].astype(F32)
        for i in range(nz - 1):
            sums_z_came(i)
            total = total + o.ms3[i].astype(F32)
        o.om[...] = total
        others(lambda k: sums_z(k).wait_send())

        @pl.when(dec)
        def _():
            o.mo1[...] = total
            sums_across().start()
            o.om[CROSS_AT : CROSS_AT + 1, :] = total[CROSS_AT + 1 : CROSS_AT + 2, :]
            sums_across().wait_send()

        @pl.when(enc)
        def _():
            sums_across().wait_recv()
            o.om[CROSS_AT : CROSS_AT + 1, :] = o.mo2[CROSS_AT : CROSS_AT + 1, :]


    def piece(c, slot):
        return pltpu.make_async_copy(
            o.table.at[pl.ds(pl.multiple_of(c * PIECE, PIECE), PIECE)],
            o.exs.at[slot, pl.ds(0, PIECE)],
            o.tg.at[slot],
        )

    def pick_rows():
        n_piece = o.table.shape[0] // PIECE
        piece(0, 0).start()
        rows_done(2)
        for k in range(4):
            o.idr[:, k * held : (k + 1) * held] = o.mq[k, 0:1, :held]
        o.gres[...] = jnp.zeros(o.gres.shape, F32)

        @pl.loop(0, n_piece)
        def _(c):
            slot = lax.rem(c, 2)
            pl.when(c + 1 < n_piece)(lambda: piece(c + 1, 1 - slot).start())
            at = lax.broadcasted_iota(jnp.int32, (PIECE, L), 0) + c * PIECE
            hit = jnp.where(at == o.idr[...], 1.0, 0.0).astype(BF)
            piece(c, slot).wait()
            o.gres[...] += dot_tn(hit, o.exs[slot, :PIECE, :])

        def one(rows):
            o.nb[rows, :] = o.gres[rows, :].astype(BF)

        rows_loop(one)


    def rs_y(r, k):
        g, at, width = REDUCE[r]
        cols = pl.ds(at, width)
        return remote(
            W[g].at[1 - y, chunk(k), cols],
            RY[g].at[chunk(k), cols],
            o.rs_s.at[r, k],
            o.rs_r.at[r, k],
            beside,
        )

    mate = z + 1 - 2 * lax.rem(z, 2)
    far = 2 - 2 * (z // 2)
    TAKES = (far + lax.rem(mate, 2), mate, far + lax.rem(z, 2), z)
    GOES = (mate, mate, far + lax.rem(z, 2), z)

    def by_step(i, values):
        if nz == 1:
            return z
        weights = (
            (1 - i) * (2 - i) * (3 - i) // 6,
            i * (2 - i) * (3 - i) // 2,
            i * (i - 1) * (3 - i) // 2,
            i * (i - 1) * (i - 2) // 6,
        )
        return sum(value * weight for value, weight in zip(values, weights))

    def rs_z(r, i):
        g, at, width = REDUCE[r]
        cols = pl.ds(at, width)
        return remote(
            RY[g].at[chunk(by_step(i, TAKES)), cols],
            RZ[g].at[i, :, cols],
            o.rz_s.at[r, i],
            o.rz_r.at[r, i],
            (p, by_step(i, GOES), t),
        )

    def rs_start(r):
        for i in range(nz):
            rs_y(r, by_step(i, TAKES)).start()


    kv_cols = slice(at_kv, at_ext)
    kv_lanes = pl.ds(at_kv, 2 * hs)

    def kv_slot(own, i):
        return RZ[A].at[i, :, kv_lanes] if own else RY[A].at[chunk(i), kv_lanes]

    def kv_z(own, i):
        a = y if own else 1 - y
        return remote(
            W[A].at[a, chunk(TAKES[i]), kv_lanes],
            kv_slot(own, i),
            o.kq.at[own, i],
            o.kq.at[2 + own, i],
            (p, GOES[i], t),
        )

    kv_y = remote(
        W[A].at[1 - y, chunk(z), kv_lanes],
        RY[A].at[chunk(nz - 1), kv_lanes],
        o.kq.at[0, nz - 1],
        o.kq.at[2, nz - 1],
        beside,
    )

    def kv_add(k, terms, put):
        start = pl.multiple_of(k * chunk_rows, 16)

        @pl.loop(0, chunk_rows // 32)
        def _(n):
            rows = pl.ds(pl.multiple_of(start + n * 32, 16), 32)
            near = pl.ds(pl.multiple_of(n * 32, 16), 32)
            put(rows, near, sum(term(rows, near).astype(F32) for term in terms))

    def kv_term(own, i):
        if own:
            return lambda rows, near: RZ[A][i, near, kv_cols]
        return lambda rows, near: RY[A][
            pl.ds(pl.multiple_of(i * chunk_rows + near.start, 16), 32), kv_cols
        ]

    def kv_mine(own):
        a = y if own else 1 - y
        return lambda rows, near: W[A][a, rows, kv_cols]

    def kv_keep(own):
        a = y if own else 1 - y

        def put(rows, near, value):
            W[A][a, rows, kv_cols] = value.astype(BF)

        return put

    def kv_start(own):
        if nz > 1:
            kv_z(own, 0).start()
            kv_z(own, 1).start()

    def kv_mid():
        if nz == 1:
            rs_mid(RK)
            return
        for own in (0, 1):
            kv_z(own, 0).wait_recv()
            kv_add(TAKES[2], [kv_mine(own), kv_term(own, 0)], kv_keep(own))
            kv_z(own, 2).start()

    def kv_cross():
        if nz == 1:
            return
        kv_z(0, 1).wait_recv()
        kv_z(0, 2).wait_recv()
        kv_add(z, [kv_mine(0), kv_term(0, 1), kv_term(0, 2)], kv_keep(0))
        kv_y.start()

    def kv_out():
        if nz == 1:
            rs_out(RK)
            return
        out, buffer, first, into = LEAVE[RK]
        kv_z(1, 1).wait_recv()
        kv_z(1, 2).wait_recv()
        kv_y.wait_recv()

        def put(rows, near, value):
            to = pl.ds(pl.multiple_of(near.start + first, 16), 32)
            buffer[to, into : into + 2 * hs] = value

        kv_add(
            z, [kv_mine(1), kv_term(1, 1), kv_term(1, 2), kv_term(0, nz - 1)], put
        )
        rs_leave(RK).start()
        for own in (0, 1):
            for i in range(nz - 1):
                kv_z(own, i).wait_send()
        kv_y.wait_send()

    def rs_mid(r, first=0, last=nz):
        g, at, width = REDUCE[r]
        cols = slice(at, at + width)

        @pl.loop(min(first, nz), min(last, nz))
        def _(i):
            k = by_step(i, TAKES)
            rs_y(r, k).wait_recv()
            start = pl.multiple_of(k * chunk_rows, 16)

            def add(more):
                @pl.loop(0, chunk_rows // 32)
                def _(n):
                    rows = pl.ds(pl.multiple_of(start + n * 32, 16), 32)
                    both = W[g][y, rows, cols].astype(F32) + RY[g][rows, cols].astype(F32)
                    if more:
                        near = pl.ds(pl.multiple_of(n * 32, 16), 32)
                        both = both + RZ[g][0, near, cols].astype(F32)
                    RY[g][rows, cols] = both.astype(BF)

            if nz == 1:
                add(False)
                return

            @pl.when(i == 2)
            def _():
                rs_z(r, 0).wait_recv()
                add(True)

            pl.when(i != 2)(lambda: add(False))
            pl.when(i < nz - 1)(lambda: rs_z(r, i).start())

    def rs_end(r, put):
        g, at, width = REDUCE[r]
        cols = slice(at, at + width)
        if nz > 1:
            rs_z(r, 1).wait_recv()
            rs_z(r, 2).wait_recv()
        start = pl.multiple_of(z * chunk_rows, 16)

        @pl.loop(0, chunk_rows // 32)
        def _(n):
            rows = pl.ds(pl.multiple_of(n * 32, 16), 32)
            total = RY[g][pl.ds(pl.multiple_of(start + n * 32, 16), 32), cols].astype(F32)
            if nz > 1:
                total = total + RZ[g][1, rows, cols].astype(F32)
                total = total + RZ[g][2, rows, cols].astype(F32)
            put(rows, total)

    def rs_sent(r):
        for i in range(nz):
            rs_y(r, by_step(i, TAKES)).wait_send()
            if i < nz - 1:
                rs_z(r, i).wait_send()

    def rs_leave(r):
        g, at, width = REDUCE[r]
        out, buffer, first, into = LEAVE[r]
        return pltpu.make_async_copy(
            buffer.at[pl.ds(first, chunk_rows), pl.ds(into, width)],
            out.at[:, pl.ds(at, width)],
            o.lc.at[r],
        )

    def rs_out(r):
        g, at, width = REDUCE[r]
        out, buffer, first, into = LEAVE[r]
        if nz == 1:

            @pl.loop(0, chunk_rows // 32)
            def _(n):
                rows = pl.ds(pl.multiple_of(n * 32, 16), 32)
                out[rows, at : at + width] = RY[g][rows, at : at + width]

        else:

            def put(rows, total):
                buffer[pl.ds(pl.multiple_of(rows.start + first, 16), 32), into : into + width] = (
                    total
                )

            rs_end(r, put)
            rs_leave(r).start()
        rs_sent(r)


    def rows_sib(i, k, n):
        own, landing = ROWS[i]
        src = own.at[y] if n == 0 else landing.at[k]
        return remote(src, landing.at[k], o.qs.at[i, n], o.qr.at[i, n], sibling)

    def rows_beside(i, k):
        own, landing = ROWS[i]
        return remote(own.at[1 - y], landing.at[k], o.qs.at[i, 2], o.qr.at[i, 2], beside)

    def rows_own(i):
        own, landing = ROWS[i]
        return pltpu.make_async_copy(own.at[y], landing.at[t], o.ql.at[i])

    def rows_start(i):
        rows_own(i).start()
        rows_beside(i, t).start()
        rows_sib(i, t, 0).start()

    other = lax.rem(t + 2, 4)

    def rows_pass(i):
        rows_beside(i, other).wait_recv()
        rows_sib(i, other, 1).start()

    def rows_done(i):
        rows_own(i).wait()
        rows_sib(i, t, 0).wait()
        rows_sib(i, other, 1).wait()
        rows_beside(i, t).wait_send()

    def rows_join(i, out_ref):
        landing = ROWS[i][1]
        wide = 256

        @pl.loop(0, 2)
        def _(k):
            @pl.loop(0, D // wide)
            def _(n):
                cols = pl.ds(pl.multiple_of(n * wide, 128), wide)
                value = jnp.concatenate(
                    [landing[2 * k + j, :held, cols].astype(F32) for j in range(2)], axis=0
                )
                rows = pl.ds(pl.multiple_of(2 * k * held, 16), 2 * held)
                out_ref[rows, cols] = value.astype(out_ref.dtype)


    def home_copy(i):
        return remote(o.hs.at[i], o.hr.at[i], o.hx.at[i], o.hy.at[i], beside)

    def home_block(buffer, k):
        value = buffer[pl.ds(pl.multiple_of(k * held, 8), held), :]
        pad = o.hs.shape[1] - held
        return jnp.concatenate([value, jnp.zeros((pad, D), F32)], axis=0).astype(BF)

    def home_send(i, buffer):
        o.hs[i] = home_block(buffer, other)
        home_copy(i).start()

    home_out = (
        pltpu.make_async_copy(o.ho, o.oh.at[y], o.lh.at[0]),
        pltpu.make_async_copy(o.hr.at[0], o.oh.at[1 - y], o.lh.at[1]),
        pltpu.make_async_copy(
            o.gres.at[pl.ds(pl.multiple_of(t * held, 8), held)], o.gh.at[y], o.lh.at[2]
        ),
        pltpu.make_async_copy(o.ext.at[pl.ds(0, held)], o.gh.at[1 - y], o.lh.at[3]),
    )

    barrier = pltpu.get_barrier_semaphore()
    for g in (A, B, C):
        own_copy(g).start()
    when(dec, cross_own.start)
    for peer in (sibling, across, beside, skew):
        pl.semaphore_signal(barrier, inc=1, device_id=peer, device_id_type=MESH)
    for i in range(1, nz):
        pl.semaphore_signal(
            barrier, inc=1, device_id=(p, lax.rem(d + i, nz), t), device_id_type=MESH
        )
    pl.semaphore_wait(barrier, 4 + nz - 1)
    tiles_start()
    rows_start(0)
    when(enc, lambda: rows_start(2))
    own_copy(A).wait()
    ag_hop(A, 0)
    when(enc, cross_in.start)
    own_copy(B).wait()
    ag_hop(B, 0, False)
    when(enc, lambda: ag_side(B, 0))
    own_copy(C).wait()

    lane = lax.broadcasted_iota(jnp.int32, (1, 128), 1)
    lo = jnp.where(lane < 64, 1.0, 0.0).astype(BF)
    hi = jnp.where(lane < 64, 0.0, 1.0).astype(BF)

    def rows_loop(fn, step=RT):
        @pl.loop(0, L // step)
        def _(i):
            fn(pl.ds(pl.multiple_of(i * step, step), step))

    def half_rows(h):
        return pl.ds(pl.multiple_of(h * half, 16), half)

    def tile_rows(h, j):
        return pl.ds(pl.multiple_of(h * half + j * RT, 16), RT)

    def halves(fn, ready=None, before=None, after=None):
        @pl.loop(0, 2)
        def _(i):
            h = lax.rem(core + i, 2)
            if ready is not None:
                ready(i, h)

            @pl.loop(0, half // RT)
            def _(j):
                if before is not None:
                    before(i, h, j)
                fn(tile_rows(h, j))
                if after is not None:
                    pl.when(i == 0)(lambda: after(j))

    def normed(v, gain_no):
        r = lax.rsqrt(jnp.mean(v * v, axis=-1, keepdims=True) + EPSILON)
        return (v * r * o.g[gain_no : gain_no + 1, :]).astype(BF)

    def norm_rows(x_ref, gain_no, out_ref):
        def one(rows):
            out_ref[rows, :] = normed(x_ref[rows, :].astype(F32), gain_no)

        rows_loop(one)

    def ex_copy(slot, h):
        rows = half_rows(h)
        return remote(
            o.exs.at[slot, rows], o.exr.at[slot, rows], o.ss.at[slot, h], o.rs.at[slot, h], sibling
        )

    def exchange(slot, fn):
        @pl.loop(0, 2)
        def _(i):
            h = lax.rem(1 - core + i, 2)
            rows = half_rows(h)
            o.exs[slot, rows, :] = fn(rows).astype(BF)
            ex_copy(slot, h).start()

    def arrived(slot):
        return lambda i, h: ex_copy(slot, h).wait()

    def ex_rows(slot, rows):
        return o.exs[slot, rows, :].astype(F32) + o.exr[slot, rows, :].astype(F32)

    def residual(slot, base_ref, put, after=None):
        def one(rows):
            put(rows, base_ref[rows, :].astype(F32) + ex_rows(slot, rows))

        halves(one, arrived(slot), after=after)

    def keep(ref, gain_no=None, normed_ref=None):
        def put(rows, value):
            ref[rows, :] = value
            if gain_no is not None:
                normed_ref[rows, :] = normed(value, gain_no)

        return put

    def norm_back(slot, x_ref, gain_no, put, after=None):
        o.dgacc[gain_no] = jnp.zeros((8, D), F32)

        def one(rows):
            dh = ex_rows(slot, rows)
            v = x_ref[rows, :].astype(F32)
            r = lax.rsqrt(jnp.mean(v * v, axis=-1, keepdims=True) + EPSILON)
            n = v * r
            dhg = dh * o.g[gain_no : gain_no + 1, :]
            mu = jnp.mean(dhg * n, axis=-1, keepdims=True)
            put(rows, r * (dhg - n * mu))
            o.dgacc[gain_no] += jnp.sum((dh * n).reshape(RT // 8, 8, D), axis=0)

        halves(one, arrived(slot), after=after)

    def split(a):
        return slice(a * hs, (a + 1) * hs)

    def both_shards(fn):
        @pl.loop(0, 2)
        def _(a):
            fn(a)

    def side_first(fn, r):
        @pl.loop(0, 2)
        def _(i):
            fn(lax.rem(1 - y + i, 2))
            if r is not None:
                pl.when(i == 0)(lambda: rs_start(r))

    def kv_project():
        def one(a):
            o.dkv[a] = dot(o.ns[...], W[A][a, :, at_kv:at_ext]).astype(BF)

        both_shards(one)
        for a in range(2):
            o.ks[:, split(a)] = o.dkv[a, :, :hs]
            o.vs[:, split(a)] = o.dkv[a, :, hs:]

    def pair_stack(block):
        return jnp.concatenate([block * lo, block * hi], axis=0)

    def pair_pick(stacked):
        return jnp.where(lane < 64, stacked[:qb_rows], stacked[qb_rows:])

    def attn_fwd(q_ref, mix_ref, mem, own, causal, hooks=()):
        @pl.loop(0, n_blk)
        def _(b):
            for i, hook in enumerate(hooks):
                pl.when(b == i)(hook)
            rows = pl.ds(pl.multiple_of(b * qb_rows, 16), qb_rows)
            wrows = pl.ds(pl.multiple_of(b * qb_rows, 16), win_w)
            sq = o.segq[rows, :]
            if mem:
                o.mm[...] = jnp.where(sq == o.srcseg[...], 0.0, NEG)
            if own:
                allowed = sq == o.segw[b]
                if causal:
                    qi = lax.broadcasted_iota(jnp.int32, (qb_rows, win_w), 0)
                    kj = lax.broadcasted_iota(jnp.int32, (qb_rows, win_w), 1)
                    allowed = allowed & (kj - HALO <= qi)
                o.mo[...] = jnp.where(allowed, 0.0, NEG)

            @pl.loop(0, n_pair)
            def _(j):
                cols = pl.ds(pl.multiple_of(j * 128, 128), 128)
                q2 = pair_stack(q_ref[rows, cols])
                parts = []
                if mem:
                    s = dot_nt(q2, o.ks[:, cols]).reshape(2, qb_rows, L)
                    parts.append(s + o.mm[...][None])
                if own:
                    s = dot_nt(q2, o.kp[wrows, cols]).reshape(2, qb_rows, win_w)
                    parts.append(s + o.tb[pl.ds(2 * j, 2)] + o.mo[...][None])
                top = [jnp.max(s, axis=-1, keepdims=True) for s in parts]
                top = functools.reduce(jnp.maximum, top)
                exps = [jnp.exp(s - top) for s in parts]
                total = sum(jnp.sum(e, axis=-1, keepdims=True) for e in exps)
                inv = 1.0 / total
                probs = [(e * inv).astype(BF).reshape(2 * qb_rows, -1) for e in exps]
                mixed = 0.0
                if mem:
                    o.pm[b * n_pair + j] = probs[0]
                    mixed = mixed + dot(probs[0], o.vs[:, cols])
                if own:
                    o.po[b * n_pair + j] = probs[-1]
                    mixed = mixed + dot(probs[-1], o.vp[wrows, cols])
                mix_ref[rows, cols] = pair_pick(mixed).astype(BF)

    def attn_back(q_ref, mix_ref, mem, own, hooks=()):
        if mem:
            o.dks[...] = jnp.zeros(o.dks.shape, F32)
            o.dvs[...] = jnp.zeros(o.dvs.shape, F32)
        if own:
            o.dkp[...] = jnp.zeros(o.dkp.shape, F32)
            o.dvp[...] = jnp.zeros(o.dvp.shape, F32)
            o.tb[...] = jnp.zeros(o.tb.shape, F32)

        @pl.loop(0, n_blk)
        def _(b):
            for i, hook in enumerate(hooks):
                pl.when(b == i)(hook)
            rows = pl.ds(pl.multiple_of(b * qb_rows, 16), qb_rows)
            wrows = pl.ds(pl.multiple_of(b * qb_rows, 16), win_w)

            @pl.loop(0, n_pair)
            def _(j):
                cols = pl.ds(pl.multiple_of(j * 128, 128), 128)
                q2 = pair_stack(q_ref[rows, cols])
                do2 = pair_stack(o.dmix[rows, cols])
                mix = mix_ref[rows, cols].astype(F32)
                delta = jnp.sum(
                    do2.astype(F32).reshape(2, qb_rows, 128) * mix[None], axis=-1, keepdims=True
                ).reshape(2 * qb_rows, 1)
                dq2 = 0.0
                if mem:
                    probs = o.pm[b * n_pair + j]
                    dp = dot_nt(do2, o.vs[:, cols])
                    ds = (probs.astype(F32) * (dp - delta)).astype(BF)
                    dq2 = dq2 + dot(ds, o.ks[:, cols])
                    o.dks[:, cols] += dot_tn(ds, q2)
                    o.dvs[:, cols] += dot_tn(probs, do2)
                if own:
                    probs = o.po[b * n_pair + j]
                    dp = dot_nt(do2, o.vp[wrows, cols])
                    ds = (probs.astype(F32) * (dp - delta)).astype(BF)
                    dq2 = dq2 + dot(ds, o.kp[wrows, cols])
                    o.dkp[wrows, cols] += dot_tn(ds, q2)
                    o.dvp[wrows, cols] += dot_tn(probs, do2)
                    o.tb[pl.ds(2 * j, 2)] += ds.astype(F32).reshape(2, qb_rows, win_w)
                o.dq[rows, cols] = (pair_pick(dq2) * (HD**-0.5)).astype(BF)

    def out_project(slot, mix_ref, weight_ref, at):
        exchange(
            slot,
            lambda rows: sum(
                dot_nt(mix_ref[rows, split(a)], weight_ref[a, :, at : at + hs]) for a in range(2)
            ),
        )

    def mix_grads(weight_ref, at):
        for a in range(2):
            o.dmix[:, split(a)] = dot(o.gb[...], weight_ref[a, :, at : at + hs]).astype(BF)

    fw = fs // 2

    def ff_half(n):
        a = n // 2
        return a, pl.ds(pl.multiple_of((n - 2 * a) * fw, 128), fw)

    def shard_cols(a):
        return slice(a * fs, (a + 1) * fs)

    def ff_fwd():
        ag_wait(B)

        @pl.loop(0, 4)
        def _(n):
            a, half_cols = ff_half(n)
            cols = pl.ds(pl.multiple_of(n * fw, 128), fw)
            o.pre[...] = dot(o.nc[...], W[B][a, :, half_cols])

            def one(rows):
                v = o.pre[rows, :]
                v2 = v * v
                th = jnp.tanh(0.7978845608028654 * v * (1.0 + 0.044715 * v2))
                cdf = 0.5 * (1.0 + th)
                slope = (0.5 * 0.7978845608028654) * v * (1.0 - th * th)
                o.hidden[rows, cols] = (v * cdf).astype(BF)
                o.gp[rows, cols] = (cdf + slope * (1.0 + (3 * 0.044715) * v2)).astype(BF)

            rows_loop(one, 32)

        ag_wait(C)
        when(dec, lambda: ag_also_hop(3))
        exchange(
            2,
            lambda rows: sum(dot_nt(o.hidden[rows, shard_cols(a)], W[C][a]) for a in range(2)),
        )

    def side_cols(a, width):
        return pl.ds(pl.multiple_of(a * width, 128), width)

    def ff_pre(n):
        a, half_cols = ff_half(n)
        cols = pl.ds(pl.multiple_of(n * fw, 128), fw)
        o.gp[:, cols] = (
            dot(o.gb[...], W[C][a, :, half_cols]) * o.gp[:, cols].astype(F32)
        ).astype(BF)

    def ff_out_weights():
        def one(a):
            W[C][a] = dot_tn(o.gb[...], o.hidden[:, side_cols(a, fs)]).astype(BF)

        side_first(one, RC)

    def ff_in_weights():
        def one(a):
            W[B][a] = dot_tn(o.nc[...], o.gp[:, side_cols(a, fs)]).astype(BF)

        side_first(one, RB)

    def ff_back():
        ag_finish(B)
        ag_finish(C)
        if nz > 1:
            when(dec, ag_also_sent)

        @pl.loop(0, 4)
        def _(n):
            ff_pre(n)

        exchange(
            0, lambda rows: sum(dot_nt(o.gp[rows, shard_cols(a)], W[B][a]) for a in range(2))
        )
        ff_out_weights()

        def put(rows, dv):
            new = o.gres[rows, :] + dv
            o.gres[rows, :] = new
            o.gb[rows, :] = new.astype(BF)

        norm_back(0, o.xlate, 1, put)

    n_tile = half // RT

    def x_copy(way, j):
        rows = tile_rows(core, j)
        return remote(
            o.xsend.at[rows], o.xbuf.at[rows], o.xss.at[way, 0, j], o.xrs.at[way, 0, j], across
        )

    def x_pass(way, h, j):
        rows = tile_rows(h, j)
        return remote(
            o.xbuf.at[rows], o.xbuf.at[rows], o.xss.at[way, 1, j], o.xrs.at[way, 1, j], sibling
        )

    def x_sent(way):
        @pl.loop(0, n_tile)
        def _(j):
            x_copy(way, j).wait_send()

    def x_halves(way, fn):
        def before(i, h, j):
            @pl.when(i == 0)
            def _():
                x_copy(way, j).wait_recv()
                x_pass(way, h, j).start()

            pl.when(i == 1)(lambda: x_pass(way, h, j).wait_recv())

        halves(fn, before=before)

        @pl.loop(0, n_tile)
        def _(j):
            x_pass(way, core, j).wait_send()

    def kv_weights():
        def one(a):
            W[A][a, :, at_kv:at_ext] = dot_tn(o.ns[...], o.dkv[a]).astype(BF)

        side_first(one, RK if nz == 1 else None)
        kv_start(0)
        kv_start(1)

    def dkv_grads():
        for a in range(2):
            o.dkv[a, :, :hs] = o.dks[:, split(a)].astype(BF)
            o.dkv[a, :, hs:] = o.dvs[:, split(a)].astype(BF)
        exchange(
            2,
            lambda rows: sum(
                dot_nt(o.dkv[a, rows, :], W[A][a, :, at_kv:at_ext]) for a in range(2)
            ),
        )

    when(enc, lambda: rows_pass(2))

    def first_cross():
        cross_own.wait()
        cross_in.wait_recv()
        ag_hop(X, 0)

    when(dec, first_cross)
    ag_hop(A, 1)
    ag_hop(C, 0, False)
    tiles_pass()
    if STAGE:
        when(dec, lambda: ag_pass_on(A))
    ag_side(C, 0)
    when(enc, pick_rows)
    ag_hop(A, 2)
    ag_hop(B, 1, False)
    when(enc, lambda: ag_side(B, 1))
    when(dec, lambda: ag_hop(X, 1))
    rows_pass(0)
    ag_hop(C, 1, False)
    if STAGE:
        when(dec, lambda: ag_pass_on(C))
    ag_hop(A, 3)
    ag_side(C, 1)
    ag_hop(B, 2, False)
    when(enc, lambda: ag_side(B, 2))
    when(dec, lambda: ag_hop(X, 2))
    rows_done(0)
    rows_join(0, o.x)

    @pl.when(dec)
    def _():
        ag_hop(X, 3)
        ag_side(B, 0)
        ag_side(B, 1)
        ag_side(B, 2)

    ag_wait(A)
    ag_hop(C, 2)
    tiles_done()
    for a in range(2):
        rel_lines = dot(o.rl[a].astype(BF), o.hot[...])
        for h in range(n_rel):
            o.tb[a * n_rel + h] = pltpu.roll(
                jnp.broadcast_to(rel_lines[h : h + 1, :], (qb_rows, win_w)),
                0,
                1,
                stride=1,
                stride_axis=0,
            )
    pad = jnp.zeros((HALO, hc), BF)
    for ref in (o.kp, o.vp):
        ref[:HALO, :] = pad
        ref[HALO + L :, :] = pad
    norm_rows(o.x, 0, o.na)

    def project_own(a):
        o.dqkv[a] = dot(o.na[...], W[A][a, :, :at_o]).astype(BF)

    both_shards(project_own)
    for a in range(2):
        o.q[:, split(a)] = (o.dqkv[a, :, :hs] * (HD**-0.5)).astype(BF)
        o.kp[HALO : HALO + L, split(a)] = o.dqkv[a, :, hs : 2 * hs]
        o.vp[HALO : HALO + L, split(a)] = o.dqkv[a, :, 2 * hs :]
    hooks = (lambda: ag_hop(B, 3), lambda: ag_hop(C, 3))

    @pl.when(enc)
    def _():
        norm_rows(o.nb, 2, o.ns)
        kv_project()
        attn_fwd(o.q, o.mixa, True, True, False, hooks)

    @pl.when(dec)
    def _():
        ag_also_hop(0)
        attn_fwd(o.q, o.mixa, False, True, True, hooks)

    out_project(0, o.mixa, W[A], at_o)
    when(dec, lambda: rows_start(1))

    @pl.when(enc)
    def _():
        residual(0, o.x, keep(o.xlate, 1, o.nc))

    @pl.when(dec)
    def _():
        ag_wait(X)
        ag_finish(X)
        if STAGE:
            ag_relay(A).wait_send()
            ag_relay(C).wait_send()

        def whole(a):
            for k in range(nz):
                for part in range(2):
                    at = part * (D // 2) + k * cross_rows
                    start = k * chunk_rows + part * cross_rows
                    o.xg[a, at : at + cross_rows, :] = W[X][a, start : start + cross_rows, :]

        both_shards(whole)
        residual(0, o.x, keep(o.xmid, 3, o.nb))
        for a in range(2):
            r = dot(o.nb[...], o.xg[a, :, :hs]).astype(BF)
            o.qb[:, split(a)] = (r * (HD**-0.5)).astype(BF)

        def one(rows):
            o.ns[rows, :] = normed(o.xbuf[rows, :].astype(F32), 2)

        ag_also_hop(1)
        x_halves(0, one)
        kv_project()
        attn_fwd(o.qb, o.mixb, True, False, False)
        ag_also_hop(2)
        out_project(1, o.mixb, o.xg, hs)
        residual(1, o.xmid, keep(o.xlate, 1, o.nc))


    ff_fwd()

    def put_out(rows, value):
        o.gres[rows, :] = value
        o.xsend[rows, :] = value.astype(BF)

    residual(2, o.xlate, put_out, lambda j: pl.when(enc)(lambda: x_copy(0, j).start()))
    when(enc, lambda: rows_start(1))
    home_send(0, o.gres)
    o.ho[...] = home_block(o.gres, t)
    home_out[0].start()
    ag_finish(A)
    rows_pass(1)
    rows_done(1)
    rows_join(1, o.gres)

    @pl.when(enc)
    def _():
        o.dgacc[3] = jnp.zeros((8, D), F32)
        x_sent(0)

        def one(rows):
            value = o.gres[rows, :] + o.xbuf[rows, :].astype(F32)
            o.gres[rows, :] = value
            o.gb[rows, :] = value.astype(BF)

        x_halves(1, one)

    when(dec, lambda: rows_join(1, o.gb))


    ff_back()

    @pl.when(dec)
    def _():
        mix_grads(o.xg, hs)
        attn_back(o.qb, o.mixb, True, False)
        dkv_grads()
        exchange(
            1, lambda rows: sum(dot_nt(o.dq[rows, split(a)], o.xg[a, :, :hs]) for a in range(2))
        )

        def put_source(rows, dv):
            o.xsend[rows, :] = dv.astype(BF)

        norm_back(2, o.xbuf, 2, put_source, lambda j: x_copy(1, j).start())
        rs_mid(RC, 0, 2)

        def put_mid(rows, dv):
            new = o.gres[rows, :] + dv
            o.gres[rows, :] = new
            o.xbuf[rows, :] = new.astype(BF)

        norm_back(1, o.xmid, 3, put_mid)
        for a in range(2):
            o.dqkv[a, :, :hs] = o.dq[:, split(a)]
            o.dqkv[a, :, hs : 2 * hs] = o.mixb[:, split(a)]

        def cross_weights(a):
            full = jnp.concatenate(
                [
                    dot_tn(o.nb[...], o.dqkv[a, :, :hs]).astype(BF),
                    dot_tn(o.gb[...], o.dqkv[a, :, hs : 2 * hs]).astype(BF),
                ],
                axis=1,
            )
            for k in range(nz):
                for part in range(2):
                    at = part * (D // 2) + k * cross_rows
                    to = k * chunk_rows + part * cross_rows
                    W[X][a, to : to + cross_rows, :] = full[at : at + cross_rows]

        both_shards(cross_weights)
        rs_start(RX)
        x_sent(1)
        o.gb[...] = o.xbuf[...]

    ff_in_weights()
    mix_grads(W[A], at_o)
    for a in range(2):
        W[A][a, :, at_o : at_o + hs] = dot_tn(o.gb[...], o.mixa[:, split(a)]).astype(BF)
    steps = tuple(functools.partial(rs_mid, RC, i, i + 1) for i in range(3))

    @pl.when(enc)
    def _():
        attn_back(o.q, o.mixa, True, True, steps)
        dkv_grads()

    @pl.when(dec)
    def _():
        attn_back(o.q, o.mixa, False, True)
        rs_mid(RC, 2, 3)

    kv_weights()
    rs_mid(RC, 3)
    for a in range(2):
        o.dqkv[a, :, :hs] = o.dq[:, split(a)]
        o.dqkv[a, :, hs : 2 * hs] = o.dkp[HALO : HALO + L, split(a)].astype(BF)
        o.dqkv[a, :, 2 * hs :] = o.dvp[HALO : HALO + L, split(a)].astype(BF)
    last_slot = 1 - p
    exchange(
        last_slot,
        lambda rows: sum(dot_nt(o.dqkv[a, rows, :], W[A][a, :, :at_o]) for a in range(2)),
    )

    @pl.when(enc)
    def _():
        def put_source(rows, dv):
            pass

        norm_back(2, o.nb, 2, put_source)

    heads = 2 * n_pair
    acc = jnp.zeros((heads * 8, win_w), F32)
    for k in range(qb_rows // 8):
        part = o.tb[:, 8 * k : 8 * k + 8, :].reshape(heads * 8, win_w)
        acc = acc + (part if k == 0 else pltpu.roll(part, win_w - 8 * k, 1))
    sub = lax.rem(lax.broadcasted_iota(jnp.int32, (heads * 8, win_w), 0), 8)
    diag = jnp.zeros((heads * 8, win_w), F32)
    for k in range(8):
        turned = acc if k == 0 else pltpu.roll(acc, win_w - k, 1)
        diag = diag + jnp.where(sub == k, turned, 0.0)
    lines = jnp.sum(diag.reshape(heads, 8, win_w), axis=1)

    def put_in(rows, dv):
        o.gres[rows, :] = o.gres[rows, :] + dv

    norm_back(last_slot, o.x, 0, put_in)
    home_send(1, o.gres)
    home_out[2].start()
    sums_start(lines)

    def own_weights(a):
        W[A][a, :, :at_o] = dot_tn(o.na[...], o.dqkv[a]).astype(BF)

    side_first(own_weights, RQ)

    home_copy(0).wait()
    home_out[1].start()
    kv_mid()
    rs_mid(RB)
    rs_out(RC)
    kv_cross()
    sums_mid()
    when(dec, lambda: rs_mid(RX))
    rs_mid(RQ, 0, 2)
    rs_out(RB)
    sums_end()
    rs_mid(RQ, 2)
    kv_out()

    @pl.when(dec)
    def _():
        def put(rows, total):
            o.xt[rows, :] = total

        rs_end(RX, put)
        rs_sent(RX)
        o.xo[...] = o.xt[:cross_rows, :]
        cross_out.start()
        o.ox[...] = o.xt[cross_rows:, :].astype(o.ox.dtype)
        cross_out.wait_send()

    @pl.when(enc)
    def _():
        cross_in.wait_send()
        cross_out.wait_recv()
        o.ox[...] = o.xi[...].astype(o.ox.dtype)

    home_copy(1).wait()
    o.ext[...] = o.hr[1].astype(F32)
    home_out[3].start()
    rs_out(RQ)
    for copy in home_out:
        copy.wait()
    if nz > 1:
        for r in LEAVE:
            rs_leave(r).wait()


def run_kernel(dims, given):
    L, D, hs, fs, nz, qb_rows, win_w = dims
    hc, fc = 2 * hs, 2 * fs
    n_blk, n_pair = L // qb_rows, hc // 128
    LP = L + 2 * HALO
    LBP = -(-(L // 4) // 16) * 16
    CR = D // nz
    widths = dict(a=6 * hs, b=fs, c=fs, x=2 * hs)
    MW = -(-CR // 128) * 128
    S = jax.ShapeDtypeStruct
    SUM = F32 if nz > 1 else BF
    outs = dict(
        oh=S((2, LBP, D), BF),
        gh=S((2, L // 4, D), F32),
        oa=S((CR, widths["a"]), SUM),
        ob=S((CR, widths["b"]), SUM),
        oc=S((CR, widths["c"]), SUM),
        ox=S((CR // 2, widths["x"]), SUM),
        om=S((TILE, MW), F32),
    )
    V = pltpu.VMEM
    LD, LH, LF = (L, D), (L, hc), (L, fc)
    scratch = dict(
        na=V(LD, BF), ns=V(LD, BF), nb=V(LD, BF), nc=V(LD, BF),
        xmid=V(LD, F32), xlate=V(LD, F32), gres=V(LD, F32),
        q=V(LH, BF), kp=V((LP, hc), BF), vp=V((LP, hc), BF), ks=V(LH, BF), vs=V(LH, BF),
        qb=V(LH, BF), mixa=V(LH, BF), mixb=V(LH, BF),
        pm=V((n_blk * n_pair, 2 * qb_rows, L), BF), po=V((n_blk * n_pair, 2 * qb_rows, win_w), BF),
        hidden=V(LF, BF), gp=V(LF, BF), pre=V((L, fs // 2), F32),
        tb=V((2 * n_pair, qb_rows, win_w), F32),
        mm=V((qb_rows, L), F32), mo=V((qb_rows, win_w), F32),
        dmix=V(LH, BF), dq=V(LH, BF), dqkv=V((2, L, 3 * hs), BF), dkv=V((2, L, 2 * hs), BF),
        dkp=V((LP, hc), F32), dvp=V((LP, hc), F32), dks=V(LH, F32), dvs=V(LH, F32),
        gb=V(LD, BF), xbuf=V(LD, BF), xsend=V(LD, BF),
        exs=V((3, L, D), BF), exr=V((3, L, D), BF), dgacc=V((4, 8, D), F32),
        g=V((8, D), F32), ext=V((LBP, D), F32), lines=V((TILE, win_w), F32),
        m=V((3, nz, TILE, MW), BF), ms1=V((2, nz, TILE, MW), BF), ms2=V((nz, TILE, MW), BF),
        ms3=V((max(nz - 1, 1), TILE, MW), BF), mf=V((TILE, MW), F32), mo1=V((TILE, MW), F32),
        mo2=V((TILE, MW), F32), dgl=V((8, D), F32), rl=V((2, TILE, 128), F32),
        idr=V((1, L), jnp.int32),
        x=V(LD, BF), xq=V((4, LBP, D), BF), cq=V((4, LBP, D), BF), mq=V((4, 8, 128), jnp.int32),
        hs=V((2, LBP, D), BF), hr=V((2, LBP, D), BF), ho=V((LBP, D), BF),
        xg=V((2, D, widths["x"]), BF), xt=V((CR, widths["x"]), F32),
        xo=V((CR // 2, widths["x"]), F32), xi=V((CR // 2, widths["x"]), F32),
    )
    for g, width in widths.items():
        scratch["w" + g] = V((2, D, width), BF)
        scratch["y" + g] = V((D, width), BF)
        scratch["z" + g] = V((nz - 1, CR, width) if nz > 1 else (1, 16, width), BF)
    sem = pltpu.SemaphoreType.DMA
    scratch.update(ss=sem((3, 2)), rs=sem((3, 2)), gd=sem((3, 3)), ga=sem((2, nz)), gb2=sem((nz,)), mt=sem((8, nz)), mx=sem((6,)), tg=sem((2,)), xss=sem((2, 2, L // 2 // RT)), xrs=sem((2, 2, L // 2 // RT)))
    scratch.update(xw=sem((4,)), oc_sem=sem((4,)), kq=sem((4, nz)), lc=sem((6,)), lh=sem((4,)))
    scratch.update(qs=sem((3, 3)), qr=sem((3, 3)), ql=sem((3,)), hx=sem((2,)), hy=sem((2,)))
    for name in ("gr", "gl", "gs", "gz", "gy"):
        scratch[name] = sem((4, nz))
    for name in ("rs_s", "rs_r", "rz_s", "rz_r"):
        scratch[name] = sem((6, nz))
    spec = pl.BlockSpec(memory_space=pltpu.VMEM)
    far = pl.BlockSpec(memory_space=pl.ANY)
    names = list(given) + list(outs) + list(scratch)
    FAR = ["sa", "sb", "sc", "sx", "xs", "cs", "ms", "table", "oh", "gh"]
    if nz > 1:
        FAR += ["oa", "ob", "oc"]
    return pl.pallas_call(
        functools.partial(kernel, dims, names),
        out_shape=list(outs.values()),
        in_specs=[far if name in FAR else spec for name in given],
        out_specs=[far if name in FAR else spec for name in outs],
        scratch_shapes=list(scratch.values()),
        compiler_params=pltpu.CompilerParams(
            collective_id=0, has_side_effects=True, vmem_limit_bytes=63 << 20
        ),
        name="layers",
    )(*given.values())


def prep_kernel(dims, n_dp, names, *refs):
    L, D, hs, fs, nz, qb_rows, win_w = dims
    o = Refs()
    for name, ref in zip(names, refs, strict=True):
        setattr(o, name, ref)
    section = lax.axis_index("pipe")
    y = lax.axis_index("tensor") // 2
    rows = D // n_dp
    held = L // 4
    for raw, out in ((o.li, o.xs), (o.co, o.cs)):
        o.tmp[...] = raw[...].astype(F32)
        pad = jnp.zeros((out.shape[1] - held, D), F32)
        for r in range(2):
            out[r] = jnp.concatenate([o.tmp[:, r, :], pad], axis=0).astype(BF)
    for i in range(3):
        o.sa[:, i * hs : (i + 1) * hs] = o.qkv[i]
    o.sa[:, 3 * hs : 4 * hs] = o.so[...].astype(F32).T.astype(BF)
    for i in range(2):
        o.kvt[...] = o.kv[...].astype(F32)
        o.sa[:, (4 + i) * hs : (5 + i) * hs] = o.kvt[:, i, :].astype(BF)
    n_gain = o.gain.shape[0]
    heads = o.rel.shape[0]
    o.mf[...] = jnp.zeros(o.mf.shape, F32)
    o.mf[:n_gain, : o.gain.shape[1]] = o.gain[...].astype(F32)
    o.mf[CROSS_AT : CROSS_AT + 1, : o.cg.shape[1]] = o.cg[...].astype(F32)
    o.mf[REL_AT : REL_AT + heads, : o.rel.shape[1]] = o.rel[...].astype(F32)
    o.sm[...] = o.mf[...].astype(BF)
    o.sx[:, :hs] = o.cq[...]
    o.sx[:, hs : 2 * hs] = o.cw[...].astype(F32).T.astype(BF)
    o.ms[...] = jnp.zeros(o.ms.shape, jnp.int32)
    for r in range(2):
        o.ms[r, 0:1, :held] = o.ids[r : r + 1, :]
    own = o.seg[section, pl.ds(y, 1), :]
    first = o.seg[0, pl.ds(y, 1), :]
    o.segq[...] = jnp.broadcast_to(own.astype(F32), (8, L)).T[:, :1].astype(jnp.int32)
    slots = lax.broadcasted_iota(jnp.int32, (1, L), 1).astype(F32)
    slots = jnp.floor((slots + 0.5) * (1.0 / MEM)).astype(jnp.int32)
    o.srcseg[...] = jnp.where(section == 0, slots, first)
    o.line[...] = jnp.full(o.line.shape, -1, jnp.int32)
    o.line[:, HALO : HALO + L] = own
    for b in range(L // qb_rows):
        o.segw[b] = o.line[:, b * qb_rows : b * qb_rows + win_w]
    o.win[...] = jnp.full(o.win.shape, -1, jnp.int32)
    o.win[:, : 2 * HALO] = o.buckets[:, L - HALO : L + HALO]
    at = lax.broadcasted_iota(jnp.int32, (128, win_w), 0)
    o.hot[...] = jnp.where(at == o.win[...], 1.0, 0.0).astype(BF)


def run_prep(dims, n_dp, given):
    L, D, hs, fs, nz, qb_rows, win_w = dims
    rows, held = D // n_dp, L // 4
    MW = -(-(D // nz) // 128) * 128
    LBP = -(-held // 16) * 16
    S = jax.ShapeDtypeStruct
    outs = dict(
        xs=S((2, LBP, D), BF),
        cs=S((2, LBP, D), BF),
        sa=S((rows, 6 * hs), BF),
        sx=S((rows // 2, 2 * hs), BF),
        sm=S((TILE, MW), BF),
        ms=S((2, 8, 128), jnp.int32),
        segq=S((L, 1), jnp.int32),
        segw=S((L // qb_rows, 1, win_w), jnp.int32),
        srcseg=S((1, L), jnp.int32),
        hot=S((128, win_w), BF),
    )
    V = pltpu.VMEM
    scratch = dict(
        tmp=V((held, 2, D), F32),
        kvt=V((rows, 2, hs), F32),
        mf=V((TILE, MW), F32),
        line=V((1, L + 2 * HALO), jnp.int32),
        win=V((1, win_w), jnp.int32),
    )
    spec = pl.BlockSpec(memory_space=pltpu.VMEM)
    names = list(given) + list(outs) + list(scratch)
    return pl.pallas_call(
        functools.partial(prep_kernel, dims, n_dp, names),
        out_shape=list(outs.values()),
        in_specs=[spec] * len(given),
        out_specs=[spec] * len(outs),
        scratch_shapes=list(scratch.values()),
        compiler_params=pltpu.CompilerParams(vmem_limit_bytes=60 << 20),
        name="prep",
    )(*given.values())


def finish_kernel(dims, names, *refs):
    L, D, hs, fs, nz, qb_rows, win_w = dims
    o = Refs()
    for name, ref in zip(names, refs, strict=True):
        setattr(o, name, ref)
    o.ffi[...] = o.gb[...]
    o.ffo[...] = o.gc[...]
    for r in range(2):
        o.gin[:, r, :] = o.gh[r]
        o.tmp[:, r, :] = o.oh[r, : L // 4].astype(F32)
    o.out[...] = o.tmp[...].astype(BF)
    for i in range(3):
        o.qkv[i] = o.ga[:, i * hs : (i + 1) * hs]
    o.so[...] = o.ga[:, 3 * hs : 4 * hs].T
    for i in range(2):
        o.kv[:, i, :] = o.ga[:, (4 + i) * hs : (5 + i) * hs]
    rows = o.ga.shape[0]
    for i in range(o.gain.shape[0]):
        o.gain[i] = o.gm[i : i + 1, :rows]
    heads, _, nb_rows = o.rel.shape
    for i in range(heads):
        o.rel[i] = o.gm[REL_AT + i : REL_AT + i + 1, :nb_rows]
    o.cq[...] = o.gx[:, :hs]
    o.co[...] = o.gx[:, hs : 2 * hs].T
    o.cg[...] = o.gm[CROSS_AT : CROSS_AT + 1, : rows // 2]


def run_finish(dims, rel_shape, sums):
    L, D, hs, fs, nz, qb_rows, win_w = dims
    rows = sums[2].shape[0]
    held = L // 4
    S = jax.ShapeDtypeStruct
    outs = dict(
        out=S((held, 2, D), BF),
        gin=S((held, 2, D), F32),
        qkv=S((3, rows, hs), F32),
        so=S((hs, rows), F32),
        kv=S((rows, 2, hs), F32),
        rel=S((rel_shape[1], 1, rel_shape[0]), F32),
        gain=S((3, 1, rows), F32),
        cq=S((rows // 2, hs), F32),
        co=S((hs, rows // 2), F32),
        cg=S((1, rows // 2), F32),
        ffi=S((rows, fs), F32),
        ffo=S((rows, fs), F32),
    )
    spec = pl.BlockSpec(memory_space=pltpu.VMEM)
    return pl.pallas_call(
        functools.partial(
            finish_kernel, dims, ["oh", "gh", "ga", "gb", "gc", "gx", "gm", *outs, "tmp"]
        ),
        out_shape=list(outs.values()),
        in_specs=[spec] * 7,
        out_specs=[spec] * len(outs),
        scratch_shapes=[pltpu.VMEM((held, 2, D), F32)],
        compiler_params=pltpu.CompilerParams(vmem_limit_bytes=60 << 20),
        name="finish",
    )(*sums)


def body(
    layer_inputs,
    segment_ids,
    slot_ids,
    memory_table,
    buckets,
    self_qkv,
    self_out,
    source_kv,
    ff_in,
    ff_out,
    rel_bias,
    gains,
    cross_query,
    cross_out,
    cross_gain,
    cotangents,
):
    nt = lax.axis_size("tensor")
    n_dp = lax.axis_size("dp")
    assert nt == 4 and layer_inputs.shape[2] == 2
    D = layer_inputs.shape[3]
    L = segment_ids.shape[2]
    hs = self_qkv.shape[3]
    fs = ff_in.shape[2]
    qb_rows, win_w = 160, 256
    rows = D // n_dp
    nz = 4 if n_dp == 4 and (rows // 2) % 32 == 0 else 1
    dims = (L, D, hs, fs, nz, qb_rows, win_w)
    held = L // nt
    gain, rel, cross_g = gains[0], rel_bias[0].T, cross_gain[None]
    if nz != n_dp:
        gain = lax.all_gather(gain, "dp", axis=1, tiled=True)
        rel = lax.all_gather(rel, "dp", axis=1, tiled=True)
        cross_g = lax.all_gather(cross_g, "dp", axis=1, tiled=True)
    prepared = run_prep(
        dims,
        n_dp,
        dict(
            li=layer_inputs[0],
            co=cotangents[0],
            qkv=self_qkv[0].transpose(1, 0, 2),
            so=self_out[0],
            kv=source_kv[0],
            gain=gain,
            rel=rel,
            cq=cross_query,
            cw=cross_out,
            cg=cross_g,
            seg=segment_ids,
            ids=slot_ids.T,
            buckets=buckets[None],
        ),
    )
    xs, cs, sa, sx, sm, ms, segq, segw, srcseg, hot = prepared
    shards = [sa, ff_in[0], ff_out[0].T, sx]
    if nz != n_dp:
        shards = [lax.all_gather(shard, "dp", axis=0, tiled=True) for shard in shards]
    given = dict(
        xs=xs, cs=cs, ms=ms, table=memory_table, sm=sm, segq=segq, segw=segw, srcseg=srcseg, hot=hot,
        sa=shards[0], sb=shards[1], sc=shards[2], sx=shards[3],
    )
    oh, gh, *sums, gm = run_kernel(dims, given)
    if nz != n_dp:
        sums = [
            lax.psum_scatter(full, "dp", scatter_dimension=0, tiled=True).astype(F32)
            for full in sums
        ]

        def share(first, count, width):
            mine = lax.psum_scatter(
                gm[first : first + count, :width], "dp", scatter_dimension=1, tiled=True
            )
            below = TILE - first - count
            return jnp.pad(mine, ((first, below), (0, 128 - mine.shape[1])))

        gm = (
            share(0, CROSS_AT, D)
            + share(CROSS_AT, 1, D // 2)
            + share(REL_AT, rel_bias.shape[2], NB)
        )
    done = run_finish(dims, rel_bias.shape[1:], [oh, gh, *sums, gm])
    out, gin, qkv, so, kv, rel, gain, cq, co, cg, ff_i, ff_o = done
    return (
        out[None],
        gin[None],
        qkv.transpose(1, 0, 2)[None],
        so[None],
        kv[None],
        ff_i[None],
        ff_o.T[None],
        rel.transpose(1, 2, 0),
        gain.transpose(1, 0, 2),
        cq,
        co,
        cg[0],
    )


def solution(mesh):
    placed = (
        P("pipe", "tensor", "dp", None),
        P(None, "dp", None),
        P("tensor", "dp"),
        P(),
        P(),
        P("pipe", "dp", None, "tensor"),
        P("pipe", "tensor", "dp"),
        P("pipe", "dp", None, "tensor"),
        P("pipe", "dp", "tensor"),
        P("pipe", "tensor", "dp"),
        P("pipe", "dp", "tensor"),
        P("pipe", None, "dp"),
        P(("pipe", "dp"), "tensor"),
        P("tensor", ("pipe", "dp")),
        P(("pipe", "dp")),
        P("pipe", "tensor", "dp", None),
    )
    return jax.shard_map(
        body,
        mesh=mesh,
        in_specs=placed,
        out_specs=(
            P("pipe", "tensor", "dp", None),
            P("pipe", "tensor", "dp", None),
            P("pipe", "dp", None, "tensor"),
            P("pipe", "tensor", "dp"),
            P("pipe", "dp", None, "tensor"),
            P("pipe", "dp", "tensor"),
            P("pipe", "tensor", "dp"),
            P("pipe", "dp", "tensor"),
            P("pipe", None, "dp"),
            P(("pipe", "dp"), "tensor"),
            P("tensor", ("pipe", "dp")),
            P(("pipe", "dp")),
        ),
        check_vma=False,
    )
```

```python
import functools

import jax
import jax.numpy as jnp
from jax import lax
from jax.experimental import pallas as pl
from jax.experimental.pallas import tpu as pltpu
from jax.sharding import PartitionSpec as P

HD = 64
NB = 32
MEM = 20
HALO = 48
TILE = 16
CROSS_AT = 3
REL_AT = 8
PIECE = 256
EPSILON = 1e-06
NEG = -1000000000.0
BF = jnp.bfloat16
F32 = jnp.float32
MESH = pl.DeviceIdType.MESH
RT = 48


def dot(a, b):
    return lax.dot_general(a, b, (((1,), (0,)), ((), ())), preferred_element_type=F32)


def dot_nt(a, b):
    return lax.dot_general(a, b, (((1,), (1,)), ((), ())), preferred_element_type=F32)


def dot_tn(a, b):
    return lax.dot_general(a, b, (((0,), (0,)), ((), ())), preferred_element_type=F32)


class Refs:
    pass


def kernel(dims, names, *refs):
    L, D, hs, fs, nz, qb_rows, win_w = dims
    hc, fc = 2 * hs, 2 * fs
    at_o, at_kv, at_ext = 3 * hs, 4 * hs, 6 * hs
    chunk_rows = D // nz
    cross_rows = chunk_rows // 2
    n_blk = L // qb_rows
    n_pair = hc // 128
    o = Refs()
    for name, ref in zip(names, refs, strict=True):
        setattr(o, name, ref)
    p = lax.axis_index("pipe")
    d = lax.axis_index("dp")
    t = lax.axis_index("tensor")
    enc, dec = p == 0, p == 1
    core = lax.rem(t, 2)
    y = t // 2
    z = d if nz > 1 else 0
    skew = (1 - p, d, lax.rem(t + 2, 4))
    sibling = (p, d, t + 1 - 2 * core)
    across = (1 - p, d, t)
    beside = (p, d, lax.rem(t + 2, 4))
    half = L // 2
    held = L // 4
    A, B, C, X = range(4)
    shard = (o.sa, o.sb, o.sc, o.sx)
    W = (o.wa, o.wb, o.wc, o.wx)
    RY = (o.ya, o.yb, o.yc, o.yx)
    RZ = (o.za, o.zb, o.zc, o.zx)
    RB, RC, RX, RQ, RK = range(5)
    REDUCE = {
        RB: (B, 0, fs),
        RC: (C, 0, fs),
        RX: (X, 0, 2 * hs),
        RQ: (A, 0, at_kv),
        RK: (A, at_kv, 2 * hs),
    }
    LEAVE = {
        RB: (o.ob, o.xlate, 0, 0),
        RC: (o.oc, o.xmid, 0, 0),
        RQ: (o.oa, o.xmid, chunk_rows, 0),
        RK: (o.oa, o.xlate, chunk_rows, 0),
    }
    STAGE = {} if nz == 1 else {
        A: o.hidden.at[pl.ds(0, chunk_rows), pl.ds(0, 6 * hs)],
        C: o.gp.at[pl.ds(0, chunk_rows), pl.ds(fs, fs)],
    }
    ROWS = ((o.xs, o.xq), (o.cs, o.cq), (o.ms, o.mq))

    def chunk(k):
        return pl.ds(pl.multiple_of(k * chunk_rows, 16), chunk_rows)

    def remote(src, dst, send, recv, device):
        return pltpu.make_async_remote_copy(
            src_ref=src,
            dst_ref=dst,
            send_sem=send,
            recv_sem=recv,
            device_id=device,
            device_id_type=MESH,
        )


    def ag_right(g, k):
        slot = W[g].at[y, chunk(k)]
        return remote(slot, slot, o.gr.at[g, k], o.gz.at[g, k], (p, d + 1, t))

    def ag_left(g, k):
        slot = W[g].at[y, chunk(k)]
        return remote(slot, slot, o.gl.at[g, k], o.gz.at[g, k], (p, d - 1, t))

    def ag_beside(g, k):
        slot = W[g].at[y, chunk(k)]
        return remote(slot, slot, o.gs.at[g, k], o.gy.at[g, k], beside)

    def ag_came(g, k):
        slot = W[g].at[y, chunk(k)]
        remote(slot, slot, o.gr.at[g, k], o.gz.at[g, k], beside).wait_recv()

    def ag_each(g, h, act):
        if h == 0:
            act(z, z + 1 < nz, z > 0, True)
        else:
            act(z - h, z + 1 < nz, False, z - h >= 0)
            act(z + h, False, z > 0, z + h < nz)

    def when(cond, fn):
        if cond is True:
            fn()
        elif cond is not False:
            pl.when(cond)(fn)


    def ag_skew(g):
        return remote(W[g].at[y, chunk(z)], STAGE[g], o.gd.at[g, 0], o.gd.at[g, 1], skew)

    def ag_relay(g):
        slot = W[g].at[1 - y, chunk(z)]
        return remote(STAGE[g], slot, o.gd.at[g, 2], o.gy.at[g, z], across)

    def ag_pass_on(g):
        ag_skew(g).wait_recv()
        ag_relay(g).start()

    def ag_aside(g, k, own, wait):
        act = (lambda c: c.wait_send()) if wait else (lambda c: c.start())
        if own and g in STAGE:
            pl.when(enc)(lambda: act(ag_skew(g)))
            pl.when(dec)(lambda: act(ag_beside(g, k)))
        elif not own and g == C:
            pl.when(enc)(lambda: act(ag_beside(g, k)))
        else:
            act(ag_beside(g, k))


    def ag_also(k, way):
        slot = W[C].at[1 - y, chunk(k)]
        return remote(slot, slot, o.ga.at[way, k], o.gb2.at[k], (p, d + (1, -1)[way], t))

    def ag_also_hop(h):
        if h >= nz or nz == 1:
            return

        def act(k, right, left, here):
            def go():
                slot = W[C].at[1 - y, chunk(k)]
                if h == 0:
                    remote(slot, slot, o.gs.at[C, k], o.gy.at[C, k], beside).wait_recv()
                else:
                    remote(slot, slot, o.ga.at[0, k], o.gb2.at[k], beside).wait_recv()
                when(right, lambda: ag_also(k, 0).start())
                when(left, lambda: ag_also(k, 1).start())

            when(here, go)

        ag_each(C, h, act)

    def ag_also_sent():
        for h in range(nz):

            def act(k, right, left, here):
                def go():
                    when(right, lambda: ag_also(k, 0).wait_send())
                    when(left, lambda: ag_also(k, 1).wait_send())

                when(here, go)

            ag_each(C, h, act)

    def ag_hop(g, h, aside=True):
        if h >= nz:
            return

        def act(k, right, left, here):
            def go():
                if h > 0:
                    ag_came(g, k)
                if nz > 1:
                    when(right, lambda: ag_right(g, k).start())
                    when(left, lambda: ag_left(g, k).start())
                if aside:
                    ag_aside(g, k, h == 0, False)

            when(here, go)

        ag_each(g, h, act)

    def ag_side(g, h):
        if h >= nz:
            return

        def act(k, right, left, here):
            when(here, lambda: ag_aside(g, k, h == 0, False))

        ag_each(g, h, act)

    def ag_wait(g):
        if g == C and nz > 1:
            pl.when(enc)(lambda: ag_wait_all(g))
        else:
            ag_wait_all(g)

    def ag_wait_all(g):
        for k in range(nz):
            slot = W[g].at[1 - y, chunk(k)]
            remote(slot, slot, o.gs.at[g, k], o.gy.at[g, k], beside).wait_recv()

    def ag_finish(g):
        for h in range(nz):

            def act(k, right, left, here):
                def go():
                    if nz > 1:
                        when(right, lambda: ag_right(g, k).wait_send())
                        when(left, lambda: ag_left(g, k).wait_send())
                    ag_aside(g, k, h == 0, True)

                when(here, go)

            ag_each(g, h, act)

    def own_copy(g):
        return pltpu.make_async_copy(shard[g], W[g].at[y, chunk(z)], o.oc_sem.at[g])

    def cross_part(k, part):
        start = k * chunk_rows + part * cross_rows
        return pl.ds(pl.multiple_of(start, 16), cross_rows)

    cross_own = pltpu.make_async_copy(o.sx, W[X].at[y, cross_part(z, 1)], o.oc_sem.at[X])
    cross_in = remote(
        o.sx, W[X].at[y, cross_part(z, 0)], o.xw.at[0], o.xw.at[1], across
    )
    cross_out = remote(o.xo, o.xi, o.xw.at[2], o.xw.at[3], across)


    nb_each = NB // nz
    n_rel = hs // HD

    def others(fn):
        if nz > 1:

            @pl.loop(1, nz)
            def _(i):
                fn(lax.rem(z + i, nz))

    def tile_z(a, k, to, sems):
        slot = o.m.at[a, k]
        return remote(slot, slot, o.mt.at[sems, to], o.mt.at[sems + 1, k], (p, to, t))

    def tile_beside(k):
        slot = o.m.at[y, k]
        return remote(slot, slot, o.mt.at[2, k], o.mt.at[3, k], beside)

    def tile_across():
        return remote(o.m.at[y, z], o.m.at[2, z], o.mx.at[0], o.mx.at[1], across)

    def tiles_start():
        o.m[y, z] = o.sm[...]

        @pl.when(enc)
        def _():
            o.m[2] = jnp.zeros(o.m.shape[1:], BF)

        others(lambda k: tile_z(y, z, k, 0).start())
        tile_beside(z).start()
        when(enc, lambda: tile_across().start())

    def tiles_pass():
        def one(k):
            tile_z(y, k, k, 0).wait_recv()
            tile_beside(k).start()

        others(one)

        @pl.when(dec)
        def _():
            tile_across().wait_recv()
            others(lambda k: tile_z(2, z, k, 4).start())

    def tiles_done():
        @pl.loop(0, nz)
        def _(k):
            slot = o.m.at[1 - y, k]
            remote(slot, slot, o.mt.at[2, k], o.mt.at[3, k], beside).wait_recv()
            tile_beside(k).wait_send()

        others(lambda k: tile_z(y, z, k, 0).wait_send())
        when(enc, lambda: tile_across().wait_send())

        @pl.when(dec)
        def _():
            others(lambda k: tile_z(2, k, k, 4).wait_recv())
            others(lambda k: tile_z(2, z, k, 4).wait_send())

        o.rl[...] = jnp.zeros(o.rl.shape, F32)
        for k in range(nz):
            block = o.m[y, k].astype(F32)
            o.g[:CROSS_AT, k * chunk_rows : (k + 1) * chunk_rows] = block[:CROSS_AT, :chunk_rows]
            for part in range(2):
                cross = block if part else o.m[2, k].astype(F32)
                at = part * (D // 2) + k * cross_rows
                o.g[CROSS_AT : CROSS_AT + 1, at : at + cross_rows] = cross[
                    CROSS_AT : CROSS_AT + 1, :cross_rows
                ]
            for a in range(2):
                rel = o.m[a, k].astype(F32)
                o.rl[a, :n_rel, k * nb_each : (k + 1) * nb_each] = rel[
                    REL_AT : REL_AT + n_rel, :nb_each
                ]

    def sums_y():
        return remote(o.ms1.at[1 - y], o.ms2, o.mx.at[2], o.mx.at[3], beside)

    def sums_z(k):
        away = lax.rem(z + nz - 1 - k, nz)
        return remote(o.ms2.at[k], o.ms3.at[away], o.mt.at[6, k], o.mt.at[7, away], (p, k, t))

    def sums_z_came(i):
        remote(o.ms2.at[z], o.ms3.at[i], o.mt.at[6, z], o.mt.at[7, i], beside).wait_recv()

    def sums_across():
        return remote(o.mo1, o.mo2, o.mx.at[4], o.mx.at[5], across)

    def sums_start(lines):
        o.dgl[...] = jnp.zeros(o.dgl.shape, F32)
        for i in range(4):
            o.dgl[i : i + 1, :] = jnp.sum(o.dgacc[i], axis=0, keepdims=True)
        for a in range(2):
            o.lines[...] = jnp.zeros(o.lines.shape, F32)
            o.lines[:n_rel, :] = lines[n_rel * a : n_rel * (a + 1), :]
            whole = o.lines[...]
            high = whole.astype(BF)
            low = (whole - high.astype(F32)).astype(BF)
            o.rl[a] = dot_nt(high, o.hot[...]) + dot_nt(low, o.hot[...])
            for k in range(nz):
                o.mf[...] = jnp.zeros(o.mf.shape, F32)
                o.mf[:CROSS_AT, :chunk_rows] = o.dgl[
                    :CROSS_AT, k * chunk_rows : (k + 1) * chunk_rows
                ]
                for part in range(2):
                    at = part * (D // 2) + k * cross_rows
                    row = CROSS_AT + part
                    o.mf[row : row + 1, :cross_rows] = o.dgl[
                        CROSS_AT : CROSS_AT + 1, at : at + cross_rows
                    ]
                o.mf[REL_AT : REL_AT + n_rel, :nb_each] = o.rl[
                    a, :n_rel, k * nb_each : (k + 1) * nb_each
                ]
                o.ms1[a, k] = o.mf[...].astype(BF)
        sums_y().start()

    def sums_mid():
        sums_y().wait()
        for k in range(nz):
            both = o.ms1[y, k].astype(F32) + o.ms2[k].astype(F32)
            o.ms2[k] = both.astype(BF)
        others(lambda k: sums_z(k).start())

    def sums_end():
        total = o.ms2[z].astype(F32)
        for i in range(nz - 1):
            sums_z_came(i)
            total = total + o.ms3[i].astype(F32)
        o.om[...] = total
        others(lambda k: sums_z(k).wait_send())

        @pl.when(dec)
        def _():
            o.mo1[...] = total
            sums_across().start()
            o.om[CROSS_AT : CROSS_AT + 1, :] = total[CROSS_AT + 1 : CROSS_AT + 2, :]
            sums_across().wait_send()

        @pl.when(enc)
        def _():
            sums_across().wait_recv()
            o.om[CROSS_AT : CROSS_AT + 1, :] = o.mo2[CROSS_AT : CROSS_AT + 1, :]


    def piece(c, slot):
        return pltpu.make_async_copy(
            o.table.at[pl.ds(pl.multiple_of(c * PIECE, PIECE), PIECE)],
            o.exs.at[slot, pl.ds(0, PIECE)],
            o.tg.at[slot],
        )

    def pick_rows():
        n_piece = o.table.shape[0] // PIECE
        piece(0, 0).start()
        rows_done(2)
        for k in range(4):
            o.idr[:, k * held : (k + 1) * held] = o.mq[k, 0:1, :held]
        o.gres[...] = jnp.zeros(o.gres.shape, F32)

        @pl.loop(0, n_piece)
        def _(c):
            slot = lax.rem(c, 2)
            pl.when(c + 1 < n_piece)(lambda: piece(c + 1, 1 - slot).start())
            at = lax.broadcasted_iota(jnp.int32, (PIECE, L), 0) + c * PIECE
            hit = jnp.where(at == o.idr[...], 1.0, 0.0).astype(BF)
            piece(c, slot).wait()
            o.gres[...] += dot_tn(hit, o.exs[slot, :PIECE, :])

        def one(rows):
            o.nb[rows, :] = o.gres[rows, :].astype(BF)

        rows_loop(one)


    def rs_y(r, k):
        g, at, width = REDUCE[r]
        cols = pl.ds(at, width)
        return remote(
            W[g].at[1 - y, chunk(k), cols],
            RY[g].at[chunk(k), cols],
            o.rs_s.at[r, k],
            o.rs_r.at[r, k],
            beside,
        )

    mate = z + 1 - 2 * lax.rem(z, 2)
    far = 2 - 2 * (z // 2)
    TAKES = (far + lax.rem(mate, 2), mate, far + lax.rem(z, 2), z)
    GOES = (mate, mate, far + lax.rem(z, 2), z)

    def by_step(i, values):
        if nz == 1:
            return z
        weights = (
            (1 - i) * (2 - i) * (3 - i) // 6,
            i * (2 - i) * (3 - i) // 2,
            i * (i - 1) * (3 - i) // 2,
            i * (i - 1) * (i - 2) // 6,
        )
        return sum(value * weight for value, weight in zip(values, weights))

    def rs_z(r, i):
        g, at, width = REDUCE[r]
        cols = pl.ds(at, width)
        return remote(
            RY[g].at[chunk(by_step(i, TAKES)), cols],
            RZ[g].at[i, :, cols],
            o.rz_s.at[r, i],
            o.rz_r.at[r, i],
            (p, by_step(i, GOES), t),
        )

    def rs_start(r):
        for i in range(nz):
            rs_y(r, by_step(i, TAKES)).start()


    kv_cols = slice(at_kv, at_ext)
    kv_lanes = pl.ds(at_kv, 2 * hs)

    def kv_slot(own, i):
        return RZ[A].at[i, :, kv_lanes] if own else RY[A].at[chunk(i), kv_lanes]

    def kv_z(own, i):
        a = y if own else 1 - y
        return remote(
            W[A].at[a, chunk(TAKES[i]), kv_lanes],
            kv_slot(own, i),
            o.kq.at[own, i],
            o.kq.at[2 + own, i],
            (p, GOES[i], t),
        )

    kv_y = remote(
        W[A].at[1 - y, chunk(z), kv_lanes],
        RY[A].at[chunk(nz - 1), kv_lanes],
        o.kq.at[0, nz - 1],
        o.kq.at[2, nz - 1],
        beside,
    )

    def kv_add(k, terms, put):
        start = pl.multiple_of(k * chunk_rows, 16)

        @pl.loop(0, chunk_rows // 32)
        def _(n):
            rows = pl.ds(pl.multiple_of(start + n * 32, 16), 32)
            near = pl.ds(pl.multiple_of(n * 32, 16), 32)
            put(rows, near, sum(term(rows, near).astype(F32) for term in terms))

    def kv_term(own, i):
        if own:
            return lambda rows, near: RZ[A][i, near, kv_cols]
        return lambda rows, near: RY[A][
            pl.ds(pl.multiple_of(i * chunk_rows + near.start, 16), 32), kv_cols
        ]

    def kv_mine(own):
        a = y if own else 1 - y
        return lambda rows, near: W[A][a, rows, kv_cols]

    def kv_keep(own):
        a = y if own else 1 - y

        def put(rows, near, value):
            W[A][a, rows, kv_cols] = value.astype(BF)

        return put

    def kv_start(own):
        if nz > 1:
            kv_z(own, 0).start()
            kv_z(own, 1).start()

    def kv_mid():
        if nz == 1:
            rs_mid(RK)
            return
        for own in (0, 1):
            kv_z(own, 0).wait_recv()
            kv_add(TAKES[2], [kv_mine(own), kv_term(own, 0)], kv_keep(own))
            kv_z(own, 2).start()

    def kv_cross():
        if nz == 1:
            return
        kv_z(0, 1).wait_recv()
        kv_z(0, 2).wait_recv()
        kv_add(z, [kv_mine(0), kv_term(0, 1), kv_term(0, 2)], kv_keep(0))
        kv_y.start()

    def kv_out():
        if nz == 1:
            rs_out(RK)
            return
        out, buffer, first, into = LEAVE[RK]
        kv_z(1, 1).wait_recv()
        kv_z(1, 2).wait_recv()
        kv_y.wait_recv()

        def put(rows, near, value):
            to = pl.ds(pl.multiple_of(near.start + first, 16), 32)
            buffer[to, into : into + 2 * hs] = value

        kv_add(
            z, [kv_mine(1), kv_term(1, 1), kv_term(1, 2), kv_term(0, nz - 1)], put
        )
        rs_leave(RK).start()
        for own in (0, 1):
            for i in range(nz - 1):
                kv_z(own, i).wait_send()
        kv_y.wait_send()

    def rs_mid(r, first=0, last=nz):
        g, at, width = REDUCE[r]
        cols = slice(at, at + width)

        @pl.loop(min(first, nz), min(last, nz))
        def _(i):
            k = by_step(i, TAKES)
            rs_y(r, k).wait_recv()
            start = pl.multiple_of(k * chunk_rows, 16)

            def add(more):
                @pl.loop(0, chunk_rows // 32)
                def _(n):
                    rows = pl.ds(pl.multiple_of(start + n * 32, 16), 32)
                    both = W[g][y, rows, cols].astype(F32) + RY[g][rows, cols].astype(F32)
                    if more:
                        near = pl.ds(pl.multiple_of(n * 32, 16), 32)
                        both = both + RZ[g][0, near, cols].astype(F32)
                    RY[g][rows, cols] = both.astype(BF)

            if nz == 1:
                add(False)
                return

            @pl.when(i == 2)
            def _():
                rs_z(r, 0).wait_recv()
                add(True)

            pl.when(i != 2)(lambda: add(False))
            pl.when(i < nz - 1)(lambda: rs_z(r, i).start())

    def rs_end(r, put):
        g, at, width = REDUCE[r]
        cols = slice(at, at + width)
        if nz > 1:
            rs_z(r, 1).wait_recv()
            rs_z(r, 2).wait_recv()
        start = pl.multiple_of(z * chunk_rows, 16)

        @pl.loop(0, chunk_rows // 32)
        def _(n):
            rows = pl.ds(pl.multiple_of(n * 32, 16), 32)
            total = RY[g][pl.ds(pl.multiple_of(start + n * 32, 16), 32), cols].astype(F32)
            if nz > 1:
                total = total + RZ[g][1, rows, cols].astype(F32)
                total = total + RZ[g][2, rows, cols].astype(F32)
            put(rows, total)

    def rs_sent(r):
        for i in range(nz):
            rs_y(r, by_step(i, TAKES)).wait_send()
            if i < nz - 1:
                rs_z(r, i).wait_send()

    def rs_leave(r):
        g, at, width = REDUCE[r]
        out, buffer, first, into = LEAVE[r]
        return pltpu.make_async_copy(
            buffer.at[pl.ds(first, chunk_rows), pl.ds(into, width)],
            out.at[:, pl.ds(at, width)],
            o.lc.at[r],
        )

    def rs_out(r):
        g, at, width = REDUCE[r]
        out, buffer, first, into = LEAVE[r]
        if nz == 1:

            @pl.loop(0, chunk_rows // 32)
            def _(n):
                rows = pl.ds(pl.multiple_of(n * 32, 16), 32)
                out[rows, at : at + width] = RY[g][rows, at : at + width]

        else:

            def put(rows, total):
                buffer[pl.ds(pl.multiple_of(rows.start + first, 16), 32), into : into + width] = (
                    total
                )

            rs_end(r, put)
            rs_leave(r).start()
        rs_sent(r)


    def rows_sib(i, k, n):
        own, landing = ROWS[i]
        src = own.at[y] if n == 0 else landing.at[k]
        return remote(src, landing.at[k], o.qs.at[i, n], o.qr.at[i, n], sibling)

    def rows_beside(i, k):
        own, landing = ROWS[i]
        return remote(own.at[1 - y], landing.at[k], o.qs.at[i, 2], o.qr.at[i, 2], beside)

    def rows_own(i):
        own, landing = ROWS[i]
        return pltpu.make_async_copy(own.at[y], landing.at[t], o.ql.at[i])

    def rows_start(i):
        rows_own(i).start()
        rows_beside(i, t).start()
        rows_sib(i, t, 0).start()

    other = lax.rem(t + 2, 4)

    def rows_pass(i):
        rows_beside(i, other).wait_recv()
        rows_sib(i, other, 1).start()

    def rows_done(i):
        rows_own(i).wait()
        rows_sib(i, t, 0).wait()
        rows_sib(i, other, 1).wait()
        rows_beside(i, t).wait_send()

    def rows_join(i, out_ref):
        landing = ROWS[i][1]
        wide = 256

        @pl.loop(0, 2)
        def _(k):
            @pl.loop(0, D // wide)
            def _(n):
                cols = pl.ds(pl.multiple_of(n * wide, 128), wide)
                value = jnp.concatenate(
                    [landing[2 * k + j, :held, cols].astype(F32) for j in range(2)], axis=0
                )
                rows = pl.ds(pl.multiple_of(2 * k * held, 16), 2 * held)
                out_ref[rows, cols] = value.astype(out_ref.dtype)


    def home_copy(i):
        return remote(o.hs.at[i], o.hr.at[i], o.hx.at[i], o.hy.at[i], beside)

    def home_block(buffer, k):
        value = buffer[pl.ds(pl.multiple_of(k * held, 8), held), :]
        pad = o.hs.shape[1] - held
        return jnp.concatenate([value, jnp.zeros((pad, D), F32)], axis=0).astype(BF)

    def home_send(i, buffer):
        o.hs[i] = home_block(buffer, other)
        home_copy(i).start()

    home_out = (
        pltpu.make_async_copy(o.ho, o.oh.at[y], o.lh.at[0]),
        pltpu.make_async_copy(o.hr.at[0], o.oh.at[1 - y], o.lh.at[1]),
        pltpu.make_async_copy(
            o.gres.at[pl.ds(pl.multiple_of(t * held, 8), held)], o.gh.at[y], o.lh.at[2]
        ),
        pltpu.make_async_copy(o.ext.at[pl.ds(0, held)], o.gh.at[1 - y], o.lh.at[3]),
    )

    barrier = pltpu.get_barrier_semaphore()
    for g in (A, B, C):
        own_copy(g).start()
    when(dec, cross_own.start)
    for peer in (sibling, across, beside, skew):
        pl.semaphore_signal(barrier, inc=1, device_id=peer, device_id_type=MESH)
    for i in range(1, nz):
        pl.semaphore_signal(
            barrier, inc=1, device_id=(p, lax.rem(d + i, nz), t), device_id_type=MESH
        )
    pl.semaphore_wait(barrier, 4 + nz - 1)
    tiles_start()
    rows_start(0)
    when(enc, lambda: rows_start(2))
    own_copy(A).wait()
    ag_hop(A, 0)
    when(enc, cross_in.start)
    own_copy(B).wait()
    ag_hop(B, 0, False)
    when(enc, lambda: ag_side(B, 0))
    own_copy(C).wait()

    lane = lax.broadcasted_iota(jnp.int32, (1, 128), 1)
    lo = jnp.where(lane < 64, 1.0, 0.0).astype(BF)
    hi = jnp.where(lane < 64, 0.0, 1.0).astype(BF)

    def rows_loop(fn, step=RT):
        @pl.loop(0, L // step)
        def _(i):
            fn(pl.ds(pl.multiple_of(i * step, step), step))

    def half_rows(h):
        return pl.ds(pl.multiple_of(h * half, 16), half)

    def tile_rows(h, j):
        return pl.ds(pl.multiple_of(h * half + j * RT, 16), RT)

    def halves(fn, ready=None, before=None, after=None):
        @pl.loop(0, 2)
        def _(i):
            h = lax.rem(core + i, 2)
            if ready is not None:
                ready(i, h)

            @pl.loop(0, half // RT)
            def _(j):
                if before is not None:
                    before(i, h, j)
                fn(tile_rows(h, j))
                if after is not None:
                    pl.when(i == 0)(lambda: after(j))

    def normed(v, gain_no):
        r = lax.rsqrt(jnp.mean(v * v, axis=-1, keepdims=True) + EPSILON)
        return (v * r * o.g[gain_no : gain_no + 1, :]).astype(BF)

    def norm_rows(x_ref, gain_no, out_ref):
        def one(rows):
            out_ref[rows, :] = normed(x_ref[rows, :].astype(F32), gain_no)

        rows_loop(one)

    def ex_copy(slot, h):
        rows = half_rows(h)
        return remote(
            o.exs.at[slot, rows], o.exr.at[slot, rows], o.ss.at[slot, h], o.rs.at[slot, h], sibling
        )

    def exchange(slot, fn):
        @pl.loop(0, 2)
        def _(i):
            h = lax.rem(1 - core + i, 2)
            rows = half_rows(h)
            o.exs[slot, rows, :] = fn(rows).astype(BF)
            ex_copy(slot, h).start()

    def arrived(slot):
        return lambda i, h: ex_copy(slot, h).wait()

    def ex_rows(slot, rows):
        return o.exs[slot, rows, :].astype(F32) + o.exr[slot, rows, :].astype(F32)

    def residual(slot, base_ref, put, after=None):
        def one(rows):
            put(rows, base_ref[rows, :].astype(F32) + ex_rows(slot, rows))

        halves(one, arrived(slot), after=after)

    def keep(ref, gain_no=None, normed_ref=None):
        def put(rows, value):
            ref[rows, :] = value
            if gain_no is not None:
                normed_ref[rows, :] = normed(value, gain_no)

        return put

    def norm_back(slot, x_ref, gain_no, put, after=None):
        o.dgacc[gain_no] = jnp.zeros((8, D), F32)

        def one(rows):
            dh = ex_rows(slot, rows)
            v = x_ref[rows, :].astype(F32)
            r = lax.rsqrt(jnp.mean(v * v, axis=-1, keepdims=True) + EPSILON)
            n = v * r
            dhg = dh * o.g[gain_no : gain_no + 1, :]
            mu = jnp.mean(dhg * n, axis=-1, keepdims=True)
            put(rows, r * (dhg - n * mu))
            o.dgacc[gain_no] += jnp.sum((dh * n).reshape(RT // 8, 8, D), axis=0)

        halves(one, arrived(slot), after=after)

    def split(a):
        return slice(a * hs, (a + 1) * hs)

    def both_shards(fn):
        @pl.loop(0, 2)
        def _(a):
            fn(a)

    def side_first(fn, r):
        @pl.loop(0, 2)
        def _(i):
            fn(lax.rem(1 - y + i, 2))
            if r is not None:
                pl.when(i == 0)(lambda: rs_start(r))

    def kv_project():
        def one(a):
            o.dkv[a] = dot(o.ns[...], W[A][a, :, at_kv:at_ext]).astype(BF)

        both_shards(one)
        for a in range(2):
            o.ks[:, split(a)] = o.dkv[a, :, :hs]
            o.vs[:, split(a)] = o.dkv[a, :, hs:]

    def pair_stack(block):
        return jnp.concatenate([block * lo, block * hi], axis=0)

    def pair_pick(stacked):
        return jnp.where(lane < 64, stacked[:qb_rows], stacked[qb_rows:])

    def attn_fwd(q_ref, mix_ref, mem, own, causal, hooks=()):
        @pl.loop(0, n_blk)
        def _(b):
            for i, hook in enumerate(hooks):
                pl.when(b == i)(hook)
            rows = pl.ds(pl.multiple_of(b * qb_rows, 16), qb_rows)
            wrows = pl.ds(pl.multiple_of(b * qb_rows, 16), win_w)
            sq = o.segq[rows, :]
            if mem:
                o.mm[...] = jnp.where(sq == o.srcseg[...], 0.0, NEG)
            if own:
                allowed = sq == o.segw[b]
                if causal:
                    qi = lax.broadcasted_iota(jnp.int32, (qb_rows, win_w), 0)
                    kj = lax.broadcasted_iota(jnp.int32, (qb_rows, win_w), 1)
                    allowed = allowed & (kj - HALO <= qi)
                o.mo[...] = jnp.where(allowed, 0.0, NEG)

            @pl.loop(0, n_pair)
            def _(j):
                cols = pl.ds(pl.multiple_of(j * 128, 128), 128)
                q2 = pair_stack(q_ref[rows, cols])
                parts = []
                if mem:
                    s = dot_nt(q2, o.ks[:, cols]).reshape(2, qb_rows, L)
                    parts.append(s + o.mm[...][None])
                if own:
                    s = dot_nt(q2, o.kp[wrows, cols]).reshape(2, qb_rows, win_w)
                    parts.append(s + o.tb[pl.ds(2 * j, 2)] + o.mo[...][None])
                top = [jnp.max(s, axis=-1, keepdims=True) for s in parts]
                top = functools.reduce(jnp.maximum, top)
                exps = [jnp.exp(s - top) for s in parts]
                total = sum(jnp.sum(e, axis=-1, keepdims=True) for e in exps)
                inv = 1.0 / total
                probs = [(e * inv).astype(BF).reshape(2 * qb_rows, -1) for e in exps]
                mixed = 0.0
                if mem:
                    o.pm[b * n_pair + j] = probs[0]
                    mixed = mixed + dot(probs[0], o.vs[:, cols])
                if own:
                    o.po[b * n_pair + j] = probs[-1]
                    mixed = mixed + dot(probs[-1], o.vp[wrows, cols])
                mix_ref[rows, cols] = pair_pick(mixed).astype(BF)

    def attn_back(q_ref, mix_ref, mem, own, hooks=()):
        if mem:
            o.dks[...] = jnp.zeros(o.dks.shape, F32)
            o.dvs[...] = jnp.zeros(o.dvs.shape, F32)
        if own:
            o.dkp[...] = jnp.zeros(o.dkp.shape, F32)
            o.dvp[...] = jnp.zeros(o.dvp.shape, F32)
            o.tb[...] = jnp.zeros(o.tb.shape, F32)

        @pl.loop(0, n_blk)
        def _(b):
            for i, hook in enumerate(hooks):
                pl.when(b == i)(hook)
            rows = pl.ds(pl.multiple_of(b * qb_rows, 16), qb_rows)
            wrows = pl.ds(pl.multiple_of(b * qb_rows, 16), win_w)

            @pl.loop(0, n_pair)
            def _(j):
                cols = pl.ds(pl.multiple_of(j * 128, 128), 128)
                q2 = pair_stack(q_ref[rows, cols])
                do2 = pair_stack(o.dmix[rows, cols])
                mix = mix_ref[rows, cols].astype(F32)
                delta = jnp.sum(
                    do2.astype(F32).reshape(2, qb_rows, 128) * mix[None], axis=-1, keepdims=True
                ).reshape(2 * qb_rows, 1)
                dq2 = 0.0
                if mem:
                    probs = o.pm[b * n_pair + j]
                    dp = dot_nt(do2, o.vs[:, cols])
                    ds = (probs.astype(F32) * (dp - delta)).astype(BF)
                    dq2 = dq2 + dot(ds, o.ks[:, cols])
                    o.dks[:, cols] += dot_tn(ds, q2)
                    o.dvs[:, cols] += dot_tn(probs, do2)
                if own:
                    probs = o.po[b * n_pair + j]
                    dp = dot_nt(do2, o.vp[wrows, cols])
                    ds = (probs.astype(F32) * (dp - delta)).astype(BF)
                    dq2 = dq2 + dot(ds, o.kp[wrows, cols])
                    o.dkp[wrows, cols] += dot_tn(ds, q2)
                    o.dvp[wrows, cols] += dot_tn(probs, do2)
                    o.tb[pl.ds(2 * j, 2)] += ds.astype(F32).reshape(2, qb_rows, win_w)
                o.dq[rows, cols] = (pair_pick(dq2) * (HD**-0.5)).astype(BF)

    def out_project(slot, mix_ref, weight_ref, at):
        exchange(
            slot,
            lambda rows: sum(
                dot_nt(mix_ref[rows, split(a)], weight_ref[a, :, at : at + hs]) for a in range(2)
            ),
        )

    def mix_grads(weight_ref, at):
        for a in range(2):
            o.dmix[:, split(a)] = dot(o.gb[...], weight_ref[a, :, at : at + hs]).astype(BF)

    fw = fs // 2

    def ff_half(n):
        a = n // 2
        return a, pl.ds(pl.multiple_of((n - 2 * a) * fw, 128), fw)

    def shard_cols(a):
        return slice(a * fs, (a + 1) * fs)

    def ff_fwd():
        ag_wait(B)

        @pl.loop(0, 4)
        def _(n):
            a, half_cols = ff_half(n)
            cols = pl.ds(pl.multiple_of(n * fw, 128), fw)
            o.pre[...] = dot(o.nc[...], W[B][a, :, half_cols])

            def one(rows):
                v = o.pre[rows, :]
                v2 = v * v
                th = jnp.tanh(0.7978845608028654 * v * (1.0 + 0.044715 * v2))
                cdf = 0.5 * (1.0 + th)
                slope = (0.5 * 0.7978845608028654) * v * (1.0 - th * th)
                o.hidden[rows, cols] = (v * cdf).astype(BF)
                o.gp[rows, cols] = (cdf + slope * (1.0 + (3 * 0.044715) * v2)).astype(BF)

            rows_loop(one, 32)

        ag_wait(C)
        when(dec, lambda: ag_also_hop(3))
        exchange(
            2,
            lambda rows: sum(dot_nt(o.hidden[rows, shard_cols(a)], W[C][a]) for a in range(2)),
        )

    def side_cols(a, width):
        return pl.ds(pl.multiple_of(a * width, 128), width)

    def ff_pre(n):
        a, half_cols = ff_half(n)
        cols = pl.ds(pl.multiple_of(n * fw, 128), fw)
        o.gp[:, cols] = (
            dot(o.gb[...], W[C][a, :, half_cols]) * o.gp[:, cols].astype(F32)
        ).astype(BF)

    def ff_out_weights():
        def one(a):
            W[C][a] = dot_tn(o.gb[...], o.hidden[:, side_cols(a, fs)]).astype(BF)

        side_first(one, RC)

    def ff_in_weights():
        def one(a):
            W[B][a] = dot_tn(o.nc[...], o.gp[:, side_cols(a, fs)]).astype(BF)

        side_first(one, RB)

    def ff_back():
        ag_finish(B)
        ag_finish(C)
        if nz > 1:
            when(dec, ag_also_sent)

        @pl.loop(0, 4)
        def _(n):
            ff_pre(n)

        exchange(
            0, lambda rows: sum(dot_nt(o.gp[rows, shard_cols(a)], W[B][a]) for a in range(2))
        )
        ff_out_weights()

        def put(rows, dv):
            new = o.gres[rows, :] + dv
            o.gres[rows, :] = new
            o.gb[rows, :] = new.astype(BF)

        norm_back(0, o.xlate, 1, put)

    n_tile = half // RT

    def x_copy(way, j):
        rows = tile_rows(core, j)
        return remote(
            o.xsend.at[rows], o.xbuf.at[rows], o.xss.at[way, 0, j], o.xrs.at[way, 0, j], across
        )

    def x_pass(way, h, j):
        rows = tile_rows(h, j)
        return remote(
            o.xbuf.at[rows], o.xbuf.at[rows], o.xss.at[way, 1, j], o.xrs.at[way, 1, j], sibling
        )

    def x_sent(way):
        @pl.loop(0, n_tile)
        def _(j):
            x_copy(way, j).wait_send()

    def x_halves(way, fn):
        def before(i, h, j):
            @pl.when(i == 0)
            def _():
                x_copy(way, j).wait_recv()
                x_pass(way, h, j).start()

            pl.when(i == 1)(lambda: x_pass(way, h, j).wait_recv())

        halves(fn, before=before)

        @pl.loop(0, n_tile)
        def _(j):
            x_pass(way, core, j).wait_send()

    def kv_weights():
        def one(a):
            W[A][a, :, at_kv:at_ext] = dot_tn(o.ns[...], o.dkv[a]).astype(BF)

        side_first(one, RK if nz == 1 else None)
        kv_start(0)
        kv_start(1)

    def dkv_grads():
        for a in range(2):
            o.dkv[a, :, :hs] = o.dks[:, split(a)].astype(BF)
            o.dkv[a, :, hs:] = o.dvs[:, split(a)].astype(BF)
        exchange(
            2,
            lambda rows: sum(
                dot_nt(o.dkv[a, rows, :], W[A][a, :, at_kv:at_ext]) for a in range(2)
            ),
        )

    when(enc, lambda: rows_pass(2))

    def first_cross():
        cross_own.wait()
        cross_in.wait_recv()
        ag_hop(X, 0)

    when(dec, first_cross)
    ag_hop(A, 1)
    ag_hop(C, 0, False)
    tiles_pass()
    if STAGE:
        when(dec, lambda: ag_pass_on(A))
    ag_side(C, 0)
    when(enc, pick_rows)
    ag_hop(A, 2)
    ag_hop(B, 1, False)
    when(enc, lambda: ag_side(B, 1))
    when(dec, lambda: ag_hop(X, 1))
    rows_pass(0)
    ag_hop(C, 1, False)
    if STAGE:
        when(dec, lambda: ag_pass_on(C))
    ag_hop(A, 3)
    ag_side(C, 1)
    ag_hop(B, 2, False)
    when(enc, lambda: ag_side(B, 2))
    when(dec, lambda: ag_hop(X, 2))
    rows_done(0)
    rows_join(0, o.x)

    @pl.when(dec)
    def _():
        ag_hop(X, 3)
        ag_side(B, 0)
        ag_side(B, 1)
        ag_side(B, 2)

    ag_wait(A)
    ag_hop(C, 2)
    tiles_done()
    for a in range(2):
        rel_lines = dot(o.rl[a].astype(BF), o.hot[...])
        for h in range(n_rel):
            o.tb[a * n_rel + h] = pltpu.roll(
                jnp.broadcast_to(rel_lines[h : h + 1, :], (qb_rows, win_w)),
                0,
                1,
                stride=1,
                stride_axis=0,
            )
    pad = jnp.zeros((HALO, hc), BF)
    for ref in (o.kp, o.vp):
        ref[:HALO, :] = pad
        ref[HALO + L :, :] = pad
    norm_rows(o.x, 0, o.na)

    def project_own(a):
        o.dqkv[a] = dot(o.na[...], W[A][a, :, :at_o]).astype(BF)

    both_shards(project_own)
    for a in range(2):
        o.q[:, split(a)] = (o.dqkv[a, :, :hs] * (HD**-0.5)).astype(BF)
        o.kp[HALO : HALO + L, split(a)] = o.dqkv[a, :, hs : 2 * hs]
        o.vp[HALO : HALO + L, split(a)] = o.dqkv[a, :, 2 * hs :]
    hooks = (lambda: ag_hop(B, 3), lambda: ag_hop(C, 3))

    @pl.when(enc)
    def _():
        norm_rows(o.nb, 2, o.ns)
        kv_project()
        attn_fwd(o.q, o.mixa, True, True, False, hooks)

    @pl.when(dec)
    def _():
        ag_also_hop(0)
        attn_fwd(o.q, o.mixa, False, True, True, hooks)

    out_project(0, o.mixa, W[A], at_o)
    when(dec, lambda: rows_start(1))

    @pl.when(enc)
    def _():
        residual(0, o.x, keep(o.xlate, 1, o.nc))

    @pl.when(dec)
    def _():
        ag_wait(X)
        ag_finish(X)
        if STAGE:
            ag_relay(A).wait_send()
            ag_relay(C).wait_send()

        def whole(a):
            for k in range(nz):
                for part in range(2):
                    at = part * (D // 2) + k * cross_rows
                    start = k * chunk_rows + part * cross_rows
                    o.xg[a, at : at + cross_rows, :] = W[X][a, start : start + cross_rows, :]

        both_shards(whole)
        residual(0, o.x, keep(o.xmid, 3, o.nb))
        for a in range(2):
            r = dot(o.nb[...], o.xg[a, :, :hs]).astype(BF)
            o.qb[:, split(a)] = (r * (HD**-0.5)).astype(BF)

        def one(rows):
            o.ns[rows, :] = normed(o.xbuf[rows, :].astype(F32), 2)

        ag_also_hop(1)
        x_halves(0, one)
        kv_project()
        attn_fwd(o.qb, o.mixb, True, False, False)
        ag_also_hop(2)
        out_project(1, o.mixb, o.xg, hs)
        residual(1, o.xmid, keep(o.xlate, 1, o.nc))


    ff_fwd()

    def put_out(rows, value):
        o.gres[rows, :] = value
        o.xsend[rows, :] = value.astype(BF)

    residual(2, o.xlate, put_out, lambda j: pl.when(enc)(lambda: x_copy(0, j).start()))
    when(enc, lambda: rows_start(1))
    home_send(0, o.gres)
    o.ho[...] = home_block(o.gres, t)
    home_out[0].start()
    ag_finish(A)
    rows_pass(1)
    rows_done(1)
    rows_join(1, o.gres)

    @pl.when(enc)
    def _():
        o.dgacc[3] = jnp.zeros((8, D), F32)
        x_sent(0)

        def one(rows):
            value = o.gres[rows, :] + o.xbuf[rows, :].astype(F32)
            o.gres[rows, :] = value
            o.gb[rows, :] = value.astype(BF)

        x_halves(1, one)

    when(dec, lambda: rows_join(1, o.gb))


    ff_back()

    @pl.when(dec)
    def _():
        mix_grads(o.xg, hs)
        attn_back(o.qb, o.mixb, True, False)
        dkv_grads()
        exchange(
            1, lambda rows: sum(dot_nt(o.dq[rows, split(a)], o.xg[a, :, :hs]) for a in range(2))
        )

        def put_source(rows, dv):
            o.xsend[rows, :] = dv.astype(BF)

        norm_back(2, o.xbuf, 2, put_source, lambda j: x_copy(1, j).start())
        rs_mid(RC, 0, 2)

        def put_mid(rows, dv):
            new = o.gres[rows, :] + dv
            o.gres[rows, :] = new
            o.xbuf[rows, :] = new.astype(BF)

        norm_back(1, o.xmid, 3, put_mid)
        for a in range(2):
            o.dqkv[a, :, :hs] = o.dq[:, split(a)]
            o.dqkv[a, :, hs : 2 * hs] = o.mixb[:, split(a)]

        def cross_weights(a):
            full = jnp.concatenate(
                [
                    dot_tn(o.nb[...], o.dqkv[a, :, :hs]).astype(BF),
                    dot_tn(o.gb[...], o.dqkv[a, :, hs : 2 * hs]).astype(BF),
                ],
                axis=1,
            )
            for k in range(nz):
                for part in range(2):
                    at = part * (D // 2) + k * cross_rows
                    to = k * chunk_rows + part * cross_rows
                    W[X][a, to : to + cross_rows, :] = full[at : at + cross_rows]

        both_shards(cross_weights)
        rs_start(RX)
        x_sent(1)
        o.gb[...] = o.xbuf[...]

    ff_in_weights()
    mix_grads(W[A], at_o)
    for a in range(2):
        W[A][a, :, at_o : at_o + hs] = dot_tn(o.gb[...], o.mixa[:, split(a)]).astype(BF)
    steps = tuple(functools.partial(rs_mid, RC, i, i + 1) for i in range(3))

    @pl.when(enc)
    def _():
        attn_back(o.q, o.mixa, True, True, steps)
        dkv_grads()

    @pl.when(dec)
    def _():
        attn_back(o.q, o.mixa, False, True)
        rs_mid(RC, 2, 3)

    kv_weights()
    rs_mid(RC, 3)
    for a in range(2):
        o.dqkv[a, :, :hs] = o.dq[:, split(a)]
        o.dqkv[a, :, hs : 2 * hs] = o.dkp[HALO : HALO + L, split(a)].astype(BF)
        o.dqkv[a, :, 2 * hs :] = o.dvp[HALO : HALO + L, split(a)].astype(BF)
    last_slot = 1 - p
    exchange(
        last_slot,
        lambda rows: sum(dot_nt(o.dqkv[a, rows, :], W[A][a, :, :at_o]) for a in range(2)),
    )

    @pl.when(enc)
    def _():
        def put_source(rows, dv):
            pass

        norm_back(2, o.nb, 2, put_source)

    heads = 2 * n_pair
    acc = jnp.zeros((heads * 8, win_w), F32)
    for k in range(qb_rows // 8):
        part = o.tb[:, 8 * k : 8 * k + 8, :].reshape(heads * 8, win_w)
        acc = acc + (part if k == 0 else pltpu.roll(part, win_w - 8 * k, 1))
    sub = lax.rem(lax.broadcasted_iota(jnp.int32, (heads * 8, win_w), 0), 8)
    diag = jnp.zeros((heads * 8, win_w), F32)
    for k in range(8):
        turned = acc if k == 0 else pltpu.roll(acc, win_w - k, 1)
        diag = diag + jnp.where(sub == k, turned, 0.0)
    lines = jnp.sum(diag.reshape(heads, 8, win_w), axis=1)

    def put_in(rows, dv):
        o.gres[rows, :] = o.gres[rows, :] + dv

    norm_back(last_slot, o.x, 0, put_in)
    home_send(1, o.gres)
    home_out[2].start()
    sums_start(lines)

    def own_weights(a):
        W[A][a, :, :at_o] = dot_tn(o.na[...], o.dqkv[a]).astype(BF)

    side_first(own_weights, RQ)

    home_copy(0).wait()
    home_out[1].start()
    rs_mid(RB, 0, 2)
    kv_mid()
    rs_mid(RB, 2)
    rs_out(RC)
    kv_cross()
    sums_mid()
    when(dec, lambda: rs_mid(RX))
    rs_mid(RQ, 0, 2)
    rs_out(RB)
    sums_end()
    rs_mid(RQ, 2)
    kv_out()

    @pl.when(dec)
    def _():
        def put(rows, total):
            o.xt[rows, :] = total

        rs_end(RX, put)
        rs_sent(RX)
        o.xo[...] = o.xt[:cross_rows, :]
        cross_out.start()
        o.ox[...] = o.xt[cross_rows:, :].astype(o.ox.dtype)
        cross_out.wait_send()

    @pl.when(enc)
    def _():
        cross_in.wait_send()
        cross_out.wait_recv()
        o.ox[...] = o.xi[...].astype(o.ox.dtype)

    home_copy(1).wait()
    o.ext[...] = o.hr[1].astype(F32)
    home_out[3].start()
    rs_out(RQ)
    for copy in home_out:
        copy.wait()
    if nz > 1:
        for r in LEAVE:
            rs_leave(r).wait()


def run_kernel(dims, given):
    L, D, hs, fs, nz, qb_rows, win_w = dims
    hc, fc = 2 * hs, 2 * fs
    n_blk, n_pair = L // qb_rows, hc // 128
    LP = L + 2 * HALO
    LBP = -(-(L // 4) // 16) * 16
    CR = D // nz
    widths = dict(a=6 * hs, b=fs, c=fs, x=2 * hs)
    MW = -(-CR // 128) * 128
    S = jax.ShapeDtypeStruct
    SUM = F32 if nz > 1 else BF
    outs = dict(
        oh=S((2, LBP, D), BF),
        gh=S((2, L // 4, D), F32),
        oa=S((CR, widths["a"]), SUM),
        ob=S((CR, widths["b"]), SUM),
        oc=S((CR, widths["c"]), SUM),
        ox=S((CR // 2, widths["x"]), SUM),
        om=S((TILE, MW), F32),
    )
    V = pltpu.VMEM
    LD, LH, LF = (L, D), (L, hc), (L, fc)
    scratch = dict(
        na=V(LD, BF), ns=V(LD, BF), nb=V(LD, BF), nc=V(LD, BF),
        xmid=V(LD, F32), xlate=V(LD, F32), gres=V(LD, F32),
        q=V(LH, BF), kp=V((LP, hc), BF), vp=V((LP, hc), BF), ks=V(LH, BF), vs=V(LH, BF),
        qb=V(LH, BF), mixa=V(LH, BF), mixb=V(LH, BF),
        pm=V((n_blk * n_pair, 2 * qb_rows, L), BF), po=V((n_blk * n_pair, 2 * qb_rows, win_w), BF),
        hidden=V(LF, BF), gp=V(LF, BF), pre=V((L, fs // 2), F32),
        tb=V((2 * n_pair, qb_rows, win_w), F32),
        mm=V((qb_rows, L), F32), mo=V((qb_rows, win_w), F32),
        dmix=V(LH, BF), dq=V(LH, BF), dqkv=V((2, L, 3 * hs), BF), dkv=V((2, L, 2 * hs), BF),
        dkp=V((LP, hc), F32), dvp=V((LP, hc), F32), dks=V(LH, F32), dvs=V(LH, F32),
        gb=V(LD, BF), xbuf=V(LD, BF), xsend=V(LD, BF),
        exs=V((3, L, D), BF), exr=V((3, L, D), BF), dgacc=V((4, 8, D), F32),
        g=V((8, D), F32), ext=V((LBP, D), F32), lines=V((TILE, win_w), F32),
        m=V((3, nz, TILE, MW), BF), ms1=V((2, nz, TILE, MW), BF), ms2=V((nz, TILE, MW), BF),
        ms3=V((max(nz - 1, 1), TILE, MW), BF), mf=V((TILE, MW), F32), mo1=V((TILE, MW), F32),
        mo2=V((TILE, MW), F32), dgl=V((8, D), F32), rl=V((2, TILE, 128), F32),
        idr=V((1, L), jnp.int32),
        x=V(LD, BF), xq=V((4, LBP, D), BF), cq=V((4, LBP, D), BF), mq=V((4, 8, 128), jnp.int32),
        hs=V((2, LBP, D), BF), hr=V((2, LBP, D), BF), ho=V((LBP, D), BF),
        xg=V((2, D, widths["x"]), BF), xt=V((CR, widths["x"]), F32),
        xo=V((CR // 2, widths["x"]), F32), xi=V((CR // 2, widths["x"]), F32),
    )
    for g, width in widths.items():
        scratch["w" + g] = V((2, D, width), BF)
        scratch["y" + g] = V((D, width), BF)
        scratch["z" + g] = V((nz - 1, CR, width) if nz > 1 else (1, 16, width), BF)
    sem = pltpu.SemaphoreType.DMA
    scratch.update(ss=sem((3, 2)), rs=sem((3, 2)), gd=sem((3, 3)), ga=sem((2, nz)), gb2=sem((nz,)), mt=sem((8, nz)), mx=sem((6,)), tg=sem((2,)), xss=sem((2, 2, L // 2 // RT)), xrs=sem((2, 2, L // 2 // RT)))
    scratch.update(xw=sem((4,)), oc_sem=sem((4,)), kq=sem((4, nz)), lc=sem((6,)), lh=sem((4,)))
    scratch.update(qs=sem((3, 3)), qr=sem((3, 3)), ql=sem((3,)), hx=sem((2,)), hy=sem((2,)))
    for name in ("gr", "gl", "gs", "gz", "gy"):
        scratch[name] = sem((4, nz))
    for name in ("rs_s", "rs_r", "rz_s", "rz_r"):
        scratch[name] = sem((6, nz))
    spec = pl.BlockSpec(memory_space=pltpu.VMEM)
    far = pl.BlockSpec(memory_space=pl.ANY)
    names = list(given) + list(outs) + list(scratch)
    FAR = ["sa", "sb", "sc", "sx", "xs", "cs", "ms", "table", "oh", "gh"]
    if nz > 1:
        FAR += ["oa", "ob", "oc"]
    return pl.pallas_call(
        functools.partial(kernel, dims, names),
        out_shape=list(outs.values()),
        in_specs=[far if name in FAR else spec for name in given],
        out_specs=[far if name in FAR else spec for name in outs],
        scratch_shapes=list(scratch.values()),
        compiler_params=pltpu.CompilerParams(
            collective_id=0, has_side_effects=True, vmem_limit_bytes=63 << 20
        ),
        name="layers",
    )(*given.values())


def prep_kernel(dims, n_dp, names, *refs):
    L, D, hs, fs, nz, qb_rows, win_w = dims
    o = Refs()
    for name, ref in zip(names, refs, strict=True):
        setattr(o, name, ref)
    section = lax.axis_index("pipe")
    y = lax.axis_index("tensor") // 2
    rows = D // n_dp
    held = L // 4
    for raw, out in ((o.li, o.xs), (o.co, o.cs)):
        o.tmp[...] = raw[...].astype(F32)
        pad = jnp.zeros((out.shape[1] - held, D), F32)
        for r in range(2):
            out[r] = jnp.concatenate([o.tmp[:, r, :], pad], axis=0).astype(BF)
    for i in range(3):
        o.sa[:, i * hs : (i + 1) * hs] = o.qkv[i]
    o.sa[:, 3 * hs : 4 * hs] = o.so[...].astype(F32).T.astype(BF)
    for i in range(2):
        o.kvt[...] = o.kv[...].astype(F32)
        o.sa[:, (4 + i) * hs : (5 + i) * hs] = o.kvt[:, i, :].astype(BF)
    n_gain = o.gain.shape[0]
    heads = o.rel.shape[0]
    o.mf[...] = jnp.zeros(o.mf.shape, F32)
    o.mf[:n_gain, : o.gain.shape[1]] = o.gain[...].astype(F32)
    o.mf[CROSS_AT : CROSS_AT + 1, : o.cg.shape[1]] = o.cg[...].astype(F32)
    o.mf[REL_AT : REL_AT + heads, : o.rel.shape[1]] = o.rel[...].astype(F32)
    o.sm[...] = o.mf[...].astype(BF)
    o.sx[:, :hs] = o.cq[...]
    o.sx[:, hs : 2 * hs] = o.cw[...].astype(F32).T.astype(BF)
    o.ms[...] = jnp.zeros(o.ms.shape, jnp.int32)
    for r in range(2):
        o.ms[r, 0:1, :held] = o.ids[r : r + 1, :]
    own = o.seg[section, pl.ds(y, 1), :]
    first = o.seg[0, pl.ds(y, 1), :]
    o.segq[...] = jnp.broadcast_to(own.astype(F32), (8, L)).T[:, :1].astype(jnp.int32)
    slots = lax.broadcasted_iota(jnp.int32, (1, L), 1).astype(F32)
    slots = jnp.floor((slots + 0.5) * (1.0 / MEM)).astype(jnp.int32)
    o.srcseg[...] = jnp.where(section == 0, slots, first)
    o.line[...] = jnp.full(o.line.shape, -1, jnp.int32)
    o.line[:, HALO : HALO + L] = own
    for b in range(L // qb_rows):
        o.segw[b] = o.line[:, b * qb_rows : b * qb_rows + win_w]
    o.win[...] = jnp.full(o.win.shape, -1, jnp.int32)
    o.win[:, : 2 * HALO] = o.buckets[:, L - HALO : L + HALO]
    at = lax.broadcasted_iota(jnp.int32, (128, win_w), 0)
    o.hot[...] = jnp.where(at == o.win[...], 1.0, 0.0).astype(BF)


def run_prep(dims, n_dp, given):
    L, D, hs, fs, nz, qb_rows, win_w = dims
    rows, held = D // n_dp, L // 4
    MW = -(-(D // nz) // 128) * 128
    LBP = -(-held // 16) * 16
    S = jax.ShapeDtypeStruct
    outs = dict(
        xs=S((2, LBP, D), BF),
        cs=S((2, LBP, D), BF),
        sa=S((rows, 6 * hs), BF),
        sx=S((rows // 2, 2 * hs), BF),
        sm=S((TILE, MW), BF),
        ms=S((2, 8, 128), jnp.int32),
        segq=S((L, 1), jnp.int32),
        segw=S((L // qb_rows, 1, win_w), jnp.int32),
        srcseg=S((1, L), jnp.int32),
        hot=S((128, win_w), BF),
    )
    V = pltpu.VMEM
    scratch = dict(
        tmp=V((held, 2, D), F32),
        kvt=V((rows, 2, hs), F32),
        mf=V((TILE, MW), F32),
        line=V((1, L + 2 * HALO), jnp.int32),
        win=V((1, win_w), jnp.int32),
    )
    spec = pl.BlockSpec(memory_space=pltpu.VMEM)
    names = list(given) + list(outs) + list(scratch)
    return pl.pallas_call(
        functools.partial(prep_kernel, dims, n_dp, names),
        out_shape=list(outs.values()),
        in_specs=[spec] * len(given),
        out_specs=[spec] * len(outs),
        scratch_shapes=list(scratch.values()),
        compiler_params=pltpu.CompilerParams(vmem_limit_bytes=60 << 20),
        name="prep",
    )(*given.values())


def finish_kernel(dims, names, *refs):
    L, D, hs, fs, nz, qb_rows, win_w = dims
    o = Refs()
    for name, ref in zip(names, refs, strict=True):
        setattr(o, name, ref)
    o.ffi[...] = o.gb[...]
    o.ffo[...] = o.gc[...]
    for r in range(2):
        o.gin[:, r, :] = o.gh[r]
        o.tmp[:, r, :] = o.oh[r, : L // 4].astype(F32)
    o.out[...] = o.tmp[...].astype(BF)
    for i in range(3):
        o.qkv[i] = o.ga[:, i * hs : (i + 1) * hs]
    o.so[...] = o.ga[:, 3 * hs : 4 * hs].T
    for i in range(2):
        o.kv[:, i, :] = o.ga[:, (4 + i) * hs : (5 + i) * hs]
    rows = o.ga.shape[0]
    for i in range(o.gain.shape[0]):
        o.gain[i] = o.gm[i : i + 1, :rows]
    heads, _, nb_rows = o.rel.shape
    for i in range(heads):
        o.rel[i] = o.gm[REL_AT + i : REL_AT + i + 1, :nb_rows]
    o.cq[...] = o.gx[:, :hs]
    o.co[...] = o.gx[:, hs : 2 * hs].T
    o.cg[...] = o.gm[CROSS_AT : CROSS_AT + 1, : rows // 2]


def run_finish(dims, rel_shape, sums):
    L, D, hs, fs, nz, qb_rows, win_w = dims
    rows = sums[2].shape[0]
    held = L // 4
    S = jax.ShapeDtypeStruct
    outs = dict(
        out=S((held, 2, D), BF),
        gin=S((held, 2, D), F32),
        qkv=S((3, rows, hs), F32),
        so=S((hs, rows), F32),
        kv=S((rows, 2, hs), F32),
        rel=S((rel_shape[1], 1, rel_shape[0]), F32),
        gain=S((3, 1, rows), F32),
        cq=S((rows // 2, hs), F32),
        co=S((hs, rows // 2), F32),
        cg=S((1, rows // 2), F32),
        ffi=S((rows, fs), F32),
        ffo=S((rows, fs), F32),
    )
    spec = pl.BlockSpec(memory_space=pltpu.VMEM)
    return pl.pallas_call(
        functools.partial(
            finish_kernel, dims, ["oh", "gh", "ga", "gb", "gc", "gx", "gm", *outs, "tmp"]
        ),
        out_shape=list(outs.values()),
        in_specs=[spec] * 7,
        out_specs=[spec] * len(outs),
        scratch_shapes=[pltpu.VMEM((held, 2, D), F32)],
        compiler_params=pltpu.CompilerParams(vmem_limit_bytes=60 << 20),
        name="finish",
    )(*sums)


def body(
    layer_inputs,
    segment_ids,
    slot_ids,
    memory_table,
    buckets,
    self_qkv,
    self_out,
    source_kv,
    ff_in,
    ff_out,
    rel_bias,
    gains,
    cross_query,
    cross_out,
    cross_gain,
    cotangents,
):
    nt = lax.axis_size("tensor")
    n_dp = lax.axis_size("dp")
    assert nt == 4 and layer_inputs.shape[2] == 2
    D = layer_inputs.shape[3]
    L = segment_ids.shape[2]
    hs = self_qkv.shape[3]
    fs = ff_in.shape[2]
    qb_rows, win_w = 160, 256
    rows = D // n_dp
    nz = 4 if n_dp == 4 and (rows // 2) % 32 == 0 else 1
    dims = (L, D, hs, fs, nz, qb_rows, win_w)
    held = L // nt
    gain, rel, cross_g = gains[0], rel_bias[0].T, cross_gain[None]
    if nz != n_dp:
        gain = lax.all_gather(gain, "dp", axis=1, tiled=True)
        rel = lax.all_gather(rel, "dp", axis=1, tiled=True)
        cross_g = lax.all_gather(cross_g, "dp", axis=1, tiled=True)
    prepared = run_prep(
        dims,
        n_dp,
        dict(
            li=layer_inputs[0],
            co=cotangents[0],
            qkv=self_qkv[0].transpose(1, 0, 2),
            so=self_out[0],
            kv=source_kv[0],
            gain=gain,
            rel=rel,
            cq=cross_query,
            cw=cross_out,
            cg=cross_g,
            seg=segment_ids,
            ids=slot_ids.T,
            buckets=buckets[None],
        ),
    )
    xs, cs, sa, sx, sm, ms, segq, segw, srcseg, hot = prepared
    shards = [sa, ff_in[0], ff_out[0].T, sx]
    if nz != n_dp:
        shards = [lax.all_gather(shard, "dp", axis=0, tiled=True) for shard in shards]
    given = dict(
        xs=xs, cs=cs, ms=ms, table=memory_table, sm=sm, segq=segq, segw=segw, srcseg=srcseg, hot=hot,
        sa=shards[0], sb=shards[1], sc=shards[2], sx=shards[3],
    )
    oh, gh, *sums, gm = run_kernel(dims, given)
    if nz != n_dp:
        sums = [
            lax.psum_scatter(full, "dp", scatter_dimension=0, tiled=True).astype(F32)
            for full in sums
        ]

        def share(first, count, width):
            mine = lax.psum_scatter(
                gm[first : first + count, :width], "dp", scatter_dimension=1, tiled=True
            )
            below = TILE - first - count
            return jnp.pad(mine, ((first, below), (0, 128 - mine.shape[1])))

        gm = (
            share(0, CROSS_AT, D)
            + share(CROSS_AT, 1, D // 2)
            + share(REL_AT, rel_bias.shape[2], NB)
        )
    done = run_finish(dims, rel_bias.shape[1:], [oh, gh, *sums, gm])
    out, gin, qkv, so, kv, rel, gain, cq, co, cg, ff_i, ff_o = done
    return (
        out[None],
        gin[None],
        qkv.transpose(1, 0, 2)[None],
        so[None],
        kv[None],
        ff_i[None],
        ff_o.T[None],
        rel.transpose(1, 2, 0),
        gain.transpose(1, 0, 2),
        cq,
        co,
        cg[0],
    )


def solution(mesh):
    placed = (
        P("pipe", "tensor", "dp", None),
        P(None, "dp", None),
        P("tensor", "dp"),
        P(),
        P(),
        P("pipe", "dp", None, "tensor"),
        P("pipe", "tensor", "dp"),
        P("pipe", "dp", None, "tensor"),
        P("pipe", "dp", "tensor"),
        P("pipe", "tensor", "dp"),
        P("pipe", "dp", "tensor"),
        P("pipe", None, "dp"),
        P(("pipe", "dp"), "tensor"),
        P("tensor", ("pipe", "dp")),
        P(("pipe", "dp")),
        P("pipe", "tensor", "dp", None),
    )
    return jax.shard_map(
        body,
        mesh=mesh,
        in_specs=placed,
        out_specs=(
            P("pipe", "tensor", "dp", None),
            P("pipe", "tensor", "dp", None),
            P("pipe", "dp", None, "tensor"),
            P("pipe", "tensor", "dp"),
            P("pipe", "dp", None, "tensor"),
            P("pipe", "dp", "tensor"),
            P("pipe", "tensor", "dp"),
            P("pipe", "dp", "tensor"),
            P("pipe", None, "dp"),
            P(("pipe", "dp"), "tensor"),
            P("tensor", ("pipe", "dp")),
            P(("pipe", "dp")),
        ),
        check_vma=False,
    )
```
